32 devices in a mesh: snap: 2 (over y), curve: 4 (over z), chan: 2 (over x), rep: 2 (over core).
Axes of the slice: x: 2, y: 2, z: 4, core: 2. Of those that a mesh axis runs over, the one named last changes fastest.
Arguments:
- children: bfloat16 [8, 128, 12288], P(None, None, ('snap', 'curve', 'rep')), parts along dimension 2, may hold values from -6 to 6
- child_mask: int32 [8, 12288], P(None, ('snap', 'curve', 'rep')), parts along dimension 1, may hold values from 0 to 1, as said below
- neighbours: int32 [27, 12288], P(None, ('snap', 'curve', 'rep')), parts along dimension 1, may hold values from -1 to 6143, as said below
- down_weight: bfloat16 [8, 256, 128], P(None, 'chan'), may hold values from -0.25 to 0.25
- conv_weight: bfloat16 [27, 256, 256], P(None, 'chan'), may hold values from -0.125 to 0.125
- cotangent: bfloat16 [256, 12288], P('chan', ('snap', 'curve', 'rep')), parts along dimension 1, may hold values from -6 to 6
Outputs:
- features_out: bfloat16 [256, 12288], P('chan', ('snap', 'curve', 'rep')), parts along dimension 1
- children_grad: bfloat16 [8, 128, 12288], P(None, 'chan', ('snap', 'curve', 'rep')), parts along dimension 2
- conv_weight_grad: float32 [54, 256, 256], P('snap', 'chan'), parts along dimension 0
- down_weight_grad: float32 [16, 256, 128], P('snap', 'chan'), parts along dimension 0
The draws below stay inside these ranges and needn't reach their ends.
There are 2 independent parts, one for each index of `snap`. The reference program is written for one: setup_inputs(seed, part) draws one part's arguments, and reference() takes and returns one part's arrays. A program takes and returns all parts, laid end to end along the dimension named above; an argument that names none is the same for every part. Nothing has to cross between parts.
Inputs may be any that keep to these rules, and one draw needn't show every extreme that they name: Entry k of site p names the slot of the site at offset (k // 9 - 1, k // 3 % 3 - 1, k % 3 - 1) cells from p, or -1 where that cell is empty; entry 13 of an occupied site is p itself; neighbours[26 - k, neighbours[k, p]] = p wherever neighbours[k, p] >= 0; a site in slots j * 768 to (j + 1) * 768 - 1 names only sites in slots (j - 1) * 768 to (j + 2) * 768 - 1; empty slots hold -1 in all 27 entries. `child_mask`: 1 where the child cell is occupied; every occupied coarse site has at least one occupied child, empty slots have none.
All inputs are finite; a program needn't handle non-finite values.
Results may differ from the reference program's by a relative error of at most 0.0067.
Values may be sent and summed in bfloat16 or wider, within the bound.
No kernel may reach another device: no remote copies, remote signals or barrier semaphores. Data moves between devices by JAX's collectives and lax.ppermute only.
A program may use at most 128 MiB of HBM per device.

```python
import jax
import jax.numpy as jnp
from jax import lax

C1 = 128
C2 = 256
SD2 = 768
SHARDS = 8
SITES = 6144
GROUP = 128
N_CHAN = 2


def slab_layout(key):
    base = jax.random.fold_in(key, 101)
    first, second, third = jax.random.split(base, 3)
    cells = 2 * SD2
    pieces = jnp.arange(SHARDS, dtype=jnp.int32)
    counts = jax.random.randint(first, (SHARDS,), SD2 // 2, SD2 + 1)
    fullest = jax.random.randint(second, (), 0, SHARDS)
    counts = jnp.where((pieces == fullest) | (pieces == SHARDS - 1), SD2, counts)
    scores = jax.random.randint(third, (SHARDS, cells), 0, 2 ** 19) * cells + jnp.arange(cells, dtype=jnp.int32)[None, :]
    ranking = jnp.argsort(jnp.argsort(scores, axis=1), axis=1)
    occupied = ranking < counts[:, None]
    slots = jnp.cumsum(occupied.astype(jnp.int32), axis=1) - 1
    table = jnp.where(occupied, pieces[:, None] * SD2 + slots, -1)
    cell_index = jnp.arange(cells, dtype=jnp.int32)[None, :]
    order = jnp.argsort(jnp.where(occupied, cell_index, cells + cell_index), axis=1)[:, :SD2].astype(jnp.int32)
    live = jnp.arange(SD2, dtype=jnp.int32)[None, :] < counts[:, None]
    return (table, order, live)


def draw_neighbours(key, part):
    table, order, live = slab_layout(key)
    rows = SD2 // 16
    plane = order // (rows * 16)
    across = order // 16 % rows
    depth = order % 16
    global_x = jnp.arange(SHARDS, dtype=jnp.int32)[:, None] * 2 + plane
    result = []
    for offset in range(27):
        step_x = offset // 9 - 1
        step_y = offset // 3 % 3 - 1
        step_z = offset % 3 - 1
        near_x = global_x + step_x
        near_y = across + step_y
        near_z = depth + step_z
        inside = (near_x >= 0) & (near_x < 2 * SHARDS) & (near_y >= 0) & (near_y < rows) & (near_z >= 0) & (near_z < 16)
        owner = jnp.clip(near_x // 2, 0, SHARDS - 1)
        cell = (jnp.clip(near_x, 0, 2 * SHARDS - 1) % 2 * rows + jnp.clip(near_y, 0, rows - 1)) * 16 + jnp.clip(near_z, 0, 15)
        found = table[owner, cell]
        result.append(jnp.where(inside & live, found, -1).reshape(SITES))
    return jnp.stack(result).astype(jnp.int32)


def draw_child_mask(key, part):
    table, order, live = slab_layout(key)
    key = jax.random.fold_in(key, 11)
    first, second = jax.random.split(key)
    bits = jax.random.randint(first, (8, SHARDS, SD2), 0, 20) < 11
    forced = jax.random.randint(second, (SHARDS, SD2), 0, 8)
    marked = bits | (jnp.arange(8, dtype=jnp.int32)[:, None, None] == forced[None, :, :])
    marked = marked & live[None, :, :]
    return marked.astype(jnp.int32).reshape(8, SITES)


def steps_of(key, dims, cuts, least, high):
    level, own = 1.0, jax.random.fold_in(key, 6)
    for axis_at, shards_of in cuts:
        steps = jnp.exp(jax.random.uniform(jax.random.fold_in(own, axis_at), (shards_of,), jnp.float32, least / len(cuts), high / len(cuts)))
        level = level * jnp.repeat(steps, dims[axis_at] // shards_of).reshape([-1 if axis == axis_at else 1 for axis in range(len(dims))])
    return level


def gaussian(key, extent, deviation, most, cuts=(), kind=jnp.bfloat16):
    values = deviation * jax.random.normal(key, extent, jnp.float32)
    if cuts:
        values = values * steps_of(key, extent, cuts, -0.22, 0.18)
    return jnp.clip(values, -most, most).astype(kind)


def setup_inputs(seed: int = 0, part: int = 0) -> dict:
    streams_of = jax.random.split(jax.random.key(seed), 7)
    part_keys = jax.random.split(jax.random.fold_in(streams_of[6], part), 7)
    children = gaussian(part_keys[0], (8, C1, SITES), 1.0, 6.0, ((2, 8),))
    child_mask = draw_child_mask(jax.random.fold_in(jax.random.fold_in(streams_of[6], part), 71), part)
    neighbours = draw_neighbours(jax.random.fold_in(jax.random.fold_in(streams_of[6], part), 71), part)
    down_weight = gaussian(streams_of[3], (8, C2, C1), (4 * C1) ** -0.5, 0.25, ((1, 2),))
    conv_weight = gaussian(streams_of[4], (27, C2, C2), (8 * C2) ** -0.5, 0.125, ((1, 2),))
    cotangent = gaussian(part_keys[5], (C2, SITES), 1.0, 6.0, ((0, 2), (1, 8)))
    return {"children": children, "child_mask": child_mask, "neighbours": neighbours, "down_weight": down_weight, "conv_weight": conv_weight, "cotangent": cotangent}


def silu_slope(value):
    sigma = jax.nn.sigmoid(value)
    return sigma * (1.0 + value * (1.0 - sigma))


def pick_columns(field, columns):
    picked = jnp.take(field, jnp.maximum(columns, 0), axis=1)
    return jnp.where(columns[None, :] >= 0, picked, jnp.zeros_like(picked))


def reference(children, child_mask, neighbours, down_weight, conv_weight, cotangent):
    masked = children * child_mask[:, None, :].astype(children.dtype)
    pre = jnp.einsum("oci,oip->cp", down_weight.astype(jnp.float32), masked.astype(jnp.float32))
    coarse = jax.nn.silu(pre).astype(jnp.bfloat16)
    conv = jnp.zeros((C2, SITES), jnp.float32)
    for offset in range(27):
        conv = conv + jnp.dot(conv_weight[offset], pick_columns(coarse, neighbours[offset]), preferred_element_type=jnp.float32)
    features_out = jax.nn.silu(conv).astype(jnp.bfloat16)
    conv_grad = (cotangent.astype(jnp.float32) * silu_slope(conv)).astype(jnp.bfloat16)
    scale = 1.0 / (SITES ** 0.5)
    weight_rows = []
    coarse_grad = jnp.zeros((C2, SITES), jnp.float32)
    for offset in range(27):
        picked = pick_columns(coarse, neighbours[offset])
        weight_rows.append(jnp.dot(conv_grad, picked.T, preferred_element_type=jnp.float32) * scale)
        term = jnp.dot(conv_weight[offset].T, conv_grad, preferred_element_type=jnp.float32)
        valid = neighbours[offset] >= 0
        term = jnp.where(valid[None, :], term, jnp.zeros_like(term))
        coarse_grad = coarse_grad.at[:, jnp.maximum(neighbours[offset], 0)].add(term)
    conv_weight_grad = jnp.stack(weight_rows)
    pre_grad = (coarse_grad * silu_slope(pre)).astype(jnp.bfloat16)
    down_weight_grad = jnp.einsum("cp,oip->oci", pre_grad.astype(jnp.float32), masked.astype(jnp.float32)) * scale
    child_sum = jnp.zeros((8, C1, SITES), jnp.float32)
    for block in range(N_CHAN):
        weights = down_weight[:, block * GROUP:(block + 1) * GROUP, :].astype(jnp.float32)
        grads = pre_grad[block * GROUP:(block + 1) * GROUP, :].astype(jnp.float32)
        partial_sum = jnp.einsum("oci,cp->oip", weights, grads)
        child_sum = child_sum + lax.optimization_barrier(partial_sum.astype(jnp.bfloat16)).astype(jnp.float32)
    children_grad = (child_sum * child_mask[:, None, :].astype(jnp.float32)).astype(jnp.bfloat16)
    return features_out, children_grad, conv_weight_grad, down_weight_grad
```

```python
import functools

import jax
import jax.numpy as jnp
from jax import lax
from jax.experimental import pallas as pl
from jax.experimental.pallas import tpu as pltpu
from jax.sharding import PartitionSpec as P

BLOCK = 128
SPAN = 256
GROUPS = 3
PER = 9
VMEM_LIMIT = 56 * 1024 * 1024
PIECES = ("curve", "rep")
F32 = jnp.float32
BF16 = jnp.bfloat16
NT = (((1,), (1,)), ((), ()))


def silu_slope(value):
    sigma = jax.nn.sigmoid(value)
    return sigma * (1.0 + value * (1.0 - sigma))


def passed_along(shard, axis, by):
    devices = lax.axis_size(axis)
    pairs = [(i, i + by) for i in range(devices) if 0 <= i + by < devices]
    return lax.ppermute(shard, axis, pairs)


def swapped(shard, axis):
    return lax.ppermute(shard, axis, [(0, 1), (1, 0)])


def call(kernel, out_shape, specs, scratch, flops, bytes_accessed):
    return pl.pallas_call(
        kernel,
        out_shape=out_shape,
        in_specs=specs,
        scratch_shapes=scratch,
        compiler_params=pltpu.CompilerParams(vmem_limit_bytes=VMEM_LIMIT),
        cost_estimate=pl.CostEstimate(
            flops=flops, bytes_accessed=bytes_accessed, transcendentals=0
        ),
    )


def vmem(count):
    return [pl.BlockSpec(memory_space=pltpu.VMEM)] * count


SMEM = [pl.BlockSpec(memory_space=pltpu.SMEM)]


def down_kernel(children_ref, mask_ref, weight_ref, coarse_ref, slope_ref):
    octants = children_ref.shape[0]
    total = None
    for o in range(0, octants, 2):
        masked = jnp.concatenate(
            [
                children_ref[o + j] * mask_ref[o + j : o + j + 1, :].astype(F32).astype(BF16)
                for j in range(2)
            ],
            axis=0,
        )
        weights = jnp.concatenate([weight_ref[o], weight_ref[o + 1]], axis=1)
        term = jnp.dot(weights, masked, preferred_element_type=F32)
        total = term if total is None else total + term
    slope_ref[...] = silu_slope(total)
    coarse_ref[...] = (total * jax.nn.sigmoid(total)).T.astype(BF16)


def fill_window(window_ref, pieces, order, rows):
    for at, blocks in enumerate(pieces):
        for lane, source in enumerate(order):
            width = blocks[source].shape[1]
            window_ref[at * rows : (at + 1) * rows, lane * width : (lane + 1) * width] = blocks[
                source
            ][...]
    window_ref[3 * rows :, :] = jnp.zeros_like(window_ref[3 * rows :, :])


def gather_block(scalars_ref, index_ref, window_ref, block, blocks, store, add):
    rows = pl.ds(pl.multiple_of(block * BLOCK, BLOCK), BLOCK)
    columns = index_ref[rows, :]
    lanes = lax.broadcasted_iota(jnp.int32, (BLOCK, SPAN), 1)

    def picked(group, start):
        hot = [
            jnp.where(columns[:, group * PER + j : group * PER + j + 1] - start == lanes, 1.0, 0.0)
            .astype(F32)
            .astype(BF16)
            for j in range(PER)
        ]
        span = window_ref[pl.ds(pl.multiple_of(start, 16), SPAN), :]
        return jnp.dot(jnp.concatenate(hot, axis=0), span, preferred_element_type=F32).astype(BF16)

    for group in range(GROUPS):
        low = scalars_ref[group * blocks + block]
        steps = scalars_ref[(GROUPS + group) * blocks + block]
        result = picked(group, low)
        for j in range(PER):
            store(group * PER + j, rows, result[j * BLOCK : (j + 1) * BLOCK])

        @pl.when(steps > 1)
        def _():
            def more(step, _):
                result = picked(group, low + step * SPAN)
                for j in range(PER):
                    add(group * PER + j, rows, result[j * BLOCK : (j + 1) * BLOCK])
                return 0

            lax.fori_loop(1, steps, more, 0)


def conv_kernel(chans, scale, scalars_ref, index_ref, weight_ref, cotangent_ref, *refs):
    count = len(refs) - 9
    blocks_refs, refs = refs[:count], refs[count:]
    out_ref, grad_ref, keep_ref, send_ref = refs[:4]
    window_ref, column_ref, picked_ref, conv_ref, scratch_ref = refs[4:]
    rows = index_ref.shape[1]
    blocks = rows // BLOCK
    width = window_ref.shape[1]
    channels = weight_ref.shape[1]
    per_piece = count // 3
    pieces = [blocks_refs[i * per_piece : (i + 1) * per_piece] for i in range(3)]
    chan = scalars_ref[2 * GROUPS * blocks]
    rep = scalars_ref[2 * GROUPS * blocks + 1]
    if chans == 2:
        for own in range(2):

            @pl.when(chan == own)
            def _(own=own):
                fill_window(window_ref, pieces, (own, 1 - own), rows)

    else:
        fill_window(window_ref, pieces, tuple(range(chans)), rows)
    column_ref[...] = index_ref[...].T

    def store(offset, at, value):
        lane = offset % 3 * width
        picked_ref[offset // 3, at, lane : lane + width] = value

    def add(offset, at, value):
        lane = offset % 3 * width
        picked_ref[offset // 3, at, lane : lane + width] += value

    def gather(block, _):
        gather_block(scalars_ref, column_ref, window_ref, block, blocks, store, add)
        return 0

    lax.fori_loop(0, blocks, gather, 0)

    def multiply(three, _):
        weights = jnp.concatenate([weight_ref[three * 3 + j] for j in range(3)], axis=1)
        term = lax.dot_general(picked_ref[three], weights, NT, preferred_element_type=F32)
        conv_ref[...] = jnp.where(three == 0, term, conv_ref[...] + term)
        return 0

    conv_ref[...] = jnp.zeros_like(conv_ref)
    lax.fori_loop(0, 9, multiply, 0)
    conv = conv_ref[...].T
    sigma = jax.nn.sigmoid(conv)
    out_ref[...] = (conv * sigma).astype(BF16)
    grad = cotangent_ref[...].astype(F32) * (sigma * (1.0 + conv * (1.0 - sigma)))
    grad_ref[...] = grad.T.astype(BF16)
    scratch_ref[...] = grad.astype(BF16)
    half = channels // 2

    def weigh(three, _):
        term = jnp.dot(scratch_ref[...], picked_ref[three], preferred_element_type=F32) * scale
        for j in range(3):
            both = term[:, j * width : (j + 1) * width].astype(BF16)
            keep_ref[three * 3 + j] = jnp.where(rep == 0, both[:half], both[half:])
            send_ref[three * 3 + j] = jnp.where(rep == 0, both[half:], both[:half])
        return 0

    lax.fori_loop(0, 9, weigh, 0)


def coarse_grad_kernel(scalars_ref, index_ref, weight_ref, low_ref, own_ref, high_ref, *refs):
    mine_ref, other_ref, window_ref, column_ref, picked_ref, total_ref = refs
    rows = index_ref.shape[1]
    blocks = rows // BLOCK
    offsets, channels, width = weight_ref.shape
    fill_window(window_ref, [[low_ref], [own_ref], [high_ref]], (0,), rows)
    column_ref[...] = index_ref[...].T
    chan = scalars_ref[2 * GROUPS * blocks]

    def lanes(offset):
        at = (offsets - 1 - offset) * channels
        return slice(at, at + channels)

    def store(offset, at, value):
        picked_ref[at, lanes(offset)] = value

    def add(offset, at, value):
        picked_ref[at, lanes(offset)] += value

    def step(block, _):
        gather_block(scalars_ref, column_ref, window_ref, block, blocks, store, add)
        return 0

    lax.fori_loop(0, blocks, step, 0)
    weights = weight_ref[...].reshape(offsets * channels, width)
    chans = width // channels
    result = jnp.dot(picked_ref[...], weights, preferred_element_type=F32).T
    for at in range(chans):
        total_ref[at] = result[at * channels : (at + 1) * channels]
    mine_ref[...] = total_ref[chan]
    for step in range(1, chans):
        other_ref[step - 1] = total_ref[lax.rem(chan + step, chans)].astype(BF16)


def pre_grad_kernel(scale, children_ref, mask_ref, slope_ref, mine_ref, *refs):
    others, (grad_ref, weight_grad_ref) = refs[:-2], refs[-2:]
    total = mine_ref[...]
    for other in others:
        total = total + other[...].astype(F32)
    grad = (total * slope_ref[...]).astype(BF16)
    grad_ref[...] = grad
    for o in range(children_ref.shape[0]):
        masked = children_ref[o] * mask_ref[o : o + 1, :].astype(F32).astype(BF16)
        term = lax.dot_general(grad, masked, NT, preferred_element_type=F32) * scale
        weight_grad_ref[o] = term.astype(BF16)


def children_kernel(mask_ref, *refs):
    out_ref = refs[-1]
    count = (len(refs) - 1) // 2
    grads, weights = refs[:count], refs[count:-1]
    for o in range(out_ref.shape[0]):
        total = None
        for grad, weight in zip(grads, weights):
            term = jnp.dot(weight[o], grad[...], preferred_element_type=F32)
            term = term.astype(BF16).astype(F32)
            total = term if total is None else total + term
        out_ref[o] = (total * mask_ref[o : o + 1, :].astype(F32)).astype(BF16)


def body(children, child_mask, neighbours, down_weight, conv_weight, cotangent):
    octants, fine, rows = children.shape
    offsets, channels, width = conv_weight.shape
    blocks = rows // BLOCK
    chans = lax.axis_size("chan")
    chan = lax.axis_index("chan")
    rep = lax.axis_index("rep")
    pieces = lax.axis_size(PIECES)
    position = lax.axis_index(PIECES)
    scale = 1.0 / (rows * pieces) ** 0.5
    shape = jax.ShapeDtypeStruct

    coarse, slope = call(
        down_kernel,
        [shape((rows, channels), BF16), shape((channels, rows), F32)],
        vmem(3),
        [],
        2 * octants * fine * rows * channels,
        3 * 1024 * 1024,
    )(children, child_mask, down_weight)

    valid = neighbours >= 0
    local = jnp.where(valid, neighbours - (position - 1) * rows, -(2**20))
    tiles = local.reshape(GROUPS, PER, blocks, BLOCK)
    low = jnp.min(jnp.where(tiles < 0, 2**20, tiles), axis=(1, 3))
    high = jnp.max(tiles, axis=(1, 3)) + 1
    low = jnp.where(high <= 0, 0, low // 16 * 16)
    steps = jnp.maximum(1, (high - low + SPAN - 1) // SPAN)
    scalars = jnp.concatenate(
        [low.reshape(-1), steps.reshape(-1), jnp.stack([chan, rep]).astype(jnp.int32)]
    )
    index = jnp.pad(local, ((0, 32 - offsets), (0, 0)), constant_values=-(2**20))

    if chans == 2:
        parts = [coarse, swapped(coarse, "chan")]
    else:
        every = lax.all_gather(coarse, "chan", axis=0)
        parts = [every[i] for i in range(chans)]
    before = [passed_along(part, PIECES, 1) for part in parts]
    after = [passed_along(part, PIECES, -1) for part in parts]

    half = channels // 2
    features_out, conv_grad, keep, send = call(
        functools.partial(conv_kernel, chans, scale),
        [
            shape((channels, rows), BF16),
            shape((rows, channels), BF16),
            shape((offsets, half, width), BF16),
            shape((offsets, half, width), BF16),
        ],
        SMEM + vmem(3 + 3 * chans),
        [
            pltpu.VMEM((3 * rows + SPAN, width), BF16),
            pltpu.VMEM((rows, 32), jnp.int32),
            pltpu.VMEM((9, rows, 3 * width), BF16),
            pltpu.VMEM((rows, channels), F32),
            pltpu.VMEM((channels, rows), BF16),
        ],
        2 * offsets * rows * width * (SPAN + 2 * channels),
        8 * 1024 * 1024,
    )(scalars, index, conv_weight, cotangent, *before, *parts, *after)

    grad_before = passed_along(conv_grad, PIECES, 1)
    grad_after = passed_along(conv_grad, PIECES, -1)
    summed = (keep.astype(F32) + swapped(send, "rep").astype(F32)).astype(BF16)
    summed = lax.psum(summed, "curve")

    mine, others = call(
        coarse_grad_kernel,
        [shape((channels, rows), F32), shape((chans - 1, channels, rows), BF16)],
        SMEM + vmem(5),
        [
            pltpu.VMEM((3 * rows + SPAN, channels), BF16),
            pltpu.VMEM((rows, 32), jnp.int32),
            pltpu.VMEM((rows, offsets * channels), BF16),
            pltpu.VMEM((chans, channels, rows), F32),
        ],
        2 * offsets * rows * channels * (SPAN + width),
        6 * 1024 * 1024,
    )(scalars, index, conv_weight, grad_before, conv_grad, grad_after)
    received = [
        lax.ppermute(others[by - 1], "chan", [(i, (i + by) % chans) for i in range(chans)])
        for by in range(1, chans)
    ]
    pre_grad, down_partial = call(
        functools.partial(pre_grad_kernel, scale),
        [shape((channels, rows), BF16), shape((octants, channels, fine), BF16)],
        vmem(4 + len(received)),
        [],
        2 * octants * fine * rows * channels,
        3 * 1024 * 1024,
    )(children, child_mask, slope, mine, *received)
    down_weight_grad = lax.psum(down_partial, PIECES).astype(F32)

    mine_fine = fine // chans
    grads, weights = [pre_grad], []
    turned = down_weight.transpose(0, 2, 1)
    for by in range(chans):
        start = lax.rem(chan + by, chans) * mine_fine
        part = lax.dynamic_slice_in_dim(turned, start, mine_fine, axis=1)
        pairs = [(i, (i + by) % chans) for i in range(chans)]
        if by:
            grads.append(lax.ppermute(pre_grad, "chan", pairs))
            part = lax.ppermute(part, "chan", pairs)
        weights.append(part)
    children_grad = call(
        children_kernel,
        shape((octants, mine_fine, rows), BF16),
        vmem(1 + 2 * chans),
        [],
        2 * octants * fine * rows * channels,
        3 * 1024 * 1024,
    )(child_mask, *grads, *weights)

    swap = swapped(summed, "rep")
    first = jnp.where(rep == 0, summed, swap)
    second = jnp.where(rep == 0, swap, summed)
    conv_weight_grad = jnp.concatenate([first, second], axis=1).astype(F32)
    return (features_out, children_grad, conv_weight_grad, down_weight_grad)


def solution(mesh):
    in_specs = (
        P(None, None, ("snap", "curve", "rep")),
        P(None, ("snap", "curve", "rep")),
        P(None, ("snap", "curve", "rep")),
        P(None, "chan", None),
        P(None, "chan", None),
        P("chan", ("snap", "curve", "rep")),
    )
    out_specs = (
        P("chan", ("snap", "curve", "rep")),
        P(None, "chan", ("snap", "curve", "rep")),
        P("snap", "chan", None),
        P("snap", "chan", None),
    )
    return jax.shard_map(body, mesh=mesh, in_specs=in_specs, out_specs=out_specs, check_vma=False)
```

```python
import functools

import jax
import jax.numpy as jnp
from jax import lax
from jax.experimental import pallas as pl
from jax.experimental.pallas import tpu as pltpu
from jax.sharding import PartitionSpec as P

BLOCK = 128
SPAN = 256
GROUPS = 3
PER = 9
VMEM_LIMIT = 56 * 1024 * 1024
PIECES = ("curve", "rep")
F32 = jnp.float32
BF16 = jnp.bfloat16
NT = (((1,), (1,)), ((), ()))


def silu_slope(value):
    sigma = jax.nn.sigmoid(value)
    return sigma * (1.0 + value * (1.0 - sigma))


def passed_along(shard, axis, by):
    devices = lax.axis_size(axis)
    pairs = [(i, i + by) for i in range(devices) if 0 <= i + by < devices]
    return lax.ppermute(shard, axis, pairs)


def swapped(shard, axis):
    return lax.ppermute(shard, axis, [(0, 1), (1, 0)])


def call(kernel, out_shape, specs, scratch, flops, bytes_accessed):
    return pl.pallas_call(
        kernel,
        out_shape=out_shape,
        in_specs=specs,
        scratch_shapes=scratch,
        compiler_params=pltpu.CompilerParams(vmem_limit_bytes=VMEM_LIMIT),
        cost_estimate=pl.CostEstimate(
            flops=flops, bytes_accessed=bytes_accessed, transcendentals=0
        ),
    )


def vmem(count):
    return [pl.BlockSpec(memory_space=pltpu.VMEM)] * count


SMEM = [pl.BlockSpec(memory_space=pltpu.SMEM)]


def down_kernel(children_ref, mask_ref, weight_ref, coarse_ref, slope_ref):
    octants = children_ref.shape[0]
    total = None
    for o in range(0, octants, 2):
        masked = jnp.concatenate(
            [
                children_ref[o + j] * mask_ref[o + j : o + j + 1, :].astype(F32).astype(BF16)
                for j in range(2)
            ],
            axis=0,
        )
        weights = jnp.concatenate([weight_ref[o], weight_ref[o + 1]], axis=1)
        term = jnp.dot(weights, masked, preferred_element_type=F32)
        total = term if total is None else total + term
    slope_ref[...] = silu_slope(total)
    coarse_ref[...] = (total * jax.nn.sigmoid(total)).T.astype(BF16)


def fill_window(window_ref, pieces, order, rows):
    for at, blocks in enumerate(pieces):
        for lane, source in enumerate(order):
            width = blocks[source].shape[1]
            window_ref[at * rows : (at + 1) * rows, lane * width : (lane + 1) * width] = blocks[
                source
            ][...]
    window_ref[3 * rows :, :] = jnp.zeros_like(window_ref[3 * rows :, :])


def gather(scalars_ref, column_ref, window_ref, blocks, store, add):
    lanes = lax.broadcasted_iota(jnp.int32, (BLOCK, SPAN), 1).astype(F32).astype(BF16)

    def picked(group, rows, start):
        columns = jnp.clip(column_ref[group, rows, :] - start, -1, SPAN).astype(F32)
        hot = [
            jnp.where(
                jnp.broadcast_to(columns[:, j : j + 1], (BLOCK, SPAN)).astype(BF16) == lanes,
                jnp.ones((), BF16),
                jnp.zeros((), BF16),
            )
            for j in range(PER)
        ]
        span = window_ref[pl.ds(pl.multiple_of(start, 16), SPAN), :]
        return jnp.dot(jnp.concatenate(hot, axis=0), span, preferred_element_type=F32).astype(BF16)

    def first(block, _):
        rows = pl.ds(pl.multiple_of(block * BLOCK, BLOCK), BLOCK)
        for group in range(GROUPS):
            result = picked(group, rows, scalars_ref[group * blocks + block])
            for j in range(PER):
                store(group, j, rows, result[j * BLOCK : (j + 1) * BLOCK])
        return 0

    lax.fori_loop(0, blocks, first, 0)

    def rest(at, _):
        group, block = at // blocks, at % blocks
        rows = pl.ds(pl.multiple_of(block * BLOCK, BLOCK), BLOCK)

        def more(step, _):
            result = picked(group, rows, scalars_ref[at] + step * SPAN)
            for j in range(PER):
                add(group, j, rows, result[j * BLOCK : (j + 1) * BLOCK])
            return 0

        lax.fori_loop(1, scalars_ref[GROUPS * blocks + at], more, 0)
        return 0

    lax.fori_loop(0, GROUPS * blocks, rest, 0)


def turn(scratch_ref, value, shards, scalars_ref, at):
    half = value.shape[0] // 2
    size = half // shards
    scratch_ref[0] = value
    place, rep = scalars_ref[at + 1], scalars_ref[at + 2]
    for core in range(2):
        for step in range(shards):
            source = (rep + core) % 2 * half + (place + step) % shards * size
            target = core * half + step * size
            scratch_ref[1, target : target + size] = scratch_ref[
                0, pl.ds(pl.multiple_of(source, size), size)
            ]


def conv_kernel(chans, shards, scale, scalars_ref, index_ref, weight_ref, cotangent_ref, *refs):
    count = 3 * chans
    blocks_refs, refs = refs[:count], refs[count:]
    out_ref, grad_ref, keep_ref, send_ref = refs[:4]
    window_ref, column_ref, picked_ref, conv_ref, scratch_ref = refs[4:]
    rows = index_ref.shape[2]
    blocks = rows // BLOCK
    width = window_ref.shape[1]
    channels = weight_ref.shape[1]
    pieces = [blocks_refs[i * chans : (i + 1) * chans] for i in range(3)]
    chan = scalars_ref[2 * GROUPS * blocks]
    if chans == 2:
        for own in range(2):

            @pl.when(chan == own)
            def _(own=own):
                fill_window(window_ref, pieces, (own, 1 - own), rows)

    else:
        fill_window(window_ref, pieces, tuple(range(chans)), rows)
    for group in range(GROUPS):
        column_ref[group] = index_ref[group].T

    def store(group, j, at, value):
        lane = j % 3 * width
        picked_ref[group * 3 + j // 3, at, lane : lane + width] = value

    def add(group, j, at, value):
        lane = j % 3 * width
        picked_ref[group * 3 + j // 3, at, lane : lane + width] += value

    gather(scalars_ref, column_ref, window_ref, blocks, store, add)

    def multiply(three, _):
        weights = jnp.concatenate([weight_ref[three * 3 + j] for j in range(3)], axis=1)
        term = lax.dot_general(picked_ref[three], weights, NT, preferred_element_type=F32)
        conv_ref[...] += term
        return 0

    conv_ref[...] = jnp.zeros_like(conv_ref)
    lax.fori_loop(0, 9, multiply, 0)
    conv = conv_ref[...].T
    sigma = jax.nn.sigmoid(conv)
    out_ref[...] = (conv * sigma).astype(BF16)
    grad = cotangent_ref[...].astype(F32) * (sigma * (1.0 + conv * (1.0 - sigma)))
    grad_ref[...] = grad.T.astype(BF16)
    turn(scratch_ref, grad.astype(BF16), shards, scalars_ref, 2 * GROUPS * blocks)
    half = channels // 2
    size = half // shards

    def weigh(three, _):
        term = jnp.dot(scratch_ref[1], picked_ref[three], preferred_element_type=F32) * scale
        for j in range(3):
            both = term[:, j * width : (j + 1) * width].astype(BF16)
            for step in range(shards):
                at = step * size
                keep_ref[step, three * 3 + j] = both[at : at + size]
                send_ref[step, three * 3 + j] = both[half + at : half + at + size]
        return 0

    lax.fori_loop(0, 9, weigh, 0)


def coarse_grad_kernel(scalars_ref, index_ref, weight_ref, low_ref, own_ref, high_ref, *refs):
    mine_ref, other_ref, window_ref, column_ref, picked_ref, total_ref = refs
    rows = index_ref.shape[2]
    blocks = rows // BLOCK
    offsets, channels, width = weight_ref.shape
    fill_window(window_ref, [[low_ref], [own_ref], [high_ref]], (0,), rows)
    for group in range(GROUPS):
        column_ref[group] = index_ref[group].T
    chan = scalars_ref[2 * GROUPS * blocks]

    def store(group, j, at, value):
        lane = (PER - 1 - j) * channels
        picked_ref[GROUPS - 1 - group, at, lane : lane + channels] = value

    def add(group, j, at, value):
        lane = (PER - 1 - j) * channels
        picked_ref[GROUPS - 1 - group, at, lane : lane + channels] += value

    gather(scalars_ref, column_ref, window_ref, blocks, store, add)
    result = None
    for group in range(GROUPS):
        weights = weight_ref[group * PER : (group + 1) * PER].reshape(PER * channels, width)
        term = jnp.dot(picked_ref[group], weights, preferred_element_type=F32)
        result = term if result is None else result + term
    result = result.T
    chans = width // channels
    for at in range(chans):
        total_ref[at] = result[at * channels : (at + 1) * channels]
    mine_ref[...] = total_ref[chan]
    for step in range(1, chans):
        other_ref[step - 1] = total_ref[lax.rem(chan + step, chans)].astype(BF16)


def pre_grad_kernel(shards, scale, scalars_ref, children_ref, mask_ref, slope_ref, mine_ref, *refs):
    others, refs = refs[:-4], refs[-4:]
    grad_ref, keep_ref, send_ref, scratch_ref = refs
    total = mine_ref[...]
    for other in others:
        total = total + other[...].astype(F32)
    grad = (total * slope_ref[...]).astype(BF16)
    grad_ref[...] = grad
    blocks = grad.shape[1] // BLOCK
    turn(scratch_ref, grad, shards, scalars_ref, 2 * GROUPS * blocks)
    half = grad.shape[0] // 2
    size = half // shards
    for o in range(children_ref.shape[0]):
        masked = children_ref[o] * mask_ref[o : o + 1, :].astype(F32).astype(BF16)
        term = lax.dot_general(scratch_ref[1], masked, NT, preferred_element_type=F32) * scale
        both = term.astype(BF16)
        for step in range(shards):
            at = step * size
            keep_ref[step, o] = both[at : at + size]
            send_ref[step, o] = both[half + at : half + at + size]


def children_kernel(mask_ref, *refs):
    out_ref = refs[-1]
    count = (len(refs) - 1) // 2
    grads, weights = refs[:count], refs[count:-1]
    for o in range(out_ref.shape[0]):
        total = None
        for grad, weight in zip(grads, weights):
            term = jnp.dot(weight[o], grad[...], preferred_element_type=F32)
            term = term.astype(BF16).astype(F32)
            total = term if total is None else total + term
        out_ref[o] = (total * mask_ref[o : o + 1, :].astype(F32)).astype(BF16)


def spread_kernel(shards, scalars_ref, *refs):
    mine, theirs, out_ref = refs[:shards], refs[shards:-1], refs[-1]
    half = out_ref.shape[1] // 2
    size = half // shards
    place, rep = scalars_ref[0], scalars_ref[1]
    for step in range(shards):
        row = (place + shards - step) % shards * size
        for core, source in ((rep, mine[step]), (1 - rep, theirs[step])):
            at = pl.ds(pl.multiple_of(core * half + row, size), size)
            out_ref[:, at, :] = source[...].astype(F32)


def summed(keep, send, shards, place):
    total = (keep.astype(F32) + swapped(send, "rep").astype(F32)).astype(BF16)
    if shards == 1:
        mine = [lax.psum(total, "curve")[0]]
    else:
        pairs = [[(i, (i + by) % shards) for i in range(shards)] for by in range(shards)]
        terms = [total[0]] + [
            lax.ppermute(total[by], "curve", pairs[by]) for by in range(1, shards)
        ]
        own = sum(term.astype(F32) for term in terms).astype(BF16)
        mine = [own] + [lax.ppermute(own, "curve", pairs[by]) for by in range(1, shards)]
    theirs = [swapped(part, "rep") for part in mine]
    count, size, width = mine[0].shape
    steps = 4 if count % 4 == 0 else 3
    part = pl.BlockSpec((count // steps, size, width), lambda i: (i, 0, 0))
    whole = pl.BlockSpec((count // steps, 2 * shards * size, width), lambda i: (i, 0, 0))
    return pl.pallas_call(
        functools.partial(spread_kernel, shards),
        grid=(steps,),
        out_shape=jax.ShapeDtypeStruct((count, 2 * shards * size, width), F32),
        in_specs=SMEM + [part] * (2 * shards),
        out_specs=whole,
        compiler_params=pltpu.CompilerParams(vmem_limit_bytes=VMEM_LIMIT),
    )(place, *mine, *theirs)


def body(children, child_mask, neighbours, down_weight, conv_weight, cotangent):
    octants, fine, rows = children.shape
    offsets, channels, width = conv_weight.shape
    blocks = rows // BLOCK
    chans = lax.axis_size("chan")
    chan = lax.axis_index("chan")
    rep = lax.axis_index("rep")
    curve = lax.axis_index("curve")
    pieces = lax.axis_size(PIECES)
    position = lax.axis_index(PIECES)
    scale = 1.0 / (rows * pieces) ** 0.5
    shape = jax.ShapeDtypeStruct
    half = channels // 2
    shards = lax.axis_size("curve")
    if half % (16 * shards):
        shards = 1
    size = half // shards

    coarse, slope = call(
        down_kernel,
        [shape((rows, channels), BF16), shape((channels, rows), F32)],
        vmem(3),
        [],
        2 * octants * fine * rows * channels,
        3 * 1024 * 1024,
    )(children, child_mask, down_weight)

    valid = neighbours >= 0
    local = jnp.where(valid, neighbours - (position - 1) * rows, -(2**20))
    tiles = local.reshape(GROUPS, PER, blocks, BLOCK)
    low = jnp.min(jnp.where(tiles < 0, 2**20, tiles), axis=(1, 3))
    high = jnp.max(tiles, axis=(1, 3)) + 1
    low = jnp.where(high <= 0, 0, low // 16 * 16)
    steps = jnp.maximum(1, (high - low + SPAN - 1) // SPAN)
    place = jnp.stack([curve, rep]).astype(jnp.int32)
    scalars = jnp.concatenate(
        [low.reshape(-1), steps.reshape(-1), chan[None].astype(jnp.int32), place]
    )
    index = jnp.pad(
        local.reshape(GROUPS, PER, rows),
        ((0, 0), (0, 16 - PER), (0, 0)),
        constant_values=-(2**20),
    )

    if chans == 2:
        parts = [coarse, swapped(coarse, "chan")]
    else:
        every = lax.all_gather(coarse, "chan", axis=0)
        parts = [every[i] for i in range(chans)]
    before = [passed_along(part, PIECES, 1) for part in parts]
    after = [passed_along(part, PIECES, -1) for part in parts]

    features_out, conv_grad, keep, send = call(
        functools.partial(conv_kernel, chans, shards, scale),
        [
            shape((channels, rows), BF16),
            shape((rows, channels), BF16),
            shape((shards, offsets, size, width), BF16),
            shape((shards, offsets, size, width), BF16),
        ],
        SMEM + vmem(3 + 3 * chans),
        [
            pltpu.VMEM((3 * rows + SPAN, width), BF16),
            pltpu.VMEM((GROUPS, rows, 16), jnp.int32),
            pltpu.VMEM((9, rows, 3 * width), BF16),
            pltpu.VMEM((rows, channels), F32),
            pltpu.VMEM((2, channels, rows), BF16),
        ],
        2 * offsets * rows * width * (SPAN + 2 * channels),
        8 * 1024 * 1024,
    )(scalars, index, conv_weight, cotangent, *before, *parts, *after)
    conv_weight_grad = summed(keep, send, shards, place)

    grad_before = passed_along(conv_grad, PIECES, 1)
    grad_after = passed_along(conv_grad, PIECES, -1)
    mine, others = call(
        coarse_grad_kernel,
        [shape((channels, rows), F32), shape((chans - 1, channels, rows), BF16)],
        SMEM + vmem(5),
        [
            pltpu.VMEM((3 * rows + SPAN, channels), BF16),
            pltpu.VMEM((GROUPS, rows, 16), jnp.int32),
            pltpu.VMEM((GROUPS, rows, PER * channels), BF16),
            pltpu.VMEM((chans, channels, rows), F32),
        ],
        2 * offsets * rows * channels * (SPAN + width),
        6 * 1024 * 1024,
    )(scalars, index, conv_weight, grad_before, conv_grad, grad_after)
    received = [
        lax.ppermute(others[by - 1], "chan", [(i, (i + by) % chans) for i in range(chans)])
        for by in range(1, chans)
    ]
    pre_grad, keep, send = call(
        functools.partial(pre_grad_kernel, shards, scale),
        [
            shape((channels, rows), BF16),
            shape((shards, octants, size, fine), BF16),
            shape((shards, octants, size, fine), BF16),
        ],
        SMEM + vmem(4 + len(received)),
        [pltpu.VMEM((2, channels, rows), BF16)],
        2 * octants * fine * rows * channels,
        3 * 1024 * 1024,
    )(scalars, children, child_mask, slope, mine, *received)
    down_weight_grad = summed(keep, send, shards, place)

    mine_fine = fine // chans
    grads, weights = [pre_grad], []
    turned = down_weight.transpose(0, 2, 1)
    for by in range(chans):
        start = lax.rem(chan + by, chans) * mine_fine
        part = lax.dynamic_slice_in_dim(turned, start, mine_fine, axis=1)
        pairs = [(i, (i + by) % chans) for i in range(chans)]
        if by:
            grads.append(lax.ppermute(pre_grad, "chan", pairs))
            part = lax.ppermute(part, "chan", pairs)
        weights.append(part)
    children_grad = call(
        children_kernel,
        shape((octants, mine_fine, rows), BF16),
        vmem(1 + 2 * chans),
        [],
        2 * octants * fine * rows * channels,
        3 * 1024 * 1024,
    )(child_mask, *grads, *weights)
    return (features_out, children_grad, conv_weight_grad, down_weight_grad)


def solution(mesh):
    in_specs = (
        P(None, None, ("snap", "curve", "rep")),
        P(None, ("snap", "curve", "rep")),
        P(None, ("snap", "curve", "rep")),
        P(None, "chan", None),
        P(None, "chan", None),
        P("chan", ("snap", "curve", "rep")),
    )
    out_specs = (
        P("chan", ("snap", "curve", "rep")),
        P(None, "chan", ("snap", "curve", "rep")),
        P("snap", "chan", None),
        P("snap", "chan", None),
    )
    return jax.shard_map(body, mesh=mesh, in_specs=in_specs, out_specs=out_specs, check_vma=False)
```

```python
import functools

import jax
import jax.numpy as jnp
from jax import lax
from jax.experimental import pallas as pl
from jax.experimental.pallas import tpu as pltpu
from jax.sharding import PartitionSpec as P

BLOCK = 128
SPAN = 256
GROUPS = 3
PER = 9
VMEM_LIMIT = 56 * 1024 * 1024
PIECES = ("curve", "rep")
F32 = jnp.float32
BF16 = jnp.bfloat16
NT = (((1,), (1,)), ((), ()))


def silu_slope(value):
    sigma = jax.nn.sigmoid(value)
    return sigma * (1.0 + value * (1.0 - sigma))


def met(shard):
    devices = lax.axis_size(PIECES)
    pairs = [(i, i + 1) for i in range(1, devices - 1, 2)]
    pairs += [(j, i) for i, j in pairs]
    return [lax.ppermute(shard, PIECES, pairs), swapped(shard, "rep")]


def swapped(shard, axis):
    return lax.ppermute(shard, axis, [(0, 1), (1, 0)])


def call(kernel, out_shape, in_specs, scratch, out_specs=None):
    options = {} if out_specs is None else {"out_specs": out_specs}
    return pl.pallas_call(
        kernel,
        out_shape=out_shape,
        in_specs=in_specs,
        scratch_shapes=scratch,
        compiler_params=pltpu.CompilerParams(vmem_limit_bytes=VMEM_LIMIT),
        cost_estimate=pl.CostEstimate(flops=0, bytes_accessed=0, transcendentals=0),
        **options,
    )


def anywhere(count):
    return [pl.BlockSpec(memory_space=pl.ANY)] * count


def vmem(count):
    return [pl.BlockSpec(memory_space=pltpu.VMEM)] * count


SMEM = [pl.BlockSpec(memory_space=pltpu.SMEM)]


def down_kernel(children_ref, mask_ref, weight_ref, coarse_ref, slope_ref):
    octants = children_ref.shape[0]
    total = None
    for o in range(0, octants, 2):
        masked = jnp.concatenate(
            [
                children_ref[o + j] * mask_ref[o + j : o + j + 1, :].astype(F32).astype(BF16)
                for j in range(2)
            ],
            axis=0,
        )
        weights = jnp.concatenate([weight_ref[o], weight_ref[o + 1]], axis=1)
        term = jnp.dot(weights, masked, preferred_element_type=F32)
        total = term if total is None else total + term
    slope_ref[...] = silu_slope(total)
    coarse_ref[...] = (total * jax.nn.sigmoid(total)).T.astype(BF16)


def window_copies(window_ref, parts, slots, rep, semaphores):
    rows = parts[0][0].shape[0]
    places = (rows, rep * 2 * rows, (1 - rep) * 2 * rows)
    copies = []
    for part, slot in zip(parts, slots):
        for source, place in zip(part, places):
            target = window_ref.at[slot, pl.ds(pl.multiple_of(place, 16), rows)]
            copies.append(pltpu.make_async_copy(source, target, semaphores.at[len(copies)]))
    return copies


def gather(scalars_ref, column_ref, window_ref, blocks, store, add):
    lanes = lax.broadcasted_iota(jnp.int32, (BLOCK, SPAN), 1).astype(F32).astype(BF16)

    def picked(group, rows, start):
        columns = jnp.clip(column_ref[group, rows, :] - start, -1, SPAN).astype(F32)
        hot = [
            jnp.where(
                jnp.broadcast_to(columns[:, j : j + 1], (BLOCK, SPAN)).astype(BF16) == lanes,
                jnp.ones((), BF16),
                jnp.zeros((), BF16),
            )
            for j in range(PER)
        ]
        at = pl.ds(pl.multiple_of(start, 16), SPAN)
        span = jnp.concatenate([window_ref[c, at, :] for c in range(window_ref.shape[0])], axis=1)
        return jnp.dot(jnp.concatenate(hot, axis=0), span, preferred_element_type=F32).astype(BF16)

    def first(block, _):
        rows = pl.ds(pl.multiple_of(block * BLOCK, BLOCK), BLOCK)
        for group in range(GROUPS):
            result = picked(group, rows, scalars_ref[group * blocks + block])
            for j in range(PER):
                store(group, j, rows, result[j * BLOCK : (j + 1) * BLOCK])
        return 0

    lax.fori_loop(0, blocks, first, 0)

    def rest(at, _):
        group, block = at // blocks, at % blocks
        rows = pl.ds(pl.multiple_of(block * BLOCK, BLOCK), BLOCK)

        def more(step, _):
            result = picked(group, rows, scalars_ref[at] + step * SPAN)
            for j in range(PER):
                add(group, j, rows, result[j * BLOCK : (j + 1) * BLOCK])
            return 0

        lax.fori_loop(1, scalars_ref[GROUPS * blocks + at], more, 0)
        return 0

    lax.fori_loop(0, GROUPS * blocks, rest, 0)


def turn(scratch_ref, value, shards, scalars_ref, at):
    half = value.shape[0] // 2
    size = half // shards
    scratch_ref[0] = value
    place, rep = scalars_ref[at + 1], scalars_ref[at + 2]
    for core in range(2):
        for step in range(shards):
            source = (rep + core) % 2 * half + (place ^ step) * size
            target = core * half + step * size
            scratch_ref[1, target : target + size] = scratch_ref[
                0, pl.ds(pl.multiple_of(source, size), size)
            ]


def conv_kernel(chans, shards, scale, scalars_ref, index_ref, weight_hbm, cotangent_hbm, *refs):
    parts, refs = [refs[3 * i : 3 * i + 3] for i in range(chans)], refs[3 * chans :]
    out_hbm, grad_hbm, keep_hbm, send_hbm = refs[:4]
    window_ref, column_ref, picked_ref, conv_ref, scratch_ref = refs[4:9]
    weight_ref, cotangent_ref, out_ref, grad_ref, keep_ref, send_ref = refs[9:15]
    window_sems, sems, keep_sems, send_sems = refs[15:]
    rows = index_ref.shape[2]
    blocks = rows // BLOCK
    width = chans * window_ref.shape[2]
    channels = weight_ref.shape[1]
    chan = scalars_ref[2 * GROUPS * blocks]
    rep = scalars_ref[2 * GROUPS * blocks + 2]
    slots = (chan, 1 - chan) if chans == 2 else range(chans)
    copies = window_copies(window_ref, parts, slots, rep, window_sems)
    weight_copy = pltpu.make_async_copy(weight_hbm, weight_ref, sems.at[0])
    cotangent_copy = pltpu.make_async_copy(cotangent_hbm, cotangent_ref, sems.at[1])
    out_copy = pltpu.make_async_copy(out_ref, out_hbm, sems.at[2])
    grad_copy = pltpu.make_async_copy(grad_ref, grad_hbm, sems.at[3])
    for copy in copies:
        copy.start()
    weight_copy.start()
    cotangent_copy.start()
    window_ref[:, 3 * rows :, :] = jnp.zeros((chans, SPAN, channels), BF16)
    for group in range(GROUPS):
        column_ref[group] = index_ref[group].T
    for copy in copies:
        copy.wait()

    def store(group, j, at, value):
        lane = j % 3 * width
        picked_ref[group * 3 + j // 3, at, lane : lane + width] = value

    def add(group, j, at, value):
        lane = j % 3 * width
        picked_ref[group * 3 + j // 3, at, lane : lane + width] += value

    gather(scalars_ref, column_ref, window_ref, blocks, store, add)

    def multiply(three, _):
        weights = jnp.concatenate([weight_ref[three * 3 + j] for j in range(3)], axis=1)
        term = lax.dot_general(picked_ref[three], weights, NT, preferred_element_type=F32)
        conv_ref[...] += term
        return 0

    conv_ref[...] = jnp.zeros_like(conv_ref)
    weight_copy.wait()
    lax.fori_loop(0, 9, multiply, 0)
    conv = conv_ref[...].T
    cotangent_copy.wait()
    sigma = jax.nn.sigmoid(conv)
    out_ref[...] = (conv * sigma).astype(BF16)
    grad = cotangent_ref[...].astype(F32) * (sigma * (1.0 + conv * (1.0 - sigma)))
    grad_ref[...] = grad.T.astype(BF16)
    out_copy.start()
    grad_copy.start()
    turn(scratch_ref, grad.astype(BF16), shards, scalars_ref, 2 * GROUPS * blocks)
    half = channels // 2
    size = half // shards

    def leave(three):
        at = pl.ds(three * 3, 3)
        return (
            pltpu.make_async_copy(keep_ref.at[:, at], keep_hbm.at[:, at], keep_sems.at[three]),
            pltpu.make_async_copy(send_ref.at[:, at], send_hbm.at[:, at], send_sems.at[three]),
        )

    def weigh(three, _):
        term = jnp.dot(scratch_ref[1], picked_ref[three], preferred_element_type=F32) * scale
        for j in range(3):
            both = term[:, j * width : (j + 1) * width].astype(BF16)
            for step in range(shards):
                at = step * size
                keep_ref[step, three * 3 + j] = both[at : at + size]
                send_ref[step, three * 3 + j] = both[half + at : half + at + size]
        for copy in leave(three):
            copy.start()
        return 0

    lax.fori_loop(0, 9, weigh, 0)

    def finish(three, _):
        for copy in leave(three):
            copy.wait()
        return 0

    lax.fori_loop(0, 9, finish, 0)
    out_copy.wait()
    grad_copy.wait()


def coarse_grad_kernel(scalars_ref, index_ref, weight_hbm, *refs):
    part, refs = refs[:3], refs[3:]
    mine_ref, other_ref, window_ref, column_ref, picked_ref, total_ref, weight_ref, sems = refs
    rows = index_ref.shape[2]
    blocks = rows // BLOCK
    offsets, channels, width = weight_ref.shape
    chan = scalars_ref[2 * GROUPS * blocks]
    rep = scalars_ref[2 * GROUPS * blocks + 2]
    copies = window_copies(window_ref, [part], (0,), rep, sems)
    weight_copy = pltpu.make_async_copy(weight_hbm, weight_ref, sems.at[3])
    for copy in copies:
        copy.start()
    weight_copy.start()
    window_ref[0, 3 * rows :, :] = jnp.zeros((SPAN, channels), BF16)
    for group in range(GROUPS):
        column_ref[group] = index_ref[group].T
    for copy in copies:
        copy.wait()

    def store(group, j, at, value):
        lane = (PER - 1 - j) * channels
        picked_ref[GROUPS - 1 - group, at, lane : lane + channels] = value

    def add(group, j, at, value):
        lane = (PER - 1 - j) * channels
        picked_ref[GROUPS - 1 - group, at, lane : lane + channels] += value

    gather(scalars_ref, column_ref, window_ref, blocks, store, add)
    weight_copy.wait()
    result = None
    for group in range(GROUPS):
        weights = weight_ref[group * PER : (group + 1) * PER].reshape(PER * channels, width)
        term = jnp.dot(picked_ref[group], weights, preferred_element_type=F32)
        result = term if result is None else result + term
    result = result.T
    chans = width // channels
    for at in range(chans):
        total_ref[at] = result[at * channels : (at + 1) * channels]
    mine_ref[...] = total_ref[chan]
    for step in range(1, chans):
        other_ref[step - 1] = total_ref[lax.rem(chan + step, chans)].astype(BF16)


def pre_grad_kernel(shards, scale, scalars_ref, children_ref, mask_ref, slope_ref, mine_ref, *refs):
    others, refs = refs[:-4], refs[-4:]
    grad_ref, keep_ref, send_ref, scratch_ref = refs
    total = mine_ref[...]
    for other in others:
        total = total + other[...].astype(F32)
    grad = (total * slope_ref[...]).astype(BF16)
    grad_ref[...] = grad
    blocks = grad.shape[1] // BLOCK
    turn(scratch_ref, grad, shards, scalars_ref, 2 * GROUPS * blocks)
    half = grad.shape[0] // 2
    size = half // shards
    for o in range(children_ref.shape[0]):
        masked = children_ref[o] * mask_ref[o : o + 1, :].astype(F32).astype(BF16)
        term = lax.dot_general(scratch_ref[1], masked, NT, preferred_element_type=F32) * scale
        both = term.astype(BF16)
        for step in range(shards):
            at = step * size
            keep_ref[step, o] = both[at : at + size]
            send_ref[step, o] = both[half + at : half + at + size]


def children_kernel(mask_ref, *refs):
    out_ref = refs[-1]
    count = (len(refs) - 1) // 2
    grads, weights = refs[:count], refs[count:-1]
    for o in range(out_ref.shape[0]):
        total = None
        for grad, weight in zip(grads, weights):
            term = jnp.dot(weight[o], grad[...], preferred_element_type=F32)
            term = term.astype(BF16).astype(F32)
            total = term if total is None else total + term
        out_ref[o] = (total * mask_ref[o : o + 1, :].astype(F32)).astype(BF16)


def spread_kernel(shards, scalars_ref, *refs):
    mine, theirs, out_ref = refs[:shards], refs[shards:-1], refs[-1]
    half = out_ref.shape[1] // 2
    size = half // shards
    place, rep = scalars_ref[0], scalars_ref[1]
    for step in range(shards):
        row = (place ^ step) * size
        for core, source in ((rep, mine[step]), (1 - rep, theirs[step])):
            at = pl.ds(pl.multiple_of(core * half + row, size), size)
            out_ref[:, at, :] = source[...].astype(F32)


def apart(shard, by):
    return lax.ppermute(shard, "curve", [(i, i ^ by) for i in range(lax.axis_size("curve"))])


def added(*terms):
    return sum(term.astype(F32) for term in terms).astype(BF16)


def sum_over_curve(total):
    first = added(total[2], apart(total[3], 1))
    own = added(total[0], apart(total[1], 1), apart(first, 2))
    across = apart(own, 2)
    return first, own, [own, apart(own, 1), across, apart(across, 1)]


def spread(mine, theirs, place):
    shards = len(mine)
    count, size, width = mine[0].shape
    steps = 4 if count % 4 == 0 else 3
    part = pl.BlockSpec((count // steps, size, width), lambda i: (i, 0, 0))
    whole = pl.BlockSpec((count // steps, 2 * shards * size, width), lambda i: (i, 0, 0))
    return pl.pallas_call(
        functools.partial(spread_kernel, shards),
        grid=(steps,),
        out_shape=jax.ShapeDtypeStruct((count, 2 * shards * size, width), F32),
        in_specs=SMEM + [part] * (2 * shards),
        out_specs=whole,
        compiler_params=pltpu.CompilerParams(vmem_limit_bytes=VMEM_LIMIT),
        cost_estimate=pl.CostEstimate(flops=0, bytes_accessed=0, transcendentals=0),
    )(place, *mine, *theirs)


def after(value, *earlier):
    return lax.optimization_barrier((value, *earlier))[0]


def body(children, child_mask, neighbours, down_weight, conv_weight, cotangent):
    octants, fine, rows = children.shape
    offsets, channels, width = conv_weight.shape
    blocks = rows // BLOCK
    chans = lax.axis_size("chan")
    chan = lax.axis_index("chan")
    rep = lax.axis_index("rep")
    curve = lax.axis_index("curve")
    pieces = lax.axis_size(PIECES)
    position = lax.axis_index(PIECES)
    scale = 1.0 / (rows * pieces) ** 0.5
    shape = jax.ShapeDtypeStruct
    half = channels // 2
    shards = 4 if lax.axis_size("curve") == 4 and half % 64 == 0 else 1
    size = half // shards

    coarse, slope = call(
        down_kernel,
        [shape((rows, channels), BF16), shape((channels, rows), F32)],
        vmem(3),
        [],
    )(children, child_mask, down_weight)

    valid = neighbours >= 0
    local = jnp.where(valid, neighbours - (position - 1) * rows, -(2**20))
    tiles = local.reshape(GROUPS, PER, blocks, BLOCK)
    low = jnp.min(jnp.where(tiles < 0, 2**20, tiles), axis=(1, 3))
    high = jnp.max(tiles, axis=(1, 3)) + 1
    low = jnp.where(high <= 0, 0, low // 16 * 16)
    steps = jnp.maximum(1, (high - low + SPAN - 1) // SPAN)
    place = jnp.stack([curve if shards == 4 else 0 * curve, rep]).astype(jnp.int32)
    scalars = jnp.concatenate(
        [low.reshape(-1), steps.reshape(-1), chan[None].astype(jnp.int32), place]
    )
    index = jnp.pad(
        local.reshape(GROUPS, PER, rows),
        ((0, 0), (0, 16 - PER), (0, 0)),
        constant_values=-(2**20),
    )

    if chans == 2:
        parts = [coarse, swapped(coarse, "chan")]
    else:
        every = lax.all_gather(coarse, "chan", axis=0)
        parts = [every[i] for i in range(chans)]
    windows = [array for part in parts for array in [part] + met(part)]

    features_out, conv_grad, keep, send = call(
        functools.partial(conv_kernel, chans, shards, scale),
        [
            shape((channels, rows), BF16),
            shape((rows, channels), BF16),
            shape((shards, offsets, size, width), BF16),
            shape((shards, offsets, size, width), BF16),
        ],
        SMEM + vmem(1) + anywhere(2 + 3 * chans),
        [
            pltpu.VMEM((chans, 3 * rows + SPAN, channels), BF16),
            pltpu.VMEM((GROUPS, rows, 16), jnp.int32),
            pltpu.VMEM((9, rows, 3 * width), BF16),
            pltpu.VMEM((rows, channels), F32),
            pltpu.VMEM((2, channels, rows), BF16),
            pltpu.VMEM((offsets, channels, width), BF16),
            pltpu.VMEM((channels, rows), BF16),
            pltpu.VMEM((channels, rows), BF16),
            pltpu.VMEM((rows, channels), BF16),
            pltpu.VMEM((shards, offsets, size, width), BF16),
            pltpu.VMEM((shards, offsets, size, width), BF16),
            pltpu.SemaphoreType.DMA((3 * chans,)),
            pltpu.SemaphoreType.DMA((4,)),
            pltpu.SemaphoreType.DMA((9,)),
            pltpu.SemaphoreType.DMA((9,)),
        ],
        anywhere(4),
    )(scalars, index, conv_weight, cotangent, *windows)

    received = swapped(send, "rep")
    total = [added(keep[i], received[i]) for i in range(shards)]
    if shards == 4:
        first, own, mine = sum_over_curve(total)
    else:
        first = own = lax.psum(total[0], "curve")
        mine = [own]
    theirs = [swapped(part, "rep") for part in mine]
    conv_weight_grad = spread(mine, theirs, place)

    mine, others = call(
        coarse_grad_kernel,
        [shape((channels, rows), F32), shape((chans - 1, channels, rows), BF16)],
        SMEM + vmem(1) + anywhere(4),
        [
            pltpu.VMEM((1, 3 * rows + SPAN, channels), BF16),
            pltpu.VMEM((GROUPS, rows, 16), jnp.int32),
            pltpu.VMEM((GROUPS, rows, PER * channels), BF16),
            pltpu.VMEM((chans, channels, rows), F32),
            pltpu.VMEM((offsets, channels, width), BF16),
            pltpu.SemaphoreType.DMA((4,)),
        ],
    )(after(scalars, first), index, conv_weight, conv_grad, *met(conv_grad))
    received = [
        lax.ppermute(others[by - 1], "chan", [(i, (i + by) % chans) for i in range(chans)])
        for by in range(1, chans)
    ]
    pre_grad, keep, send = call(
        functools.partial(pre_grad_kernel, shards, scale),
        [
            shape((channels, rows), BF16),
            shape((shards, octants, size, fine), BF16),
            shape((shards, octants, size, fine), BF16),
        ],
        SMEM + vmem(4 + len(received)),
        [pltpu.VMEM((2, channels, rows), BF16)],
    )(after(scalars, own), children, child_mask, slope, mine, *received)

    received = swapped(send, "rep")
    total = added(keep, received)
    if shards == 4:
        terms = [total[0]] + [apart(total[by], by) for by in range(1, 4)]
        own = added(*terms)
        mine = [own] + [apart(own, by) for by in range(1, 4)]
    else:
        mine = [lax.psum(total[0], "curve")]
    theirs = swapped(jnp.stack(mine), "rep")
    down_weight_grad = spread(mine, [theirs[i] for i in range(shards)], place)

    mine_fine = fine // chans
    grads, weights = [pre_grad], []
    turned = down_weight.transpose(0, 2, 1)
    for by in range(chans):
        start = lax.rem(chan + by, chans) * mine_fine
        part = lax.dynamic_slice_in_dim(turned, start, mine_fine, axis=1)
        pairs = [(i, (i + by) % chans) for i in range(chans)]
        if by:
            grads.append(lax.ppermute(pre_grad, "chan", pairs))
            part = lax.ppermute(part, "chan", pairs)
        weights.append(part)
    children_grad = call(
        children_kernel,
        shape((octants, mine_fine, rows), BF16),
        vmem(1 + 2 * chans),
        [],
    )(child_mask, *grads, *weights)
    return (features_out, children_grad, conv_weight_grad, down_weight_grad)


def solution(mesh):
    in_specs = (
        P(None, None, ("snap", "curve", "rep")),
        P(None, ("snap", "curve", "rep")),
        P(None, ("snap", "curve", "rep")),
        P(None, "chan", None),
        P(None, "chan", None),
        P("chan", ("snap", "curve", "rep")),
    )
    out_specs = (
        P("chan", ("snap", "curve", "rep")),
        P(None, "chan", ("snap", "curve", "rep")),
        P("snap", "chan", None),
        P("snap", "chan", None),
    )
    return jax.shard_map(body, mesh=mesh, in_specs=in_specs, out_specs=out_specs, check_vma=False)
```

```python
import functools

import jax
import jax.numpy as jnp
from jax import lax
from jax.experimental import pallas as pl
from jax.experimental.pallas import tpu as pltpu
from jax.sharding import PartitionSpec as P

BLOCK = 128
SPAN = 256
GROUPS = 3
PER = 9
VMEM_LIMIT = 56 * 1024 * 1024
PIECES = ("curve", "rep")
F32 = jnp.float32
BF16 = jnp.bfloat16
NT = (((1,), (1,)), ((), ()))


def silu_slope(value):
    sigma = jax.nn.sigmoid(value)
    return sigma * (1.0 + value * (1.0 - sigma))


def met(shard):
    devices = lax.axis_size(PIECES)
    pairs = [(i, i + 1) for i in range(1, devices - 1, 2)]
    pairs += [(j, i) for i, j in pairs]
    return [lax.ppermute(shard, PIECES, pairs), swapped(shard, "rep")]


def swapped(shard, axis):
    return lax.ppermute(shard, axis, [(0, 1), (1, 0)])


def call(kernel, out_shape, in_specs, scratch, out_specs=None):
    options = {} if out_specs is None else {"out_specs": out_specs}
    return pl.pallas_call(
        kernel,
        out_shape=out_shape,
        in_specs=in_specs,
        scratch_shapes=scratch,
        compiler_params=pltpu.CompilerParams(vmem_limit_bytes=VMEM_LIMIT),
        cost_estimate=pl.CostEstimate(flops=0, bytes_accessed=0, transcendentals=0),
        **options,
    )


def anywhere(count):
    return [pl.BlockSpec(memory_space=pl.ANY)] * count


def vmem(count):
    return [pl.BlockSpec(memory_space=pltpu.VMEM)] * count


SMEM = [pl.BlockSpec(memory_space=pltpu.SMEM)]


def octant_copies(children_hbm, children_ref, semaphores):
    copies = [
        pltpu.make_async_copy(children_hbm.at[o], children_ref.at[o], semaphores.at[o])
        for o in range(children_hbm.shape[0])
    ]
    for copy in copies:
        copy.start()
    return copies


def down_kernel(children_hbm, mask_ref, weight_ref, coarse_ref, slope_ref, children_ref, sems):
    copies = octant_copies(children_hbm, children_ref, sems)
    total = None
    for o in range(0, len(copies), 2):
        copies[o].wait()
        copies[o + 1].wait()
        masked = jnp.concatenate(
            [
                children_ref[o + j] * mask_ref[o + j : o + j + 1, :].astype(F32).astype(BF16)
                for j in range(2)
            ],
            axis=0,
        )
        weights = jnp.concatenate([weight_ref[o], weight_ref[o + 1]], axis=1)
        term = jnp.dot(weights, masked, preferred_element_type=F32)
        total = term if total is None else total + term
    slope_ref[...] = silu_slope(total)
    coarse_ref[...] = (total * jax.nn.sigmoid(total)).T.astype(BF16)


def window_copies(window_ref, parts, slots, rep, semaphores):
    rows = parts[0][0].shape[0]
    places = (rows, rep * 2 * rows, (1 - rep) * 2 * rows)
    copies = []
    for part, slot in zip(parts, slots):
        for source, place in zip(part, places):
            target = window_ref.at[slot, pl.ds(pl.multiple_of(place, 16), rows)]
            copies.append(pltpu.make_async_copy(source, target, semaphores.at[len(copies)]))
    return copies


def gather(scalars_ref, column_ref, window_ref, blocks, store, add):
    lanes = lax.broadcasted_iota(jnp.int32, (BLOCK, SPAN), 1).astype(F32).astype(BF16)

    def picked(group, rows, start):
        columns = jnp.clip(column_ref[group, rows, :] - start, -1, SPAN).astype(F32)
        hot = [
            jnp.where(
                jnp.broadcast_to(columns[:, j : j + 1], (BLOCK, SPAN)).astype(BF16) == lanes,
                jnp.ones((), BF16),
                jnp.zeros((), BF16),
            )
            for j in range(PER)
        ]
        at = pl.ds(pl.multiple_of(start, 16), SPAN)
        span = jnp.concatenate([window_ref[c, at, :] for c in range(window_ref.shape[0])], axis=1)
        return jnp.dot(jnp.concatenate(hot, axis=0), span, preferred_element_type=F32).astype(BF16)

    def first(block, _):
        rows = pl.ds(pl.multiple_of(block * BLOCK, BLOCK), BLOCK)
        for group in range(GROUPS):
            result = picked(group, rows, scalars_ref[group * blocks + block])
            for j in range(PER):
                store(group, j, rows, result[j * BLOCK : (j + 1) * BLOCK])
        return 0

    lax.fori_loop(0, blocks, first, 0, unroll=2)

    def rest(at, _):
        group, block = at // blocks, at % blocks
        rows = pl.ds(pl.multiple_of(block * BLOCK, BLOCK), BLOCK)

        def more(step, _):
            result = picked(group, rows, scalars_ref[at] + step * SPAN)
            for j in range(PER):
                add(group, j, rows, result[j * BLOCK : (j + 1) * BLOCK])
            return 0

        lax.fori_loop(1, scalars_ref[GROUPS * blocks + at], more, 0)
        return 0

    lax.fori_loop(0, GROUPS * blocks, rest, 0)


def turn(scratch_ref, value, shards, scalars_ref, at):
    half = value.shape[0] // 2
    size = half // shards
    scratch_ref[0] = value
    place, rep = scalars_ref[at + 1], scalars_ref[at + 2]
    for core in range(2):
        for step in range(shards):
            source = (rep + core) % 2 * half + (place ^ step) * size
            target = core * half + step * size
            scratch_ref[1, target : target + size] = scratch_ref[
                0, pl.ds(pl.multiple_of(source, size), size)
            ]


def conv_kernel(chans, shards, scale, scalars_ref, index_ref, weight_hbm, cotangent_hbm, *refs):
    parts, refs = [refs[3 * i : 3 * i + 3] for i in range(chans)], refs[3 * chans :]
    out_hbm, grad_hbm, keep_hbm, send_hbm = refs[:4]
    window_ref, column_ref, picked_ref, conv_ref, scratch_ref = refs[4:9]
    weight_ref, cotangent_ref, out_ref, grad_ref, keep_ref, send_ref = refs[9:15]
    window_sems, sems, keep_sems, send_sems = refs[15:]
    rows = index_ref.shape[2]
    blocks = rows // BLOCK
    width = chans * window_ref.shape[2]
    channels = weight_ref.shape[1]
    chan = scalars_ref[2 * GROUPS * blocks]
    rep = scalars_ref[2 * GROUPS * blocks + 2]
    slots = (chan, 1 - chan) if chans == 2 else range(chans)
    copies = window_copies(window_ref, parts, slots, rep, window_sems)
    weight_copy = pltpu.make_async_copy(weight_hbm, weight_ref, sems.at[0])
    cotangent_copy = pltpu.make_async_copy(cotangent_hbm, cotangent_ref, sems.at[1])
    out_copy = pltpu.make_async_copy(out_ref, out_hbm, sems.at[2])
    grad_copy = pltpu.make_async_copy(grad_ref, grad_hbm, sems.at[3])
    for copy in copies:
        copy.start()
    weight_copy.start()
    cotangent_copy.start()
    window_ref[:, 3 * rows :, :] = jnp.zeros((chans, SPAN, channels), BF16)
    for group in range(GROUPS):
        column_ref[group] = index_ref[group].T
    for copy in copies:
        copy.wait()

    def store(group, j, at, value):
        lane = j % 3 * width
        picked_ref[group * 3 + j // 3, at, lane : lane + width] = value

    def add(group, j, at, value):
        lane = j % 3 * width
        picked_ref[group * 3 + j // 3, at, lane : lane + width] += value

    gather(scalars_ref, column_ref, window_ref, blocks, store, add)

    def multiply(three, _):
        weights = jnp.concatenate([weight_ref[three * 3 + j] for j in range(3)], axis=1)
        term = lax.dot_general(picked_ref[three], weights, NT, preferred_element_type=F32)
        conv_ref[...] += term
        return 0

    conv_ref[...] = jnp.zeros_like(conv_ref)
    weight_copy.wait()
    lax.fori_loop(0, 9, multiply, 0, unroll=3)
    conv = conv_ref[...].T
    cotangent_copy.wait()
    sigma = jax.nn.sigmoid(conv)
    out_ref[...] = (conv * sigma).astype(BF16)
    grad = cotangent_ref[...].astype(F32) * (sigma * (1.0 + conv * (1.0 - sigma)))
    grad_ref[...] = grad.T.astype(BF16)
    out_copy.start()
    grad_copy.start()
    turn(scratch_ref, grad.astype(BF16), shards, scalars_ref, 2 * GROUPS * blocks)
    half = channels // 2
    size = half // shards

    def leave(three):
        at = pl.ds(three * 3, 3)
        return (
            pltpu.make_async_copy(keep_ref.at[:, at], keep_hbm.at[:, at], keep_sems.at[three]),
            pltpu.make_async_copy(send_ref.at[:, at], send_hbm.at[:, at], send_sems.at[three]),
        )

    def weigh(three, _):
        term = jnp.dot(scratch_ref[1], picked_ref[three], preferred_element_type=F32) * scale
        for j in range(3):
            both = term[:, j * width : (j + 1) * width].astype(BF16)
            for step in range(shards):
                at = step * size
                keep_ref[step, three * 3 + j] = both[at : at + size]
                send_ref[step, three * 3 + j] = both[half + at : half + at + size]
        for copy in leave(three):
            copy.start()
        return 0

    lax.fori_loop(0, 9, weigh, 0, unroll=3)

    def finish(three, _):
        for copy in leave(three):
            copy.wait()
        return 0

    lax.fori_loop(0, 9, finish, 0)
    out_copy.wait()
    grad_copy.wait()


def coarse_grad_kernel(scalars_ref, index_ref, weight_hbm, *refs):
    part, refs = refs[:3], refs[3:]
    mine_ref, other_ref, window_ref, column_ref, picked_ref, total_ref, weight_ref, sems = refs
    rows = index_ref.shape[2]
    blocks = rows // BLOCK
    offsets, channels, width = weight_ref.shape
    chan = scalars_ref[2 * GROUPS * blocks]
    rep = scalars_ref[2 * GROUPS * blocks + 2]
    copies = window_copies(window_ref, [part], (0,), rep, sems)
    weight_copy = pltpu.make_async_copy(weight_hbm, weight_ref, sems.at[3])
    for copy in copies:
        copy.start()
    weight_copy.start()
    window_ref[0, 3 * rows :, :] = jnp.zeros((SPAN, channels), BF16)
    for group in range(GROUPS):
        column_ref[group] = index_ref[group].T
    for copy in copies:
        copy.wait()

    def store(group, j, at, value):
        lane = (PER - 1 - j) * channels
        picked_ref[GROUPS - 1 - group, at, lane : lane + channels] = value

    def add(group, j, at, value):
        lane = (PER - 1 - j) * channels
        picked_ref[GROUPS - 1 - group, at, lane : lane + channels] += value

    gather(scalars_ref, column_ref, window_ref, blocks, store, add)
    weight_copy.wait()
    result = None
    for group in range(GROUPS):
        weights = weight_ref[group * PER : (group + 1) * PER].reshape(PER * channels, width)
        term = jnp.dot(picked_ref[group], weights, preferred_element_type=F32)
        result = term if result is None else result + term
    result = result.T
    chans = width // channels
    for at in range(chans):
        total_ref[at] = result[at * channels : (at + 1) * channels]
    mine_ref[...] = total_ref[chan]
    for step in range(1, chans):
        other_ref[step - 1] = total_ref[lax.rem(chan + step, chans)].astype(BF16)


def pre_grad_kernel(shards, scale, scalars_ref, children_hbm, mask_ref, slope_ref, mine_ref, *refs):
    others, refs = refs[:-6], refs[-6:]
    grad_ref, keep_ref, send_ref, scratch_ref, children_ref, sems = refs
    copies = octant_copies(children_hbm, children_ref, sems)
    total = mine_ref[...]
    for other in others:
        total = total + other[...].astype(F32)
    grad = (total * slope_ref[...]).astype(BF16)
    grad_ref[...] = grad
    blocks = grad.shape[1] // BLOCK
    turn(scratch_ref, grad, shards, scalars_ref, 2 * GROUPS * blocks)
    half = grad.shape[0] // 2
    size = half // shards
    for o, copy in enumerate(copies):
        copy.wait()
        masked = children_ref[o] * mask_ref[o : o + 1, :].astype(F32).astype(BF16)
        term = lax.dot_general(scratch_ref[1], masked, NT, preferred_element_type=F32) * scale
        both = term.astype(BF16)
        for step in range(shards):
            at = step * size
            keep_ref[step, o] = both[at : at + size]
            send_ref[step, o] = both[half + at : half + at + size]


def children_kernel(mask_ref, *refs):
    out_hbm, out_ref, sems = refs[-3:]
    count = (len(refs) - 3) // 2
    grads, weights = refs[:count], refs[count:-3]
    copies = []
    for o in range(out_ref.shape[0]):
        total = None
        for grad, weight in zip(grads, weights):
            term = jnp.dot(weight[o], grad[...], preferred_element_type=F32)
            term = term.astype(BF16).astype(F32)
            total = term if total is None else total + term
        out_ref[o] = (total * mask_ref[o : o + 1, :].astype(F32)).astype(BF16)
        copies.append(pltpu.make_async_copy(out_ref.at[o], out_hbm.at[o], sems.at[o]))
        copies[-1].start()
    for copy in copies:
        copy.wait()


def spread_kernel(slots, shards, scalars_ref, *refs):
    count = len(slots)
    parts = refs[:count]
    out_hbm, narrow_ref, wide_ref, in_sems, out_sems = refs[-5:]
    half = out_hbm.shape[1] // 2
    size = half // shards
    place, rep = scalars_ref[0], scalars_ref[1]
    arriving = [
        pltpu.make_async_copy(part, narrow_ref.at[i], in_sems.at[i])
        for i, part in enumerate(parts)
    ]
    for copy in arriving:
        copy.start()
    leaving = []
    for i, (core, step) in enumerate(slots):
        row = (rep + core) % 2 * half + (place ^ step) * size
        target = out_hbm.at[:, pl.ds(pl.multiple_of(row, size), size), :]
        arriving[i].wait()
        wide_ref[i] = narrow_ref[i].astype(F32)
        leaving.append(pltpu.make_async_copy(wide_ref.at[i], target, out_sems.at[i]))
        leaving[-1].start()
    for copy in leaving:
        copy.wait()


def apart(shard, by):
    return lax.ppermute(shard, "curve", [(i, i ^ by) for i in range(lax.axis_size("curve"))])


def added(*terms):
    return sum(term.astype(F32) for term in terms).astype(BF16)


def sum_over_curve(total, beside):
    terms = [apart(total[by], by) for by in range(1, 4)]
    own = added(after(total[0], beside), *terms)
    across = apart(own, 2)
    return [own, apart(own, 1), across, apart(across, 1)]


def spread(parts, shards, place, base=None):
    slots = list(parts)
    arrays = [parts[slot] for slot in slots]
    count, size, width = arrays[0].shape
    held = [] if base is None else [base]
    return pl.pallas_call(
        functools.partial(spread_kernel, slots, shards),
        out_shape=jax.ShapeDtypeStruct((count, 2 * shards * size, width), F32),
        in_specs=SMEM + anywhere(len(arrays) + len(held)),
        out_specs=anywhere(1)[0],
        scratch_shapes=[
            pltpu.VMEM((len(arrays), count, size, width), BF16),
            pltpu.VMEM((len(arrays), count, size, width), F32),
            pltpu.SemaphoreType.DMA((len(arrays),)),
            pltpu.SemaphoreType.DMA((len(arrays),)),
        ],
        input_output_aliases={1 + len(arrays): 0} if held else {},
        compiler_params=pltpu.CompilerParams(vmem_limit_bytes=VMEM_LIMIT),
        cost_estimate=pl.CostEstimate(flops=0, bytes_accessed=0, transcendentals=0),
    )(place, *arrays, *held)


def after(value, *earlier):
    return lax.optimization_barrier((value, *earlier))[0]


def body(children, child_mask, neighbours, down_weight, conv_weight, cotangent):
    octants, fine, rows = children.shape
    offsets, channels, width = conv_weight.shape
    blocks = rows // BLOCK
    chans = lax.axis_size("chan")
    chan = lax.axis_index("chan")
    rep = lax.axis_index("rep")
    curve = lax.axis_index("curve")
    pieces = lax.axis_size(PIECES)
    position = lax.axis_index(PIECES)
    scale = 1.0 / (rows * pieces) ** 0.5
    shape = jax.ShapeDtypeStruct
    half = channels // 2
    shards = 4 if lax.axis_size("curve") == 4 and half % 64 == 0 else 1
    size = half // shards

    coarse, slope = call(
        down_kernel,
        [shape((rows, channels), BF16), shape((channels, rows), F32)],
        anywhere(1) + vmem(2),
        [pltpu.VMEM(children.shape, BF16), pltpu.SemaphoreType.DMA((octants,))],
    )(children, child_mask, down_weight)

    valid = neighbours >= 0
    local = jnp.where(valid, neighbours - (position - 1) * rows, -(2**20))
    tiles = local.reshape(GROUPS, PER, blocks, BLOCK)
    low = jnp.min(jnp.where(tiles < 0, 2**20, tiles), axis=(1, 3))
    high = jnp.max(tiles, axis=(1, 3)) + 1
    low = jnp.where(high <= 0, 0, low // 16 * 16)
    steps = jnp.maximum(1, (high - low + SPAN - 1) // SPAN)
    place = jnp.stack([curve if shards == 4 else 0 * curve, rep]).astype(jnp.int32)
    scalars = jnp.concatenate(
        [low.reshape(-1), steps.reshape(-1), chan[None].astype(jnp.int32), place]
    )
    index = jnp.pad(
        local.reshape(GROUPS, PER, rows),
        ((0, 0), (0, 16 - PER), (0, 0)),
        constant_values=-(2**20),
    )

    if chans == 2:
        parts = [coarse, swapped(coarse, "chan")]
    else:
        every = lax.all_gather(coarse, "chan", axis=0)
        parts = [every[i] for i in range(chans)]
    windows = [array for part in parts for array in [part] + met(part)]

    mine_fine = fine // chans
    turned = down_weight.transpose(0, 2, 1)
    weights = []
    for by in range(chans):
        start = lax.rem(chan + by, chans) * mine_fine
        part = lax.dynamic_slice_in_dim(turned, start, mine_fine, axis=1)
        weights.append(part)
    scalars = after(scalars, *weights)

    features_out, conv_grad, keep, send = call(
        functools.partial(conv_kernel, chans, shards, scale),
        [
            shape((channels, rows), BF16),
            shape((rows, channels), BF16),
            shape((shards, offsets, size, width), BF16),
            shape((shards, offsets, size, width), BF16),
        ],
        SMEM + vmem(1) + anywhere(2 + 3 * chans),
        [
            pltpu.VMEM((chans, 3 * rows + SPAN, channels), BF16),
            pltpu.VMEM((GROUPS, rows, 16), jnp.int32),
            pltpu.VMEM((9, rows, 3 * width), BF16),
            pltpu.VMEM((rows, channels), F32),
            pltpu.VMEM((2, channels, rows), BF16),
            pltpu.VMEM((offsets, channels, width), BF16),
            pltpu.VMEM((channels, rows), BF16),
            pltpu.VMEM((channels, rows), BF16),
            pltpu.VMEM((rows, channels), BF16),
            pltpu.VMEM((shards, offsets, size, width), BF16),
            pltpu.VMEM((shards, offsets, size, width), BF16),
            pltpu.SemaphoreType.DMA((3 * chans,)),
            pltpu.SemaphoreType.DMA((4,)),
            pltpu.SemaphoreType.DMA((9,)),
            pltpu.SemaphoreType.DMA((9,)),
        ],
        anywhere(4),
    )(scalars, index, conv_weight, cotangent, *windows)

    near = met(conv_grad)
    received = swapped(send, "rep")
    total = [added(after(keep[i], *near), received[i]) for i in range(shards)]
    mine, others = call(
        coarse_grad_kernel,
        [shape((channels, rows), F32), shape((chans - 1, channels, rows), BF16)],
        SMEM + vmem(1) + anywhere(4),
        [
            pltpu.VMEM((1, 3 * rows + SPAN, channels), BF16),
            pltpu.VMEM((GROUPS, rows, 16), jnp.int32),
            pltpu.VMEM((GROUPS, rows, PER * channels), BF16),
            pltpu.VMEM((chans, channels, rows), F32),
            pltpu.VMEM((offsets, channels, width), BF16),
            pltpu.SemaphoreType.DMA((4,)),
        ],
    )(after(scalars, *total), index, conv_weight, conv_grad, *near)
    if shards == 4:
        sums = sum_over_curve(total, mine)
    else:
        sums = [lax.psum(total[0], "curve")]
    received = [
        lax.ppermute(others[by - 1], "chan", [(i, (i + by) % chans) for i in range(chans)])
        for by in range(1, chans)
    ]
    weights = weights[:1] + [
        lax.ppermute(
            after(weights[by], *received), "chan", [(i, (i + by) % chans) for i in range(chans)]
        )
        for by in range(1, chans)
    ]
    pre_grad, keep, send = call(
        functools.partial(pre_grad_kernel, shards, scale),
        [
            shape((channels, rows), BF16),
            shape((shards, octants, size, fine), BF16),
            shape((shards, octants, size, fine), BF16),
        ],
        SMEM + anywhere(1) + vmem(3 + len(received)),
        [
            pltpu.VMEM((2, channels, rows), BF16),
            pltpu.VMEM(children.shape, BF16),
            pltpu.SemaphoreType.DMA((octants,)),
        ],
    )(after(scalars, *sums[:2]), children, child_mask, slope, mine, *received)

    grads = [pre_grad] + [
        lax.ppermute(pre_grad, "chan", [(i, (i + by) % chans) for i in range(chans)])
        for by in range(1, chans)
    ]
    children_grad = call(
        children_kernel,
        shape((octants, mine_fine, rows), BF16),
        vmem(1 + 2 * chans),
        [pltpu.VMEM((octants, mine_fine, rows), BF16), pltpu.SemaphoreType.DMA((octants,))],
        anywhere(1)[0],
    )(child_mask, *grads, *weights)
    total = added(after(keep, *sums[2:3]), swapped(send, "rep"))
    if shards == 4:
        terms = [apart(total[by], by) for by in range(1, 4)]
        own = added(after(total[0], sums[3], children_grad), *terms)
        mine = [own] + [apart(own, by) for by in range(1, 4)]
    else:
        mine = [lax.psum(total[0], "curve")]
    theirs = swapped(jnp.stack(mine), "rep")
    parts = {(0, i): part for i, part in enumerate(mine)}
    parts.update({(1, i): theirs[i] for i in range(shards)})
    down_weight_grad = spread(parts, shards, place)

    parts = {(0, i): part for i, part in enumerate(sums)}
    parts.update({(1, i): swapped(part, "rep") for i, part in enumerate(sums)})
    last = [slot for slot in parts if slot in ((0, 3), (1, 2), (1, 3))]
    early = {slot: part for slot, part in parts.items() if slot not in last}
    conv_weight_grad = spread(early, shards, after(place, children_grad))
    if last:
        late = {slot: parts[slot] for slot in last}
        conv_weight_grad = spread(
            late, shards, after(place, down_weight_grad), conv_weight_grad
        )
    return (features_out, children_grad, conv_weight_grad, down_weight_grad)


def solution(mesh):
    in_specs = (
        P(None, None, ("snap", "curve", "rep")),
        P(None, ("snap", "curve", "rep")),
        P(None, ("snap", "curve", "rep")),
        P(None, "chan", None),
        P(None, "chan", None),
        P("chan", ("snap", "curve", "rep")),
    )
    out_specs = (
        P("chan", ("snap", "curve", "rep")),
        P(None, "chan", ("snap", "curve", "rep")),
        P("snap", "chan", None),
        P("snap", "chan", None),
    )
    return jax.shard_map(body, mesh=mesh, in_specs=in_specs, out_specs=out_specs, check_vma=False)
```

```python
import functools

import jax
import jax.numpy as jnp
from jax import lax
from jax.experimental import pallas as pl
from jax.experimental.pallas import tpu as pltpu
from jax.sharding import PartitionSpec as P

BLOCK = 128
SPAN = 256
GROUPS = 3
PER = 9
VMEM_LIMIT = 56 * 1024 * 1024
PIECES = ("curve", "rep")
F32 = jnp.float32
BF16 = jnp.bfloat16
NOWHERE = -(2**20)
NT = (((1,), (1,)), ((), ()))


def silu_slope(value):
    sigma = jax.nn.sigmoid(value)
    return sigma * (1.0 + value * (1.0 - sigma))


def met(shard):
    devices = lax.axis_size(PIECES)
    pairs = [(i, i + 1) for i in range(1, devices - 1, 2)]
    pairs += [(j, i) for i, j in pairs]
    return [lax.ppermute(shard, PIECES, pairs), swapped(shard, "rep")]


def swapped(shard, axis):
    return lax.ppermute(shard, axis, [(0, 1), (1, 0)])


def call(kernel, out_shape, in_specs, scratch, out_specs=None):
    options = {} if out_specs is None else {"out_specs": out_specs}
    return pl.pallas_call(
        kernel,
        out_shape=out_shape,
        in_specs=in_specs,
        scratch_shapes=scratch,
        compiler_params=pltpu.CompilerParams(vmem_limit_bytes=VMEM_LIMIT),
        cost_estimate=pl.CostEstimate(flops=0, bytes_accessed=0, transcendentals=0),
        **options,
    )


def anywhere(count):
    return [pl.BlockSpec(memory_space=pl.ANY)] * count


def vmem(count):
    return [pl.BlockSpec(memory_space=pltpu.VMEM)] * count


SMEM = [pl.BlockSpec(memory_space=pltpu.SMEM)]


def down_kernel(children_ref, mask_ref, weight_ref, coarse_ref, slope_ref):
    octants = children_ref.shape[0]
    total = None
    for o in range(0, octants, 2):
        masked = jnp.concatenate(
            [
                children_ref[o + j] * mask_ref[o + j : o + j + 1, :].astype(F32).astype(BF16)
                for j in range(2)
            ],
            axis=0,
        )
        weights = jnp.concatenate([weight_ref[o], weight_ref[o + 1]], axis=1)
        term = jnp.dot(weights, masked, preferred_element_type=F32)
        total = term if total is None else total + term
    slope_ref[...] = silu_slope(total)
    coarse_ref[...] = (total * jax.nn.sigmoid(total)).T.astype(BF16)


def index_kernel(shards, neighbours_ref, index_ref, scalars_ref):
    offsets, rows = neighbours_ref.shape
    blocks = rows // BLOCK
    curve, rep = lax.axis_index("curve"), lax.axis_index("rep")
    names = neighbours_ref[...]
    local = jnp.where(names >= 0, names - (curve * 2 + rep - 1) * rows, NOWHERE)
    index_ref[...] = jnp.full(index_ref.shape, NOWHERE, jnp.int32)
    for group in range(GROUPS):
        part = local[group * PER : (group + 1) * PER]
        index_ref[group, :PER, :] = part
        lows = jnp.min(jnp.where(part < 0, -NOWHERE, part), axis=0, keepdims=True)
        highs = jnp.max(part, axis=0, keepdims=True)
        for block in range(blocks):
            at = slice(block * BLOCK, (block + 1) * BLOCK)
            low, high = jnp.min(lows[:, at]), jnp.max(highs[:, at]) + 1
            low = jnp.where(high <= 0, 0, low // 16 * 16)
            steps = jnp.maximum(1, (high - low + SPAN - 1) // SPAN)
            scalars_ref[group * blocks + block] = low
            scalars_ref[(GROUPS + group) * blocks + block] = steps
    last = 2 * GROUPS * blocks
    scalars_ref[last] = lax.axis_index("chan")
    scalars_ref[last + 1] = curve if shards > 1 else 0
    scalars_ref[last + 2] = rep


def window_copies(window_ref, parts, slots, rep, semaphores):
    rows = parts[0][0].shape[0]
    places = (rows, rep * 2 * rows, (1 - rep) * 2 * rows)
    copies = []
    for part, slot in zip(parts, slots):
        for source, place in zip(part, places):
            target = window_ref.at[slot, pl.ds(pl.multiple_of(place, 16), rows)]
            copies.append(pltpu.make_async_copy(source, target, semaphores.at[len(copies)]))
    return copies


def gather(scalars_ref, column_ref, window_ref, blocks, store, add):
    lanes = lax.broadcasted_iota(jnp.int32, (BLOCK, SPAN), 1).astype(F32).astype(BF16)

    def picked(group, rows, start):
        columns = jnp.clip(column_ref[group, rows, :] - start, -1, SPAN).astype(F32)
        hot = [
            jnp.where(
                jnp.broadcast_to(columns[:, j : j + 1], (BLOCK, SPAN)).astype(BF16) == lanes,
                jnp.ones((), BF16),
                jnp.zeros((), BF16),
            )
            for j in range(PER)
        ]
        at = pl.ds(pl.multiple_of(start, 16), SPAN)
        span = jnp.concatenate([window_ref[c, at, :] for c in range(window_ref.shape[0])], axis=1)
        return jnp.dot(jnp.concatenate(hot, axis=0), span, preferred_element_type=F32).astype(BF16)

    def first(block, _):
        rows = pl.ds(pl.multiple_of(block * BLOCK, BLOCK), BLOCK)
        for group in range(GROUPS):
            result = picked(group, rows, scalars_ref[group * blocks + block])
            for j in range(PER):
                store(group, j, rows, result[j * BLOCK : (j + 1) * BLOCK])
        return 0

    lax.fori_loop(0, blocks, first, 0, unroll=2)

    def rest(at, _):
        group, block = at // blocks, at % blocks
        rows = pl.ds(pl.multiple_of(block * BLOCK, BLOCK), BLOCK)

        def more(step, _):
            result = picked(group, rows, scalars_ref[at] + step * SPAN)
            for j in range(PER):
                add(group, j, rows, result[j * BLOCK : (j + 1) * BLOCK])
            return 0

        lax.fori_loop(1, scalars_ref[GROUPS * blocks + at], more, 0)
        return 0

    lax.fori_loop(0, GROUPS * blocks, rest, 0)


def turn(scratch_ref, value, shards, scalars_ref, at):
    half = value.shape[0] // 2
    size = half // shards
    scratch_ref[0] = value
    place = 0 if shards == 1 else scalars_ref[at + 1]
    rep = scalars_ref[at + 2]
    for core in range(2):
        for step in range(shards):
            source = (rep + core) % 2 * half + (place ^ step) * size
            target = core * half + step * size
            scratch_ref[1, target : target + size] = scratch_ref[
                0, pl.ds(pl.multiple_of(source, size), size)
            ]


def conv_kernel(chans, shards, scalars_ref, index_ref, weight_hbm, cotangent_hbm, *refs):
    parts, refs = [refs[3 * i : 3 * i + 3] for i in range(chans)], refs[3 * chans :]
    out_hbm, grad_hbm, turned_hbm, picked_hbm = refs[:4]
    window_ref, column_ref, picked_ref, conv_ref, scratch_ref = refs[4:9]
    weight_ref, cotangent_ref, out_ref, grad_ref = refs[9:13]
    window_sems, sems, picked_sems = refs[13:]
    rows = index_ref.shape[2]
    blocks = rows // BLOCK
    width = chans * window_ref.shape[2]
    channels = weight_ref.shape[1]
    chan = scalars_ref[2 * GROUPS * blocks]
    rep = scalars_ref[2 * GROUPS * blocks + 2]
    slots = (chan, 1 - chan) if chans == 2 else range(chans)
    copies = window_copies(window_ref, parts, slots, rep, window_sems)
    weight_copy = pltpu.make_async_copy(weight_hbm, weight_ref, sems.at[0])
    cotangent_copy = pltpu.make_async_copy(cotangent_hbm, cotangent_ref, sems.at[1])
    out_copy = pltpu.make_async_copy(out_ref, out_hbm, sems.at[2])
    grad_copy = pltpu.make_async_copy(grad_ref, grad_hbm, sems.at[3])
    turned_copy = pltpu.make_async_copy(scratch_ref.at[1], turned_hbm, sems.at[4])
    picked_copies = [
        pltpu.make_async_copy(picked_ref.at[i], picked_hbm.at[i], picked_sems.at[i])
        for i in range(9)
    ]
    for copy in copies:
        copy.start()
    weight_copy.start()
    cotangent_copy.start()
    window_ref[:, 3 * rows :, :] = jnp.zeros((chans, SPAN, channels), BF16)
    for group in range(GROUPS):
        column_ref[group] = index_ref[group].T
    for copy in copies:
        copy.wait()

    def store(group, j, at, value):
        lane = j % 3 * width
        picked_ref[group * 3 + j // 3, at, lane : lane + width] = value

    def add(group, j, at, value):
        lane = j % 3 * width
        picked_ref[group * 3 + j // 3, at, lane : lane + width] += value

    gather(scalars_ref, column_ref, window_ref, blocks, store, add)
    for copy in picked_copies:
        copy.start()

    def multiply(three, _):
        weights = jnp.concatenate([weight_ref[three * 3 + j] for j in range(3)], axis=1)
        term = lax.dot_general(picked_ref[three], weights, NT, preferred_element_type=F32)
        conv_ref[...] += term
        return 0

    conv_ref[...] = jnp.zeros_like(conv_ref)
    weight_copy.wait()
    lax.fori_loop(0, 9, multiply, 0, unroll=3)
    conv = conv_ref[...].T
    cotangent_copy.wait()
    sigma = jax.nn.sigmoid(conv)
    out_ref[...] = (conv * sigma).astype(BF16)
    grad = cotangent_ref[...].astype(F32) * (sigma * (1.0 + conv * (1.0 - sigma)))
    grad_ref[...] = grad.T.astype(BF16)
    out_copy.start()
    grad_copy.start()
    turn(scratch_ref, grad.astype(BF16), shards, scalars_ref, 2 * GROUPS * blocks)
    turned_copy.start()
    for copy in [out_copy, grad_copy, turned_copy] + picked_copies:
        copy.wait()


def weight_kernel(shards, scale, grad_ref, picked_hbm, *refs):
    keep_hbm, send_hbm, picked_ref, keep_ref, send_ref, picked_sems, keep_sems, send_sems = refs
    width = picked_ref.shape[2] // 3
    half = grad_ref.shape[0] // 2
    size = half // shards

    def arrive(three):
        return pltpu.make_async_copy(
            picked_hbm.at[three], picked_ref.at[three], picked_sems.at[three]
        )

    def leave(three):
        at = pl.ds(three * 3, 3)
        return (
            pltpu.make_async_copy(keep_ref.at[:, at], keep_hbm.at[:, at], keep_sems.at[three]),
            pltpu.make_async_copy(send_ref.at[:, at], send_hbm.at[:, at], send_sems.at[three]),
        )

    for three in range(9):
        arrive(three).start()

    def weigh(three, _):
        arrive(three).wait()
        term = jnp.dot(grad_ref[...], picked_ref[three], preferred_element_type=F32) * scale
        for j in range(3):
            both = term[:, j * width : (j + 1) * width].astype(BF16)
            for step in range(shards):
                at = step * size
                keep_ref[step, three * 3 + j] = both[at : at + size]
                send_ref[step, three * 3 + j] = both[half + at : half + at + size]
        for copy in leave(three):
            copy.start()
        return 0

    lax.fori_loop(0, 9, weigh, 0, unroll=3)

    def finish(three, _):
        for copy in leave(three):
            copy.wait()
        return 0

    lax.fori_loop(0, 9, finish, 0)


def coarse_grad_kernel(scalars_ref, index_ref, weight_hbm, *refs):
    part, refs = refs[:3], refs[3:]
    mine_ref, other_ref, window_ref, column_ref, picked_ref, total_ref, weight_ref, sems = refs
    rows = index_ref.shape[2]
    blocks = rows // BLOCK
    offsets, channels, width = weight_ref.shape
    chan = scalars_ref[2 * GROUPS * blocks]
    rep = scalars_ref[2 * GROUPS * blocks + 2]
    copies = window_copies(window_ref, [part], (0,), rep, sems)
    weight_copy = pltpu.make_async_copy(weight_hbm, weight_ref, sems.at[3])
    for copy in copies:
        copy.start()
    weight_copy.start()
    window_ref[0, 3 * rows :, :] = jnp.zeros((SPAN, channels), BF16)
    for group in range(GROUPS):
        column_ref[group] = index_ref[group].T
    for copy in copies:
        copy.wait()

    def store(group, j, at, value):
        lane = (PER - 1 - j) * channels
        picked_ref[GROUPS - 1 - group, at, lane : lane + channels] = value

    def add(group, j, at, value):
        lane = (PER - 1 - j) * channels
        picked_ref[GROUPS - 1 - group, at, lane : lane + channels] += value

    gather(scalars_ref, column_ref, window_ref, blocks, store, add)
    weight_copy.wait()
    result = None
    for group in range(GROUPS):
        weights = weight_ref[group * PER : (group + 1) * PER].reshape(PER * channels, width)
        term = jnp.dot(picked_ref[group], weights, preferred_element_type=F32)
        result = term if result is None else result + term
    result = result.T
    chans = width // channels
    for at in range(chans):
        total_ref[at] = result[at * channels : (at + 1) * channels]
    mine_ref[...] = total_ref[chan]
    for step in range(1, chans):
        other_ref[step - 1] = total_ref[lax.rem(chan + step, chans)].astype(BF16)


def pre_grad_kernel(scale, scalars_ref, children_ref, mask_ref, slope_ref, mine_ref, *refs):
    others, (grad_ref, keep_ref, send_ref, scratch_ref) = refs[:-4], refs[-4:]
    total = mine_ref[...]
    for other in others:
        total = total + other[...].astype(F32)
    grad = (total * slope_ref[...]).astype(BF16)
    grad_ref[...] = grad
    blocks = grad.shape[1] // BLOCK
    turn(scratch_ref, grad, 1, scalars_ref, 2 * GROUPS * blocks)
    half = grad.shape[0] // 2
    tiles = half // 16
    for o in range(0, children_ref.shape[0], 2):
        masked = jnp.concatenate(
            [
                children_ref[o + j] * mask_ref[o + j : o + j + 1, :].astype(F32).astype(BF16)
                for j in range(2)
            ],
            axis=0,
        )
        term = lax.dot_general(scratch_ref[1], masked, NT, preferred_element_type=F32) * scale
        both = term.astype(BF16)
        for tile in range(tiles):
            at = tile * 16
            keep_ref[o // 2 * tiles + tile] = both[at : at + 16]
            send_ref[o // 2 * tiles + tile] = both[half + at : half + at + 16]


def cut_kernel(weight_ref, out_ref, scratch_ref):
    octants, fine, _ = scratch_ref.shape
    chans = out_ref.shape[0]
    size = fine // chans
    chan = lax.axis_index("chan")
    for o in range(octants):
        scratch_ref[o] = weight_ref[o].T
    for by in range(chans):
        at = pl.ds(pl.multiple_of((chan + by) % chans * size, size), size)
        for o in range(octants):
            out_ref[by, o] = scratch_ref[o, at, :]


def empty_kernel(out_ref):
    pass


def children_kernel(mask_ref, *refs):
    out_hbm, out_ref, sems = refs[-3:]
    count = (len(refs) - 3) // 2
    grads, weights = refs[:count], refs[count:-3]
    copies = []
    for o in range(out_ref.shape[0]):
        total = None
        for grad, weight in zip(grads, weights):
            term = jnp.dot(weight[o], grad[...], preferred_element_type=F32)
            term = term.astype(BF16).astype(F32)
            total = term if total is None else total + term
        out_ref[o] = (total * mask_ref[o : o + 1, :].astype(F32)).astype(BF16)
        copies.append(pltpu.make_async_copy(out_ref.at[o], out_hbm.at[o], sems.at[o]))
        copies[-1].start()
    for copy in copies:
        copy.wait()


def join_kernel(scalars_ref, mine_ref, theirs_ref, out_ref):
    octants, channels, fine = out_ref.shape
    half = channels // 2
    tiles = half // 16
    rep = scalars_ref[scalars_ref.shape[0] - 1]
    for core, source in ((rep, mine_ref), (1 - rep, theirs_ref)):
        for o in range(0, octants, 2):
            for tile in range(tiles):
                value = source[o // 2 * tiles + tile].astype(F32)
                at = pl.ds(pl.multiple_of(core * half + tile * 16, 16), 16)
                out_ref[o, at, :] = value[:, :fine]
                out_ref[o + 1, at, :] = value[:, fine:]


def apart(shard, by):
    return lax.ppermute(shard, "curve", [(i, i ^ by) for i in range(lax.axis_size("curve"))])


def added(*terms):
    return sum(term.astype(F32) for term in terms).astype(BF16)


def sum_over_curve(total, beside):
    terms = [apart(total[by], by) for by in range(1, 4)]
    own = added(after(total[0], beside), *terms)
    across = apart(own, 2)
    return [own, apart(own, 1), across, apart(across, 1)]


def after(value, *earlier):
    return lax.optimization_barrier((value, *earlier))[0]


def body(children, child_mask, neighbours, down_weight, conv_weight, cotangent):
    octants, fine, rows = children.shape
    offsets, channels, width = conv_weight.shape
    blocks = rows // BLOCK
    chans = lax.axis_size("chan")
    chan = lax.axis_index("chan")
    rep = lax.axis_index("rep")
    curve = lax.axis_index("curve")
    pieces = lax.axis_size(PIECES)
    scale = 1.0 / (rows * pieces) ** 0.5
    shape = jax.ShapeDtypeStruct
    half = channels // 2
    shards = 4 if lax.axis_size("curve") == 4 and half % 64 == 0 else 1
    size = half // shards

    coarse, slope = call(
        down_kernel,
        [shape((rows, channels), BF16), shape((channels, rows), F32)],
        vmem(3),
        [],
    )(children, child_mask, down_weight)

    if chans == 2:
        parts = [coarse, swapped(coarse, "chan")]
    else:
        every = lax.all_gather(coarse, "chan", axis=0)
        parts = [every[i] for i in range(chans)]
    windows = [array for part in parts for array in [part] + met(part)]
    mine_fine = fine // chans
    cut = call(
        cut_kernel,
        shape((chans, octants, mine_fine, channels), BF16),
        vmem(1),
        [pltpu.VMEM((octants, fine, channels), BF16)],
    )(after(down_weight, coarse))
    index, scalars = call(
        functools.partial(index_kernel, shards),
        [shape((GROUPS, 16, rows), jnp.int32), shape((2 * GROUPS * blocks + 3,), jnp.int32)],
        vmem(1),
        [],
        vmem(1) + SMEM,
    )(after(neighbours, parts[1], cut))

    features_out, conv_grad, turned, picked = call(
        functools.partial(conv_kernel, chans, shards),
        [
            shape((channels, rows), BF16),
            shape((rows, channels), BF16),
            shape((channels, rows), BF16),
            shape((9, rows, 3 * width), BF16),
        ],
        SMEM + vmem(1) + anywhere(2 + 3 * chans),
        [
            pltpu.VMEM((chans, 3 * rows + SPAN, channels), BF16),
            pltpu.VMEM((GROUPS, rows, 16), jnp.int32),
            pltpu.VMEM((9, rows, 3 * width), BF16),
            pltpu.VMEM((rows, channels), F32),
            pltpu.VMEM((2, channels, rows), BF16),
            pltpu.VMEM((offsets, channels, width), BF16),
            pltpu.VMEM((channels, rows), BF16),
            pltpu.VMEM((channels, rows), BF16),
            pltpu.VMEM((rows, channels), BF16),
            pltpu.SemaphoreType.DMA((3 * chans,)),
            pltpu.SemaphoreType.DMA((5,)),
            pltpu.SemaphoreType.DMA((9,)),
        ],
        anywhere(4),
    )(scalars, index, conv_weight, cotangent, *windows)

    keep, send = call(
        functools.partial(weight_kernel, shards, scale),
        [shape((shards, offsets, size, width), BF16)] * 2,
        vmem(1) + anywhere(1),
        [
            pltpu.VMEM((9, rows, 3 * width), BF16),
            pltpu.VMEM((shards, offsets, size, width), BF16),
            pltpu.VMEM((shards, offsets, size, width), BF16),
            pltpu.SemaphoreType.DMA((9,)),
            pltpu.SemaphoreType.DMA((9,)),
            pltpu.SemaphoreType.DMA((9,)),
        ],
        anywhere(2),
    )(turned, picked)

    near = met(conv_grad)
    received = swapped(after(send, *near), "rep")
    conv_weight_grad = call(
        empty_kernel,
        shape((offsets, channels, width), F32),
        [],
        [],
        anywhere(1)[0],
    )()
    total = [
        added(after(keep[i], conv_weight_grad), received[i]) for i in range(shards)
    ]
    mine, others = call(
        coarse_grad_kernel,
        [shape((channels, rows), F32), shape((chans - 1, channels, rows), BF16)],
        SMEM + vmem(1) + anywhere(4),
        [
            pltpu.VMEM((1, 3 * rows + SPAN, channels), BF16),
            pltpu.VMEM((GROUPS, rows, 16), jnp.int32),
            pltpu.VMEM((GROUPS, rows, PER * channels), BF16),
            pltpu.VMEM((chans, channels, rows), F32),
            pltpu.VMEM((offsets, channels, width), BF16),
            pltpu.SemaphoreType.DMA((4,)),
        ],
    )(after(scalars, *total), index, conv_weight, conv_grad, *near)
    received = [
        lax.ppermute(others[by - 1], "chan", [(i, (i + by) % chans) for i in range(chans)])
        for by in range(1, chans)
    ]
    tiles = octants // 2 * half // 16
    pre_grad, keep, send = call(
        functools.partial(pre_grad_kernel, scale),
        [
            shape((channels, rows), BF16),
            shape((tiles, 16, 2 * fine), BF16),
            shape((tiles, 16, 2 * fine), BF16),
        ],
        SMEM + vmem(4 + len(received)),
        [pltpu.VMEM((2, channels, rows), BF16)],
    )(scalars, children, child_mask, slope, mine, *received)

    if shards == 4:
        sums = sum_over_curve(total, pre_grad)
    else:
        sums = [lax.psum(total[0], "curve")]

    grads, weights = [], []
    for by in range(chans):
        pairs = [(i, (i + by) % chans) for i in range(chans)]
        grads.append(lax.ppermute(pre_grad, "chan", pairs) if by else pre_grad)
        part = after(cut[by], pre_grad)
        weights.append(lax.ppermute(part, "chan", pairs) if by else part)
    children_grad = call(
        children_kernel,
        shape((octants, mine_fine, rows), BF16),
        vmem(1 + 2 * chans),
        [pltpu.VMEM((octants, mine_fine, rows), BF16), pltpu.SemaphoreType.DMA((octants,))],
        anywhere(1)[0],
    )(after(child_mask, sums[min(1, shards - 1)]), *grads, *weights)

    down = added(keep, swapped(send, "rep"))
    if shards == 4:
        down = added(down, apart(down, 1))
        down = added(after(down, sums[2]), apart(down, 2))
    else:
        down = lax.psum(down, "curve")
    down_weight_grad = call(
        join_kernel,
        shape((octants, channels, fine), F32),
        SMEM + vmem(2),
        [],
    )(scalars, down, swapped(down, "rep"))

    for step, part in enumerate(sums):
        for core, piece in enumerate((part, swapped(part, "rep"))):
            row = lax.rem(rep + core, 2) * half + (curve ^ step if shards > 1 else 0) * size
            conv_weight_grad = lax.dynamic_update_slice(
                conv_weight_grad, piece.astype(F32), (0, row, 0)
            )
    return (features_out, children_grad, conv_weight_grad, down_weight_grad)


def solution(mesh):
    in_specs = (
        P(None, None, ("snap", "curve", "rep")),
        P(None, ("snap", "curve", "rep")),
        P(None, ("snap", "curve", "rep")),
        P(None, "chan", None),
        P(None, "chan", None),
        P("chan", ("snap", "curve", "rep")),
    )
    out_specs = (
        P("chan", ("snap", "curve", "rep")),
        P(None, "chan", ("snap", "curve", "rep")),
        P("snap", "chan", None),
        P("snap", "chan", None),
    )
    return jax.shard_map(body, mesh=mesh, in_specs=in_specs, out_specs=out_specs, check_vma=False)
```

```python
import functools

import jax
import jax.numpy as jnp
from jax import lax
from jax.experimental import pallas as pl
from jax.experimental.pallas import tpu as pltpu
from jax.sharding import PartitionSpec as P

BLOCK = 128
SPAN = 256
GROUPS = 3
PER = 9
VMEM_LIMIT = 56 * 1024 * 1024
PIECES = ("curve", "rep")
F32 = jnp.float32
BF16 = jnp.bfloat16
NOWHERE = -(2**20)
NT = (((1,), (1,)), ((), ()))


def silu_slope(value):
    sigma = jax.nn.sigmoid(value)
    return sigma * (1.0 + value * (1.0 - sigma))


def met(shard):
    devices = lax.axis_size(PIECES)
    pairs = [(i, i + 1) for i in range(1, devices - 1, 2)]
    pairs += [(j, i) for i, j in pairs]
    return [lax.ppermute(shard, PIECES, pairs), swapped(shard, "rep")]


def swapped(shard, axis):
    return lax.ppermute(shard, axis, [(0, 1), (1, 0)])


def call(kernel, out_shape, in_specs, scratch, out_specs=None):
    options = {} if out_specs is None else {"out_specs": out_specs}
    return pl.pallas_call(
        kernel,
        out_shape=out_shape,
        in_specs=in_specs,
        scratch_shapes=scratch,
        compiler_params=pltpu.CompilerParams(vmem_limit_bytes=VMEM_LIMIT),
        cost_estimate=pl.CostEstimate(flops=0, bytes_accessed=0, transcendentals=0),
        **options,
    )


def anywhere(count):
    return [pl.BlockSpec(memory_space=pl.ANY)] * count


def vmem(count):
    return [pl.BlockSpec(memory_space=pltpu.VMEM)] * count


SMEM = [pl.BlockSpec(memory_space=pltpu.SMEM)]


def down_kernel(children_ref, mask_ref, weight_ref, coarse_ref, slope_ref):
    octants = children_ref.shape[0]
    total = None
    for o in range(0, octants, 2):
        masked = jnp.concatenate(
            [
                children_ref[o + j] * mask_ref[o + j : o + j + 1, :].astype(F32).astype(BF16)
                for j in range(2)
            ],
            axis=0,
        )
        weights = jnp.concatenate([weight_ref[o], weight_ref[o + 1]], axis=1)
        term = jnp.dot(weights, masked, preferred_element_type=F32)
        total = term if total is None else total + term
    slope_ref[...] = silu_slope(total)
    coarse_ref[...] = (total * jax.nn.sigmoid(total)).T.astype(BF16)


def index_kernel(shards, neighbours_ref, index_ref, scalars_ref):
    offsets, rows = neighbours_ref.shape
    blocks = rows // BLOCK
    curve, rep = lax.axis_index("curve"), lax.axis_index("rep")
    names = neighbours_ref[...]
    local = jnp.where(names >= 0, names - (curve * 2 + rep - 1) * rows, NOWHERE)
    index_ref[...] = jnp.full(index_ref.shape, NOWHERE, jnp.int32)
    for group in range(GROUPS):
        part = local[group * PER : (group + 1) * PER]
        index_ref[group, :PER, :] = part
        lows = jnp.min(jnp.where(part < 0, -NOWHERE, part), axis=0, keepdims=True)
        highs = jnp.max(part, axis=0, keepdims=True)
        for block in range(blocks):
            at = slice(block * BLOCK, (block + 1) * BLOCK)
            low, high = jnp.min(lows[:, at]), jnp.max(highs[:, at]) + 1
            low = jnp.where(high <= 0, 0, low // 16 * 16)
            steps = jnp.maximum(1, (high - low + SPAN - 1) // SPAN)
            scalars_ref[group * blocks + block] = low
            scalars_ref[(GROUPS + group) * blocks + block] = steps
    last = 2 * GROUPS * blocks
    scalars_ref[last] = lax.axis_index("chan")
    scalars_ref[last + 1] = curve if shards > 1 else 0
    scalars_ref[last + 2] = rep


def window_copies(window_ref, parts, slots, rep, semaphores):
    rows = parts[0][0].shape[0]
    places = (rows, rep * 2 * rows, (1 - rep) * 2 * rows)
    copies = []
    for part, slot in zip(parts, slots):
        for source, place in zip(part, places):
            target = window_ref.at[slot, pl.ds(pl.multiple_of(place, 16), rows)]
            copies.append(pltpu.make_async_copy(source, target, semaphores.at[len(copies)]))
    return copies


def gather(scalars_ref, column_ref, window_ref, blocks, store, add):
    lanes = lax.broadcasted_iota(jnp.int32, (BLOCK, SPAN), 1).astype(F32).astype(BF16)

    def picked(group, rows, start):
        columns = jnp.clip(column_ref[group, rows, :] - start, -1, SPAN).astype(F32).astype(BF16)
        hot = [
            jnp.where(
                jnp.broadcast_to(columns[:, j : j + 1], (BLOCK, SPAN)) == lanes,
                jnp.ones((), BF16),
                jnp.zeros((), BF16),
            )
            for j in range(PER)
        ]
        at = pl.ds(pl.multiple_of(start, 16), SPAN)
        span = jnp.concatenate([window_ref[c, at, :] for c in range(window_ref.shape[0])], axis=1)
        return jnp.dot(jnp.concatenate(hot, axis=0), span, preferred_element_type=F32).astype(BF16)

    def first(block, _):
        rows = pl.ds(pl.multiple_of(block * BLOCK, BLOCK), BLOCK)
        for group in range(GROUPS):
            result = picked(group, rows, scalars_ref[group * blocks + block])
            for j in range(PER):
                store(group, j, rows, result[j * BLOCK : (j + 1) * BLOCK])
        return 0

    lax.fori_loop(0, blocks, first, 0, unroll=3)

    def rest(at, _):
        group, block = at // blocks, at % blocks
        rows = pl.ds(pl.multiple_of(block * BLOCK, BLOCK), BLOCK)

        def more(step, _):
            result = picked(group, rows, scalars_ref[at] + step * SPAN)
            for j in range(PER):
                add(group, j, rows, result[j * BLOCK : (j + 1) * BLOCK])
            return 0

        lax.fori_loop(1, scalars_ref[GROUPS * blocks + at], more, 0)
        return 0

    lax.fori_loop(0, GROUPS * blocks, rest, 0)


def turn(scratch_ref, value, shards, scalars_ref, at):
    half = value.shape[0] // 2
    size = half // shards
    scratch_ref[0] = value
    place = 0 if shards == 1 else scalars_ref[at + 1]
    rep = scalars_ref[at + 2]
    for core in range(2):
        for step in range(shards):
            source = (rep + core) % 2 * half + (place ^ step) * size
            target = core * half + step * size
            scratch_ref[1, target : target + size] = scratch_ref[
                0, pl.ds(pl.multiple_of(source, size), size)
            ]


def conv_kernel(chans, shards, scale, scalars_ref, index_ref, weight_hbm, cotangent_hbm, *refs):
    parts, refs = [refs[3 * i : 3 * i + 3] for i in range(chans)], refs[3 * chans :]
    out_hbm, grad_hbm, keep_hbm, send_hbm = refs[:4]
    window_ref, column_ref, picked_ref, conv_ref, scratch_ref = refs[4:9]
    weight_ref, cotangent_ref, out_ref, grad_ref, keep_ref, send_ref = refs[9:15]
    window_sems, sems, keep_sems, send_sems = refs[15:]
    rows = index_ref.shape[2]
    blocks = rows // BLOCK
    width = chans * window_ref.shape[2]
    channels = weight_ref.shape[1]
    chan = scalars_ref[2 * GROUPS * blocks]
    rep = scalars_ref[2 * GROUPS * blocks + 2]
    slots = (chan, 1 - chan) if chans == 2 else range(chans)
    copies = window_copies(window_ref, parts, slots, rep, window_sems)
    weight_copy = pltpu.make_async_copy(weight_hbm, weight_ref, sems.at[0])
    cotangent_copy = pltpu.make_async_copy(cotangent_hbm, cotangent_ref, sems.at[1])
    out_copy = pltpu.make_async_copy(out_ref, out_hbm, sems.at[2])
    grad_copy = pltpu.make_async_copy(grad_ref, grad_hbm, sems.at[3])
    for copy in copies:
        copy.start()
    weight_copy.start()
    cotangent_copy.start()
    window_ref[:, 3 * rows :, :] = jnp.zeros((chans, SPAN, channels), BF16)
    for group in range(GROUPS):
        column_ref[group] = index_ref[group].T
    for copy in copies:
        copy.wait()

    def store(group, j, at, value):
        lane = j % 3 * width
        picked_ref[group * 3 + j // 3, at, lane : lane + width] = value

    def add(group, j, at, value):
        lane = j % 3 * width
        picked_ref[group * 3 + j // 3, at, lane : lane + width] += value

    gather(scalars_ref, column_ref, window_ref, blocks, store, add)

    def multiply(three, _):
        weights = jnp.concatenate([weight_ref[three * 3 + j] for j in range(3)], axis=1)
        term = lax.dot_general(picked_ref[three], weights, NT, preferred_element_type=F32)
        conv_ref[...] += term
        return 0

    conv_ref[...] = jnp.zeros_like(conv_ref)
    weight_copy.wait()
    lax.fori_loop(0, 9, multiply, 0, unroll=3)
    conv = conv_ref[...].T
    cotangent_copy.wait()
    sigma = jax.nn.sigmoid(conv)
    out_ref[...] = (conv * sigma).astype(BF16)
    grad = cotangent_ref[...].astype(F32) * (sigma * (1.0 + conv * (1.0 - sigma)))
    grad_ref[...] = grad.T.astype(BF16)
    out_copy.start()
    grad_copy.start()
    turn(scratch_ref, grad.astype(BF16), shards, scalars_ref, 2 * GROUPS * blocks)
    half = channels // 2
    size = half // shards

    def leave(three):
        at = pl.ds(three * 3, 3)
        return (
            pltpu.make_async_copy(keep_ref.at[:, at], keep_hbm.at[:, at], keep_sems.at[three]),
            pltpu.make_async_copy(send_ref.at[:, at], send_hbm.at[:, at], send_sems.at[three]),
        )

    def weigh(three, _):
        term = jnp.dot(scratch_ref[1], picked_ref[three], preferred_element_type=F32) * scale
        for j in range(3):
            both = term[:, j * width : (j + 1) * width].astype(BF16)
            for step in range(shards):
                at = step * size
                keep_ref[step, three * 3 + j] = both[at : at + size]
                send_ref[step, three * 3 + j] = both[half + at : half + at + size]
        for copy in leave(three):
            copy.start()
        return 0

    lax.fori_loop(0, 9, weigh, 0, unroll=3)

    def finish(three, _):
        for copy in leave(three):
            copy.wait()
        return 0

    lax.fori_loop(0, 9, finish, 0)
    out_copy.wait()
    grad_copy.wait()


def coarse_grad_kernel(scalars_ref, index_ref, weight_hbm, *refs):
    part, refs = refs[:3], refs[3:]
    mine_ref, other_ref, window_ref, column_ref, picked_ref, total_ref, weight_ref, sems = refs
    rows = index_ref.shape[2]
    blocks = rows // BLOCK
    offsets, channels, width = weight_ref.shape
    chan = scalars_ref[2 * GROUPS * blocks]
    rep = scalars_ref[2 * GROUPS * blocks + 2]
    copies = window_copies(window_ref, [part], (0,), rep, sems)
    weight_copy = pltpu.make_async_copy(weight_hbm, weight_ref, sems.at[3])
    for copy in copies:
        copy.start()
    weight_copy.start()
    window_ref[0, 3 * rows :, :] = jnp.zeros((SPAN, channels), BF16)
    for group in range(GROUPS):
        column_ref[group] = index_ref[group].T
    for copy in copies:
        copy.wait()

    def store(group, j, at, value):
        lane = (PER - 1 - j) * channels
        picked_ref[GROUPS - 1 - group, at, lane : lane + channels] = value

    def add(group, j, at, value):
        lane = (PER - 1 - j) * channels
        picked_ref[GROUPS - 1 - group, at, lane : lane + channels] += value

    gather(scalars_ref, column_ref, window_ref, blocks, store, add)
    weight_copy.wait()
    result = None
    for group in range(GROUPS):
        weights = weight_ref[group * PER : (group + 1) * PER].reshape(PER * channels, width)
        term = jnp.dot(picked_ref[group], weights, preferred_element_type=F32)
        result = term if result is None else result + term
    result = result.T
    chans = width // channels
    for at in range(chans):
        total_ref[at] = result[at * channels : (at + 1) * channels]
    mine_ref[...] = total_ref[chan]
    for step in range(1, chans):
        other_ref[step - 1] = total_ref[lax.rem(chan + step, chans)].astype(BF16)


def pre_grad_kernel(scale, scalars_ref, children_ref, mask_ref, slope_ref, mine_ref, *refs):
    others, (grad_ref, keep_ref, send_ref, scratch_ref) = refs[:-4], refs[-4:]
    total = mine_ref[...]
    for other in others:
        total = total + other[...].astype(F32)
    grad = (total * slope_ref[...]).astype(BF16)
    grad_ref[...] = grad
    blocks = grad.shape[1] // BLOCK
    turn(scratch_ref, grad, 1, scalars_ref, 2 * GROUPS * blocks)
    half = grad.shape[0] // 2
    tiles = half // 16
    for o in range(0, children_ref.shape[0], 2):
        masked = jnp.concatenate(
            [
                children_ref[o + j] * mask_ref[o + j : o + j + 1, :].astype(F32).astype(BF16)
                for j in range(2)
            ],
            axis=0,
        )
        term = lax.dot_general(scratch_ref[1], masked, NT, preferred_element_type=F32) * scale
        both = term.astype(BF16)
        for tile in range(tiles):
            at = tile * 16
            keep_ref[o // 2 * tiles + tile] = both[at : at + 16]
            send_ref[o // 2 * tiles + tile] = both[half + at : half + at + 16]


def cut_kernel(weight_ref, out_ref, scratch_ref):
    octants, fine, _ = scratch_ref.shape
    chans = out_ref.shape[0]
    size = fine // chans
    chan = lax.axis_index("chan")
    for o in range(octants):
        scratch_ref[o] = weight_ref[o].T
    for by in range(chans):
        at = pl.ds(pl.multiple_of((chan + by) % chans * size, size), size)
        for o in range(octants):
            out_ref[by, o] = scratch_ref[o, at, :]


def spread_kernel(slots, shards, scalars_ref, *refs):
    parts = refs[: len(slots)]
    out_hbm, narrow_ref, wide_ref, in_sems, out_sems = refs[-5:]
    half = out_hbm.shape[1] // 2
    size = half // shards
    last = scalars_ref.shape[0] - 1
    place, rep = scalars_ref[last - 1], scalars_ref[last]
    arriving = [
        pltpu.make_async_copy(part, narrow_ref.at[i], in_sems.at[i])
        for i, part in enumerate(parts)
    ]
    for copy in arriving:
        copy.start()
    leaving = []
    for i, (core, step) in enumerate(slots):
        row = (rep + core) % 2 * half + (place ^ step) * size
        target = out_hbm.at[:, pl.ds(pl.multiple_of(row, size), size), :]
        arriving[i].wait()
        wide_ref[i] = narrow_ref[i].astype(F32)
        leaving.append(pltpu.make_async_copy(wide_ref.at[i], target, out_sems.at[i]))
        leaving[-1].start()
    for copy in leaving:
        copy.wait()


def children_kernel(mask_ref, *refs):
    out_hbm, out_ref, sems = refs[-3:]
    count = (len(refs) - 3) // 2
    grads, weights = refs[:count], refs[count:-3]
    copies = []
    for o in range(out_ref.shape[0]):
        total = None
        for grad, weight in zip(grads, weights):
            term = jnp.dot(weight[o], grad[...], preferred_element_type=F32)
            term = term.astype(BF16).astype(F32)
            total = term if total is None else total + term
        out_ref[o] = (total * mask_ref[o : o + 1, :].astype(F32)).astype(BF16)
        copies.append(pltpu.make_async_copy(out_ref.at[o], out_hbm.at[o], sems.at[o]))
        copies[-1].start()
    for copy in copies:
        copy.wait()


def join_kernel(scalars_ref, mine_ref, theirs_ref, out_ref):
    octants, channels, fine = out_ref.shape
    half = channels // 2
    tiles = half // 16
    rep = scalars_ref[scalars_ref.shape[0] - 1]
    for core, source in ((rep, mine_ref), (1 - rep, theirs_ref)):
        for o in range(0, octants, 2):
            for tile in range(tiles):
                value = source[o // 2 * tiles + tile].astype(F32)
                at = pl.ds(pl.multiple_of(core * half + tile * 16, 16), 16)
                out_ref[o, at, :] = value[:, :fine]
                out_ref[o + 1, at, :] = value[:, fine:]


def apart(shard, by):
    return lax.ppermute(shard, "curve", [(i, i ^ by) for i in range(lax.axis_size("curve"))])


def added(*terms):
    return sum(term.astype(F32) for term in terms).astype(BF16)


def sum_over_curve(total, beside):
    terms = [apart(total[by], by) for by in range(1, 4)]
    own = added(after(total[0], beside), *terms)
    across = apart(own, 2)
    return [own, apart(own, 1), across, apart(across, 1)]


def after(value, *earlier):
    return lax.optimization_barrier((value, *earlier))[0]


def spread(parts, shards, scalars, base=None):
    slots = list(parts)
    arrays = [parts[slot] for slot in slots]
    count, size, width = arrays[0].shape
    held = [] if base is None else [base]
    return pl.pallas_call(
        functools.partial(spread_kernel, slots, shards),
        out_shape=jax.ShapeDtypeStruct((count, 2 * shards * size, width), F32),
        in_specs=SMEM + anywhere(len(arrays) + len(held)),
        out_specs=anywhere(1)[0],
        scratch_shapes=[
            pltpu.VMEM((len(arrays), count, size, width), BF16),
            pltpu.VMEM((len(arrays), count, size, width), F32),
            pltpu.SemaphoreType.DMA((len(arrays),)),
            pltpu.SemaphoreType.DMA((len(arrays),)),
        ],
        input_output_aliases={1 + len(arrays): 0} if held else {},
        compiler_params=pltpu.CompilerParams(vmem_limit_bytes=VMEM_LIMIT),
        cost_estimate=pl.CostEstimate(flops=0, bytes_accessed=0, transcendentals=0),
    )(scalars, *arrays, *held)


def body(children, child_mask, neighbours, down_weight, conv_weight, cotangent):
    octants, fine, rows = children.shape
    offsets, channels, width = conv_weight.shape
    blocks = rows // BLOCK
    chans = lax.axis_size("chan")
    chan = lax.axis_index("chan")
    rep = lax.axis_index("rep")
    curve = lax.axis_index("curve")
    pieces = lax.axis_size(PIECES)
    scale = 1.0 / (rows * pieces) ** 0.5
    shape = jax.ShapeDtypeStruct
    half = channels // 2
    shards = 4 if lax.axis_size("curve") == 4 and half % 64 == 0 else 1
    size = half // shards

    coarse, slope = call(
        down_kernel,
        [shape((rows, channels), BF16), shape((channels, rows), F32)],
        vmem(3),
        [],
    )(children, child_mask, down_weight)

    if chans == 2:
        parts = [coarse, swapped(coarse, "chan")]
    else:
        every = lax.all_gather(coarse, "chan", axis=0)
        parts = [every[i] for i in range(chans)]
    windows = [array for part in parts for array in [part] + met(part)]
    index, scalars = call(
        functools.partial(index_kernel, shards),
        [shape((GROUPS, 16, rows), jnp.int32), shape((2 * GROUPS * blocks + 3,), jnp.int32)],
        vmem(1),
        [],
        vmem(1) + SMEM,
    )(after(neighbours, parts[1]))

    features_out, conv_grad, keep, send = call(
        functools.partial(conv_kernel, chans, shards, scale),
        [
            shape((channels, rows), BF16),
            shape((rows, channels), BF16),
            shape((shards, offsets, size, width), BF16),
            shape((shards, offsets, size, width), BF16),
        ],
        SMEM + vmem(1) + anywhere(2 + 3 * chans),
        [
            pltpu.VMEM((chans, 3 * rows + SPAN, channels), BF16),
            pltpu.VMEM((GROUPS, rows, 16), jnp.int32),
            pltpu.VMEM((9, rows, 3 * width), BF16),
            pltpu.VMEM((rows, channels), F32),
            pltpu.VMEM((2, channels, rows), BF16),
            pltpu.VMEM((offsets, channels, width), BF16),
            pltpu.VMEM((channels, rows), BF16),
            pltpu.VMEM((channels, rows), BF16),
            pltpu.VMEM((rows, channels), BF16),
            pltpu.VMEM((shards, offsets, size, width), BF16),
            pltpu.VMEM((shards, offsets, size, width), BF16),
            pltpu.SemaphoreType.DMA((3 * chans,)),
            pltpu.SemaphoreType.DMA((4,)),
            pltpu.SemaphoreType.DMA((9,)),
            pltpu.SemaphoreType.DMA((9,)),
        ],
        anywhere(4),
    )(scalars, index, conv_weight, cotangent, *windows)

    near = met(conv_grad)
    received = swapped(send, "rep")
    total = [added(keep[i], received[i]) for i in range(shards)]

    mine, others = call(
        coarse_grad_kernel,
        [shape((channels, rows), F32), shape((chans - 1, channels, rows), BF16)],
        SMEM + vmem(1) + anywhere(4),
        [
            pltpu.VMEM((1, 3 * rows + SPAN, channels), BF16),
            pltpu.VMEM((GROUPS, rows, 16), jnp.int32),
            pltpu.VMEM((GROUPS, rows, PER * channels), BF16),
            pltpu.VMEM((chans, channels, rows), F32),
            pltpu.VMEM((offsets, channels, width), BF16),
            pltpu.SemaphoreType.DMA((4,)),
        ],
    )(after(scalars, *total), index, conv_weight, conv_grad, *near)
    received = [
        lax.ppermute(others[by - 1], "chan", [(i, (i + by) % chans) for i in range(chans)])
        for by in range(1, chans)
    ]
    mine_fine = fine // chans
    cut = call(
        cut_kernel,
        shape((chans, octants, mine_fine, channels), BF16),
        vmem(1),
        [pltpu.VMEM((octants, fine, channels), BF16)],
    )(after(down_weight, mine))
    tiles = octants // 2 * half // 16
    pre_grad, keep, send = call(
        functools.partial(pre_grad_kernel, scale),
        [
            shape((channels, rows), BF16),
            shape((tiles, 16, 2 * fine), BF16),
            shape((tiles, 16, 2 * fine), BF16),
        ],
        SMEM + vmem(4 + len(received)),
        [pltpu.VMEM((2, channels, rows), BF16)],
    )(after(scalars, cut), children, child_mask, slope, mine, *received)

    if shards == 4:
        sums = sum_over_curve(total, pre_grad)
    else:
        sums = [lax.psum(total[0], "curve")]
    sent_grad, send = after(pre_grad, sums[0]), after(send, sums[0])
    grads, weights = [], []
    for by in range(chans):
        pairs = [(i, (i + by) % chans) for i in range(chans)]
        grads.append(lax.ppermute(sent_grad, "chan", pairs) if by else pre_grad)
        part = after(cut[by], sums[0])
        weights.append(lax.ppermute(part, "chan", pairs) if by else part)
    children_grad = call(
        children_kernel,
        shape((octants, mine_fine, rows), BF16),
        vmem(1 + 2 * chans),
        [pltpu.VMEM((octants, mine_fine, rows), BF16), pltpu.SemaphoreType.DMA((octants,))],
        anywhere(1)[0],
    )(child_mask, *grads, *weights)

    down = added(keep, swapped(send, "rep"))
    if shards == 4:
        down = added(after(down, *grads[1:]), apart(down, 1))
        down = added(after(down, sums[2], children_grad), apart(down, 2))
    else:
        down = lax.psum(down, "curve")
    theirs = swapped(down, "rep")

    conv_weight_grad = None
    for steps in ((0,), (1, 2), (3,)):
        parts = {}
        for step in steps:
            if step < shards:
                part = sums[step] if conv_weight_grad is None else after(sums[step], conv_weight_grad)
                parts[0, step] = sums[step]
                parts[1, step] = swapped(part if step == 3 else sums[step], "rep")
        if parts:
            conv_weight_grad = spread(parts, shards, scalars, conv_weight_grad)
        if steps == (1, 2):
            down = after(down, conv_weight_grad)
    down_weight_grad = call(
        join_kernel,
        shape((octants, channels, fine), F32),
        SMEM + vmem(2),
        [],
    )(scalars, down, theirs)
    return (features_out, children_grad, conv_weight_grad, down_weight_grad)


def solution(mesh):
    in_specs = (
        P(None, None, ("snap", "curve", "rep")),
        P(None, ("snap", "curve", "rep")),
        P(None, ("snap", "curve", "rep")),
        P(None, "chan", None),
        P(None, "chan", None),
        P("chan", ("snap", "curve", "rep")),
    )
    out_specs = (
        P("chan", ("snap", "curve", "rep")),
        P(None, "chan", ("snap", "curve", "rep")),
        P("snap", "chan", None),
        P("snap", "chan", None),
    )
    return jax.shard_map(body, mesh=mesh, in_specs=in_specs, out_specs=out_specs, check_vma=False)
```

```python
import functools

import jax
import jax.numpy as jnp
from jax import lax
from jax.experimental import pallas as pl
from jax.experimental.pallas import tpu as pltpu
from jax.sharding import PartitionSpec as P

BLOCK = 128
SPAN = 256
GROUPS = 3
PER = 9
VMEM_LIMIT = 56 * 1024 * 1024
PIECES = ("curve", "rep")
F32 = jnp.float32
BF16 = jnp.bfloat16
NOWHERE = -(2**20)
NT = (((1,), (1,)), ((), ()))


def silu_slope(value):
    sigma = jax.nn.sigmoid(value)
    return sigma * (1.0 + value * (1.0 - sigma))


def met(shard):
    devices = lax.axis_size(PIECES)
    pairs = [(i, i + 1) for i in range(1, devices - 1, 2)]
    pairs += [(j, i) for i, j in pairs]
    return [lax.ppermute(shard, PIECES, pairs), swapped(shard, "rep")]


def swapped(shard, axis):
    return lax.ppermute(shard, axis, [(0, 1), (1, 0)])


def call(kernel, out_shape, in_specs, scratch, out_specs=None):
    options = {} if out_specs is None else {"out_specs": out_specs}
    return pl.pallas_call(
        kernel,
        out_shape=out_shape,
        in_specs=in_specs,
        scratch_shapes=scratch,
        compiler_params=pltpu.CompilerParams(vmem_limit_bytes=VMEM_LIMIT),
        cost_estimate=pl.CostEstimate(flops=0, bytes_accessed=0, transcendentals=0),
        **options,
    )


def anywhere(count):
    return [pl.BlockSpec(memory_space=pl.ANY)] * count


def vmem(count):
    return [pl.BlockSpec(memory_space=pltpu.VMEM)] * count


SMEM = [pl.BlockSpec(memory_space=pltpu.SMEM)]


def down_kernel(children_ref, mask_ref, weight_ref, coarse_ref, slope_ref):
    octants = children_ref.shape[0]
    total = None
    for o in range(0, octants, 2):
        masked = jnp.concatenate(
            [
                children_ref[o + j] * mask_ref[o + j : o + j + 1, :].astype(F32).astype(BF16)
                for j in range(2)
            ],
            axis=0,
        )
        weights = jnp.concatenate([weight_ref[o], weight_ref[o + 1]], axis=1)
        term = jnp.dot(weights, masked, preferred_element_type=F32)
        total = term if total is None else total + term
    slope_ref[...] = silu_slope(total)
    coarse_ref[...] = (total * jax.nn.sigmoid(total)).T.astype(BF16)


def index_kernel(shards, neighbours_ref, index_ref, scalars_ref):
    offsets, rows = neighbours_ref.shape
    blocks = rows // BLOCK
    curve, rep = lax.axis_index("curve"), lax.axis_index("rep")
    names = neighbours_ref[...]
    local = jnp.where(names >= 0, names - (curve * 2 + rep - 1) * rows, NOWHERE)
    index_ref[...] = jnp.full(index_ref.shape, NOWHERE, jnp.int32)
    for group in range(GROUPS):
        part = local[group * PER : (group + 1) * PER]
        index_ref[group, :PER, :] = part
        lows = jnp.min(jnp.where(part < 0, -NOWHERE, part), axis=0, keepdims=True)
        highs = jnp.max(part, axis=0, keepdims=True)
        for block in range(blocks):
            at = slice(block * BLOCK, (block + 1) * BLOCK)
            low, high = jnp.min(lows[:, at]), jnp.max(highs[:, at]) + 1
            low = jnp.where(high <= 0, 0, low // 16 * 16)
            steps = jnp.maximum(1, (high - low + SPAN - 1) // SPAN)
            scalars_ref[group * blocks + block] = low
            scalars_ref[(GROUPS + group) * blocks + block] = steps
    last = 2 * GROUPS * blocks
    scalars_ref[last] = lax.axis_index("chan")
    scalars_ref[last + 1] = curve if shards > 1 else 0
    scalars_ref[last + 2] = rep


def window_copies(window_ref, parts, slots, rep, semaphores):
    rows = parts[0][0].shape[0]
    places = (rows, rep * 2 * rows, (1 - rep) * 2 * rows)
    copies = []
    for part, slot in zip(parts, slots):
        for source, place in zip(part, places):
            target = window_ref.at[slot, pl.ds(pl.multiple_of(place, 16), rows)]
            copies.append(pltpu.make_async_copy(source, target, semaphores.at[len(copies)]))
    return copies


def gather(scalars_ref, column_ref, window_ref, blocks, store, add):
    lanes = lax.broadcasted_iota(jnp.int32, (BLOCK, SPAN), 1).astype(F32).astype(BF16)

    def picked(group, rows, start):
        columns = jnp.clip(column_ref[group, rows, :] - start, -1, SPAN).astype(F32).astype(BF16)
        hot = [
            jnp.where(
                jnp.broadcast_to(columns[:, j : j + 1], (BLOCK, SPAN)) == lanes,
                jnp.ones((), BF16),
                jnp.zeros((), BF16),
            )
            for j in range(PER)
        ]
        at = pl.ds(pl.multiple_of(start, 16), SPAN)
        span = jnp.concatenate([window_ref[c, at, :] for c in range(window_ref.shape[0])], axis=1)
        return jnp.dot(jnp.concatenate(hot, axis=0), span, preferred_element_type=F32).astype(BF16)

    def first(block, _):
        rows = pl.ds(pl.multiple_of(block * BLOCK, BLOCK), BLOCK)
        for group in range(GROUPS):
            result = picked(group, rows, scalars_ref[group * blocks + block])
            for j in range(PER):
                store(group, j, rows, result[j * BLOCK : (j + 1) * BLOCK])
        return 0

    lax.fori_loop(0, blocks, first, 0, unroll=3)

    def rest(at, _):
        group, block = at // blocks, at % blocks
        rows = pl.ds(pl.multiple_of(block * BLOCK, BLOCK), BLOCK)

        def more(step, _):
            result = picked(group, rows, scalars_ref[at] + step * SPAN)
            for j in range(PER):
                add(group, j, rows, result[j * BLOCK : (j + 1) * BLOCK])
            return 0

        lax.fori_loop(1, scalars_ref[GROUPS * blocks + at], more, 0)
        return 0

    lax.fori_loop(0, GROUPS * blocks, rest, 0)


def turn(scratch_ref, value, shards, scalars_ref, at):
    half = value.shape[0] // 2
    size = half // shards
    scratch_ref[0] = value
    place = 0 if shards == 1 else scalars_ref[at + 1]
    rep = scalars_ref[at + 2]
    for core in range(2):
        for step in range(shards):
            source = (rep + core) % 2 * half + (place ^ step) * size
            target = core * half + step * size
            scratch_ref[1, target : target + size] = scratch_ref[
                0, pl.ds(pl.multiple_of(source, size), size)
            ]


def conv_kernel(chans, shards, scale, scalars_ref, index_ref, weight_hbm, cotangent_hbm, *refs):
    parts, refs = [refs[3 * i : 3 * i + 3] for i in range(chans)], refs[3 * chans :]
    out_hbm, grad_hbm, keep_hbm, send_hbm, far_hbm = refs[:5]
    window_ref, column_ref, picked_ref, conv_ref, scratch_ref = refs[5:10]
    weight_ref, cotangent_ref, out_ref, grad_ref, keep_ref, send_ref, far_ref = refs[10:17]
    window_sems, sems, keep_sems, send_sems, far_sems = refs[17:]
    rows = index_ref.shape[2]
    blocks = rows // BLOCK
    width = chans * window_ref.shape[2]
    channels = weight_ref.shape[1]
    chan = scalars_ref[2 * GROUPS * blocks]
    rep = scalars_ref[2 * GROUPS * blocks + 2]
    slots = (chan, 1 - chan) if chans == 2 else range(chans)
    copies = window_copies(window_ref, parts, slots, rep, window_sems)
    weight_copy = pltpu.make_async_copy(weight_hbm, weight_ref, sems.at[0])
    cotangent_copy = pltpu.make_async_copy(cotangent_hbm, cotangent_ref, sems.at[1])
    out_copy = pltpu.make_async_copy(out_ref, out_hbm, sems.at[2])
    grad_copy = pltpu.make_async_copy(grad_ref, grad_hbm, sems.at[3])
    for copy in copies:
        copy.start()
    weight_copy.start()
    cotangent_copy.start()
    window_ref[:, 3 * rows :, :] = jnp.zeros((chans, SPAN, channels), BF16)
    for group in range(GROUPS):
        column_ref[group] = index_ref[group].T
    for copy in copies:
        copy.wait()

    def store(group, j, at, value):
        lane = j % 3 * width
        picked_ref[group * 3 + j // 3, at, lane : lane + width] = value

    def add(group, j, at, value):
        lane = j % 3 * width
        picked_ref[group * 3 + j // 3, at, lane : lane + width] += value

    gather(scalars_ref, column_ref, window_ref, blocks, store, add)

    def multiply(three, _):
        weights = jnp.concatenate([weight_ref[three * 3 + j] for j in range(3)], axis=1)
        term = lax.dot_general(picked_ref[three], weights, NT, preferred_element_type=F32)
        conv_ref[...] += term
        return 0

    conv_ref[...] = jnp.zeros_like(conv_ref)
    weight_copy.wait()
    lax.fori_loop(0, 9, multiply, 0, unroll=3)
    conv = conv_ref[...].T
    cotangent_copy.wait()
    sigma = jax.nn.sigmoid(conv)
    out_ref[...] = (conv * sigma).astype(BF16)
    grad = cotangent_ref[...].astype(F32) * (sigma * (1.0 + conv * (1.0 - sigma)))
    grad_ref[...] = grad.T.astype(BF16)
    out_copy.start()
    grad_copy.start()
    turn(scratch_ref, grad.astype(BF16), shards, scalars_ref, 2 * GROUPS * blocks)
    half = channels // 2
    size = half // shards

    def leave(three):
        at = pl.ds(three * 3, 3)
        return (
            pltpu.make_async_copy(keep_ref.at[:, at], keep_hbm.at[:, at], keep_sems.at[three]),
            pltpu.make_async_copy(send_ref.at[:, at], send_hbm.at[:, at], send_sems.at[three]),
            pltpu.make_async_copy(far_ref.at[at], far_hbm.at[at], far_sems.at[three]),
        )

    def weigh(three, _):
        term = jnp.dot(scratch_ref[1], picked_ref[three], preferred_element_type=F32) * scale
        for j in range(3):
            both = term[:, j * width : (j + 1) * width].astype(BF16)
            for step in range(shards):
                at = step * size
                keep_ref[step, three * 3 + j] = both[at : at + size]
                other = both[half + at : half + at + size]
                if step == shards - 1:
                    far_ref[three * 3 + j] = other
                if step < send_ref.shape[0]:
                    send_ref[step, three * 3 + j] = other
        for copy in leave(three):
            copy.start()
        return 0

    lax.fori_loop(0, 9, weigh, 0, unroll=3)

    def finish(three, _):
        for copy in leave(three):
            copy.wait()
        return 0

    lax.fori_loop(0, 9, finish, 0)
    out_copy.wait()
    grad_copy.wait()


def coarse_grad_kernel(scalars_ref, index_ref, weight_hbm, *refs):
    part, refs = refs[:3], refs[3:]
    mine_ref, other_ref, window_ref, column_ref, picked_ref, total_ref, weight_ref, sems = refs
    rows = index_ref.shape[2]
    blocks = rows // BLOCK
    offsets, channels, width = weight_ref.shape
    chan = scalars_ref[2 * GROUPS * blocks]
    rep = scalars_ref[2 * GROUPS * blocks + 2]
    copies = window_copies(window_ref, [part], (0,), rep, sems)
    weight_copy = pltpu.make_async_copy(weight_hbm, weight_ref, sems.at[3])
    for copy in copies:
        copy.start()
    weight_copy.start()
    window_ref[0, 3 * rows :, :] = jnp.zeros((SPAN, channels), BF16)
    for group in range(GROUPS):
        column_ref[group] = index_ref[group].T
    for copy in copies:
        copy.wait()

    def store(group, j, at, value):
        lane = (PER - 1 - j) * channels
        picked_ref[GROUPS - 1 - group, at, lane : lane + channels] = value

    def add(group, j, at, value):
        lane = (PER - 1 - j) * channels
        picked_ref[GROUPS - 1 - group, at, lane : lane + channels] += value

    gather(scalars_ref, column_ref, window_ref, blocks, store, add)
    weight_copy.wait()
    result = None
    for group in range(GROUPS):
        weights = weight_ref[group * PER : (group + 1) * PER].reshape(PER * channels, width)
        term = jnp.dot(picked_ref[group], weights, preferred_element_type=F32)
        result = term if result is None else result + term
    result = result.T
    chans = width // channels
    for at in range(chans):
        total_ref[at] = result[at * channels : (at + 1) * channels]
    mine_ref[...] = total_ref[chan]
    for step in range(1, chans):
        other_ref[step - 1] = total_ref[lax.rem(chan + step, chans)].astype(BF16)


def pre_grad_kernel(scale, scalars_ref, children_ref, mask_ref, slope_ref, mine_ref, *refs):
    others, (grad_ref, keep_ref, send_ref, scratch_ref) = refs[:-4], refs[-4:]
    total = mine_ref[...]
    for other in others:
        total = total + other[...].astype(F32)
    grad = (total * slope_ref[...]).astype(BF16)
    grad_ref[...] = grad
    blocks = grad.shape[1] // BLOCK
    turn(scratch_ref, grad, 1, scalars_ref, 2 * GROUPS * blocks)
    half = grad.shape[0] // 2
    fine = children_ref.shape[1]
    for o in range(0, children_ref.shape[0], 2):
        masked = jnp.concatenate(
            [
                children_ref[o + j] * mask_ref[o + j : o + j + 1, :].astype(F32).astype(BF16)
                for j in range(2)
            ],
            axis=0,
        )
        term = lax.dot_general(scratch_ref[1], masked, NT, preferred_element_type=F32) * scale
        both = term.astype(BF16)
        for j in range(2):
            keep_ref[o + j] = both[:half, j * fine : (j + 1) * fine]
            send_ref[o + j] = both[half:, j * fine : (j + 1) * fine]


def cut_kernel(weight_ref, *refs):
    out_refs, scratch_ref = refs[:-1], refs[-1]
    octants, fine, _ = scratch_ref.shape
    chans = len(out_refs)
    size = fine // chans
    chan = lax.axis_index("chan")
    for o in range(octants):
        scratch_ref[o] = weight_ref[o].T
    for by in range(chans):
        at = pl.ds(pl.multiple_of((chan + by) % chans * size, size), size)
        for o in range(octants):
            out_refs[by][o] = scratch_ref[o, at, :]


def children_kernel(mask_ref, *refs):
    out_hbm, out_ref, sems = refs[-3:]
    count = (len(refs) - 3) // 2
    grads, weights = refs[:count], refs[count:-3]
    copies = []
    for o in range(out_ref.shape[0]):
        total = None
        for grad, weight in zip(grads, weights):
            term = jnp.dot(weight[o], grad[...], preferred_element_type=F32)
            term = term.astype(BF16).astype(F32)
            total = term if total is None else total + term
        out_ref[o] = (total * mask_ref[o : o + 1, :].astype(F32)).astype(BF16)
        copies.append(pltpu.make_async_copy(out_ref.at[o], out_hbm.at[o], sems.at[o]))
        copies[-1].start()
    for copy in copies:
        copy.wait()


def apart(shard, by):
    return lax.ppermute(shard, "curve", [(i, i ^ by) for i in range(lax.axis_size("curve"))])


def added(*terms):
    return sum(term.astype(F32) for term in terms).astype(BF16)


def after(value, *earlier):
    return lax.optimization_barrier((value, *earlier))[0]


def body(children, child_mask, neighbours, down_weight, conv_weight, cotangent):
    octants, fine, rows = children.shape
    offsets, channels, width = conv_weight.shape
    blocks = rows // BLOCK
    chans = lax.axis_size("chan")
    chan = lax.axis_index("chan")
    rep = lax.axis_index("rep")
    curve = lax.axis_index("curve")
    pieces = lax.axis_size(PIECES)
    scale = 1.0 / (rows * pieces) ** 0.5
    shape = jax.ShapeDtypeStruct
    half = channels // 2
    shards = 4 if lax.axis_size("curve") == 4 and half % 64 == 0 else 1
    size = half // shards

    coarse, slope = call(
        down_kernel,
        [shape((rows, channels), BF16), shape((channels, rows), F32)],
        vmem(3),
        [],
    )(children, child_mask, down_weight)

    if chans == 2:
        parts = [coarse, swapped(coarse, "chan")]
    else:
        every = lax.all_gather(coarse, "chan", axis=0)
        parts = [every[i] for i in range(chans)]
    windows = [array for part in parts for array in [part] + met(part)]
    index, scalars = call(
        functools.partial(index_kernel, shards),
        [shape((GROUPS, 16, rows), jnp.int32), shape((2 * GROUPS * blocks + 3,), jnp.int32)],
        vmem(1),
        [],
        vmem(1) + SMEM,
    )(after(neighbours, parts[1]))

    features_out, conv_grad, keep, send, far = call(
        functools.partial(conv_kernel, chans, shards, scale),
        [
            shape((channels, rows), BF16),
            shape((rows, channels), BF16),
            shape((shards, offsets, size, width), BF16),
            shape((max(shards - 1, 1), offsets, size, width), BF16),
            shape((offsets, size, width), BF16),
        ],
        SMEM + vmem(1) + anywhere(2 + 3 * chans),
        [
            pltpu.VMEM((chans, 3 * rows + SPAN, channels), BF16),
            pltpu.VMEM((GROUPS, rows, 16), jnp.int32),
            pltpu.VMEM((9, rows, 3 * width), BF16),
            pltpu.VMEM((rows, channels), F32),
            pltpu.VMEM((2, channels, rows), BF16),
            pltpu.VMEM((offsets, channels, width), BF16),
            pltpu.VMEM((channels, rows), BF16),
            pltpu.VMEM((channels, rows), BF16),
            pltpu.VMEM((rows, channels), BF16),
            pltpu.VMEM((shards, offsets, size, width), BF16),
            pltpu.VMEM((max(shards - 1, 1), offsets, size, width), BF16),
            pltpu.VMEM((offsets, size, width), BF16),
            pltpu.SemaphoreType.DMA((3 * chans,)),
            pltpu.SemaphoreType.DMA((4,)),
            pltpu.SemaphoreType.DMA((9,)),
            pltpu.SemaphoreType.DMA((9,)),
            pltpu.SemaphoreType.DMA((9,)),
        ],
        anywhere(5),
    )(scalars, index, conv_weight, cotangent, *windows)

    far = added(keep[shards - 1], swapped(far, "rep"))
    first = far
    near = met(after(conv_grad, far))
    if shards == 4:
        received = swapped(after(send, far), "rep")
        total = [added(keep[i], received[i]) for i in range(3)]
        first = added(after(total[2], *near), apart(far, 1))
        terms = [apart(first, 2), apart(after(total[1], first), 1)]
    mine, others = call(
        coarse_grad_kernel,
        [shape((channels, rows), F32), shape((chans - 1, channels, rows), BF16)],
        SMEM + vmem(1) + anywhere(4),
        [
            pltpu.VMEM((1, 3 * rows + SPAN, channels), BF16),
            pltpu.VMEM((GROUPS, rows, 16), jnp.int32),
            pltpu.VMEM((GROUPS, rows, PER * channels), BF16),
            pltpu.VMEM((chans, channels, rows), F32),
            pltpu.VMEM((offsets, channels, width), BF16),
            pltpu.SemaphoreType.DMA((4,)),
        ],
    )(after(scalars, first), index, conv_weight, conv_grad, *near)
    if shards == 4:
        own = added(after(total[0], mine), *terms)
        across = apart(own, 2)
        sums = [own, apart(own, 1), across, apart(across, 1)]
    else:
        own = lax.psum(far, "curve")
        sums = [own]
    received = [
        lax.ppermute(others[by - 1], "chan", [(i, (i + by) % chans) for i in range(chans)])
        for by in range(1, chans)
    ]
    mine_fine = fine // chans
    cut = call(
        cut_kernel,
        [shape((octants, mine_fine, channels), BF16)] * chans,
        vmem(1),
        [pltpu.VMEM((octants, fine, channels), BF16)],
    )(after(down_weight, mine))
    pre_grad, keep, send = call(
        functools.partial(pre_grad_kernel, scale),
        [
            shape((channels, rows), BF16),
            shape((octants, half, fine), BF16),
            shape((octants, half, fine), BF16),
        ],
        SMEM + vmem(4 + len(received)),
        [pltpu.VMEM((2, channels, rows), BF16)],
    )(after(scalars, own, *cut), children, child_mask, slope, mine, *received)

    grads, weights = [], []
    for by in range(chans):
        pairs = [(i, (i + by) % chans) for i in range(chans)]
        grads.append(lax.ppermute(pre_grad, "chan", pairs) if by else pre_grad)
        weights.append(lax.ppermute(after(cut[by], pre_grad), "chan", pairs) if by else cut[by])
    children_grad = call(
        children_kernel,
        shape((octants, mine_fine, rows), BF16),
        vmem(1 + 2 * chans),
        [pltpu.VMEM((octants, mine_fine, rows), BF16), pltpu.SemaphoreType.DMA((octants,))],
        anywhere(1)[0],
    )(child_mask, *grads, *weights)

    down = added(after(keep, *sums[2:3]), swapped(send, "rep"))
    if shards == 4:
        down = added(after(down, *grads[1:]), apart(down, 1))
        down = added(after(down, sums[2], children_grad), apart(down, 2))
    else:
        down = lax.psum(down, "curve")
    def joined(pieces, like):
        result = jnp.broadcast_to(after(jnp.zeros((), F32), mine), like.shape)
        for row, piece in pieces:
            result = lax.dynamic_update_slice(result, piece.astype(F32), (0, row, 0))
        return result

    rows_of = [rep * half, (1 - rep) * half]
    down_weight_grad = joined(zip(rows_of, (down, swapped(down, "rep"))), down_weight)
    pieces = []
    for step, part in enumerate(sums):
        at = (curve ^ step) * size if shards > 1 else 0
        pieces += [(rows_of[0] + at, part), (rows_of[1] + at, swapped(part, "rep"))]
    conv_weight_grad = joined(pieces, conv_weight)
    return (features_out, children_grad, conv_weight_grad, down_weight_grad)


def solution(mesh):
    in_specs = (
        P(None, None, ("snap", "curve", "rep")),
        P(None, ("snap", "curve", "rep")),
        P(None, ("snap", "curve", "rep")),
        P(None, "chan", None),
        P(None, "chan", None),
        P("chan", ("snap", "curve", "rep")),
    )
    out_specs = (
        P("chan", ("snap", "curve", "rep")),
        P(None, "chan", ("snap", "curve", "rep")),
        P("snap", "chan", None),
        P("snap", "chan", None),
    )
    return jax.shard_map(body, mesh=mesh, in_specs=in_specs, out_specs=out_specs, check_vma=False)
```

```python
import functools

import jax
import jax.numpy as jnp
from jax import lax
from jax.experimental import pallas as pl
from jax.experimental.pallas import tpu as pltpu
from jax.sharding import PartitionSpec as P

BLOCK = 128
SPAN = 256
GROUPS = 3
PER = 9
VMEM_LIMIT = 56 * 1024 * 1024
PIECES = ("curve", "rep")
F32 = jnp.float32
BF16 = jnp.bfloat16
NOWHERE = -(2**20)
NT = (((1,), (1,)), ((), ()))


def silu_slope(value):
    sigma = jax.nn.sigmoid(value)
    return sigma * (1.0 + value * (1.0 - sigma))


def met(shard):
    devices = lax.axis_size(PIECES)
    pairs = [(i, i + 1) for i in range(1, devices - 1, 2)]
    pairs += [(j, i) for i, j in pairs]
    return [lax.ppermute(shard, PIECES, pairs), swapped(shard, "rep")]


def swapped(shard, axis):
    return lax.ppermute(shard, axis, [(0, 1), (1, 0)])


def call(kernel, out_shape, in_specs, scratch, out_specs=None):
    options = {} if out_specs is None else {"out_specs": out_specs}
    return pl.pallas_call(
        kernel,
        out_shape=out_shape,
        in_specs=in_specs,
        scratch_shapes=scratch,
        compiler_params=pltpu.CompilerParams(vmem_limit_bytes=VMEM_LIMIT),
        cost_estimate=pl.CostEstimate(flops=0, bytes_accessed=0, transcendentals=0),
        **options,
    )


def anywhere(count):
    return [pl.BlockSpec(memory_space=pl.ANY)] * count


def vmem(count):
    return [pl.BlockSpec(memory_space=pltpu.VMEM)] * count


SMEM = [pl.BlockSpec(memory_space=pltpu.SMEM)]


def down_kernel(children_ref, mask_ref, weight_ref, coarse_ref, slope_ref):
    octants = children_ref.shape[0]
    total = None
    for o in range(0, octants, 2):
        masked = jnp.concatenate(
            [
                children_ref[o + j] * mask_ref[o + j : o + j + 1, :].astype(F32).astype(BF16)
                for j in range(2)
            ],
            axis=0,
        )
        weights = jnp.concatenate([weight_ref[o], weight_ref[o + 1]], axis=1)
        term = jnp.dot(weights, masked, preferred_element_type=F32)
        total = term if total is None else total + term
    slope_ref[...] = silu_slope(total)
    coarse_ref[...] = (total * jax.nn.sigmoid(total)).T.astype(BF16)


def index_kernel(shards, neighbours_ref, index_ref, scalars_ref):
    offsets, rows = neighbours_ref.shape
    blocks = rows // BLOCK
    curve, rep = lax.axis_index("curve"), lax.axis_index("rep")
    names = neighbours_ref[...]
    local = jnp.where(names >= 0, names - (curve * 2 + rep - 1) * rows, NOWHERE)
    index_ref[...] = jnp.full(index_ref.shape, NOWHERE, jnp.int32)
    for group in range(GROUPS):
        part = local[group * PER : (group + 1) * PER]
        index_ref[group, :PER, :] = part
        lows = jnp.min(jnp.where(part < 0, -NOWHERE, part), axis=0, keepdims=True)
        highs = jnp.max(part, axis=0, keepdims=True)
        for block in range(blocks):
            at = slice(block * BLOCK, (block + 1) * BLOCK)
            low, high = jnp.min(lows[:, at]), jnp.max(highs[:, at]) + 1
            low = jnp.where(high <= 0, 0, low // 16 * 16)
            steps = jnp.maximum(1, (high - low + SPAN - 1) // SPAN)
            scalars_ref[group * blocks + block] = low
            scalars_ref[(GROUPS + group) * blocks + block] = steps
    last = 2 * GROUPS * blocks
    scalars_ref[last] = lax.axis_index("chan")
    scalars_ref[last + 1] = curve if shards > 1 else 0
    scalars_ref[last + 2] = rep


def window_copies(window_ref, parts, slots, rep, semaphores):
    rows = parts[0][0].shape[0]
    places = (rows, rep * 2 * rows, (1 - rep) * 2 * rows)
    copies = []
    for part, slot in zip(parts, slots):
        for source, place in zip(part, places):
            target = window_ref.at[slot, pl.ds(pl.multiple_of(place, 16), rows)]
            copies.append(pltpu.make_async_copy(source, target, semaphores.at[len(copies)]))
    return copies


def gather(scalars_ref, column_ref, window_ref, blocks, store, add):
    lanes = lax.broadcasted_iota(jnp.int32, (BLOCK, SPAN), 1).astype(F32).astype(BF16)

    def picked(group, rows, start):
        columns = jnp.clip(column_ref[group, rows, :] - start, -1, SPAN).astype(F32).astype(BF16)
        hot = [
            jnp.where(
                jnp.broadcast_to(columns[:, j : j + 1], (BLOCK, SPAN)) == lanes,
                jnp.ones((), BF16),
                jnp.zeros((), BF16),
            )
            for j in range(PER)
        ]
        at = pl.ds(pl.multiple_of(start, 16), SPAN)
        span = jnp.concatenate([window_ref[c, at, :] for c in range(window_ref.shape[0])], axis=1)
        return jnp.dot(jnp.concatenate(hot, axis=0), span, preferred_element_type=F32).astype(BF16)

    def first(block, _):
        rows = pl.ds(pl.multiple_of(block * BLOCK, BLOCK), BLOCK)
        for group in range(GROUPS):
            result = picked(group, rows, scalars_ref[group * blocks + block])
            for j in range(PER):
                store(group, j, rows, result[j * BLOCK : (j + 1) * BLOCK])
        return 0

    lax.fori_loop(0, blocks, first, 0, unroll=3)

    def rest(at, _):
        group, block = at // blocks, at % blocks
        rows = pl.ds(pl.multiple_of(block * BLOCK, BLOCK), BLOCK)

        def more(step, _):
            result = picked(group, rows, scalars_ref[at] + step * SPAN)
            for j in range(PER):
                add(group, j, rows, result[j * BLOCK : (j + 1) * BLOCK])
            return 0

        lax.fori_loop(1, scalars_ref[GROUPS * blocks + at], more, 0)
        return 0

    lax.fori_loop(0, GROUPS * blocks, rest, 0)


def turn(scratch_ref, value, shards, scalars_ref, at):
    half = value.shape[0] // 2
    size = half // shards
    scratch_ref[0] = value
    place = 0 if shards == 1 else scalars_ref[at + 1]
    rep = scalars_ref[at + 2]
    for core in range(2):
        for step in range(shards):
            source = (rep + core) % 2 * half + (place ^ step) * size
            target = core * half + step * size
            scratch_ref[1, target : target + size] = scratch_ref[
                0, pl.ds(pl.multiple_of(source, size), size)
            ]


def conv_kernel(chans, shards, scale, scalars_ref, index_ref, weight_hbm, cotangent_hbm, *refs):
    parts, refs = [refs[3 * i : 3 * i + 3] for i in range(chans)], refs[3 * chans :]
    out_hbm, grad_hbm, keep_hbm, send_hbm = refs[:4]
    window_ref, column_ref, picked_ref, conv_ref, scratch_ref = refs[4:9]
    weight_ref, cotangent_ref, out_ref, grad_ref, keep_ref, send_ref = refs[9:15]
    window_sems, sems, keep_sems, send_sems = refs[15:]
    rows = index_ref.shape[2]
    blocks = rows // BLOCK
    width = chans * window_ref.shape[2]
    channels = weight_ref.shape[1]
    chan = scalars_ref[2 * GROUPS * blocks]
    rep = scalars_ref[2 * GROUPS * blocks + 2]
    slots = (chan, 1 - chan) if chans == 2 else range(chans)
    copies = window_copies(window_ref, parts, slots, rep, window_sems)
    weight_copy = pltpu.make_async_copy(weight_hbm, weight_ref, sems.at[0])
    cotangent_copy = pltpu.make_async_copy(cotangent_hbm, cotangent_ref, sems.at[1])
    out_copy = pltpu.make_async_copy(out_ref, out_hbm, sems.at[2])
    grad_copy = pltpu.make_async_copy(grad_ref, grad_hbm, sems.at[3])
    for copy in copies:
        copy.start()
    weight_copy.start()
    cotangent_copy.start()
    window_ref[:, 3 * rows :, :] = jnp.zeros((chans, SPAN, channels), BF16)
    for group in range(GROUPS):
        column_ref[group] = index_ref[group].T
    for copy in copies:
        copy.wait()

    def store(group, j, at, value):
        lane = j % 3 * width
        picked_ref[group * 3 + j // 3, at, lane : lane + width] = value

    def add(group, j, at, value):
        lane = j % 3 * width
        picked_ref[group * 3 + j // 3, at, lane : lane + width] += value

    gather(scalars_ref, column_ref, window_ref, blocks, store, add)

    def multiply(three, _):
        weights = jnp.concatenate([weight_ref[three * 3 + j] for j in range(3)], axis=1)
        term = lax.dot_general(picked_ref[three], weights, NT, preferred_element_type=F32)
        conv_ref[...] += term
        return 0

    conv_ref[...] = jnp.zeros_like(conv_ref)
    weight_copy.wait()
    lax.fori_loop(0, 9, multiply, 0, unroll=3)
    conv = conv_ref[...].T
    cotangent_copy.wait()
    sigma = jax.nn.sigmoid(conv)
    out_ref[...] = (conv * sigma).astype(BF16)
    grad = cotangent_ref[...].astype(F32) * (sigma * (1.0 + conv * (1.0 - sigma)))
    grad_ref[...] = grad.T.astype(BF16)
    out_copy.start()
    grad_copy.start()
    turn(scratch_ref, grad.astype(BF16), shards, scalars_ref, 2 * GROUPS * blocks)
    half = channels // 2
    size = half // shards

    def leave(three):
        at = pl.ds(three * 3, 3)
        return (
            pltpu.make_async_copy(keep_ref.at[:, at], keep_hbm.at[:, at], keep_sems.at[three]),
            pltpu.make_async_copy(send_ref.at[:, at], send_hbm.at[:, at], send_sems.at[three]),
        )

    def weigh(three, _):
        term = jnp.dot(scratch_ref[1], picked_ref[three], preferred_element_type=F32) * scale
        for j in range(3):
            both = term[:, j * width : (j + 1) * width].astype(BF16)
            for step in range(shards):
                at = step * size
                keep_ref[step, three * 3 + j] = both[at : at + size]
                send_ref[step, three * 3 + j] = both[half + at : half + at + size]
        for copy in leave(three):
            copy.start()
        return 0

    lax.fori_loop(0, 9, weigh, 0, unroll=3)

    def finish(three, _):
        for copy in leave(three):
            copy.wait()
        return 0

    lax.fori_loop(0, 9, finish, 0)
    out_copy.wait()
    grad_copy.wait()


def coarse_grad_kernel(scalars_ref, index_ref, weight_hbm, *refs):
    part, refs = refs[:3], refs[3:]
    mine_ref, other_ref, window_ref, column_ref, picked_ref, total_ref, weight_ref, sems = refs
    rows = index_ref.shape[2]
    blocks = rows // BLOCK
    offsets, channels, width = weight_ref.shape
    chan = scalars_ref[2 * GROUPS * blocks]
    rep = scalars_ref[2 * GROUPS * blocks + 2]
    copies = window_copies(window_ref, [part], (0,), rep, sems)
    weight_copy = pltpu.make_async_copy(weight_hbm, weight_ref, sems.at[3])
    for copy in copies:
        copy.start()
    weight_copy.start()
    window_ref[0, 3 * rows :, :] = jnp.zeros((SPAN, channels), BF16)
    for group in range(GROUPS):
        column_ref[group] = index_ref[group].T
    for copy in copies:
        copy.wait()

    def store(group, j, at, value):
        lane = (PER - 1 - j) * channels
        picked_ref[GROUPS - 1 - group, at, lane : lane + channels] = value

    def add(group, j, at, value):
        lane = (PER - 1 - j) * channels
        picked_ref[GROUPS - 1 - group, at, lane : lane + channels] += value

    gather(scalars_ref, column_ref, window_ref, blocks, store, add)
    weight_copy.wait()
    result = None
    for group in range(GROUPS):
        weights = weight_ref[group * PER : (group + 1) * PER].reshape(PER * channels, width)
        term = jnp.dot(picked_ref[group], weights, preferred_element_type=F32)
        result = term if result is None else result + term
    result = result.T
    chans = width // channels
    for at in range(chans):
        total_ref[at] = result[at * channels : (at + 1) * channels]
    mine_ref[...] = total_ref[chan]
    for step in range(1, chans):
        other_ref[step - 1] = total_ref[lax.rem(chan + step, chans)].astype(BF16)


def pre_grad_kernel(scale, scalars_ref, children_ref, mask_ref, slope_ref, mine_ref, *refs):
    others, (grad_ref, keep_ref, send_ref, scratch_ref) = refs[:-4], refs[-4:]
    total = mine_ref[...]
    for other in others:
        total = total + other[...].astype(F32)
    grad = (total * slope_ref[...]).astype(BF16)
    grad_ref[...] = grad
    blocks = grad.shape[1] // BLOCK
    turn(scratch_ref, grad, 1, scalars_ref, 2 * GROUPS * blocks)
    half = grad.shape[0] // 2
    fine = children_ref.shape[1]
    for o in range(0, children_ref.shape[0], 2):
        masked = jnp.concatenate(
            [
                children_ref[o + j] * mask_ref[o + j : o + j + 1, :].astype(F32).astype(BF16)
                for j in range(2)
            ],
            axis=0,
        )
        term = lax.dot_general(scratch_ref[1], masked, NT, preferred_element_type=F32) * scale
        both = term.astype(BF16)
        for j in range(2):
            keep_ref[o + j] = both[:half, j * fine : (j + 1) * fine]
            send_ref[o + j] = both[half:, j * fine : (j + 1) * fine]


def cut_kernel(weight_ref, *refs):
    out_refs, scratch_ref = refs[:-1], refs[-1]
    octants, fine, _ = scratch_ref.shape
    chans = len(out_refs)
    size = fine // chans
    chan = lax.axis_index("chan")
    for o in range(octants):
        scratch_ref[o] = weight_ref[o].T
    for by in range(chans):
        at = pl.ds(pl.multiple_of((chan + by) % chans * size, size), size)
        for o in range(octants):
            out_refs[by][o] = scratch_ref[o, at, :]


def children_kernel(mask_ref, *refs):
    out_hbm, out_ref, sems = refs[-3:]
    count = (len(refs) - 3) // 2
    grads, weights = refs[:count], refs[count:-3]
    copies = []
    for o in range(out_ref.shape[0]):
        total = None
        for grad, weight in zip(grads, weights):
            term = jnp.dot(weight[o], grad[...], preferred_element_type=F32)
            term = term.astype(BF16).astype(F32)
            total = term if total is None else total + term
        out_ref[o] = (total * mask_ref[o : o + 1, :].astype(F32)).astype(BF16)
        copies.append(pltpu.make_async_copy(out_ref.at[o], out_hbm.at[o], sems.at[o]))
        copies[-1].start()
    for copy in copies:
        copy.wait()


def apart(shard, by):
    return lax.ppermute(shard, "curve", [(i, i ^ by) for i in range(lax.axis_size("curve"))])


def added(*terms):
    return sum(term.astype(F32) for term in terms).astype(BF16)


def sum_over_curve(total, beside):
    terms = [apart(total[by], by) for by in range(1, 4)]
    own = added(after(total[0], beside), *terms)
    across = apart(own, 2)
    return [own, apart(own, 1), across, apart(across, 1)]


def after(value, *earlier):
    return lax.optimization_barrier((value, *earlier))[0]


def body(children, child_mask, neighbours, down_weight, conv_weight, cotangent):
    octants, fine, rows = children.shape
    offsets, channels, width = conv_weight.shape
    blocks = rows // BLOCK
    chans = lax.axis_size("chan")
    chan = lax.axis_index("chan")
    rep = lax.axis_index("rep")
    curve = lax.axis_index("curve")
    pieces = lax.axis_size(PIECES)
    scale = 1.0 / (rows * pieces) ** 0.5
    shape = jax.ShapeDtypeStruct
    half = channels // 2
    shards = 4 if lax.axis_size("curve") == 4 and half % 64 == 0 else 1
    size = half // shards

    coarse, slope = call(
        down_kernel,
        [shape((rows, channels), BF16), shape((channels, rows), F32)],
        vmem(3),
        [],
    )(children, child_mask, down_weight)

    if chans == 2:
        parts = [coarse, swapped(coarse, "chan")]
    else:
        every = lax.all_gather(coarse, "chan", axis=0)
        parts = [every[i] for i in range(chans)]
    windows = [array for part in parts for array in [part] + met(part)]
    index, scalars = call(
        functools.partial(index_kernel, shards),
        [shape((GROUPS, 16, rows), jnp.int32), shape((2 * GROUPS * blocks + 3,), jnp.int32)],
        vmem(1),
        [],
        vmem(1) + SMEM,
    )(after(neighbours, parts[1]))

    features_out, conv_grad, keep, send = call(
        functools.partial(conv_kernel, chans, shards, scale),
        [
            shape((channels, rows), BF16),
            shape((rows, channels), BF16),
            shape((shards, offsets, size, width), BF16),
            shape((shards, offsets, size, width), BF16),
        ],
        SMEM + vmem(1) + anywhere(2 + 3 * chans),
        [
            pltpu.VMEM((chans, 3 * rows + SPAN, channels), BF16),
            pltpu.VMEM((GROUPS, rows, 16), jnp.int32),
            pltpu.VMEM((9, rows, 3 * width), BF16),
            pltpu.VMEM((rows, channels), F32),
            pltpu.VMEM((2, channels, rows), BF16),
            pltpu.VMEM((offsets, channels, width), BF16),
            pltpu.VMEM((channels, rows), BF16),
            pltpu.VMEM((channels, rows), BF16),
            pltpu.VMEM((rows, channels), BF16),
            pltpu.VMEM((shards, offsets, size, width), BF16),
            pltpu.VMEM((shards, offsets, size, width), BF16),
            pltpu.SemaphoreType.DMA((3 * chans,)),
            pltpu.SemaphoreType.DMA((4,)),
            pltpu.SemaphoreType.DMA((9,)),
            pltpu.SemaphoreType.DMA((9,)),
        ],
        anywhere(4),
    )(scalars, index, conv_weight, cotangent, *windows)

    near = met(conv_grad)
    received = swapped(send, "rep")
    total = [added(keep[i], received[i]) for i in range(shards)]

    mine, others = call(
        coarse_grad_kernel,
        [shape((channels, rows), F32), shape((chans - 1, channels, rows), BF16)],
        SMEM + vmem(1) + anywhere(4),
        [
            pltpu.VMEM((1, 3 * rows + SPAN, channels), BF16),
            pltpu.VMEM((GROUPS, rows, 16), jnp.int32),
            pltpu.VMEM((GROUPS, rows, PER * channels), BF16),
            pltpu.VMEM((chans, channels, rows), F32),
            pltpu.VMEM((offsets, channels, width), BF16),
            pltpu.SemaphoreType.DMA((4,)),
        ],
    )(after(scalars, *total), index, conv_weight, conv_grad, *near)
    received = [
        lax.ppermute(others[by - 1], "chan", [(i, (i + by) % chans) for i in range(chans)])
        for by in range(1, chans)
    ]
    mine_fine = fine // chans
    cut = call(
        cut_kernel,
        [shape((octants, mine_fine, channels), BF16)] * chans,
        vmem(1),
        [pltpu.VMEM((octants, fine, channels), BF16)],
    )(after(down_weight, mine))
    weights = [
        lax.ppermute(cut[by], "chan", [(i, (i + by) % chans) for i in range(chans)])
        if by
        else cut[by]
        for by in range(chans)
    ]
    pre_grad, keep, send = call(
        functools.partial(pre_grad_kernel, scale),
        [
            shape((channels, rows), BF16),
            shape((octants, half, fine), BF16),
            shape((octants, half, fine), BF16),
        ],
        SMEM + vmem(4 + len(received)),
        [pltpu.VMEM((2, channels, rows), BF16)],
    )(after(scalars, *weights), children, child_mask, slope, mine, *received)

    if shards == 4:
        sums = sum_over_curve(total, pre_grad)
    else:
        sums = [lax.psum(total[0], "curve")]
    sent_grad, send = after(pre_grad, sums[0]), after(send, sums[0])
    grads = [
        lax.ppermute(sent_grad, "chan", [(i, (i + by) % chans) for i in range(chans)])
        if by
        else pre_grad
        for by in range(chans)
    ]
    children_grad = call(
        children_kernel,
        shape((octants, mine_fine, rows), BF16),
        vmem(1 + 2 * chans),
        [pltpu.VMEM((octants, mine_fine, rows), BF16), pltpu.SemaphoreType.DMA((octants,))],
        anywhere(1)[0],
    )(child_mask, *grads, *weights)

    down = added(keep, swapped(send, "rep"))
    if shards == 4:
        down = added(after(down, *grads[1:]), apart(down, 1))
        down = added(after(down, sums[2], children_grad), apart(down, 2))
    else:
        down = lax.psum(down, "curve")
    def joined(pieces, like):
        result = jnp.broadcast_to(after(jnp.zeros((), F32), mine), like.shape)
        for row, piece in pieces:
            result = lax.dynamic_update_slice(result, piece.astype(F32), (0, row, 0))
        return result

    rows_of = [rep * half, (1 - rep) * half]
    down_weight_grad = joined(zip(rows_of, (down, swapped(down, "rep"))), down_weight)
    pieces = []
    for step, part in enumerate(sums):
        at = (curve ^ step) * size if shards > 1 else 0
        pieces += [(rows_of[0] + at, part), (rows_of[1] + at, swapped(part, "rep"))]
    conv_weight_grad = joined(pieces, conv_weight)
    return (features_out, children_grad, conv_weight_grad, down_weight_grad)


def solution(mesh):
    in_specs = (
        P(None, None, ("snap", "curve", "rep")),
        P(None, ("snap", "curve", "rep")),
        P(None, ("snap", "curve", "rep")),
        P(None, "chan", None),
        P(None, "chan", None),
        P("chan", ("snap", "curve", "rep")),
    )
    out_specs = (
        P("chan", ("snap", "curve", "rep")),
        P(None, "chan", ("snap", "curve", "rep")),
        P("snap", "chan", None),
        P("snap", "chan", None),
    )
    return jax.shard_map(body, mesh=mesh, in_specs=in_specs, out_specs=out_specs, check_vma=False)
```

```python
import functools

import jax
import jax.numpy as jnp
from jax import lax
from jax.experimental import pallas as pl
from jax.experimental.pallas import tpu as pltpu
from jax.sharding import PartitionSpec as P

BLOCK = 128
SPAN = 256
GROUPS = 3
PER = 9
VMEM_LIMIT = 28 * 1024 * 1024
PIECES = ("curve", "rep")
F32 = jnp.float32
BF16 = jnp.bfloat16
NOWHERE = -(2**20)
NT = (((1,), (1,)), ((), ()))


def silu_slope(value):
    sigma = jax.nn.sigmoid(value)
    return sigma * (1.0 + value * (1.0 - sigma))


def met(shard):
    devices = lax.axis_size(PIECES)
    pairs = [(i, i + 1) for i in range(1, devices - 1, 2)]
    pairs += [(j, i) for i, j in pairs]
    return [lax.ppermute(shard, PIECES, pairs), swapped(shard, "rep")]


def swapped(shard, axis):
    return lax.ppermute(shard, axis, [(0, 1), (1, 0)])


def call(kernel, out_shape, in_specs, scratch, out_specs=None):
    options = {} if out_specs is None else {"out_specs": out_specs}
    return pl.pallas_call(
        kernel,
        out_shape=out_shape,
        in_specs=in_specs,
        scratch_shapes=scratch,
        compiler_params=pltpu.CompilerParams(vmem_limit_bytes=VMEM_LIMIT),
        cost_estimate=pl.CostEstimate(flops=0, bytes_accessed=0, transcendentals=0),
        **options,
    )


def anywhere(count):
    return [pl.BlockSpec(memory_space=pl.ANY)] * count


def vmem(count):
    return [pl.BlockSpec(memory_space=pltpu.VMEM)] * count


SMEM = [pl.BlockSpec(memory_space=pltpu.SMEM)]


def down_kernel(children_ref, mask_ref, weight_ref, coarse_ref, slope_ref):
    octants = children_ref.shape[0]
    total = None
    for o in range(0, octants, 2):
        masked = jnp.concatenate(
            [
                children_ref[o + j] * mask_ref[o + j : o + j + 1, :].astype(F32).astype(BF16)
                for j in range(2)
            ],
            axis=0,
        )
        weights = jnp.concatenate([weight_ref[o], weight_ref[o + 1]], axis=1)
        term = jnp.dot(weights, masked, preferred_element_type=F32)
        total = term if total is None else total + term
    slope_ref[...] = silu_slope(total)
    coarse_ref[...] = (total * jax.nn.sigmoid(total)).T.astype(BF16)


def index_kernel(shards, neighbours_ref, index_ref, scalars_ref):
    offsets, rows = neighbours_ref.shape
    blocks = rows // BLOCK
    curve, rep = lax.axis_index("curve"), lax.axis_index("rep")
    names = neighbours_ref[...]
    local = jnp.where(names >= 0, names - (curve * 2 + rep - 1) * rows, NOWHERE)
    index_ref[...] = jnp.full(index_ref.shape, NOWHERE, jnp.int32)
    for group in range(GROUPS):
        part = local[group * PER : (group + 1) * PER]
        index_ref[group, :PER, :] = part
        lows = jnp.min(jnp.where(part < 0, -NOWHERE, part), axis=0, keepdims=True)
        highs = jnp.max(part, axis=0, keepdims=True)
        for block in range(blocks):
            at = slice(block * BLOCK, (block + 1) * BLOCK)
            low, high = jnp.min(lows[:, at]), jnp.max(highs[:, at]) + 1
            low = jnp.where(high <= 0, 0, low // 16 * 16)
            steps = jnp.maximum(1, (high - low + SPAN - 1) // SPAN)
            scalars_ref[group * blocks + block] = low
            scalars_ref[(GROUPS + group) * blocks + block] = steps
    last = 2 * GROUPS * blocks
    scalars_ref[last] = lax.axis_index("chan")
    scalars_ref[last + 1] = curve if shards > 1 else 0
    scalars_ref[last + 2] = rep


def window_copies(window_ref, parts, slots, rep, semaphores):
    rows = parts[0][0].shape[0]
    places = (rows, rep * 2 * rows, (1 - rep) * 2 * rows)
    copies = []
    for part, slot in zip(parts, slots):
        for source, place in zip(part, places):
            target = window_ref.at[slot, pl.ds(pl.multiple_of(place, 16), rows)]
            copies.append(pltpu.make_async_copy(source, target, semaphores.at[len(copies)]))
    return copies


def gather(scalars_ref, column_ref, window_ref, blocks, store, add):
    lanes = lax.broadcasted_iota(jnp.int32, (BLOCK, SPAN), 1).astype(F32).astype(BF16)

    def picked(group, rows, start):
        columns = jnp.clip(column_ref[group, rows, :] - start, -1, SPAN).astype(F32).astype(BF16)
        hot = [
            jnp.where(
                jnp.broadcast_to(columns[:, j : j + 1], (BLOCK, SPAN)) == lanes,
                jnp.ones((), BF16),
                jnp.zeros((), BF16),
            )
            for j in range(PER)
        ]
        at = pl.ds(pl.multiple_of(start, 16), SPAN)
        span = jnp.concatenate([window_ref[c, at, :] for c in range(window_ref.shape[0])], axis=1)
        return jnp.dot(jnp.concatenate(hot, axis=0), span, preferred_element_type=F32).astype(BF16)

    def first(block, _):
        rows = pl.ds(pl.multiple_of(block * BLOCK, BLOCK), BLOCK)
        for group in range(GROUPS):
            result = picked(group, rows, scalars_ref[group * blocks + block])
            for j in range(PER):
                store(group, j, rows, result[j * BLOCK : (j + 1) * BLOCK])
        return 0

    lax.fori_loop(0, blocks, first, 0, unroll=3)

    def rest(at, _):
        group, block = at // blocks, at % blocks
        rows = pl.ds(pl.multiple_of(block * BLOCK, BLOCK), BLOCK)

        def more(step, _):
            result = picked(group, rows, scalars_ref[at] + step * SPAN)
            for j in range(PER):
                add(group, j, rows, result[j * BLOCK : (j + 1) * BLOCK])
            return 0

        lax.fori_loop(1, scalars_ref[GROUPS * blocks + at], more, 0)
        return 0

    lax.fori_loop(0, GROUPS * blocks, rest, 0)


def turn(scratch_ref, value, shards, scalars_ref, at):
    half = value.shape[0] // 2
    size = half // shards
    scratch_ref[0] = value
    place = 0 if shards == 1 else scalars_ref[at + 1]
    rep = scalars_ref[at + 2]
    for core in range(2):
        for step in range(shards):
            source = (rep + core) % 2 * half + (place ^ step) * size
            target = core * half + step * size
            scratch_ref[1, target : target + size] = scratch_ref[
                0, pl.ds(pl.multiple_of(source, size), size)
            ]


def conv_kernel(chans, shards, scale, scalars_ref, index_ref, weight_hbm, cotangent_hbm, *refs):
    parts, refs = [refs[3 * i : 3 * i + 3] for i in range(chans)], refs[3 * chans :]
    out_hbm, grad_hbm, keep_hbm, send_hbm = refs[:4]
    window_ref, column_ref, picked_ref, conv_ref, scratch_ref = refs[4:9]
    weight_ref, cotangent_ref, out_ref, grad_ref, keep_ref, send_ref = refs[9:15]
    window_sems, sems, keep_sems, send_sems = refs[15:]
    rows = index_ref.shape[2]
    blocks = rows // BLOCK
    width = chans * window_ref.shape[2]
    channels = weight_ref.shape[1]
    chan = scalars_ref[2 * GROUPS * blocks]
    rep = scalars_ref[2 * GROUPS * blocks + 2]
    slots = (chan, 1 - chan) if chans == 2 else range(chans)
    copies = window_copies(window_ref, parts, slots, rep, window_sems)
    weight_copy = pltpu.make_async_copy(weight_hbm, weight_ref, sems.at[0])
    cotangent_copy = pltpu.make_async_copy(cotangent_hbm, cotangent_ref, sems.at[1])
    out_copy = pltpu.make_async_copy(out_ref, out_hbm, sems.at[2])
    grad_copy = pltpu.make_async_copy(grad_ref, grad_hbm, sems.at[3])
    for copy in copies:
        copy.start()
    weight_copy.start()
    cotangent_copy.start()
    window_ref[:, 3 * rows :, :] = jnp.zeros((chans, SPAN, channels), BF16)
    for group in range(GROUPS):
        column_ref[group] = index_ref[group].T
    for copy in copies:
        copy.wait()

    def store(group, j, at, value):
        lane = j % 3 * width
        picked_ref[group * 3 + j // 3, at, lane : lane + width] = value

    def add(group, j, at, value):
        lane = j % 3 * width
        picked_ref[group * 3 + j // 3, at, lane : lane + width] += value

    gather(scalars_ref, column_ref, window_ref, blocks, store, add)

    def multiply(three, _):
        weights = jnp.concatenate([weight_ref[three * 3 + j] for j in range(3)], axis=1)
        term = lax.dot_general(picked_ref[three], weights, NT, preferred_element_type=F32)
        conv_ref[...] += term
        return 0

    conv_ref[...] = jnp.zeros_like(conv_ref)
    weight_copy.wait()
    lax.fori_loop(0, 9, multiply, 0, unroll=3)
    conv = conv_ref[...].T
    cotangent_copy.wait()
    sigma = jax.nn.sigmoid(conv)
    out_ref[...] = (conv * sigma).astype(BF16)
    grad = cotangent_ref[...].astype(F32) * (sigma * (1.0 + conv * (1.0 - sigma)))
    grad_ref[...] = grad.T.astype(BF16)
    out_copy.start()
    grad_copy.start()
    turn(scratch_ref, grad.astype(BF16), shards, scalars_ref, 2 * GROUPS * blocks)
    half = channels // 2
    size = half // shards

    def leave(three):
        at = pl.ds(three * 3, 3)
        return (
            pltpu.make_async_copy(keep_ref.at[:, at], keep_hbm.at[:, at], keep_sems.at[three]),
            pltpu.make_async_copy(send_ref.at[:, at], send_hbm.at[:, at], send_sems.at[three]),
        )

    def weigh(three, _):
        term = jnp.dot(scratch_ref[1], picked_ref[three], preferred_element_type=F32) * scale
        for j in range(3):
            both = term[:, j * width : (j + 1) * width].astype(BF16)
            for step in range(shards):
                at = step * size
                keep_ref[step, three * 3 + j] = both[at : at + size]
                send_ref[step, three * 3 + j] = both[half + at : half + at + size]
        for copy in leave(three):
            copy.start()
        return 0

    lax.fori_loop(0, 9, weigh, 0, unroll=3)

    def finish(three, _):
        for copy in leave(three):
            copy.wait()
        return 0

    lax.fori_loop(0, 9, finish, 0)
    out_copy.wait()
    grad_copy.wait()


def coarse_grad_kernel(scalars_ref, index_ref, weight_hbm, *refs):
    part, refs = refs[:3], refs[3:]
    mine_ref, other_ref, window_ref, column_ref, picked_ref, total_ref, weight_ref, sems = refs
    rows = index_ref.shape[2]
    blocks = rows // BLOCK
    offsets, channels, width = weight_ref.shape
    chan = scalars_ref[2 * GROUPS * blocks]
    rep = scalars_ref[2 * GROUPS * blocks + 2]
    copies = window_copies(window_ref, [part], (0,), rep, sems)
    weight_copy = pltpu.make_async_copy(weight_hbm, weight_ref, sems.at[3])
    for copy in copies:
        copy.start()
    weight_copy.start()
    window_ref[0, 3 * rows :, :] = jnp.zeros((SPAN, channels), BF16)
    for group in range(GROUPS):
        column_ref[group] = index_ref[group].T
    for copy in copies:
        copy.wait()

    def store(group, j, at, value):
        lane = (PER - 1 - j) * channels
        picked_ref[GROUPS - 1 - group, at, lane : lane + channels] = value

    def add(group, j, at, value):
        lane = (PER - 1 - j) * channels
        picked_ref[GROUPS - 1 - group, at, lane : lane + channels] += value

    gather(scalars_ref, column_ref, window_ref, blocks, store, add)
    weight_copy.wait()
    result = None
    for group in range(GROUPS):
        weights = weight_ref[group * PER : (group + 1) * PER].reshape(PER * channels, width)
        term = jnp.dot(picked_ref[group], weights, preferred_element_type=F32)
        result = term if result is None else result + term
    result = result.T
    chans = width // channels
    for at in range(chans):
        total_ref[at] = result[at * channels : (at + 1) * channels]
    mine_ref[...] = total_ref[chan]
    for step in range(1, chans):
        other_ref[step - 1] = total_ref[lax.rem(chan + step, chans)].astype(BF16)


def pre_grad_kernel(scale, scalars_ref, children_ref, mask_ref, slope_ref, mine_ref, *refs):
    others, (grad_ref, keep_ref, send_ref, scratch_ref) = refs[:-4], refs[-4:]
    total = mine_ref[...]
    for other in others:
        total = total + other[...].astype(F32)
    grad = (total * slope_ref[...]).astype(BF16)
    grad_ref[...] = grad
    blocks = grad.shape[1] // BLOCK
    turn(scratch_ref, grad, 1, scalars_ref, 2 * GROUPS * blocks)
    half = grad.shape[0] // 2
    fine = children_ref.shape[1]
    for o in range(0, children_ref.shape[0], 2):
        masked = jnp.concatenate(
            [
                children_ref[o + j] * mask_ref[o + j : o + j + 1, :].astype(F32).astype(BF16)
                for j in range(2)
            ],
            axis=0,
        )
        term = lax.dot_general(scratch_ref[1], masked, NT, preferred_element_type=F32) * scale
        both = term.astype(BF16)
        for j in range(2):
            keep_ref[o + j] = both[:half, j * fine : (j + 1) * fine]
            send_ref[o + j] = both[half:, j * fine : (j + 1) * fine]


def cut_kernel(weight_ref, *refs):
    out_refs, scratch_ref = refs[:-1], refs[-1]
    octants, fine, _ = scratch_ref.shape
    chans = len(out_refs)
    size = fine // chans
    chan = lax.axis_index("chan")
    for o in range(octants):
        scratch_ref[o] = weight_ref[o].T
    for by in range(chans):
        at = pl.ds(pl.multiple_of((chan + by) % chans * size, size), size)
        for o in range(octants):
            out_refs[by][o] = scratch_ref[o, at, :]


def children_kernel(mask_ref, *refs):
    out_hbm, out_ref, sems = refs[-3:]
    count = (len(refs) - 3) // 2
    grads, weights = refs[:count], refs[count:-3]
    copies = []
    for o in range(out_ref.shape[0]):
        total = None
        for grad, weight in zip(grads, weights):
            term = jnp.dot(weight[o], grad[...], preferred_element_type=F32)
            term = term.astype(BF16).astype(F32)
            total = term if total is None else total + term
        out_ref[o] = (total * mask_ref[o : o + 1, :].astype(F32)).astype(BF16)
        copies.append(pltpu.make_async_copy(out_ref.at[o], out_hbm.at[o], sems.at[o]))
        copies[-1].start()
    for copy in copies:
        copy.wait()


def apart(shard, by):
    return lax.ppermute(shard, "curve", [(i, i ^ by) for i in range(lax.axis_size("curve"))])


def added(*terms):
    return sum(term.astype(F32) for term in terms).astype(BF16)


def sum_over_curve(total, beside):
    terms = [apart(total[by], by) for by in range(1, 4)]
    own = added(after(total[0], beside), *terms)
    across = apart(own, 2)
    return [own, apart(own, 1), across, apart(across, 1)]


def after(value, *earlier):
    return lax.optimization_barrier((value, *earlier))[0]


def body(children, child_mask, neighbours, down_weight, conv_weight, cotangent):
    octants, fine, rows = children.shape
    offsets, channels, width = conv_weight.shape
    blocks = rows // BLOCK
    chans = lax.axis_size("chan")
    chan = lax.axis_index("chan")
    rep = lax.axis_index("rep")
    curve = lax.axis_index("curve")
    pieces = lax.axis_size(PIECES)
    scale = 1.0 / (rows * pieces) ** 0.5
    shape = jax.ShapeDtypeStruct
    half = channels // 2
    shards = 4 if lax.axis_size("curve") == 4 and half % 64 == 0 else 1
    size = half // shards

    coarse, slope = call(
        down_kernel,
        [shape((rows, channels), BF16), shape((channels, rows), F32)],
        vmem(3),
        [],
    )(children, child_mask, down_weight)

    if chans == 2:
        parts = [coarse, swapped(coarse, "chan")]
    else:
        every = lax.all_gather(coarse, "chan", axis=0)
        parts = [every[i] for i in range(chans)]
    windows = [array for part in parts for array in [part] + met(part)]
    index, scalars = call(
        functools.partial(index_kernel, shards),
        [shape((GROUPS, 16, rows), jnp.int32), shape((2 * GROUPS * blocks + 3,), jnp.int32)],
        vmem(1),
        [],
        vmem(1) + SMEM,
    )(after(neighbours, parts[1]))

    features_out, conv_grad, keep, send = call(
        functools.partial(conv_kernel, chans, shards, scale),
        [
            shape((channels, rows), BF16),
            shape((rows, channels), BF16),
            shape((shards, offsets, size, width), BF16),
            shape((shards, offsets, size, width), BF16),
        ],
        SMEM + vmem(1) + anywhere(2 + 3 * chans),
        [
            pltpu.VMEM((chans, 3 * rows + SPAN, channels), BF16),
            pltpu.VMEM((GROUPS, rows, 16), jnp.int32),
            pltpu.VMEM((9, rows, 3 * width), BF16),
            pltpu.VMEM((rows, channels), F32),
            pltpu.VMEM((2, channels, rows), BF16),
            pltpu.VMEM((offsets, channels, width), BF16),
            pltpu.VMEM((channels, rows), BF16),
            pltpu.VMEM((channels, rows), BF16),
            pltpu.VMEM((rows, channels), BF16),
            pltpu.VMEM((shards, offsets, size, width), BF16),
            pltpu.VMEM((shards, offsets, size, width), BF16),
            pltpu.SemaphoreType.DMA((3 * chans,)),
            pltpu.SemaphoreType.DMA((4,)),
            pltpu.SemaphoreType.DMA((9,)),
            pltpu.SemaphoreType.DMA((9,)),
        ],
        anywhere(4),
    )(scalars, index, conv_weight, cotangent, *windows)

    near = met(conv_grad)
    received = swapped(send, "rep")
    total = [added(keep[i], received[i]) for i in range(shards)]

    mine, others = call(
        coarse_grad_kernel,
        [shape((channels, rows), F32), shape((chans - 1, channels, rows), BF16)],
        SMEM + vmem(1) + anywhere(4),
        [
            pltpu.VMEM((1, 3 * rows + SPAN, channels), BF16),
            pltpu.VMEM((GROUPS, rows, 16), jnp.int32),
            pltpu.VMEM((GROUPS, rows, PER * channels), BF16),
            pltpu.VMEM((chans, channels, rows), F32),
            pltpu.VMEM((offsets, channels, width), BF16),
            pltpu.SemaphoreType.DMA((4,)),
        ],
    )(after(scalars, *total), index, conv_weight, conv_grad, *near)
    received = [
        lax.ppermute(others[by - 1], "chan", [(i, (i + by) % chans) for i in range(chans)])
        for by in range(1, chans)
    ]
    mine_fine = fine // chans
    cut = call(
        cut_kernel,
        [shape((octants, mine_fine, channels), BF16)] * chans,
        vmem(1),
        [pltpu.VMEM((octants, fine, channels), BF16)],
    )(after(down_weight, mine))
    blank = [
        jnp.broadcast_to(after(jnp.zeros((), F32), mine), like.shape)
        for like in (conv_weight, down_weight)
    ]
    pre_grad, keep, send = call(
        functools.partial(pre_grad_kernel, scale),
        [
            shape((channels, rows), BF16),
            shape((octants, half, fine), BF16),
            shape((octants, half, fine), BF16),
        ],
        SMEM + vmem(4 + len(received)),
        [pltpu.VMEM((2, channels, rows), BF16)],
    )(after(scalars, *cut, *blank), children, child_mask, slope, mine, *received)

    if shards == 4:
        sums = sum_over_curve(total, pre_grad)
    else:
        sums = [lax.psum(total[0], "curve")]
    own = sums[0]
    sent_grad, send = after(pre_grad, own), after(send, own)
    grads = [
        lax.ppermute(sent_grad, "chan", [(i, (i + by) % chans) for i in range(chans)])
        if by
        else pre_grad
        for by in range(chans)
    ]
    weights = [
        lax.ppermute(after(cut[by], own), "chan", [(i, (i + by) % chans) for i in range(chans)])
        if by
        else cut[by]
        for by in range(chans)
    ]
    children_grad = call(
        children_kernel,
        shape((octants, mine_fine, rows), BF16),
        vmem(1 + 2 * chans),
        [pltpu.VMEM((octants, mine_fine, rows), BF16), pltpu.SemaphoreType.DMA((octants,))],
        anywhere(1)[0],
    )(child_mask, *grads, *weights)

    down = added(keep, swapped(send, "rep"))
    if shards == 4:
        down = added(after(down, *grads[1:]), apart(down, 1))
        down = added(after(down, sums[2], children_grad), apart(down, 2))
    else:
        down = lax.psum(down, "curve")
    def joined(result, pieces):
        for row, piece in pieces:
            result = lax.dynamic_update_slice(result, piece.astype(F32), (0, row, 0))
        return result

    rows_of = [rep * half, (1 - rep) * half]
    down_weight_grad = joined(blank[1], zip(rows_of, (down, swapped(down, "rep"))))
    pieces = []
    for step, part in enumerate(sums):
        at = (curve ^ step) * size if shards > 1 else 0
        mine = part if step else after(part, *sums[2:3])
        pieces += [(rows_of[0] + at, mine), (rows_of[1] + at, swapped(part, "rep"))]
    conv_weight_grad = joined(blank[0], pieces)
    return (features_out, children_grad, conv_weight_grad, down_weight_grad)


def solution(mesh):
    in_specs = (
        P(None, None, ("snap", "curve", "rep")),
        P(None, ("snap", "curve", "rep")),
        P(None, ("snap", "curve", "rep")),
        P(None, "chan", None),
        P(None, "chan", None),
        P("chan", ("snap", "curve", "rep")),
    )
    out_specs = (
        P("chan", ("snap", "curve", "rep")),
        P(None, "chan", ("snap", "curve", "rep")),
        P("snap", "chan", None),
        P("snap", "chan", None),
    )
    return jax.shard_map(body, mesh=mesh, in_specs=in_specs, out_specs=out_specs, check_vma=False)
```

```python
import functools

import jax
import jax.numpy as jnp
from jax import lax
from jax.experimental import pallas as pl
from jax.experimental.pallas import tpu as pltpu
from jax.sharding import PartitionSpec as P

BLOCK = 128
SPAN = 256
GROUPS = 3
PER = 9
VMEM_LIMIT = 28 * 1024 * 1024
WHOLE_LIMIT = 60 * 1024 * 1024
PIECES = ("curve", "rep")
F32 = jnp.float32
BF16 = jnp.bfloat16
NOWHERE = -(2**20)
NT = (((1,), (1,)), ((), ()))


def silu_slope(value):
    sigma = jax.nn.sigmoid(value)
    return sigma * (1.0 + value * (1.0 - sigma))


def met(shard):
    devices = lax.axis_size(PIECES)
    pairs = [(i, i + 1) for i in range(1, devices - 1, 2)]
    pairs += [(j, i) for i, j in pairs]
    return [lax.ppermute(shard, PIECES, pairs), swapped(shard, "rep")]


def swapped(shard, axis):
    return lax.ppermute(shard, axis, [(0, 1), (1, 0)])


def call(kernel, out_shape, in_specs, scratch, out_specs=None, limit=VMEM_LIMIT):
    options = {} if out_specs is None else {"out_specs": out_specs}
    return pl.pallas_call(
        kernel,
        out_shape=out_shape,
        in_specs=in_specs,
        scratch_shapes=scratch,
        compiler_params=pltpu.CompilerParams(vmem_limit_bytes=limit),
        cost_estimate=pl.CostEstimate(flops=0, bytes_accessed=0, transcendentals=0),
        **options,
    )


def anywhere(count):
    return [pl.BlockSpec(memory_space=pl.ANY)] * count


def vmem(count):
    return [pl.BlockSpec(memory_space=pltpu.VMEM)] * count


SMEM = [pl.BlockSpec(memory_space=pltpu.SMEM)]


def down_kernel(children_ref, mask_ref, weight_ref, coarse_ref, slope_ref):
    octants = children_ref.shape[0]
    total = None
    for o in range(0, octants, 2):
        masked = jnp.concatenate(
            [
                children_ref[o + j] * mask_ref[o + j : o + j + 1, :].astype(F32).astype(BF16)
                for j in range(2)
            ],
            axis=0,
        )
        weights = jnp.concatenate([weight_ref[o], weight_ref[o + 1]], axis=1)
        term = jnp.dot(weights, masked, preferred_element_type=F32)
        total = term if total is None else total + term
    slope_ref[...] = silu_slope(total)
    coarse_ref[...] = (total * jax.nn.sigmoid(total)).T.astype(BF16)


def index_kernel(shards, neighbours_ref, index_ref, scalars_ref):
    offsets, rows = neighbours_ref.shape
    blocks = rows // BLOCK
    curve, rep = lax.axis_index("curve"), lax.axis_index("rep")
    names = neighbours_ref[...]
    local = jnp.where(names >= 0, names - (curve * 2 + rep - 1) * rows, NOWHERE)
    index_ref[...] = jnp.full(index_ref.shape, NOWHERE, jnp.int32)
    for group in range(GROUPS):
        part = local[group * PER : (group + 1) * PER]
        index_ref[group, :PER, :] = part
        lows = jnp.min(jnp.where(part < 0, -NOWHERE, part), axis=0, keepdims=True)
        highs = jnp.max(part, axis=0, keepdims=True)
        for block in range(blocks):
            at = slice(block * BLOCK, (block + 1) * BLOCK)
            low, high = jnp.min(lows[:, at]), jnp.max(highs[:, at]) + 1
            low = jnp.where(high <= 0, 0, low // 16 * 16)
            steps = jnp.maximum(1, (high - low + SPAN - 1) // SPAN)
            scalars_ref[group * blocks + block] = low
            scalars_ref[(GROUPS + group) * blocks + block] = steps
    last = 2 * GROUPS * blocks
    scalars_ref[last] = lax.axis_index("chan")
    scalars_ref[last + 1] = curve if shards > 1 else 0
    scalars_ref[last + 2] = rep


def fill_window(window_ref, parts, slots, rep):
    rows = parts[0][0].shape[0]
    places = (rows, rep * 2 * rows, (1 - rep) * 2 * rows)
    for part, slot in zip(parts, slots):
        for source, place in zip(part, places):
            window_ref[slot, pl.ds(pl.multiple_of(place, 16), rows), :] = source[...]
    blank = (window_ref.shape[0], window_ref.shape[1] - 3 * rows, window_ref.shape[2])
    window_ref[:, 3 * rows :, :] = jnp.zeros(blank, BF16)


def gather(scalars_ref, column_ref, window_ref, blocks, store, add):
    lanes = lax.broadcasted_iota(jnp.int32, (BLOCK, SPAN), 1).astype(F32).astype(BF16)

    def picked(group, rows, start):
        columns = jnp.clip(column_ref[group, rows, :] - start, -1, SPAN).astype(F32).astype(BF16)
        hot = [
            jnp.where(
                jnp.broadcast_to(columns[:, j : j + 1], (BLOCK, SPAN)) == lanes,
                jnp.ones((), BF16),
                jnp.zeros((), BF16),
            )
            for j in range(PER)
        ]
        at = pl.ds(pl.multiple_of(start, 16), SPAN)
        span = jnp.concatenate([window_ref[c, at, :] for c in range(window_ref.shape[0])], axis=1)
        return jnp.dot(jnp.concatenate(hot, axis=0), span, preferred_element_type=F32).astype(BF16)

    def first(block, _):
        rows = pl.ds(pl.multiple_of(block * BLOCK, BLOCK), BLOCK)
        for group in range(GROUPS):
            result = picked(group, rows, scalars_ref[group * blocks + block])
            for j in range(PER):
                store(group, j, rows, result[j * BLOCK : (j + 1) * BLOCK])
        return 0

    lax.fori_loop(0, blocks, first, 0, unroll=3)

    def rest(at, _):
        group, block = at // blocks, at % blocks
        rows = pl.ds(pl.multiple_of(block * BLOCK, BLOCK), BLOCK)

        def more(step, _):
            result = picked(group, rows, scalars_ref[at] + step * SPAN)
            for j in range(PER):
                add(group, j, rows, result[j * BLOCK : (j + 1) * BLOCK])
            return 0

        lax.fori_loop(1, scalars_ref[GROUPS * blocks + at], more, 0)
        return 0

    lax.fori_loop(0, GROUPS * blocks, rest, 0)


def turn(scratch_ref, value, shards, scalars_ref, at):
    half = value.shape[0] // 2
    size = half // shards
    scratch_ref[0] = value
    place = 0 if shards == 1 else scalars_ref[at + 1]
    rep = scalars_ref[at + 2]
    for core in range(2):
        for step in range(shards):
            source = (rep + core) % 2 * half + (place ^ step) * size
            target = core * half + step * size
            scratch_ref[1, target : target + size] = scratch_ref[
                0, pl.ds(pl.multiple_of(source, size), size)
            ]


def conv_kernel(chans, shards, scale, scalars_ref, index_ref, weight_ref, cotangent_ref, *refs):
    parts, refs = [refs[3 * i : 3 * i + 3] for i in range(chans)], refs[3 * chans :]
    out_ref, grad_ref, keep_ref, send_ref = refs[:4]
    window_ref, column_ref, picked_ref, conv_ref, scratch_ref = refs[4:]
    rows = index_ref.shape[2]
    blocks = rows // BLOCK
    width = chans * window_ref.shape[2]
    channels = weight_ref.shape[1]
    chan = scalars_ref[2 * GROUPS * blocks]
    rep = scalars_ref[2 * GROUPS * blocks + 2]
    slots = (chan, 1 - chan) if chans == 2 else range(chans)
    fill_window(window_ref, parts, slots, rep)
    for group in range(GROUPS):
        column_ref[group] = index_ref[group].T

    def store(group, j, at, value):
        lane = j % 3 * width
        picked_ref[group * 3 + j // 3, at, lane : lane + width] = value

    def add(group, j, at, value):
        lane = j % 3 * width
        picked_ref[group * 3 + j // 3, at, lane : lane + width] += value

    gather(scalars_ref, column_ref, window_ref, blocks, store, add)

    def multiply(three, _):
        weights = jnp.concatenate([weight_ref[three * 3 + j] for j in range(3)], axis=1)
        term = lax.dot_general(picked_ref[three], weights, NT, preferred_element_type=F32)
        conv_ref[...] += term
        return 0

    conv_ref[...] = jnp.zeros_like(conv_ref)
    lax.fori_loop(0, 9, multiply, 0, unroll=3)
    conv = conv_ref[...].T
    sigma = jax.nn.sigmoid(conv)
    out_ref[...] = (conv * sigma).astype(BF16)
    grad = cotangent_ref[...].astype(F32) * (sigma * (1.0 + conv * (1.0 - sigma)))
    grad_ref[...] = grad.T.astype(BF16)
    turn(scratch_ref, grad.astype(BF16), shards, scalars_ref, 2 * GROUPS * blocks)
    half = channels // 2
    size = half // shards

    def weigh(three, _):
        term = jnp.dot(scratch_ref[1], picked_ref[three], preferred_element_type=F32) * scale
        for j in range(3):
            both = term[:, j * width : (j + 1) * width].astype(BF16)
            for step in range(shards):
                at = step * size
                keep_ref[step, three * 3 + j] = both[at : at + size]
                send_ref[step, three * 3 + j] = both[half + at : half + at + size]
        return 0

    lax.fori_loop(0, 9, weigh, 0, unroll=3)


def coarse_grad_kernel(scalars_ref, index_ref, weight_ref, *refs):
    part, refs = refs[:3], refs[3:]
    mine_ref, other_ref, window_ref, column_ref, picked_ref, total_ref = refs
    rows = index_ref.shape[2]
    blocks = rows // BLOCK
    offsets, channels, width = weight_ref.shape
    chan = scalars_ref[2 * GROUPS * blocks]
    rep = scalars_ref[2 * GROUPS * blocks + 2]
    fill_window(window_ref, [part], (0,), rep)
    for group in range(GROUPS):
        column_ref[group] = index_ref[group].T

    def store(group, j, at, value):
        lane = (PER - 1 - j) * channels
        picked_ref[GROUPS - 1 - group, at, lane : lane + channels] = value

    def add(group, j, at, value):
        lane = (PER - 1 - j) * channels
        picked_ref[GROUPS - 1 - group, at, lane : lane + channels] += value

    gather(scalars_ref, column_ref, window_ref, blocks, store, add)
    result = None
    for group in range(GROUPS):
        weights = weight_ref[group * PER : (group + 1) * PER].reshape(PER * channels, width)
        term = jnp.dot(picked_ref[group], weights, preferred_element_type=F32)
        result = term if result is None else result + term
    result = result.T
    chans = width // channels
    for at in range(chans):
        total_ref[at] = result[at * channels : (at + 1) * channels]
    mine_ref[...] = total_ref[chan]
    for step in range(1, chans):
        other_ref[step - 1] = total_ref[lax.rem(chan + step, chans)].astype(BF16)


def pre_grad_kernel(scale, scalars_ref, children_ref, mask_ref, slope_ref, mine_ref, *refs):
    others, (grad_ref, keep_ref, send_ref, scratch_ref) = refs[:-4], refs[-4:]
    total = mine_ref[...]
    for other in others:
        total = total + other[...].astype(F32)
    grad = (total * slope_ref[...]).astype(BF16)
    grad_ref[...] = grad
    blocks = grad.shape[1] // BLOCK
    turn(scratch_ref, grad, 1, scalars_ref, 2 * GROUPS * blocks)
    half = grad.shape[0] // 2
    fine = children_ref.shape[1]
    for o in range(0, children_ref.shape[0], 2):
        masked = jnp.concatenate(
            [
                children_ref[o + j] * mask_ref[o + j : o + j + 1, :].astype(F32).astype(BF16)
                for j in range(2)
            ],
            axis=0,
        )
        term = lax.dot_general(scratch_ref[1], masked, NT, preferred_element_type=F32) * scale
        both = term.astype(BF16)
        for j in range(2):
            keep_ref[o + j] = both[:half, j * fine : (j + 1) * fine]
            send_ref[o + j] = both[half:, j * fine : (j + 1) * fine]


def cut_kernel(weight_ref, *refs):
    out_refs, scratch_ref = refs[:-1], refs[-1]
    octants, fine, _ = scratch_ref.shape
    chans = len(out_refs)
    size = fine // chans
    chan = lax.axis_index("chan")
    for o in range(octants):
        scratch_ref[o] = weight_ref[o].T
    for by in range(chans):
        at = pl.ds(pl.multiple_of((chan + by) % chans * size, size), size)
        for o in range(octants):
            out_refs[by][o] = scratch_ref[o, at, :]


def children_kernel(mask_ref, *refs):
    out_hbm, out_ref, sems = refs[-3:]
    count = (len(refs) - 3) // 2
    grads, weights = refs[:count], refs[count:-3]
    copies = []
    for o in range(out_ref.shape[0]):
        total = None
        for grad, weight in zip(grads, weights):
            term = jnp.dot(weight[o], grad[...], preferred_element_type=F32)
            term = term.astype(BF16).astype(F32)
            total = term if total is None else total + term
        out_ref[o] = (total * mask_ref[o : o + 1, :].astype(F32)).astype(BF16)
        copies.append(pltpu.make_async_copy(out_ref.at[o], out_hbm.at[o], sems.at[o]))
        copies[-1].start()
    for copy in copies:
        copy.wait()


def apart(shard, by):
    return lax.ppermute(shard, "curve", [(i, i ^ by) for i in range(lax.axis_size("curve"))])


def added(*terms):
    return sum(term.astype(F32) for term in terms).astype(BF16)


def sum_over_curve(total, beside):
    terms = [apart(total[by], by) for by in range(1, 4)]
    own = added(after(total[0], beside), *terms)
    across = apart(own, 2)
    return [own, apart(own, 1), across, apart(across, 1)]


def after(value, *earlier):
    return lax.optimization_barrier((value, *earlier))[0]


def body(children, child_mask, neighbours, down_weight, conv_weight, cotangent):
    octants, fine, rows = children.shape
    offsets, channels, width = conv_weight.shape
    blocks = rows // BLOCK
    chans = lax.axis_size("chan")
    chan = lax.axis_index("chan")
    rep = lax.axis_index("rep")
    curve = lax.axis_index("curve")
    pieces = lax.axis_size(PIECES)
    scale = 1.0 / (rows * pieces) ** 0.5
    shape = jax.ShapeDtypeStruct
    half = channels // 2
    shards = 4 if lax.axis_size("curve") == 4 and half % 64 == 0 else 1
    size = half // shards

    coarse, slope = call(
        down_kernel,
        [shape((rows, channels), BF16), shape((channels, rows), F32)],
        vmem(3),
        [],
        limit=WHOLE_LIMIT,
    )(children, child_mask, down_weight)

    if chans == 2:
        parts = [coarse, swapped(coarse, "chan")]
    else:
        every = lax.all_gather(coarse, "chan", axis=0)
        parts = [every[i] for i in range(chans)]
    windows = [array for part in parts for array in [part] + met(part)]
    conv_weight = conv_weight * after(jnp.ones((), BF16), coarse)
    index, scalars = call(
        functools.partial(index_kernel, shards),
        [shape((GROUPS, 16, rows), jnp.int32), shape((2 * GROUPS * blocks + 3,), jnp.int32)],
        vmem(1),
        [],
        vmem(1) + SMEM,
    )(after(neighbours, parts[1]))

    features_out, conv_grad, keep, send = call(
        functools.partial(conv_kernel, chans, shards, scale),
        [
            shape((channels, rows), BF16),
            shape((rows, channels), BF16),
            shape((shards, offsets, size, width), BF16),
            shape((shards, offsets, size, width), BF16),
        ],
        SMEM + vmem(3 + 3 * chans),
        [
            pltpu.VMEM((chans, 3 * rows + SPAN, channels), BF16),
            pltpu.VMEM((GROUPS, rows, 16), jnp.int32),
            pltpu.VMEM((9, rows, 3 * width), BF16),
            pltpu.VMEM((rows, channels), F32),
            pltpu.VMEM((2, channels, rows), BF16),
        ],
    )(scalars, index, conv_weight, cotangent, *windows)

    near = met(conv_grad)
    received = swapped(send, "rep")
    total = [added(keep[i], received[i]) for i in range(shards)]

    mine, others = call(
        coarse_grad_kernel,
        [shape((channels, rows), F32), shape((chans - 1, channels, rows), BF16)],
        SMEM + vmem(5),
        [
            pltpu.VMEM((1, 3 * rows + SPAN, channels), BF16),
            pltpu.VMEM((GROUPS, rows, 16), jnp.int32),
            pltpu.VMEM((GROUPS, rows, PER * channels), BF16),
            pltpu.VMEM((chans, channels, rows), F32),
        ],
    )(after(scalars, *total), index, conv_weight, conv_grad, *near)
    received = [
        lax.ppermute(others[by - 1], "chan", [(i, (i + by) % chans) for i in range(chans)])
        for by in range(1, chans)
    ]
    mine_fine = fine // chans
    cut = call(
        cut_kernel,
        [shape((octants, mine_fine, channels), BF16)] * chans,
        vmem(1),
        [pltpu.VMEM((octants, fine, channels), BF16)],
    )(after(down_weight, mine))
    blank = [
        jnp.broadcast_to(after(jnp.zeros((), F32), mine), like.shape)
        for like in (conv_weight, down_weight)
    ]
    pre_grad, keep, send = call(
        functools.partial(pre_grad_kernel, scale),
        [
            shape((channels, rows), BF16),
            shape((octants, half, fine), BF16),
            shape((octants, half, fine), BF16),
        ],
        SMEM + vmem(4 + len(received)),
        [pltpu.VMEM((2, channels, rows), BF16)],
    )(after(scalars, *cut, *blank), children, child_mask, slope, mine, *received)

    if shards == 4:
        sums = sum_over_curve(total, pre_grad)
    else:
        sums = [lax.psum(total[0], "curve")]
    own = sums[0]
    sent_grad, send = after(pre_grad, own), after(send, own)
    grads = [
        lax.ppermute(sent_grad, "chan", [(i, (i + by) % chans) for i in range(chans)])
        if by
        else pre_grad
        for by in range(chans)
    ]
    weights = [
        lax.ppermute(after(cut[by], own), "chan", [(i, (i + by) % chans) for i in range(chans)])
        if by
        else cut[by]
        for by in range(chans)
    ]
    children_grad = call(
        children_kernel,
        shape((octants, mine_fine, rows), BF16),
        vmem(1 + 2 * chans),
        [pltpu.VMEM((octants, mine_fine, rows), BF16), pltpu.SemaphoreType.DMA((octants,))],
        anywhere(1)[0],
    )(after(child_mask, *sums[2:3]), *grads, *weights)

    down = added(keep, swapped(send, "rep"))
    if shards == 4:
        down = added(down, apart(down, 1))
        down = added(after(down, children_grad), apart(down, 2))
    else:
        down = lax.psum(down, "curve")
    def joined(result, pieces):
        for row, piece in pieces:
            result = lax.dynamic_update_slice(result, piece.astype(F32), (0, row, 0))
        return result

    rows_of = [rep * half, (1 - rep) * half]
    down_weight_grad = joined(blank[1], zip(rows_of, (down, swapped(down, "rep"))))
    pieces = []
    for step, part in enumerate(sums):
        at = (curve ^ step) * size if shards > 1 else 0
        mine = part if step else after(part, *sums[2:3])
        pieces += [(rows_of[0] + at, mine), (rows_of[1] + at, swapped(part, "rep"))]
    conv_weight_grad = joined(blank[0], pieces)
    return (features_out, children_grad, conv_weight_grad, down_weight_grad)


def solution(mesh):
    in_specs = (
        P(None, None, ("snap", "curve", "rep")),
        P(None, ("snap", "curve", "rep")),
        P(None, ("snap", "curve", "rep")),
        P(None, "chan", None),
        P(None, "chan", None),
        P("chan", ("snap", "curve", "rep")),
    )
    out_specs = (
        P("chan", ("snap", "curve", "rep")),
        P(None, "chan", ("snap", "curve", "rep")),
        P("snap", "chan", None),
        P("snap", "chan", None),
    )
    return jax.shard_map(body, mesh=mesh, in_specs=in_specs, out_specs=out_specs, check_vma=False)
```

```python
import functools

import jax
import jax.numpy as jnp
from jax import lax
from jax.experimental import pallas as pl
from jax.experimental.pallas import tpu as pltpu
from jax.sharding import PartitionSpec as P

BLOCK = 128
SPAN = 256
GROUPS = 3
PER = 9
VMEM_LIMIT = 28 * 1024 * 1024
WHOLE_LIMIT = 60 * 1024 * 1024
PIECES = ("curve", "rep")
F32 = jnp.float32
BF16 = jnp.bfloat16
NOWHERE = -(2**20)
NT = (((1,), (1,)), ((), ()))


def silu_slope(value):
    sigma = jax.nn.sigmoid(value)
    return sigma * (1.0 + value * (1.0 - sigma))


def met(shard):
    devices = lax.axis_size(PIECES)
    pairs = [(i, i + 1) for i in range(1, devices - 1, 2)]
    pairs += [(j, i) for i, j in pairs]
    return [lax.ppermute(shard, PIECES, pairs), swapped(shard, "rep")]


def swapped(shard, axis):
    return lax.ppermute(shard, axis, [(0, 1), (1, 0)])


def call(kernel, out_shape, in_specs, scratch, out_specs=None, limit=VMEM_LIMIT):
    options = {} if out_specs is None else {"out_specs": out_specs}
    return pl.pallas_call(
        kernel,
        out_shape=out_shape,
        in_specs=in_specs,
        scratch_shapes=scratch,
        compiler_params=pltpu.CompilerParams(vmem_limit_bytes=limit),
        cost_estimate=pl.CostEstimate(flops=0, bytes_accessed=0, transcendentals=0),
        **options,
    )


def anywhere(count):
    return [pl.BlockSpec(memory_space=pl.ANY)] * count


def vmem(count):
    return [pl.BlockSpec(memory_space=pltpu.VMEM)] * count


SMEM = [pl.BlockSpec(memory_space=pltpu.SMEM)]


def down_kernel(children_ref, mask_ref, weight_ref, coarse_ref, slope_ref):
    octants = children_ref.shape[0]
    total = None
    for o in range(0, octants, 2):
        masked = jnp.concatenate(
            [
                children_ref[o + j] * mask_ref[o + j : o + j + 1, :].astype(F32).astype(BF16)
                for j in range(2)
            ],
            axis=0,
        )
        weights = jnp.concatenate([weight_ref[o], weight_ref[o + 1]], axis=1)
        term = jnp.dot(weights, masked, preferred_element_type=F32)
        total = term if total is None else total + term
    slope_ref[...] = silu_slope(total)
    coarse_ref[...] = (total * jax.nn.sigmoid(total)).T.astype(BF16)


def index_kernel(shards, neighbours_ref, index_ref, scalars_ref):
    offsets, rows = neighbours_ref.shape
    blocks = rows // BLOCK
    curve, rep = lax.axis_index("curve"), lax.axis_index("rep")
    names = neighbours_ref[...]
    local = jnp.where(names >= 0, names - (curve * 2 + rep - 1) * rows, NOWHERE)
    index_ref[...] = jnp.full(index_ref.shape, NOWHERE, jnp.int32)
    for group in range(GROUPS):
        part = local[group * PER : (group + 1) * PER]
        index_ref[group, :PER, :] = part
        lows = jnp.min(jnp.where(part < 0, -NOWHERE, part), axis=0, keepdims=True)
        highs = jnp.max(part, axis=0, keepdims=True)
        for block in range(blocks):
            at = slice(block * BLOCK, (block + 1) * BLOCK)
            low, high = jnp.min(lows[:, at]), jnp.max(highs[:, at]) + 1
            low = jnp.where(high <= 0, 0, low // 16 * 16)
            steps = jnp.maximum(1, (high - low + SPAN - 1) // SPAN)
            scalars_ref[group * blocks + block] = low
            scalars_ref[(GROUPS + group) * blocks + block] = steps
    last = 2 * GROUPS * blocks
    scalars_ref[last] = lax.axis_index("chan")
    scalars_ref[last + 1] = curve if shards > 1 else 0
    scalars_ref[last + 2] = rep


def fill_window(window_ref, parts, slots, rep):
    rows = parts[0][0].shape[0]
    places = (rows, rep * 2 * rows, (1 - rep) * 2 * rows)
    for part, slot in zip(parts, slots):
        for source, place in zip(part, places):
            window_ref[slot, pl.ds(pl.multiple_of(place, 16), rows), :] = source[...]
    blank = (window_ref.shape[0], window_ref.shape[1] - 3 * rows, window_ref.shape[2])
    window_ref[:, 3 * rows :, :] = jnp.zeros(blank, BF16)


def gather(scalars_ref, column_ref, window_ref, blocks, store, add):
    lanes = lax.broadcasted_iota(jnp.int32, (BLOCK, SPAN), 1).astype(F32).astype(BF16)

    def picked(group, rows, start):
        columns = jnp.clip(column_ref[group, rows, :] - start, -1, SPAN).astype(F32).astype(BF16)
        hot = [
            jnp.where(
                jnp.broadcast_to(columns[:, j : j + 1], (BLOCK, SPAN)) == lanes,
                jnp.ones((), BF16),
                jnp.zeros((), BF16),
            )
            for j in range(PER)
        ]
        at = pl.ds(pl.multiple_of(start, 16), SPAN)
        span = jnp.concatenate([window_ref[c, at, :] for c in range(window_ref.shape[0])], axis=1)
        return jnp.dot(jnp.concatenate(hot, axis=0), span, preferred_element_type=F32).astype(BF16)

    def first(block, _):
        rows = pl.ds(pl.multiple_of(block * BLOCK, BLOCK), BLOCK)
        for group in range(GROUPS):
            result = picked(group, rows, scalars_ref[group * blocks + block])
            for j in range(PER):
                store(group, j, rows, result[j * BLOCK : (j + 1) * BLOCK])
        return 0

    lax.fori_loop(0, blocks, first, 0, unroll=3)

    def rest(at, _):
        group, block = at // blocks, at % blocks
        rows = pl.ds(pl.multiple_of(block * BLOCK, BLOCK), BLOCK)

        def more(step, _):
            result = picked(group, rows, scalars_ref[at] + step * SPAN)
            for j in range(PER):
                add(group, j, rows, result[j * BLOCK : (j + 1) * BLOCK])
            return 0

        lax.fori_loop(1, scalars_ref[GROUPS * blocks + at], more, 0)
        return 0

    lax.fori_loop(0, GROUPS * blocks, rest, 0)


def turn(scratch_ref, value, shards, scalars_ref, at):
    half = value.shape[0] // 2
    size = half // shards
    scratch_ref[0] = value
    place = 0 if shards == 1 else scalars_ref[at + 1]
    rep = scalars_ref[at + 2]
    for core in range(2):
        for step in range(shards):
            source = (rep + core) % 2 * half + (place ^ step) * size
            target = core * half + step * size
            scratch_ref[1, target : target + size] = scratch_ref[
                0, pl.ds(pl.multiple_of(source, size), size)
            ]


def conv_kernel(chans, shards, scale, scalars_ref, index_ref, weight_ref, cotangent_ref, *refs):
    parts, refs = [refs[3 * i : 3 * i + 3] for i in range(chans)], refs[3 * chans :]
    out_ref, grad_ref, keep_ref, send_ref, far_ref = refs[:5]
    window_ref, column_ref, picked_ref, conv_ref, scratch_ref = refs[5:]
    rows = index_ref.shape[2]
    blocks = rows // BLOCK
    width = chans * window_ref.shape[2]
    channels = weight_ref.shape[1]
    chan = scalars_ref[2 * GROUPS * blocks]
    rep = scalars_ref[2 * GROUPS * blocks + 2]
    slots = (chan, 1 - chan) if chans == 2 else range(chans)
    fill_window(window_ref, parts, slots, rep)
    for group in range(GROUPS):
        column_ref[group] = index_ref[group].T

    def store(group, j, at, value):
        lane = j % 3 * width
        picked_ref[group * 3 + j // 3, at, lane : lane + width] = value

    def add(group, j, at, value):
        lane = j % 3 * width
        picked_ref[group * 3 + j // 3, at, lane : lane + width] += value

    gather(scalars_ref, column_ref, window_ref, blocks, store, add)

    def multiply(three, _):
        weights = jnp.concatenate([weight_ref[three * 3 + j] for j in range(3)], axis=1)
        term = lax.dot_general(picked_ref[three], weights, NT, preferred_element_type=F32)
        conv_ref[...] += term
        return 0

    conv_ref[...] = jnp.zeros_like(conv_ref)
    lax.fori_loop(0, 9, multiply, 0, unroll=3)
    conv = conv_ref[...].T
    sigma = jax.nn.sigmoid(conv)
    out_ref[...] = (conv * sigma).astype(BF16)
    grad = cotangent_ref[...].astype(F32) * (sigma * (1.0 + conv * (1.0 - sigma)))
    grad_ref[...] = grad.T.astype(BF16)
    turn(scratch_ref, grad.astype(BF16), shards, scalars_ref, 2 * GROUPS * blocks)
    half = channels // 2
    size = half // shards

    def weigh(three, _):
        term = jnp.dot(scratch_ref[1], picked_ref[three], preferred_element_type=F32) * scale
        for j in range(3):
            both = term[:, j * width : (j + 1) * width].astype(BF16)
            for step in range(shards):
                at = step * size
                keep_ref[step, three * 3 + j] = both[at : at + size]
                other = both[half + at : half + at + size]
                if step == shards - 1:
                    far_ref[three * 3 + j] = other
                if step < send_ref.shape[0]:
                    send_ref[step, three * 3 + j] = other
        return 0

    lax.fori_loop(0, 9, weigh, 0, unroll=3)


def coarse_grad_kernel(scalars_ref, index_ref, weight_ref, *refs):
    part, refs = refs[:3], refs[3:]
    mine_ref, other_ref, window_ref, column_ref, picked_ref, total_ref = refs
    rows = index_ref.shape[2]
    blocks = rows // BLOCK
    offsets, channels, width = weight_ref.shape
    chan = scalars_ref[2 * GROUPS * blocks]
    rep = scalars_ref[2 * GROUPS * blocks + 2]
    fill_window(window_ref, [part], (0,), rep)
    for group in range(GROUPS):
        column_ref[group] = index_ref[group].T

    def store(group, j, at, value):
        lane = (PER - 1 - j) * channels
        picked_ref[GROUPS - 1 - group, at, lane : lane + channels] = value

    def add(group, j, at, value):
        lane = (PER - 1 - j) * channels
        picked_ref[GROUPS - 1 - group, at, lane : lane + channels] += value

    gather(scalars_ref, column_ref, window_ref, blocks, store, add)
    result = None
    for group in range(GROUPS):
        weights = weight_ref[group * PER : (group + 1) * PER].reshape(PER * channels, width)
        term = jnp.dot(picked_ref[group], weights, preferred_element_type=F32)
        result = term if result is None else result + term
    result = result.T
    chans = width // channels
    for at in range(chans):
        total_ref[at] = result[at * channels : (at + 1) * channels]
    mine_ref[...] = total_ref[chan]
    for step in range(1, chans):
        other_ref[step - 1] = total_ref[lax.rem(chan + step, chans)].astype(BF16)


def pre_grad_kernel(scale, scalars_ref, children_ref, mask_ref, slope_ref, mine_ref, *refs):
    others, (grad_ref, keep_ref, send_ref, scratch_ref) = refs[:-4], refs[-4:]
    total = mine_ref[...]
    for other in others:
        total = total + other[...].astype(F32)
    grad = (total * slope_ref[...]).astype(BF16)
    grad_ref[...] = grad
    blocks = grad.shape[1] // BLOCK
    turn(scratch_ref, grad, 1, scalars_ref, 2 * GROUPS * blocks)
    half = grad.shape[0] // 2
    fine = children_ref.shape[1]
    for o in range(0, children_ref.shape[0], 2):
        masked = jnp.concatenate(
            [
                children_ref[o + j] * mask_ref[o + j : o + j + 1, :].astype(F32).astype(BF16)
                for j in range(2)
            ],
            axis=0,
        )
        term = lax.dot_general(scratch_ref[1], masked, NT, preferred_element_type=F32) * scale
        both = term.astype(BF16)
        for j in range(2):
            keep_ref[o + j] = both[:half, j * fine : (j + 1) * fine]
            send_ref[o + j] = both[half:, j * fine : (j + 1) * fine]


def cut_kernel(weight_ref, *refs):
    out_refs, scratch_ref = refs[:-1], refs[-1]
    octants, fine, _ = scratch_ref.shape
    chans = len(out_refs)
    size = fine // chans
    chan = lax.axis_index("chan")
    for o in range(octants):
        scratch_ref[o] = weight_ref[o].T
    for by in range(chans):
        at = pl.ds(pl.multiple_of((chan + by) % chans * size, size), size)
        for o in range(octants):
            out_refs[by][o] = scratch_ref[o, at, :]


def children_kernel(mask_ref, *refs):
    out_hbm, out_ref, sems = refs[-3:]
    count = (len(refs) - 3) // 2
    grads, weights = refs[:count], refs[count:-3]
    copies = []
    for o in range(out_ref.shape[0]):
        total = None
        for grad, weight in zip(grads, weights):
            term = jnp.dot(weight[o], grad[...], preferred_element_type=F32)
            term = term.astype(BF16).astype(F32)
            total = term if total is None else total + term
        out_ref[o] = (total * mask_ref[o : o + 1, :].astype(F32)).astype(BF16)
        copies.append(pltpu.make_async_copy(out_ref.at[o], out_hbm.at[o], sems.at[o]))
        copies[-1].start()
    for copy in copies:
        copy.wait()


def apart(shard, by):
    return lax.ppermute(shard, "curve", [(i, i ^ by) for i in range(lax.axis_size("curve"))])


def added(*terms):
    return sum(term.astype(F32) for term in terms).astype(BF16)


def after(value, *earlier):
    return lax.optimization_barrier((value, *earlier))[0]


def body(children, child_mask, neighbours, down_weight, conv_weight, cotangent):
    octants, fine, rows = children.shape
    offsets, channels, width = conv_weight.shape
    blocks = rows // BLOCK
    chans = lax.axis_size("chan")
    chan = lax.axis_index("chan")
    rep = lax.axis_index("rep")
    curve = lax.axis_index("curve")
    pieces = lax.axis_size(PIECES)
    scale = 1.0 / (rows * pieces) ** 0.5
    shape = jax.ShapeDtypeStruct
    half = channels // 2
    shards = 4 if lax.axis_size("curve") == 4 and half % 64 == 0 else 1
    size = half // shards

    coarse, slope = call(
        down_kernel,
        [shape((rows, channels), BF16), shape((channels, rows), F32)],
        vmem(3),
        [],
        limit=WHOLE_LIMIT,
    )(children, child_mask, down_weight)

    if chans == 2:
        parts = [coarse, swapped(coarse, "chan")]
    else:
        every = lax.all_gather(coarse, "chan", axis=0)
        parts = [every[i] for i in range(chans)]
    windows = [array for part in parts for array in [part] + met(part)]
    conv_weight = conv_weight * after(jnp.ones((), BF16), coarse)
    index, scalars = call(
        functools.partial(index_kernel, shards),
        [shape((GROUPS, 16, rows), jnp.int32), shape((2 * GROUPS * blocks + 3,), jnp.int32)],
        vmem(1),
        [],
        vmem(1) + SMEM,
    )(after(neighbours, parts[1]))

    features_out, conv_grad, keep, send, far = call(
        functools.partial(conv_kernel, chans, shards, scale),
        [
            shape((channels, rows), BF16),
            shape((rows, channels), BF16),
            shape((shards, offsets, size, width), BF16),
            shape((max(shards - 1, 1), offsets, size, width), BF16),
            shape((offsets, size, width), BF16),
        ],
        SMEM + vmem(3 + 3 * chans),
        [
            pltpu.VMEM((chans, 3 * rows + SPAN, channels), BF16),
            pltpu.VMEM((GROUPS, rows, 16), jnp.int32),
            pltpu.VMEM((9, rows, 3 * width), BF16),
            pltpu.VMEM((rows, channels), F32),
            pltpu.VMEM((2, channels, rows), BF16),
        ],
    )(scalars, index, conv_weight, cotangent, *windows)

    far = added(keep[shards - 1], swapped(far, "rep"))
    first = far
    if shards == 4:
        received = swapped(after(send, far), "rep")
        total = [added(keep[i], received[i]) for i in range(3)]
        near = met(after(conv_grad, total[2]))
        first = added(after(total[2], *near), apart(far, 1))
        terms = [apart(first, 2), apart(after(total[1], first), 1)]
    else:
        near = met(conv_grad)

    mine, others = call(
        coarse_grad_kernel,
        [shape((channels, rows), F32), shape((chans - 1, channels, rows), BF16)],
        SMEM + vmem(5),
        [
            pltpu.VMEM((1, 3 * rows + SPAN, channels), BF16),
            pltpu.VMEM((GROUPS, rows, 16), jnp.int32),
            pltpu.VMEM((GROUPS, rows, PER * channels), BF16),
            pltpu.VMEM((chans, channels, rows), F32),
        ],
    )(after(scalars, first), index, conv_weight, conv_grad, *near)
    received = [
        lax.ppermute(others[by - 1], "chan", [(i, (i + by) % chans) for i in range(chans)])
        for by in range(1, chans)
    ]
    mine_fine = fine // chans
    cut = call(
        cut_kernel,
        [shape((octants, mine_fine, channels), BF16)] * chans,
        vmem(1),
        [pltpu.VMEM((octants, fine, channels), BF16)],
    )(after(down_weight, mine))
    blank = [
        jnp.broadcast_to(after(jnp.zeros((), F32), mine), like.shape)
        for like in (conv_weight, down_weight)
    ]
    pre_grad, keep, send = call(
        functools.partial(pre_grad_kernel, scale),
        [
            shape((channels, rows), BF16),
            shape((octants, half, fine), BF16),
            shape((octants, half, fine), BF16),
        ],
        SMEM + vmem(4 + len(received)),
        [pltpu.VMEM((2, channels, rows), BF16)],
    )(after(scalars, *cut, *blank), children, child_mask, slope, mine, *received)

    if shards == 4:
        own = added(after(total[0], pre_grad), *terms)
        across = apart(own, 2)
        sums = [own, apart(own, 1), across, apart(across, 1)]
    else:
        own = lax.psum(far, "curve")
        sums = [own]
    sent_grad = after(pre_grad, own)
    grads = [
        lax.ppermute(sent_grad, "chan", [(i, (i + by) % chans) for i in range(chans)])
        if by
        else pre_grad
        for by in range(chans)
    ]
    weights = [
        lax.ppermute(after(cut[by], own), "chan", [(i, (i + by) % chans) for i in range(chans)])
        if by
        else cut[by]
        for by in range(chans)
    ]
    children_grad = call(
        children_kernel,
        shape((octants, mine_fine, rows), BF16),
        vmem(1 + 2 * chans),
        [pltpu.VMEM((octants, mine_fine, rows), BF16), pltpu.SemaphoreType.DMA((octants,))],
        anywhere(1)[0],
    )(child_mask, *grads, *weights)

    down = added(keep, swapped(send, "rep"))
    if shards == 4:
        down = added(after(down, sums[2], children_grad), apart(down, 1))
        down = added(down, apart(down, 2))
    else:
        down = lax.psum(down, "curve")
    def joined(result, pieces):
        for row, piece in pieces:
            result = lax.dynamic_update_slice(result, piece.astype(F32), (0, row, 0))
        return result

    rows_of = [rep * half, (1 - rep) * half]
    down_weight_grad = joined(blank[1], zip(rows_of, (down, swapped(down, "rep"))))
    pieces = []
    for step, part in enumerate(sums):
        at = (curve ^ step) * size if shards > 1 else 0
        mine = part if step else after(part, *grads[1:])
        pieces += [(rows_of[0] + at, mine), (rows_of[1] + at, swapped(part, "rep"))]
    conv_weight_grad = joined(blank[0], pieces)
    return (features_out, children_grad, conv_weight_grad, down_weight_grad)


def solution(mesh):
    in_specs = (
        P(None, None, ("snap", "curve", "rep")),
        P(None, ("snap", "curve", "rep")),
        P(None, ("snap", "curve", "rep")),
        P(None, "chan", None),
        P(None, "chan", None),
        P("chan", ("snap", "curve", "rep")),
    )
    out_specs = (
        P("chan", ("snap", "curve", "rep")),
        P(None, "chan", ("snap", "curve", "rep")),
        P("snap", "chan", None),
        P("snap", "chan", None),
    )
    return jax.shard_map(body, mesh=mesh, in_specs=in_specs, out_specs=out_specs, check_vma=False)
```

```python
import functools

import jax
import jax.numpy as jnp
from jax import lax
from jax.experimental import pallas as pl
from jax.experimental.pallas import tpu as pltpu
from jax.sharding import PartitionSpec as P

BLOCK = 128
SPAN = 256
GROUPS = 3
PER = 9
VMEM_LIMIT = 28 * 1024 * 1024
WHOLE_LIMIT = 60 * 1024 * 1024
PIECES = ("curve", "rep")
F32 = jnp.float32
BF16 = jnp.bfloat16
NOWHERE = -(2**20)
NT = (((1,), (1,)), ((), ()))


def silu_slope(value):
    sigma = jax.nn.sigmoid(value)
    return sigma * (1.0 + value * (1.0 - sigma))


def met(shard):
    devices = lax.axis_size(PIECES)
    pairs = [(i, i + 1) for i in range(1, devices - 1, 2)]
    pairs += [(j, i) for i, j in pairs]
    return [lax.ppermute(shard, PIECES, pairs), swapped(shard, "rep")]


def swapped(shard, axis):
    return lax.ppermute(shard, axis, [(0, 1), (1, 0)])


def call(kernel, out_shape, in_specs, scratch, out_specs=None, limit=VMEM_LIMIT):
    options = {} if out_specs is None else {"out_specs": out_specs}
    return pl.pallas_call(
        kernel,
        out_shape=out_shape,
        in_specs=in_specs,
        scratch_shapes=scratch,
        compiler_params=pltpu.CompilerParams(vmem_limit_bytes=limit),
        cost_estimate=pl.CostEstimate(flops=0, bytes_accessed=0, transcendentals=0),
        **options,
    )


def anywhere(count):
    return [pl.BlockSpec(memory_space=pl.ANY)] * count


def vmem(count):
    return [pl.BlockSpec(memory_space=pltpu.VMEM)] * count


SMEM = [pl.BlockSpec(memory_space=pltpu.SMEM)]


def down_kernel(children_ref, mask_ref, weight_ref, coarse_ref, slope_ref):
    octants = children_ref.shape[0]
    total = None
    for o in range(0, octants, 2):
        masked = jnp.concatenate(
            [
                children_ref[o + j] * mask_ref[o + j : o + j + 1, :].astype(F32).astype(BF16)
                for j in range(2)
            ],
            axis=0,
        )
        weights = jnp.concatenate([weight_ref[o], weight_ref[o + 1]], axis=1)
        term = jnp.dot(weights, masked, preferred_element_type=F32)
        total = term if total is None else total + term
    slope_ref[...] = silu_slope(total)
    coarse_ref[...] = (total * jax.nn.sigmoid(total)).T.astype(BF16)


def index_kernel(shards, neighbours_ref, index_ref, scalars_ref):
    offsets, rows = neighbours_ref.shape
    blocks = rows // BLOCK
    curve, rep = lax.axis_index("curve"), lax.axis_index("rep")
    names = neighbours_ref[...]
    local = jnp.where(names >= 0, names - (curve * 2 + rep - 1) * rows, NOWHERE)
    index_ref[...] = jnp.full(index_ref.shape, NOWHERE, jnp.int32)
    for group in range(GROUPS):
        part = local[group * PER : (group + 1) * PER]
        index_ref[group, :PER, :] = part
        lows = jnp.min(jnp.where(part < 0, -NOWHERE, part), axis=0, keepdims=True)
        highs = jnp.max(part, axis=0, keepdims=True)
        for block in range(blocks):
            at = slice(block * BLOCK, (block + 1) * BLOCK)
            low, high = jnp.min(lows[:, at]), jnp.max(highs[:, at]) + 1
            low = jnp.where(high <= 0, 0, low // 16 * 16)
            steps = jnp.maximum(1, (high - low + SPAN - 1) // SPAN)
            scalars_ref[group * blocks + block] = low
            scalars_ref[(GROUPS + group) * blocks + block] = steps
    last = 2 * GROUPS * blocks
    scalars_ref[last] = lax.axis_index("chan")
    scalars_ref[last + 1] = curve if shards > 1 else 0
    scalars_ref[last + 2] = rep


def fill_window(window_ref, parts, slots, rep):
    rows = parts[0][0].shape[0]
    places = (rows, rep * 2 * rows, (1 - rep) * 2 * rows)
    for part, slot in zip(parts, slots):
        for source, place in zip(part, places):
            window_ref[slot, pl.ds(pl.multiple_of(place, 16), rows), :] = source[...]
    blank = (window_ref.shape[0], window_ref.shape[1] - 3 * rows, window_ref.shape[2])
    window_ref[:, 3 * rows :, :] = jnp.zeros(blank, BF16)


def gather(scalars_ref, column_ref, window_ref, blocks, store, add):
    lanes = lax.broadcasted_iota(jnp.int32, (BLOCK, SPAN), 1).astype(F32).astype(BF16)

    def picked(group, rows, start):
        columns = jnp.clip(column_ref[group, rows, :] - start, -1, SPAN).astype(F32).astype(BF16)
        hot = [
            jnp.where(
                jnp.broadcast_to(columns[:, j : j + 1], (BLOCK, SPAN)) == lanes,
                jnp.ones((), BF16),
                jnp.zeros((), BF16),
            )
            for j in range(PER)
        ]
        at = pl.ds(pl.multiple_of(start, 16), SPAN)
        span = jnp.concatenate([window_ref[c, at, :] for c in range(window_ref.shape[0])], axis=1)
        return jnp.dot(jnp.concatenate(hot, axis=0), span, preferred_element_type=F32).astype(BF16)

    def first(block, _):
        rows = pl.ds(pl.multiple_of(block * BLOCK, BLOCK), BLOCK)
        for group in range(GROUPS):
            result = picked(group, rows, scalars_ref[group * blocks + block])
            for j in range(PER):
                store(group, j, rows, result[j * BLOCK : (j + 1) * BLOCK])
        return 0

    lax.fori_loop(0, blocks, first, 0, unroll=3)

    def rest(at, _):
        group, block = at // blocks, at % blocks
        rows = pl.ds(pl.multiple_of(block * BLOCK, BLOCK), BLOCK)

        def more(step, _):
            result = picked(group, rows, scalars_ref[at] + step * SPAN)
            for j in range(PER):
                add(group, j, rows, result[j * BLOCK : (j + 1) * BLOCK])
            return 0

        lax.fori_loop(1, scalars_ref[GROUPS * blocks + at], more, 0)
        return 0

    lax.fori_loop(0, GROUPS * blocks, rest, 0)


def turn(scratch_ref, value, shards, scalars_ref, at):
    half = value.shape[0] // 2
    size = half // shards
    scratch_ref[0] = value
    place = 0 if shards == 1 else scalars_ref[at + 1]
    rep = scalars_ref[at + 2]
    for core in range(2):
        for step in range(shards):
            source = (rep + core) % 2 * half + (place ^ step) * size
            target = core * half + step * size
            scratch_ref[1, target : target + size] = scratch_ref[
                0, pl.ds(pl.multiple_of(source, size), size)
            ]


def conv_kernel(chans, shards, scale, scalars_ref, index_ref, weight_ref, cotangent_ref, *refs):
    parts, refs = [refs[3 * i : 3 * i + 3] for i in range(chans)], refs[3 * chans :]
    out_ref, grad_ref, keep_ref, send_ref = refs[:4]
    window_ref, column_ref, picked_ref, conv_ref, scratch_ref = refs[4:]
    rows = index_ref.shape[2]
    blocks = rows // BLOCK
    width = chans * window_ref.shape[2]
    channels = weight_ref.shape[1]
    chan = scalars_ref[2 * GROUPS * blocks]
    rep = scalars_ref[2 * GROUPS * blocks + 2]
    slots = (chan, 1 - chan) if chans == 2 else range(chans)
    fill_window(window_ref, parts, slots, rep)
    for group in range(GROUPS):
        column_ref[group] = index_ref[group].T

    def store(group, j, at, value):
        lane = j % 3 * width
        picked_ref[group * 3 + j // 3, at, lane : lane + width] = value

    def add(group, j, at, value):
        lane = j % 3 * width
        picked_ref[group * 3 + j // 3, at, lane : lane + width] += value

    gather(scalars_ref, column_ref, window_ref, blocks, store, add)

    def multiply(three, _):
        weights = jnp.concatenate([weight_ref[three * 3 + j] for j in range(3)], axis=1)
        term = lax.dot_general(picked_ref[three], weights, NT, preferred_element_type=F32)
        conv_ref[...] += term
        return 0

    conv_ref[...] = jnp.zeros_like(conv_ref)
    lax.fori_loop(0, 9, multiply, 0, unroll=3)
    conv = conv_ref[...].T
    sigma = jax.nn.sigmoid(conv)
    out_ref[...] = (conv * sigma).astype(BF16)
    grad = cotangent_ref[...].astype(F32) * (sigma * (1.0 + conv * (1.0 - sigma)))
    grad_ref[...] = grad.T.astype(BF16)
    turn(scratch_ref, grad.astype(BF16), shards, scalars_ref, 2 * GROUPS * blocks)
    half = channels // 2
    size = half // shards

    def weigh(three, _):
        term = jnp.dot(scratch_ref[1], picked_ref[three], preferred_element_type=F32) * scale
        for j in range(3):
            both = term[:, j * width : (j + 1) * width].astype(BF16)
            for step in range(shards):
                at = step * size
                keep_ref[step, three * 3 + j] = both[at : at + size]
                send_ref[step, three * 3 + j] = both[half + at : half + at + size]
        return 0

    lax.fori_loop(0, 9, weigh, 0, unroll=3)


def coarse_grad_kernel(scalars_ref, index_ref, weight_ref, *refs):
    part, refs = refs[:3], refs[3:]
    mine_ref, other_ref, window_ref, column_ref, picked_ref, total_ref = refs
    rows = index_ref.shape[2]
    blocks = rows // BLOCK
    offsets, channels, width = weight_ref.shape
    chan = scalars_ref[2 * GROUPS * blocks]
    rep = scalars_ref[2 * GROUPS * blocks + 2]
    fill_window(window_ref, [part], (0,), rep)
    for group in range(GROUPS):
        column_ref[group] = index_ref[group].T

    def store(group, j, at, value):
        lane = (PER - 1 - j) * channels
        picked_ref[GROUPS - 1 - group, at, lane : lane + channels] = value

    def add(group, j, at, value):
        lane = (PER - 1 - j) * channels
        picked_ref[GROUPS - 1 - group, at, lane : lane + channels] += value

    gather(scalars_ref, column_ref, window_ref, blocks, store, add)
    result = None
    for group in range(GROUPS):
        weights = weight_ref[group * PER : (group + 1) * PER].reshape(PER * channels, width)
        term = jnp.dot(picked_ref[group], weights, preferred_element_type=F32)
        result = term if result is None else result + term
    result = result.T
    chans = width // channels
    for at in range(chans):
        total_ref[at] = result[at * channels : (at + 1) * channels]
    mine_ref[...] = total_ref[chan]
    for step in range(1, chans):
        other_ref[step - 1] = total_ref[lax.rem(chan + step, chans)].astype(BF16)


def pre_grad_kernel(scale, scalars_ref, children_ref, mask_ref, slope_ref, mine_ref, *refs):
    others, (grad_ref, keep_ref, send_ref, scratch_ref) = refs[:-4], refs[-4:]
    total = mine_ref[...]
    for other in others:
        total = total + other[...].astype(F32)
    grad = (total * slope_ref[...]).astype(BF16)
    grad_ref[...] = grad
    blocks = grad.shape[1] // BLOCK
    turn(scratch_ref, grad, 1, scalars_ref, 2 * GROUPS * blocks)
    half = grad.shape[0] // 2
    fine = children_ref.shape[1]
    for o in range(0, children_ref.shape[0], 2):
        masked = jnp.concatenate(
            [
                children_ref[o + j] * mask_ref[o + j : o + j + 1, :].astype(F32).astype(BF16)
                for j in range(2)
            ],
            axis=0,
        )
        term = lax.dot_general(scratch_ref[1], masked, NT, preferred_element_type=F32) * scale
        both = term.astype(BF16)
        for j in range(2):
            keep_ref[o + j] = both[:half, j * fine : (j + 1) * fine]
            send_ref[o + j] = both[half:, j * fine : (j + 1) * fine]


def cut_kernel(weight_ref, *refs):
    out_refs, scratch_ref = refs[:-1], refs[-1]
    octants, fine, _ = scratch_ref.shape
    chans = len(out_refs)
    size = fine // chans
    chan = lax.axis_index("chan")
    for o in range(octants):
        scratch_ref[o] = weight_ref[o].T
    for by in range(chans):
        at = pl.ds(pl.multiple_of((chan + by) % chans * size, size), size)
        for o in range(octants):
            out_refs[by][o] = scratch_ref[o, at, :]


def children_kernel(mask_ref, *refs):
    out_hbm, out_ref, sems = refs[-3:]
    count = (len(refs) - 3) // 2
    grads, weights = refs[:count], refs[count:-3]
    copies = []
    for o in range(out_ref.shape[0]):
        total = None
        for grad, weight in zip(grads, weights):
            term = jnp.dot(weight[o], grad[...], preferred_element_type=F32)
            term = term.astype(BF16).astype(F32)
            total = term if total is None else total + term
        out_ref[o] = (total * mask_ref[o : o + 1, :].astype(F32)).astype(BF16)
        copies.append(pltpu.make_async_copy(out_ref.at[o], out_hbm.at[o], sems.at[o]))
        copies[-1].start()
    for copy in copies:
        copy.wait()


def apart(shard, by):
    return lax.ppermute(shard, "curve", [(i, i ^ by) for i in range(lax.axis_size("curve"))])


def added(*terms):
    return sum(term.astype(F32) for term in terms).astype(BF16)


def sum_over_curve(total, beside):
    terms = [apart(total[by], by) for by in range(1, 4)]
    own = added(after(total[0], beside), *terms)
    across = apart(own, 2)
    return [own, apart(own, 1), across, apart(across, 1)]


def after(value, *earlier):
    return lax.optimization_barrier((value, *earlier))[0]


def body(children, child_mask, neighbours, down_weight, conv_weight, cotangent):
    octants, fine, rows = children.shape
    offsets, channels, width = conv_weight.shape
    blocks = rows // BLOCK
    chans = lax.axis_size("chan")
    chan = lax.axis_index("chan")
    rep = lax.axis_index("rep")
    curve = lax.axis_index("curve")
    pieces = lax.axis_size(PIECES)
    scale = 1.0 / (rows * pieces) ** 0.5
    shape = jax.ShapeDtypeStruct
    half = channels // 2
    shards = 4 if lax.axis_size("curve") == 4 and half % 64 == 0 else 1
    size = half // shards

    coarse, slope = call(
        down_kernel,
        [shape((rows, channels), BF16), shape((channels, rows), F32)],
        vmem(3),
        [],
        limit=WHOLE_LIMIT,
    )(children, child_mask, down_weight)

    if chans == 2:
        parts = [coarse, swapped(coarse, "chan")]
    else:
        every = lax.all_gather(coarse, "chan", axis=0)
        parts = [every[i] for i in range(chans)]
    windows = [array for part in parts for array in [part] + met(part)]
    conv_weight = conv_weight * after(jnp.ones((), BF16), coarse)
    index, scalars = call(
        functools.partial(index_kernel, shards),
        [shape((GROUPS, 16, rows), jnp.int32), shape((2 * GROUPS * blocks + 3,), jnp.int32)],
        vmem(1),
        [],
        vmem(1) + SMEM,
    )(after(neighbours, parts[1]))

    features_out, conv_grad, keep, send = call(
        functools.partial(conv_kernel, chans, shards, scale),
        [
            shape((channels, rows), BF16),
            shape((rows, channels), BF16),
            shape((shards, offsets, size, width), BF16),
            shape((shards, offsets, size, width), BF16),
        ],
        SMEM + vmem(3 + 3 * chans),
        [
            pltpu.VMEM((chans, 3 * rows + SPAN, channels), BF16),
            pltpu.VMEM((GROUPS, rows, 16), jnp.int32),
            pltpu.VMEM((9, rows, 3 * width), BF16),
            pltpu.VMEM((rows, channels), F32),
            pltpu.VMEM((2, channels, rows), BF16),
        ],
    )(scalars, index, conv_weight, cotangent, *windows)

    near = met(conv_grad)
    received = swapped(send, "rep")
    total = [added(keep[i], received[i]) for i in range(shards)]

    mine, others = call(
        coarse_grad_kernel,
        [shape((channels, rows), F32), shape((chans - 1, channels, rows), BF16)],
        SMEM + vmem(5),
        [
            pltpu.VMEM((1, 3 * rows + SPAN, channels), BF16),
            pltpu.VMEM((GROUPS, rows, 16), jnp.int32),
            pltpu.VMEM((GROUPS, rows, PER * channels), BF16),
            pltpu.VMEM((chans, channels, rows), F32),
        ],
    )(after(scalars, *total), index, conv_weight, conv_grad, *near)
    received = [
        lax.ppermute(others[by - 1], "chan", [(i, (i + by) % chans) for i in range(chans)])
        for by in range(1, chans)
    ]
    mine_fine = fine // chans
    cut = call(
        cut_kernel,
        [shape((octants, mine_fine, channels), BF16)] * chans,
        vmem(1),
        [pltpu.VMEM((octants, fine, channels), BF16)],
    )(after(down_weight, mine))
    blank = [
        jnp.broadcast_to(after(jnp.zeros((), F32), mine), like.shape)
        for like in (conv_weight, down_weight)
    ]
    pre_grad, keep, send = call(
        functools.partial(pre_grad_kernel, scale),
        [
            shape((channels, rows), BF16),
            shape((octants, half, fine), BF16),
            shape((octants, half, fine), BF16),
        ],
        SMEM + vmem(4 + len(received)),
        [pltpu.VMEM((2, channels, rows), BF16)],
    )(after(scalars, *cut, *blank), children, child_mask, slope, mine, *received)

    if shards == 4:
        sums = sum_over_curve(total, pre_grad)
    else:
        sums = [lax.psum(total[0], "curve")]
    own = sums[0]
    sent_grad, send = after(pre_grad, own), after(send, own)
    grads = [
        lax.ppermute(sent_grad, "chan", [(i, (i + by) % chans) for i in range(chans)])
        if by
        else pre_grad
        for by in range(chans)
    ]
    down = core_sum = added(keep, swapped(send, "rep"))
    if shards == 4:
        down = added(down, apart(down, 1))
    else:
        down = lax.psum(down, "curve")
    weights = [
        lax.ppermute(after(cut[by], own), "chan", [(i, (i + by) % chans) for i in range(chans)])
        if by
        else cut[by]
        for by in range(chans)
    ]
    children_grad = call(
        children_kernel,
        shape((octants, mine_fine, rows), BF16),
        vmem(1 + 2 * chans),
        [pltpu.VMEM((octants, mine_fine, rows), BF16), pltpu.SemaphoreType.DMA((octants,))],
        anywhere(1)[0],
    )(after(child_mask, down), *grads, *weights)
    if shards == 4:
        down = added(after(down, children_grad), apart(after(down, sums[2]), 2))

    def joined(result, pieces):
        for row, piece in pieces:
            result = lax.dynamic_update_slice(result, piece.astype(F32), (0, row, 0))
        return result

    rows_of = [rep * half, (1 - rep) * half]
    down_weight_grad = joined(blank[1], zip(rows_of, (down, swapped(down, "rep"))))
    pieces = []
    for step, part in enumerate(sums):
        at = (curve ^ step) * size if shards > 1 else 0
        mine = part if step else after(part, core_sum)
        pieces += [(rows_of[0] + at, mine), (rows_of[1] + at, swapped(part, "rep"))]
    conv_weight_grad = joined(blank[0], pieces)
    return (features_out, children_grad, conv_weight_grad, down_weight_grad)


def solution(mesh):
    in_specs = (
        P(None, None, ("snap", "curve", "rep")),
        P(None, ("snap", "curve", "rep")),
        P(None, ("snap", "curve", "rep")),
        P(None, "chan", None),
        P(None, "chan", None),
        P("chan", ("snap", "curve", "rep")),
    )
    out_specs = (
        P("chan", ("snap", "curve", "rep")),
        P(None, "chan", ("snap", "curve", "rep")),
        P("snap", "chan", None),
        P("snap", "chan", None),
    )
    return jax.shard_map(body, mesh=mesh, in_specs=in_specs, out_specs=out_specs, check_vma=False)
```

```python
import functools

import jax
import jax.numpy as jnp
from jax import lax
from jax.experimental import pallas as pl
from jax.experimental.pallas import tpu as pltpu
from jax.sharding import PartitionSpec as P

BLOCK = 128
SPAN = 256
GROUPS = 3
PER = 9
VMEM_LIMIT = 28 * 1024 * 1024
WHOLE_LIMIT = 60 * 1024 * 1024
PIECES = ("curve", "rep")
F32 = jnp.float32
BF16 = jnp.bfloat16
NOWHERE = -(2**20)
NT = (((1,), (1,)), ((), ()))


def silu_slope(value):
    sigma = jax.nn.sigmoid(value)
    return sigma * (1.0 + value * (1.0 - sigma))


def met(shard):
    devices = lax.axis_size(PIECES)
    pairs = [(i, i + 1) for i in range(1, devices - 1, 2)]
    pairs += [(j, i) for i, j in pairs]
    return [lax.ppermute(shard, PIECES, pairs), swapped(shard, "rep")]


def swapped(shard, axis):
    return lax.ppermute(shard, axis, [(0, 1), (1, 0)])


def call(kernel, out_shape, in_specs, scratch, out_specs=None, limit=VMEM_LIMIT):
    options = {} if out_specs is None else {"out_specs": out_specs}
    return pl.pallas_call(
        kernel,
        out_shape=out_shape,
        in_specs=in_specs,
        scratch_shapes=scratch,
        compiler_params=pltpu.CompilerParams(vmem_limit_bytes=limit),
        cost_estimate=pl.CostEstimate(flops=0, bytes_accessed=0, transcendentals=0),
        **options,
    )


def anywhere(count):
    return [pl.BlockSpec(memory_space=pl.ANY)] * count


def vmem(count):
    return [pl.BlockSpec(memory_space=pltpu.VMEM)] * count


SMEM = [pl.BlockSpec(memory_space=pltpu.SMEM)]


def down_kernel(children_ref, mask_ref, weight_ref, coarse_ref, slope_ref):
    octants = children_ref.shape[0]
    total = None
    for o in range(0, octants, 2):
        masked = jnp.concatenate(
            [
                children_ref[o + j] * mask_ref[o + j : o + j + 1, :].astype(F32).astype(BF16)
                for j in range(2)
            ],
            axis=0,
        )
        weights = jnp.concatenate([weight_ref[o], weight_ref[o + 1]], axis=1)
        term = jnp.dot(weights, masked, preferred_element_type=F32)
        total = term if total is None else total + term
    slope_ref[...] = silu_slope(total)
    coarse_ref[...] = (total * jax.nn.sigmoid(total)).T.astype(BF16)


def index_kernel(shards, neighbours_ref, index_ref, scalars_ref):
    offsets, rows = neighbours_ref.shape
    blocks = rows // BLOCK
    curve, rep = lax.axis_index("curve"), lax.axis_index("rep")
    names = neighbours_ref[...]
    local = jnp.where(names >= 0, names - (curve * 2 + rep - 1) * rows, NOWHERE)
    index_ref[...] = jnp.full(index_ref.shape, NOWHERE, jnp.int32)
    for group in range(GROUPS):
        part = local[group * PER : (group + 1) * PER]
        index_ref[group, :PER, :] = part
        lows = jnp.min(jnp.where(part < 0, -NOWHERE, part), axis=0, keepdims=True)
        highs = jnp.max(part, axis=0, keepdims=True)
        for block in range(blocks):
            at = slice(block * BLOCK, (block + 1) * BLOCK)
            low, high = jnp.min(lows[:, at]), jnp.max(highs[:, at]) + 1
            low = jnp.where(high <= 0, 0, low // 16 * 16)
            steps = jnp.maximum(1, (high - low + SPAN - 1) // SPAN)
            scalars_ref[group * blocks + block] = low
            scalars_ref[(GROUPS + group) * blocks + block] = steps
    last = 2 * GROUPS * blocks
    scalars_ref[last] = lax.axis_index("chan")
    scalars_ref[last + 1] = curve if shards > 1 else 0
    scalars_ref[last + 2] = rep


def fill_window(window_ref, parts, slots, rep):
    rows = parts[0][0].shape[0]
    places = (rows, rep * 2 * rows, (1 - rep) * 2 * rows)
    for part, slot in zip(parts, slots):
        for source, place in zip(part, places):
            window_ref[slot, pl.ds(pl.multiple_of(place, 16), rows), :] = source[...]
    blank = (window_ref.shape[0], window_ref.shape[1] - 3 * rows, window_ref.shape[2])
    window_ref[:, 3 * rows :, :] = jnp.zeros(blank, BF16)


def gather(scalars_ref, column_ref, window_ref, blocks, store, add):
    lanes = lax.broadcasted_iota(jnp.int32, (BLOCK, SPAN), 1).astype(F32).astype(BF16)

    def picked(group, rows, start):
        columns = jnp.clip(column_ref[group, rows, :] - start, -1, SPAN).astype(F32).astype(BF16)
        hot = [
            jnp.where(
                jnp.broadcast_to(columns[:, j : j + 1], (BLOCK, SPAN)) == lanes,
                jnp.ones((), BF16),
                jnp.zeros((), BF16),
            )
            for j in range(PER)
        ]
        at = pl.ds(pl.multiple_of(start, 16), SPAN)
        span = jnp.concatenate([window_ref[c, at, :] for c in range(window_ref.shape[0])], axis=1)
        return jnp.dot(jnp.concatenate(hot, axis=0), span, preferred_element_type=F32).astype(BF16)

    def first(block, _):
        rows = pl.ds(pl.multiple_of(block * BLOCK, BLOCK), BLOCK)
        for group in range(GROUPS):
            result = picked(group, rows, scalars_ref[group * blocks + block])
            for j in range(PER):
                store(group, j, rows, result[j * BLOCK : (j + 1) * BLOCK])
        return 0

    lax.fori_loop(0, blocks, first, 0, unroll=True)

    def rest(at, _):
        group, block = at // blocks, at % blocks
        rows = pl.ds(pl.multiple_of(block * BLOCK, BLOCK), BLOCK)

        def more(step, _):
            result = picked(group, rows, scalars_ref[at] + step * SPAN)
            for j in range(PER):
                add(group, j, rows, result[j * BLOCK : (j + 1) * BLOCK])
            return 0

        lax.fori_loop(1, scalars_ref[GROUPS * blocks + at], more, 0)
        return 0

    lax.fori_loop(0, GROUPS * blocks, rest, 0)


def turn(scratch_ref, value, shards, scalars_ref, at):
    half = value.shape[0] // 2
    size = half // shards
    scratch_ref[0] = value
    place = 0 if shards == 1 else scalars_ref[at + 1]
    rep = scalars_ref[at + 2]
    for core in range(2):
        for step in range(shards):
            source = (rep + core) % 2 * half + (place ^ step) * size
            target = core * half + step * size
            scratch_ref[1, target : target + size] = scratch_ref[
                0, pl.ds(pl.multiple_of(source, size), size)
            ]


def conv_kernel(chans, shards, scale, scalars_ref, index_ref, weight_ref, cotangent_ref, *refs):
    parts, refs = [refs[3 * i : 3 * i + 3] for i in range(chans)], refs[3 * chans :]
    out_ref, grad_ref, keep_ref, send_ref = refs[:4]
    window_ref, column_ref, picked_ref, conv_ref, scratch_ref = refs[4:]
    rows = index_ref.shape[2]
    blocks = rows // BLOCK
    width = chans * window_ref.shape[2]
    channels = weight_ref.shape[1]
    chan = scalars_ref[2 * GROUPS * blocks]
    rep = scalars_ref[2 * GROUPS * blocks + 2]
    slots = (chan, 1 - chan) if chans == 2 else range(chans)
    fill_window(window_ref, parts, slots, rep)
    for group in range(GROUPS):
        column_ref[group] = index_ref[group].T

    def store(group, j, at, value):
        lane = j % 3 * width
        picked_ref[group * 3 + j // 3, at, lane : lane + width] = value

    def add(group, j, at, value):
        lane = j % 3 * width
        picked_ref[group * 3 + j // 3, at, lane : lane + width] += value

    gather(scalars_ref, column_ref, window_ref, blocks, store, add)

    def multiply(three, _):
        weights = jnp.concatenate([weight_ref[three * 3 + j] for j in range(3)], axis=1)
        term = lax.dot_general(picked_ref[three], weights, NT, preferred_element_type=F32)
        conv_ref[...] += term
        return 0

    conv_ref[...] = jnp.zeros_like(conv_ref)
    lax.fori_loop(0, 9, multiply, 0, unroll=True)
    conv = conv_ref[...].T
    sigma = jax.nn.sigmoid(conv)
    out_ref[...] = (conv * sigma).astype(BF16)
    grad = cotangent_ref[...].astype(F32) * (sigma * (1.0 + conv * (1.0 - sigma)))
    grad_ref[...] = grad.T.astype(BF16)
    turn(scratch_ref, grad.astype(BF16), shards, scalars_ref, 2 * GROUPS * blocks)
    half = channels // 2
    size = half // shards

    def weigh(three, _):
        term = jnp.dot(scratch_ref[1], picked_ref[three], preferred_element_type=F32) * scale
        for j in range(3):
            both = term[:, j * width : (j + 1) * width].astype(BF16)
            for step in range(shards):
                at = step * size
                keep_ref[step, three * 3 + j] = both[at : at + size]
                send_ref[step, three * 3 + j] = both[half + at : half + at + size]
        return 0

    lax.fori_loop(0, 9, weigh, 0, unroll=True)


def coarse_grad_kernel(scalars_ref, index_ref, weight_ref, *refs):
    part, refs = refs[:3], refs[3:]
    mine_ref, other_ref, window_ref, column_ref, picked_ref, total_ref = refs
    rows = index_ref.shape[2]
    blocks = rows // BLOCK
    offsets, channels, width = weight_ref.shape
    chan = scalars_ref[2 * GROUPS * blocks]
    rep = scalars_ref[2 * GROUPS * blocks + 2]
    fill_window(window_ref, [part], (0,), rep)
    for group in range(GROUPS):
        column_ref[group] = index_ref[group].T

    def store(group, j, at, value):
        lane = (PER - 1 - j) * channels
        picked_ref[GROUPS - 1 - group, at, lane : lane + channels] = value

    def add(group, j, at, value):
        lane = (PER - 1 - j) * channels
        picked_ref[GROUPS - 1 - group, at, lane : lane + channels] += value

    gather(scalars_ref, column_ref, window_ref, blocks, store, add)
    result = None
    for group in range(GROUPS):
        weights = weight_ref[group * PER : (group + 1) * PER].reshape(PER * channels, width)
        term = jnp.dot(picked_ref[group], weights, preferred_element_type=F32)
        result = term if result is None else result + term
    result = result.T
    chans = width // channels
    for at in range(chans):
        total_ref[at] = result[at * channels : (at + 1) * channels]
    mine_ref[...] = total_ref[chan]
    for step in range(1, chans):
        other_ref[step - 1] = total_ref[lax.rem(chan + step, chans)].astype(BF16)


def pre_grad_kernel(scale, scalars_ref, children_ref, mask_ref, slope_ref, mine_ref, *refs):
    others, (grad_ref, keep_ref, send_ref, scratch_ref) = refs[:-4], refs[-4:]
    total = mine_ref[...]
    for other in others:
        total = total + other[...].astype(F32)
    grad = (total * slope_ref[...]).astype(BF16)
    grad_ref[...] = grad
    blocks = grad.shape[1] // BLOCK
    turn(scratch_ref, grad, 1, scalars_ref, 2 * GROUPS * blocks)
    half = grad.shape[0] // 2
    fine = children_ref.shape[1]
    for o in range(0, children_ref.shape[0], 2):
        masked = jnp.concatenate(
            [
                children_ref[o + j] * mask_ref[o + j : o + j + 1, :].astype(F32).astype(BF16)
                for j in range(2)
            ],
            axis=0,
        )
        term = lax.dot_general(scratch_ref[1], masked, NT, preferred_element_type=F32) * scale
        both = term.astype(BF16)
        for j in range(2):
            keep_ref[o + j] = both[:half, j * fine : (j + 1) * fine]
            send_ref[o + j] = both[half:, j * fine : (j + 1) * fine]


def cut_kernel(weight_ref, *refs):
    out_refs, scratch_ref = refs[:-1], refs[-1]
    octants, fine, _ = scratch_ref.shape
    chans = len(out_refs)
    size = fine // chans
    chan = lax.axis_index("chan")
    for o in range(octants):
        scratch_ref[o] = weight_ref[o].T
    for by in range(chans):
        at = pl.ds(pl.multiple_of((chan + by) % chans * size, size), size)
        for o in range(octants):
            out_refs[by][o] = scratch_ref[o, at, :]


def children_kernel(mask_ref, *refs):
    out_hbm, out_ref, sems = refs[-3:]
    count = (len(refs) - 3) // 2
    grads, weights = refs[:count], refs[count:-3]
    copies = []
    for o in range(out_ref.shape[0]):
        total = None
        for grad, weight in zip(grads, weights):
            term = jnp.dot(weight[o], grad[...], preferred_element_type=F32)
            term = term.astype(BF16).astype(F32)
            total = term if total is None else total + term
        out_ref[o] = (total * mask_ref[o : o + 1, :].astype(F32)).astype(BF16)
        copies.append(pltpu.make_async_copy(out_ref.at[o], out_hbm.at[o], sems.at[o]))
        copies[-1].start()
    for copy in copies:
        copy.wait()


def apart(shard, by):
    return lax.ppermute(shard, "curve", [(i, i ^ by) for i in range(lax.axis_size("curve"))])


def added(*terms):
    return sum(term.astype(F32) for term in terms).astype(BF16)


def sum_over_curve(total, beside):
    terms = [apart(total[by], by) for by in range(1, 4)]
    own = added(after(total[0], beside), *terms)
    across = apart(own, 2)
    return [own, apart(own, 1), across, apart(across, 1)]


def after(value, *earlier):
    return lax.optimization_barrier((value, *earlier))[0]


def body(children, child_mask, neighbours, down_weight, conv_weight, cotangent):
    octants, fine, rows = children.shape
    offsets, channels, width = conv_weight.shape
    blocks = rows // BLOCK
    chans = lax.axis_size("chan")
    chan = lax.axis_index("chan")
    rep = lax.axis_index("rep")
    curve = lax.axis_index("curve")
    pieces = lax.axis_size(PIECES)
    scale = 1.0 / (rows * pieces) ** 0.5
    shape = jax.ShapeDtypeStruct
    half = channels // 2
    shards = 4 if lax.axis_size("curve") == 4 and half % 64 == 0 else 1
    size = half // shards

    coarse, slope = call(
        down_kernel,
        [shape((rows, channels), BF16), shape((channels, rows), F32)],
        vmem(3),
        [],
        limit=WHOLE_LIMIT,
    )(children, child_mask, down_weight)

    if chans == 2:
        parts = [coarse, swapped(coarse, "chan")]
    else:
        every = lax.all_gather(coarse, "chan", axis=0)
        parts = [every[i] for i in range(chans)]
    conv_weight = conv_weight * after(jnp.ones((), BF16), coarse)
    parts[1:] = [after(part, conv_weight) for part in parts[1:]]
    windows = [array for part in parts for array in [part] + met(part)]
    index, scalars = call(
        functools.partial(index_kernel, shards),
        [shape((GROUPS, 16, rows), jnp.int32), shape((2 * GROUPS * blocks + 3,), jnp.int32)],
        vmem(1),
        [],
        vmem(1) + SMEM,
    )(after(neighbours, parts[1]))

    features_out, conv_grad, keep, send = call(
        functools.partial(conv_kernel, chans, shards, scale),
        [
            shape((channels, rows), BF16),
            shape((rows, channels), BF16),
            shape((shards, offsets, size, width), BF16),
            shape((shards, offsets, size, width), BF16),
        ],
        SMEM + vmem(3 + 3 * chans),
        [
            pltpu.VMEM((chans, 3 * rows + SPAN, channels), BF16),
            pltpu.VMEM((GROUPS, rows, 16), jnp.int32),
            pltpu.VMEM((9, rows, 3 * width), BF16),
            pltpu.VMEM((rows, channels), F32),
            pltpu.VMEM((2, channels, rows), BF16),
        ],
    )(scalars, index, conv_weight, cotangent, *windows)

    near = met(conv_grad)
    received = swapped(send, "rep")
    keep = after(keep, *near)
    total = [added(keep[i], received[i]) for i in range(shards)]

    mine, others = call(
        coarse_grad_kernel,
        [shape((channels, rows), F32), shape((chans - 1, channels, rows), BF16)],
        SMEM + vmem(5),
        [
            pltpu.VMEM((1, 3 * rows + SPAN, channels), BF16),
            pltpu.VMEM((GROUPS, rows, 16), jnp.int32),
            pltpu.VMEM((GROUPS, rows, PER * channels), BF16),
            pltpu.VMEM((chans, channels, rows), F32),
        ],
    )(after(scalars, *total), index, conv_weight, conv_grad, *near)
    received = [
        lax.ppermute(others[by - 1], "chan", [(i, (i + by) % chans) for i in range(chans)])
        for by in range(1, chans)
    ]
    mine_fine = fine // chans
    cut = call(
        cut_kernel,
        [shape((octants, mine_fine, channels), BF16)] * chans,
        vmem(1),
        [pltpu.VMEM((octants, fine, channels), BF16)],
    )(after(down_weight, mine))
    blank = [
        jnp.broadcast_to(after(jnp.zeros((), F32), mine), like.shape)
        for like in (conv_weight, down_weight)
    ]
    pre_grad, keep, send = call(
        functools.partial(pre_grad_kernel, scale),
        [
            shape((channels, rows), BF16),
            shape((octants, half, fine), BF16),
            shape((octants, half, fine), BF16),
        ],
        SMEM + vmem(4 + len(received)),
        [pltpu.VMEM((2, channels, rows), BF16)],
    )(after(scalars, *cut, *blank), children, child_mask, slope, mine, *received)

    if shards == 4:
        sums = sum_over_curve(total, pre_grad)
    else:
        sums = [lax.psum(total[0], "curve")]
    own = sums[0]
    sent_grad, send = after(pre_grad, own), after(send, own)
    grads = [
        lax.ppermute(sent_grad, "chan", [(i, (i + by) % chans) for i in range(chans)])
        if by
        else pre_grad
        for by in range(chans)
    ]
    down = core_sum = added(keep, swapped(send, "rep"))
    if shards == 4:
        down = added(down, apart(down, 1))
    else:
        down = lax.psum(down, "curve")
    weights = [
        lax.ppermute(after(cut[by], own), "chan", [(i, (i + by) % chans) for i in range(chans)])
        if by
        else cut[by]
        for by in range(chans)
    ]
    children_grad = call(
        children_kernel,
        shape((octants, mine_fine, rows), BF16),
        vmem(1 + 2 * chans),
        [pltpu.VMEM((octants, mine_fine, rows), BF16), pltpu.SemaphoreType.DMA((octants,))],
        anywhere(1)[0],
    )(after(child_mask, down), *grads, *weights)
    if shards == 4:
        down = added(after(down, children_grad), apart(after(down, sums[2]), 2))

    def joined(result, pieces):
        for row, piece in pieces:
            result = lax.dynamic_update_slice(result, piece.astype(F32), (0, row, 0))
        return result

    rows_of = [rep * half, (1 - rep) * half]
    down_weight_grad = joined(blank[1], zip(rows_of, (down, swapped(down, "rep"))))
    pieces = []
    for step, part in enumerate(sums):
        at = (curve ^ step) * size if shards > 1 else 0
        mine = part if step else after(part, core_sum)
        pieces += [(rows_of[0] + at, mine), (rows_of[1] + at, swapped(part, "rep"))]
    conv_weight_grad = joined(blank[0], pieces)
    return (features_out, children_grad, conv_weight_grad, down_weight_grad)


def solution(mesh):
    in_specs = (
        P(None, None, ("snap", "curve", "rep")),
        P(None, ("snap", "curve", "rep")),
        P(None, ("snap", "curve", "rep")),
        P(None, "chan", None),
        P(None, "chan", None),
        P("chan", ("snap", "curve", "rep")),
    )
    out_specs = (
        P("chan", ("snap", "curve", "rep")),
        P(None, "chan", ("snap", "curve", "rep")),
        P("snap", "chan", None),
        P("snap", "chan", None),
    )
    return jax.shard_map(body, mesh=mesh, in_specs=in_specs, out_specs=out_specs, check_vma=False)
```

```python
import functools

import jax
import jax.numpy as jnp
from jax import lax
from jax.experimental import pallas as pl
from jax.experimental.pallas import tpu as pltpu
from jax.sharding import PartitionSpec as P

BLOCK = 128
SPAN = 256
GROUPS = 3
PER = 9
VMEM_LIMIT = 28 * 1024 * 1024
WHOLE_LIMIT = 60 * 1024 * 1024
PIECES = ("curve", "rep")
F32 = jnp.float32
BF16 = jnp.bfloat16
NOWHERE = -(2**20)
NT = (((1,), (1,)), ((), ()))


def silu_slope(value):
    sigma = jax.nn.sigmoid(value)
    return sigma * (1.0 + value * (1.0 - sigma))


def met(shard):
    devices = lax.axis_size(PIECES)
    pairs = [(i, i + 1) for i in range(1, devices - 1, 2)]
    pairs += [(j, i) for i, j in pairs]
    return [lax.ppermute(shard, PIECES, pairs), swapped(shard, "rep")]


def swapped(shard, axis):
    return lax.ppermute(shard, axis, [(0, 1), (1, 0)])


def call(kernel, out_shape, in_specs, scratch, out_specs=None, limit=VMEM_LIMIT):
    options = {} if out_specs is None else {"out_specs": out_specs}
    return pl.pallas_call(
        kernel,
        out_shape=out_shape,
        in_specs=in_specs,
        scratch_shapes=scratch,
        compiler_params=pltpu.CompilerParams(vmem_limit_bytes=limit),
        cost_estimate=pl.CostEstimate(flops=0, bytes_accessed=0, transcendentals=0),
        **options,
    )


def anywhere(count):
    return [pl.BlockSpec(memory_space=pl.ANY)] * count


def vmem(count):
    return [pl.BlockSpec(memory_space=pltpu.VMEM)] * count


SMEM = [pl.BlockSpec(memory_space=pltpu.SMEM)]


def down_kernel(children_ref, mask_ref, weight_ref, coarse_ref, slope_ref):
    octants = children_ref.shape[0]
    total = None
    for o in range(0, octants, 2):
        masked = jnp.concatenate(
            [
                children_ref[o + j] * mask_ref[o + j : o + j + 1, :].astype(F32).astype(BF16)
                for j in range(2)
            ],
            axis=0,
        )
        weights = jnp.concatenate([weight_ref[o], weight_ref[o + 1]], axis=1)
        term = jnp.dot(weights, masked, preferred_element_type=F32)
        total = term if total is None else total + term
    slope_ref[...] = silu_slope(total)
    coarse_ref[...] = (total * jax.nn.sigmoid(total)).T.astype(BF16)


def index_kernel(shards, neighbours_ref, index_ref, scalars_ref):
    offsets, rows = neighbours_ref.shape
    blocks = rows // BLOCK
    curve, rep = lax.axis_index("curve"), lax.axis_index("rep")
    names = neighbours_ref[...]
    local = jnp.where(names >= 0, names - (curve * 2 + rep - 1) * rows, NOWHERE)
    index_ref[...] = jnp.full(index_ref.shape, NOWHERE, jnp.int32)
    for group in range(GROUPS):
        part = local[group * PER : (group + 1) * PER]
        index_ref[group, :PER, :] = part
        lows = jnp.min(jnp.where(part < 0, -NOWHERE, part), axis=0, keepdims=True)
        highs = jnp.max(part, axis=0, keepdims=True)
        for block in range(blocks):
            at = slice(block * BLOCK, (block + 1) * BLOCK)
            low, high = jnp.min(lows[:, at]), jnp.max(highs[:, at]) + 1
            low = jnp.where(high <= 0, 0, low // 16 * 16)
            steps = jnp.maximum(1, (high - low + SPAN - 1) // SPAN)
            scalars_ref[group * blocks + block] = low
            scalars_ref[(GROUPS + group) * blocks + block] = steps
    last = 2 * GROUPS * blocks
    scalars_ref[last] = lax.axis_index("chan")
    scalars_ref[last + 1] = curve if shards > 1 else 0
    scalars_ref[last + 2] = rep


def fill_window(window_ref, parts, slots, rep):
    rows = parts[0][0].shape[0]
    places = (rows, rep * 2 * rows, (1 - rep) * 2 * rows)
    for part, slot in zip(parts, slots):
        for source, place in zip(part, places):
            window_ref[slot, pl.ds(pl.multiple_of(place, 16), rows), :] = source[...]
    blank = (window_ref.shape[0], window_ref.shape[1] - 3 * rows, window_ref.shape[2])
    window_ref[:, 3 * rows :, :] = jnp.zeros(blank, BF16)


def gather(scalars_ref, column_ref, window_ref, blocks, store, add):
    lanes = lax.broadcasted_iota(jnp.int32, (BLOCK, SPAN), 1).astype(F32).astype(BF16)

    def picked(group, rows, start):
        columns = jnp.clip(column_ref[group, rows, :] - start, -1, SPAN).astype(F32).astype(BF16)
        hot = [
            jnp.where(
                jnp.broadcast_to(columns[:, j : j + 1], (BLOCK, SPAN)) == lanes,
                jnp.ones((), BF16),
                jnp.zeros((), BF16),
            )
            for j in range(PER)
        ]
        at = pl.ds(pl.multiple_of(start, 16), SPAN)
        span = jnp.concatenate([window_ref[c, at, :] for c in range(window_ref.shape[0])], axis=1)
        return jnp.dot(jnp.concatenate(hot, axis=0), span, preferred_element_type=F32).astype(BF16)

    def first(block, _):
        rows = pl.ds(pl.multiple_of(block * BLOCK, BLOCK), BLOCK)
        for group in range(GROUPS):
            result = picked(group, rows, scalars_ref[group * blocks + block])
            for j in range(PER):
                store(group, j, rows, result[j * BLOCK : (j + 1) * BLOCK])
        return 0

    lax.fori_loop(0, blocks, first, 0, unroll=True)

    def rest(at, _):
        group, block = at // blocks, at % blocks
        rows = pl.ds(pl.multiple_of(block * BLOCK, BLOCK), BLOCK)

        def more(step, _):
            result = picked(group, rows, scalars_ref[at] + step * SPAN)
            for j in range(PER):
                add(group, j, rows, result[j * BLOCK : (j + 1) * BLOCK])
            return 0

        lax.fori_loop(1, scalars_ref[GROUPS * blocks + at], more, 0)
        return 0

    lax.fori_loop(0, GROUPS * blocks, rest, 0)


def turn(scratch_ref, value, shards, scalars_ref, at):
    half = value.shape[0] // 2
    size = half // shards
    scratch_ref[0] = value
    place = 0 if shards == 1 else scalars_ref[at + 1]
    rep = scalars_ref[at + 2]
    for core in range(2):
        for step in range(shards):
            source = (rep + core) % 2 * half + (place ^ step) * size
            target = core * half + step * size
            scratch_ref[1, target : target + size] = scratch_ref[
                0, pl.ds(pl.multiple_of(source, size), size)
            ]


def conv_kernel(chans, shards, scalars_ref, index_ref, weight_ref, cotangent_ref, *refs):
    parts, refs = [refs[3 * i : 3 * i + 3] for i in range(chans)], refs[3 * chans :]
    out_ref, grad_ref, turned_ref, picked_ref = refs[:4]
    window_ref, column_ref, conv_ref, scratch_ref = refs[4:]
    rows = index_ref.shape[2]
    blocks = rows // BLOCK
    width = chans * window_ref.shape[2]
    channels = weight_ref.shape[1]
    chan = scalars_ref[2 * GROUPS * blocks]
    rep = scalars_ref[2 * GROUPS * blocks + 2]
    slots = (chan, 1 - chan) if chans == 2 else range(chans)
    fill_window(window_ref, parts, slots, rep)
    for group in range(GROUPS):
        column_ref[group] = index_ref[group].T

    def store(group, j, at, value):
        lane = j % 3 * width
        picked_ref[group * 3 + j // 3, at, lane : lane + width] = value

    def add(group, j, at, value):
        lane = j % 3 * width
        picked_ref[group * 3 + j // 3, at, lane : lane + width] += value

    gather(scalars_ref, column_ref, window_ref, blocks, store, add)

    def multiply(three, _):
        weights = jnp.concatenate([weight_ref[three * 3 + j] for j in range(3)], axis=1)
        term = lax.dot_general(picked_ref[three], weights, NT, preferred_element_type=F32)
        conv_ref[...] += term
        return 0

    conv_ref[...] = jnp.zeros_like(conv_ref)
    lax.fori_loop(0, 9, multiply, 0, unroll=3)
    conv = conv_ref[...].T
    sigma = jax.nn.sigmoid(conv)
    out_ref[...] = (conv * sigma).astype(BF16)
    grad = cotangent_ref[...].astype(F32) * (sigma * (1.0 + conv * (1.0 - sigma)))
    grad_ref[...] = grad.T.astype(BF16)
    turn(scratch_ref, grad.astype(BF16), shards, scalars_ref, 2 * GROUPS * blocks)
    turned_ref[...] = scratch_ref[1]


def weight_kernel(shards, scale, turned_ref, picked_ref, keep_ref, send_ref):
    width = picked_ref.shape[2] // 3
    half = turned_ref.shape[0] // 2
    size = half // shards

    def weigh(three, _):
        term = jnp.dot(turned_ref[...], picked_ref[three], preferred_element_type=F32) * scale
        for j in range(3):
            both = term[:, j * width : (j + 1) * width].astype(BF16)
            for step in range(shards):
                at = step * size
                keep_ref[step, three * 3 + j] = both[at : at + size]
                send_ref[step, three * 3 + j] = both[half + at : half + at + size]
        return 0

    lax.fori_loop(0, 9, weigh, 0, unroll=3)


def coarse_grad_kernel(scalars_ref, index_ref, weight_ref, *refs):
    part, refs = refs[:3], refs[3:]
    mine_ref, other_ref, window_ref, column_ref, picked_ref, total_ref = refs
    rows = index_ref.shape[2]
    blocks = rows // BLOCK
    offsets, channels, width = weight_ref.shape
    chan = scalars_ref[2 * GROUPS * blocks]
    rep = scalars_ref[2 * GROUPS * blocks + 2]
    fill_window(window_ref, [part], (0,), rep)
    for group in range(GROUPS):
        column_ref[group] = index_ref[group].T

    def store(group, j, at, value):
        lane = (PER - 1 - j) * channels
        picked_ref[GROUPS - 1 - group, at, lane : lane + channels] = value

    def add(group, j, at, value):
        lane = (PER - 1 - j) * channels
        picked_ref[GROUPS - 1 - group, at, lane : lane + channels] += value

    gather(scalars_ref, column_ref, window_ref, blocks, store, add)
    result = None
    for group in range(GROUPS):
        weights = weight_ref[group * PER : (group + 1) * PER].reshape(PER * channels, width)
        term = jnp.dot(picked_ref[group], weights, preferred_element_type=F32)
        result = term if result is None else result + term
    result = result.T
    chans = width // channels
    for at in range(chans):
        total_ref[at] = result[at * channels : (at + 1) * channels]
    mine_ref[...] = total_ref[chan]
    for step in range(1, chans):
        other_ref[step - 1] = total_ref[lax.rem(chan + step, chans)].astype(BF16)


def pre_grad_kernel(scale, scalars_ref, children_ref, mask_ref, slope_ref, mine_ref, *refs):
    others, (grad_ref, keep_ref, send_ref, scratch_ref) = refs[:-4], refs[-4:]
    total = mine_ref[...]
    for other in others:
        total = total + other[...].astype(F32)
    grad = (total * slope_ref[...]).astype(BF16)
    grad_ref[...] = grad
    blocks = grad.shape[1] // BLOCK
    turn(scratch_ref, grad, 1, scalars_ref, 2 * GROUPS * blocks)
    half = grad.shape[0] // 2
    fine = children_ref.shape[1]
    for o in range(0, children_ref.shape[0], 2):
        masked = jnp.concatenate(
            [
                children_ref[o + j] * mask_ref[o + j : o + j + 1, :].astype(F32).astype(BF16)
                for j in range(2)
            ],
            axis=0,
        )
        term = lax.dot_general(scratch_ref[1], masked, NT, preferred_element_type=F32) * scale
        both = term.astype(BF16)
        for j in range(2):
            keep_ref[o + j] = both[:half, j * fine : (j + 1) * fine]
            send_ref[o + j] = both[half:, j * fine : (j + 1) * fine]


def cut_kernel(weight_ref, *refs):
    out_refs, scratch_ref = refs[:-1], refs[-1]
    octants, fine, _ = scratch_ref.shape
    chans = len(out_refs)
    size = fine // chans
    chan = lax.axis_index("chan")
    for o in range(octants):
        scratch_ref[o] = weight_ref[o].T
    for by in range(chans):
        at = pl.ds(pl.multiple_of((chan + by) % chans * size, size), size)
        for o in range(octants):
            out_refs[by][o] = scratch_ref[o, at, :]


def children_kernel(mask_ref, *refs):
    out_hbm, out_ref, sems = refs[-3:]
    count = (len(refs) - 3) // 2
    grads, weights = refs[:count], refs[count:-3]
    copies = []
    for o in range(out_ref.shape[0]):
        total = None
        for grad, weight in zip(grads, weights):
            term = jnp.dot(weight[o], grad[...], preferred_element_type=F32)
            term = term.astype(BF16).astype(F32)
            total = term if total is None else total + term
        out_ref[o] = (total * mask_ref[o : o + 1, :].astype(F32)).astype(BF16)
        copies.append(pltpu.make_async_copy(out_ref.at[o], out_hbm.at[o], sems.at[o]))
        copies[-1].start()
    for copy in copies:
        copy.wait()


def apart(shard, by):
    return lax.ppermute(shard, "curve", [(i, i ^ by) for i in range(lax.axis_size("curve"))])


def added(*terms):
    return sum(term.astype(F32) for term in terms).astype(BF16)


def sum_over_curve(total, beside):
    terms = [apart(total[by], by) for by in range(1, 4)]
    own = added(after(total[0], beside), *terms)
    across = apart(own, 2)
    return [own, apart(own, 1), across, apart(across, 1)]


def after(value, *earlier):
    return lax.optimization_barrier((value, *earlier))[0]


def body(children, child_mask, neighbours, down_weight, conv_weight, cotangent):
    octants, fine, rows = children.shape
    offsets, channels, width = conv_weight.shape
    blocks = rows // BLOCK
    chans = lax.axis_size("chan")
    chan = lax.axis_index("chan")
    rep = lax.axis_index("rep")
    curve = lax.axis_index("curve")
    pieces = lax.axis_size(PIECES)
    scale = 1.0 / (rows * pieces) ** 0.5
    shape = jax.ShapeDtypeStruct
    half = channels // 2
    shards = 4 if lax.axis_size("curve") == 4 and half % 64 == 0 else 1
    size = half // shards

    coarse, slope = call(
        down_kernel,
        [shape((rows, channels), BF16), shape((channels, rows), F32)],
        vmem(3),
        [],
        limit=WHOLE_LIMIT,
    )(children, child_mask, down_weight)

    if chans == 2:
        parts = [coarse, swapped(coarse, "chan")]
    else:
        every = lax.all_gather(coarse, "chan", axis=0)
        parts = [every[i] for i in range(chans)]
    conv_weight = conv_weight * after(jnp.ones((), BF16), coarse)
    parts[1:] = [after(part, conv_weight) for part in parts[1:]]
    windows = [array for part in parts for array in [part] + met(part)]
    index, scalars = call(
        functools.partial(index_kernel, shards),
        [shape((GROUPS, 16, rows), jnp.int32), shape((2 * GROUPS * blocks + 3,), jnp.int32)],
        vmem(1),
        [],
        vmem(1) + SMEM,
    )(after(neighbours, parts[1]))

    features_out, conv_grad, turned, picked = call(
        functools.partial(conv_kernel, chans, shards),
        [
            shape((channels, rows), BF16),
            shape((rows, channels), BF16),
            shape((channels, rows), BF16),
            shape((9, rows, 3 * width), BF16),
        ],
        SMEM + vmem(3 + 3 * chans),
        [
            pltpu.VMEM((chans, 3 * rows + SPAN, channels), BF16),
            pltpu.VMEM((GROUPS, rows, 16), jnp.int32),
            pltpu.VMEM((rows, channels), F32),
            pltpu.VMEM((2, channels, rows), BF16),
        ],
    )(scalars, index, conv_weight, cotangent, *windows)
    keep, send = call(
        functools.partial(weight_kernel, shards, scale),
        [shape((shards, offsets, size, width), BF16)] * 2,
        vmem(2),
        [],
    )(turned, picked)


    near = met(conv_grad)
    received = swapped(after(send, *near), "rep")
    total = [added(keep[i], received[i]) for i in range(shards)]

    mine, others = call(
        coarse_grad_kernel,
        [shape((channels, rows), F32), shape((chans - 1, channels, rows), BF16)],
        SMEM + vmem(5),
        [
            pltpu.VMEM((1, 3 * rows + SPAN, channels), BF16),
            pltpu.VMEM((GROUPS, rows, 16), jnp.int32),
            pltpu.VMEM((GROUPS, rows, PER * channels), BF16),
            pltpu.VMEM((chans, channels, rows), F32),
        ],
    )(after(scalars, *total), index, conv_weight, conv_grad, *near)
    received = [
        lax.ppermute(others[by - 1], "chan", [(i, (i + by) % chans) for i in range(chans)])
        for by in range(1, chans)
    ]
    mine_fine = fine // chans
    cut = call(
        cut_kernel,
        [shape((octants, mine_fine, channels), BF16)] * chans,
        vmem(1),
        [pltpu.VMEM((octants, fine, channels), BF16)],
    )(after(down_weight, mine))
    blank = [
        jnp.broadcast_to(after(jnp.zeros((), F32), mine), like.shape)
        for like in (conv_weight, down_weight)
    ]
    pre_grad, keep, send = call(
        functools.partial(pre_grad_kernel, scale),
        [
            shape((channels, rows), BF16),
            shape((octants, half, fine), BF16),
            shape((octants, half, fine), BF16),
        ],
        SMEM + vmem(4 + len(received)),
        [pltpu.VMEM((2, channels, rows), BF16)],
    )(after(scalars, *cut, *blank), children, child_mask, slope, mine, *received)

    if shards == 4:
        sums = sum_over_curve(total, pre_grad)
    else:
        sums = [lax.psum(total[0], "curve")]
    own = sums[0]
    sent_grad, send = after(pre_grad, own), after(send, own)
    grads = [
        lax.ppermute(sent_grad, "chan", [(i, (i + by) % chans) for i in range(chans)])
        if by
        else pre_grad
        for by in range(chans)
    ]
    down = core_sum = added(keep, swapped(send, "rep"))
    if shards == 4:
        down = added(down, apart(down, 1))
    else:
        down = lax.psum(down, "curve")
    weights = [
        lax.ppermute(after(cut[by], own), "chan", [(i, (i + by) % chans) for i in range(chans)])
        if by
        else cut[by]
        for by in range(chans)
    ]
    children_grad = call(
        children_kernel,
        shape((octants, mine_fine, rows), BF16),
        vmem(1 + 2 * chans),
        [pltpu.VMEM((octants, mine_fine, rows), BF16), pltpu.SemaphoreType.DMA((octants,))],
        anywhere(1)[0],
    )(after(child_mask, down), *grads, *weights)
    if shards == 4:
        down = added(after(down, children_grad), apart(after(down, sums[2]), 2))

    def joined(result, pieces):
        for row, piece in pieces:
            result = lax.dynamic_update_slice(result, piece.astype(F32), (0, row, 0))
        return result

    rows_of = [rep * half, (1 - rep) * half]
    down_weight_grad = joined(blank[1], zip(rows_of, (down, swapped(down, "rep"))))
    pieces = []
    for step, part in enumerate(sums):
        at = (curve ^ step) * size if shards > 1 else 0
        mine = part if step else after(part, core_sum)
        pieces += [(rows_of[0] + at, mine), (rows_of[1] + at, swapped(part, "rep"))]
    conv_weight_grad = joined(blank[0], pieces)
    return (features_out, children_grad, conv_weight_grad, down_weight_grad)


def solution(mesh):
    in_specs = (
        P(None, None, ("snap", "curve", "rep")),
        P(None, ("snap", "curve", "rep")),
        P(None, ("snap", "curve", "rep")),
        P(None, "chan", None),
        P(None, "chan", None),
        P("chan", ("snap", "curve", "rep")),
    )
    out_specs = (
        P("chan", ("snap", "curve", "rep")),
        P(None, "chan", ("snap", "curve", "rep")),
        P("snap", "chan", None),
        P("snap", "chan", None),
    )
    return jax.shard_map(body, mesh=mesh, in_specs=in_specs, out_specs=out_specs, check_vma=False)
```

```python
import functools

import jax
import jax.numpy as jnp
from jax import lax
from jax.experimental import pallas as pl
from jax.experimental.pallas import tpu as pltpu
from jax.sharding import PartitionSpec as P

BLOCK = 128
SPAN = 256
GROUPS = 3
PER = 9
VMEM_LIMIT = 28 * 1024 * 1024
WHOLE_LIMIT = 60 * 1024 * 1024
PIECES = ("curve", "rep")
F32 = jnp.float32
BF16 = jnp.bfloat16
NOWHERE = -(2**20)
NT = (((1,), (1,)), ((), ()))


def silu_slope(value):
    sigma = jax.nn.sigmoid(value)
    return sigma * (1.0 + value * (1.0 - sigma))


def met(shard):
    devices = lax.axis_size(PIECES)
    pairs = [(i, i + 1) for i in range(1, devices - 1, 2)]
    pairs += [(j, i) for i, j in pairs]
    return [lax.ppermute(shard, PIECES, pairs), swapped(shard, "rep")]


def swapped(shard, axis):
    return lax.ppermute(shard, axis, [(0, 1), (1, 0)])


def call(kernel, out_shape, in_specs, scratch, out_specs=None, limit=VMEM_LIMIT):
    options = {} if out_specs is None else {"out_specs": out_specs}
    return pl.pallas_call(
        kernel,
        out_shape=out_shape,
        in_specs=in_specs,
        scratch_shapes=scratch,
        compiler_params=pltpu.CompilerParams(vmem_limit_bytes=limit),
        cost_estimate=pl.CostEstimate(flops=0, bytes_accessed=0, transcendentals=0),
        **options,
    )


def anywhere(count):
    return [pl.BlockSpec(memory_space=pl.ANY)] * count


def vmem(count):
    return [pl.BlockSpec(memory_space=pltpu.VMEM)] * count


SMEM = [pl.BlockSpec(memory_space=pltpu.SMEM)]


def down_kernel(children_ref, mask_ref, weight_ref, coarse_ref, slope_ref):
    octants = children_ref.shape[0]
    total = None
    for o in range(0, octants, 2):
        masked = jnp.concatenate(
            [
                children_ref[o + j] * mask_ref[o + j : o + j + 1, :].astype(F32).astype(BF16)
                for j in range(2)
            ],
            axis=0,
        )
        weights = jnp.concatenate([weight_ref[o], weight_ref[o + 1]], axis=1)
        term = jnp.dot(weights, masked, preferred_element_type=F32)
        total = term if total is None else total + term
    slope_ref[...] = silu_slope(total)
    coarse_ref[...] = (total * jax.nn.sigmoid(total)).T.astype(BF16)


def index_kernel(shards, neighbours_ref, index_ref, scalars_ref):
    offsets, rows = neighbours_ref.shape
    blocks = rows // BLOCK
    curve, rep = lax.axis_index("curve"), lax.axis_index("rep")
    names = neighbours_ref[...]
    local = jnp.where(names >= 0, names - (curve * 2 + rep - 1) * rows, NOWHERE)
    index_ref[...] = jnp.full(index_ref.shape, NOWHERE, jnp.int32)
    for group in range(GROUPS):
        part = local[group * PER : (group + 1) * PER]
        index_ref[group, :PER, :] = part
        lows = jnp.min(jnp.where(part < 0, -NOWHERE, part), axis=0, keepdims=True)
        highs = jnp.max(part, axis=0, keepdims=True)
        for block in range(blocks):
            at = slice(block * BLOCK, (block + 1) * BLOCK)
            low, high = jnp.min(lows[:, at]), jnp.max(highs[:, at]) + 1
            low = jnp.where(high <= 0, 0, low // 16 * 16)
            steps = jnp.maximum(1, (high - low + SPAN - 1) // SPAN)
            scalars_ref[group * blocks + block] = low
            scalars_ref[(GROUPS + group) * blocks + block] = steps
    last = 2 * GROUPS * blocks
    scalars_ref[last] = lax.axis_index("chan")
    scalars_ref[last + 1] = curve if shards > 1 else 0
    scalars_ref[last + 2] = rep


def fill_window(window_ref, parts, slots, rep):
    rows = parts[0][0].shape[0]
    places = (rows, rep * 2 * rows, (1 - rep) * 2 * rows)
    for part, slot in zip(parts, slots):
        for source, place in zip(part, places):
            window_ref[slot, pl.ds(pl.multiple_of(place, 16), rows), :] = source[...]
    blank = (window_ref.shape[0], window_ref.shape[1] - 3 * rows, window_ref.shape[2])
    window_ref[:, 3 * rows :, :] = jnp.zeros(blank, BF16)


def gather(scalars_ref, column_ref, window_ref, blocks, store, add):
    lanes = lax.broadcasted_iota(jnp.int32, (BLOCK, SPAN), 1).astype(F32).astype(BF16)

    def picked(group, rows, start):
        columns = jnp.clip(column_ref[group, rows, :] - start, -1, SPAN).astype(F32).astype(BF16)
        hot = [
            jnp.where(
                jnp.broadcast_to(columns[:, j : j + 1], (BLOCK, SPAN)) == lanes,
                jnp.ones((), BF16),
                jnp.zeros((), BF16),
            )
            for j in range(PER)
        ]
        at = pl.ds(pl.multiple_of(start, 16), SPAN)
        span = jnp.concatenate([window_ref[c, at, :] for c in range(window_ref.shape[0])], axis=1)
        return jnp.dot(jnp.concatenate(hot, axis=0), span, preferred_element_type=F32).astype(BF16)

    def first(block, _):
        rows = pl.ds(pl.multiple_of(block * BLOCK, BLOCK), BLOCK)
        for group in range(GROUPS):
            result = picked(group, rows, scalars_ref[group * blocks + block])
            for j in range(PER):
                store(group, j, rows, result[j * BLOCK : (j + 1) * BLOCK])
        return 0

    lax.fori_loop(0, blocks, first, 0, unroll=True)

    def rest(at, _):
        group, block = at // blocks, at % blocks
        rows = pl.ds(pl.multiple_of(block * BLOCK, BLOCK), BLOCK)

        def more(step, _):
            result = picked(group, rows, scalars_ref[at] + step * SPAN)
            for j in range(PER):
                add(group, j, rows, result[j * BLOCK : (j + 1) * BLOCK])
            return 0

        lax.fori_loop(1, scalars_ref[GROUPS * blocks + at], more, 0)
        return 0

    lax.fori_loop(0, GROUPS * blocks, rest, 0)


def turn(scratch_ref, value, shards, scalars_ref, at):
    half = value.shape[0] // 2
    size = half // shards
    scratch_ref[0] = value
    place = 0 if shards == 1 else scalars_ref[at + 1]
    rep = scalars_ref[at + 2]
    for core in range(2):
        for step in range(shards):
            source = (rep + core) % 2 * half + (place ^ step) * size
            target = core * half + step * size
            scratch_ref[1, target : target + size] = scratch_ref[
                0, pl.ds(pl.multiple_of(source, size), size)
            ]


def conv_kernel(chans, shards, scale, scalars_ref, index_ref, weight_ref, cotangent_ref, *refs):
    parts, refs = [refs[3 * i : 3 * i + 3] for i in range(chans)], refs[3 * chans :]
    out_ref, grad_ref, keep_ref, send_ref = refs[:4]
    window_ref, column_ref, picked_ref, conv_ref, scratch_ref = refs[4:]
    rows = index_ref.shape[2]
    blocks = rows // BLOCK
    width = chans * window_ref.shape[2]
    channels = weight_ref.shape[1]
    chan = scalars_ref[2 * GROUPS * blocks]
    rep = scalars_ref[2 * GROUPS * blocks + 2]
    slots = (chan, 1 - chan) if chans == 2 else range(chans)
    fill_window(window_ref, parts, slots, rep)
    for group in range(GROUPS):
        column_ref[group] = index_ref[group].T

    def store(group, j, at, value):
        lane = j % 3 * width
        picked_ref[group * 3 + j // 3, at, lane : lane + width] = value

    def add(group, j, at, value):
        lane = j % 3 * width
        picked_ref[group * 3 + j // 3, at, lane : lane + width] += value

    gather(scalars_ref, column_ref, window_ref, blocks, store, add)

    def multiply(three, _):
        weights = jnp.concatenate([weight_ref[three * 3 + j] for j in range(3)], axis=1)
        term = lax.dot_general(picked_ref[three], weights, NT, preferred_element_type=F32)
        conv_ref[...] += term
        return 0

    conv_ref[...] = jnp.zeros_like(conv_ref)
    lax.fori_loop(0, 9, multiply, 0, unroll=3)
    conv = conv_ref[...].T
    sigma = jax.nn.sigmoid(conv)
    out_ref[...] = (conv * sigma).astype(BF16)
    grad = cotangent_ref[...].astype(F32) * (sigma * (1.0 + conv * (1.0 - sigma)))
    grad_ref[...] = grad.T.astype(BF16)
    turn(scratch_ref, grad.astype(BF16), shards, scalars_ref, 2 * GROUPS * blocks)
    half = channels // 2
    size = half // shards

    def weigh(three, _):
        term = jnp.dot(scratch_ref[1], picked_ref[three], preferred_element_type=F32) * scale
        for j in range(3):
            both = term[:, j * width : (j + 1) * width].astype(BF16)
            for step in range(shards):
                at = step * size
                keep_ref[step, three * 3 + j] = both[at : at + size]
                send_ref[step, three * 3 + j] = both[half + at : half + at + size]
        return 0

    lax.fori_loop(0, 9, weigh, 0, unroll=3)


def coarse_grad_kernel(scalars_ref, index_ref, weight_ref, *refs):
    part, refs = refs[:3], refs[3:]
    mine_ref, other_ref, window_ref, column_ref, picked_ref, total_ref = refs
    rows = index_ref.shape[2]
    blocks = rows // BLOCK
    offsets, channels, width = weight_ref.shape
    chan = scalars_ref[2 * GROUPS * blocks]
    rep = scalars_ref[2 * GROUPS * blocks + 2]
    fill_window(window_ref, [part], (0,), rep)
    for group in range(GROUPS):
        column_ref[group] = index_ref[group].T

    def store(group, j, at, value):
        lane = (PER - 1 - j) * channels
        picked_ref[GROUPS - 1 - group, at, lane : lane + channels] = value

    def add(group, j, at, value):
        lane = (PER - 1 - j) * channels
        picked_ref[GROUPS - 1 - group, at, lane : lane + channels] += value

    gather(scalars_ref, column_ref, window_ref, blocks, store, add)
    result = None
    for group in range(GROUPS):
        weights = weight_ref[group * PER : (group + 1) * PER].reshape(PER * channels, width)
        term = jnp.dot(picked_ref[group], weights, preferred_element_type=F32)
        result = term if result is None else result + term
    result = result.T
    chans = width // channels
    for at in range(chans):
        total_ref[at] = result[at * channels : (at + 1) * channels]
    mine_ref[...] = total_ref[chan]
    for step in range(1, chans):
        other_ref[step - 1] = total_ref[lax.rem(chan + step, chans)].astype(BF16)


def pre_grad_kernel(scale, scalars_ref, children_ref, mask_ref, slope_ref, mine_ref, *refs):
    others, (grad_ref, keep_ref, send_ref, scratch_ref) = refs[:-4], refs[-4:]
    total = mine_ref[...]
    for other in others:
        total = total + other[...].astype(F32)
    grad = (total * slope_ref[...]).astype(BF16)
    grad_ref[...] = grad
    blocks = grad.shape[1] // BLOCK
    turn(scratch_ref, grad, 1, scalars_ref, 2 * GROUPS * blocks)
    half = grad.shape[0] // 2
    fine = children_ref.shape[1]
    for o in range(0, children_ref.shape[0], 2):
        masked = jnp.concatenate(
            [
                children_ref[o + j] * mask_ref[o + j : o + j + 1, :].astype(F32).astype(BF16)
                for j in range(2)
            ],
            axis=0,
        )
        term = lax.dot_general(scratch_ref[1], masked, NT, preferred_element_type=F32) * scale
        both = term.astype(BF16)
        for j in range(2):
            keep_ref[o + j] = both[:half, j * fine : (j + 1) * fine]
            send_ref[o + j] = both[half:, j * fine : (j + 1) * fine]


def cut_kernel(weight_ref, *refs):
    out_refs, scratch_ref = refs[:-1], refs[-1]
    octants, fine, _ = scratch_ref.shape
    chans = len(out_refs)
    size = fine // chans
    chan = lax.axis_index("chan")
    for o in range(octants):
        scratch_ref[o] = weight_ref[o].T
    for by in range(chans):
        at = pl.ds(pl.multiple_of((chan + by) % chans * size, size), size)
        for o in range(octants):
            out_refs[by][o] = scratch_ref[o, at, :]


def children_kernel(mask_ref, *refs):
    out_hbm, out_ref, sems = refs[-3:]
    count = (len(refs) - 3) // 2
    grads, weights = refs[:count], refs[count:-3]
    copies = []
    for o in range(out_ref.shape[0]):
        total = None
        for grad, weight in zip(grads, weights):
            term = jnp.dot(weight[o], grad[...], preferred_element_type=F32)
            term = term.astype(BF16).astype(F32)
            total = term if total is None else total + term
        out_ref[o] = (total * mask_ref[o : o + 1, :].astype(F32)).astype(BF16)
        copies.append(pltpu.make_async_copy(out_ref.at[o], out_hbm.at[o], sems.at[o]))
        copies[-1].start()
    for copy in copies:
        copy.wait()


def apart(shard, by):
    return lax.ppermute(shard, "curve", [(i, i ^ by) for i in range(lax.axis_size("curve"))])


def added(*terms):
    return sum(term.astype(F32) for term in terms).astype(BF16)


def after(value, *earlier):
    return lax.optimization_barrier((value, *earlier))[0]


def body(children, child_mask, neighbours, down_weight, conv_weight, cotangent):
    octants, fine, rows = children.shape
    offsets, channels, width = conv_weight.shape
    blocks = rows // BLOCK
    chans = lax.axis_size("chan")
    chan = lax.axis_index("chan")
    rep = lax.axis_index("rep")
    curve = lax.axis_index("curve")
    pieces = lax.axis_size(PIECES)
    scale = 1.0 / (rows * pieces) ** 0.5
    shape = jax.ShapeDtypeStruct
    half = channels // 2
    shards = 4 if lax.axis_size("curve") == 4 and half % 64 == 0 else 1
    size = half // shards

    coarse, slope = call(
        down_kernel,
        [shape((rows, channels), BF16), shape((channels, rows), F32)],
        vmem(3),
        [],
        limit=WHOLE_LIMIT,
    )(children, child_mask, down_weight)

    if chans == 2:
        parts = [coarse, swapped(coarse, "chan")]
    else:
        every = lax.all_gather(coarse, "chan", axis=0)
        parts = [every[i] for i in range(chans)]
    windows = [array for part in parts for array in [part] + met(part)]
    conv_weight = conv_weight * after(jnp.ones((), BF16), coarse)
    index, scalars = call(
        functools.partial(index_kernel, shards),
        [shape((GROUPS, 16, rows), jnp.int32), shape((2 * GROUPS * blocks + 3,), jnp.int32)],
        vmem(1),
        [],
        vmem(1) + SMEM,
    )(after(neighbours, parts[1]))

    features_out, conv_grad, keep, send = call(
        functools.partial(conv_kernel, chans, shards, scale),
        [
            shape((channels, rows), BF16),
            shape((rows, channels), BF16),
            shape((shards, offsets, size, width), BF16),
            shape((shards, offsets, size, width), BF16),
        ],
        SMEM + vmem(3 + 3 * chans),
        [
            pltpu.VMEM((chans, 3 * rows + SPAN, channels), BF16),
            pltpu.VMEM((GROUPS, rows, 16), jnp.int32),
            pltpu.VMEM((9, rows, 3 * width), BF16),
            pltpu.VMEM((rows, channels), F32),
            pltpu.VMEM((2, channels, rows), BF16),
        ],
    )(scalars, index, conv_weight, cotangent, *windows)

    near = met(conv_grad)
    received = swapped(send, "rep")
    total = [added(keep[i], received[i]) for i in range(shards)]
    terms = []
    if shards == 4:
        terms = [apart(after(total[by], near[1]), by) for by in (2, 3)]
        terms += [apart(total[1], 1)]

    mine, others = call(
        coarse_grad_kernel,
        [shape((channels, rows), F32), shape((chans - 1, channels, rows), BF16)],
        SMEM + vmem(5),
        [
            pltpu.VMEM((1, 3 * rows + SPAN, channels), BF16),
            pltpu.VMEM((GROUPS, rows, 16), jnp.int32),
            pltpu.VMEM((GROUPS, rows, PER * channels), BF16),
            pltpu.VMEM((chans, channels, rows), F32),
        ],
    )(after(scalars, *total), index, conv_weight, conv_grad, *near)
    received = [
        lax.ppermute(others[by - 1], "chan", [(i, (i + by) % chans) for i in range(chans)])
        for by in range(1, chans)
    ]
    mine_fine = fine // chans
    cut = call(
        cut_kernel,
        [shape((octants, mine_fine, channels), BF16)] * chans,
        vmem(1),
        [pltpu.VMEM((octants, fine, channels), BF16)],
    )(after(down_weight, mine))
    blank = [
        jnp.broadcast_to(after(jnp.zeros((), F32), mine), like.shape)
        for like in (conv_weight, down_weight)
    ]
    pre_grad, keep, send = call(
        functools.partial(pre_grad_kernel, scale),
        [
            shape((channels, rows), BF16),
            shape((octants, half, fine), BF16),
            shape((octants, half, fine), BF16),
        ],
        SMEM + vmem(4 + len(received)),
        [pltpu.VMEM((2, channels, rows), BF16)],
    )(after(scalars, *cut, *blank), children, child_mask, slope, mine, *received)

    if shards == 4:
        own = added(after(total[0], pre_grad), *terms)
    else:
        own = lax.psum(total[0], "curve")
    sent_grad, send = after(pre_grad, own), after(send, own)
    grads = [
        lax.ppermute(sent_grad, "chan", [(i, (i + by) % chans) for i in range(chans)])
        if by
        else pre_grad
        for by in range(chans)
    ]
    down = core_sum = added(keep, swapped(send, "rep"))
    sums = [own]
    if shards == 4:
        across = apart(own, 2)
        sums = [own, apart(own, 1), across, apart(across, 1)]
    if shards == 4:
        down = added(down, apart(down, 1))
    else:
        down = lax.psum(down, "curve")
    weights = [
        lax.ppermute(after(cut[by], own), "chan", [(i, (i + by) % chans) for i in range(chans)])
        if by
        else cut[by]
        for by in range(chans)
    ]
    children_grad = call(
        children_kernel,
        shape((octants, mine_fine, rows), BF16),
        vmem(1 + 2 * chans),
        [pltpu.VMEM((octants, mine_fine, rows), BF16), pltpu.SemaphoreType.DMA((octants,))],
        anywhere(1)[0],
    )(after(child_mask, down), *grads, *weights)
    if shards == 4:
        down = added(after(down, children_grad), apart(after(down, sums[2]), 2))

    def joined(result, pieces):
        for row, piece in pieces:
            result = lax.dynamic_update_slice(result, piece.astype(F32), (0, row, 0))
        return result

    rows_of = [rep * half, (1 - rep) * half]
    down_weight_grad = joined(blank[1], zip(rows_of, (down, swapped(down, "rep"))))
    pieces = []
    for step, part in enumerate(sums):
        at = (curve ^ step) * size if shards > 1 else 0
        mine = part if step else after(part, core_sum)
        pieces += [(rows_of[0] + at, mine), (rows_of[1] + at, swapped(part, "rep"))]
    conv_weight_grad = joined(blank[0], pieces)
    return (features_out, children_grad, conv_weight_grad, down_weight_grad)


def solution(mesh):
    in_specs = (
        P(None, None, ("snap", "curve", "rep")),
        P(None, ("snap", "curve", "rep")),
        P(None, ("snap", "curve", "rep")),
        P(None, "chan", None),
        P(None, "chan", None),
        P("chan", ("snap", "curve", "rep")),
    )
    out_specs = (
        P("chan", ("snap", "curve", "rep")),
        P(None, "chan", ("snap", "curve", "rep")),
        P("snap", "chan", None),
        P("snap", "chan", None),
    )
    return jax.shard_map(body, mesh=mesh, in_specs=in_specs, out_specs=out_specs, check_vma=False)
```

```python
import functools

import jax
import jax.numpy as jnp
from jax import lax
from jax.experimental import pallas as pl
from jax.experimental.pallas import tpu as pltpu
from jax.sharding import PartitionSpec as P

BLOCK = 128
SPAN = 256
GROUPS = 3
PER = 9
VMEM_LIMIT = 28 * 1024 * 1024
WHOLE_LIMIT = 60 * 1024 * 1024
PIECES = ("curve", "rep")
F32 = jnp.float32
BF16 = jnp.bfloat16
NOWHERE = -(2**20)
NT = (((1,), (1,)), ((), ()))


def silu_slope(value):
    sigma = jax.nn.sigmoid(value)
    return sigma * (1.0 + value * (1.0 - sigma))


def met(shard):
    devices = lax.axis_size(PIECES)
    pairs = [(i, i + 1) for i in range(1, devices - 1, 2)]
    pairs += [(j, i) for i, j in pairs]
    return [lax.ppermute(shard, PIECES, pairs), swapped(shard, "rep")]


def swapped(shard, axis):
    return lax.ppermute(shard, axis, [(0, 1), (1, 0)])


def call(kernel, out_shape, in_specs, scratch, out_specs=None, limit=VMEM_LIMIT):
    options = {} if out_specs is None else {"out_specs": out_specs}
    return pl.pallas_call(
        kernel,
        out_shape=out_shape,
        in_specs=in_specs,
        scratch_shapes=scratch,
        compiler_params=pltpu.CompilerParams(vmem_limit_bytes=limit),
        cost_estimate=pl.CostEstimate(flops=0, bytes_accessed=0, transcendentals=0),
        **options,
    )


def anywhere(count):
    return [pl.BlockSpec(memory_space=pl.ANY)] * count


def vmem(count):
    return [pl.BlockSpec(memory_space=pltpu.VMEM)] * count


SMEM = [pl.BlockSpec(memory_space=pltpu.SMEM)]


def down_kernel(children_ref, mask_ref, weight_ref, coarse_ref, slope_ref):
    octants = children_ref.shape[0]
    total = None
    for o in range(0, octants, 2):
        masked = jnp.concatenate(
            [
                children_ref[o + j] * mask_ref[o + j : o + j + 1, :].astype(F32).astype(BF16)
                for j in range(2)
            ],
            axis=0,
        )
        weights = jnp.concatenate([weight_ref[o], weight_ref[o + 1]], axis=1)
        term = jnp.dot(weights, masked, preferred_element_type=F32)
        total = term if total is None else total + term
    slope_ref[...] = silu_slope(total)
    coarse_ref[...] = (total * jax.nn.sigmoid(total)).T.astype(BF16)


def index_kernel(shards, neighbours_ref, index_ref, scalars_ref):
    offsets, rows = neighbours_ref.shape
    blocks = rows // BLOCK
    curve, rep = lax.axis_index("curve"), lax.axis_index("rep")
    names = neighbours_ref[...]
    local = jnp.where(names >= 0, names - (curve * 2 + rep - 1) * rows, NOWHERE)
    index_ref[...] = jnp.full(index_ref.shape, NOWHERE, jnp.int32)
    for group in range(GROUPS):
        part = local[group * PER : (group + 1) * PER]
        index_ref[group, :PER, :] = part
        lows = jnp.min(jnp.where(part < 0, -NOWHERE, part), axis=0, keepdims=True)
        highs = jnp.max(part, axis=0, keepdims=True)
        for block in range(blocks):
            at = slice(block * BLOCK, (block + 1) * BLOCK)
            low, high = jnp.min(lows[:, at]), jnp.max(highs[:, at]) + 1
            low = jnp.where(high <= 0, 0, low // 16 * 16)
            steps = jnp.maximum(1, (high - low + SPAN - 1) // SPAN)
            scalars_ref[group * blocks + block] = low
            scalars_ref[(GROUPS + group) * blocks + block] = steps
    last = 2 * GROUPS * blocks
    scalars_ref[last] = lax.axis_index("chan")
    scalars_ref[last + 1] = curve if shards > 1 else 0
    scalars_ref[last + 2] = rep


def fill_window(window_ref, parts, slots, rep):
    rows = parts[0][0].shape[0]
    places = (rows, rep * 2 * rows, (1 - rep) * 2 * rows)
    for part, slot in zip(parts, slots):
        for source, place in zip(part, places):
            window_ref[slot, pl.ds(pl.multiple_of(place, 16), rows), :] = source[...]
    blank = (window_ref.shape[0], window_ref.shape[1] - 3 * rows, window_ref.shape[2])
    window_ref[:, 3 * rows :, :] = jnp.zeros(blank, BF16)


def gather(scalars_ref, column_ref, window_ref, blocks, store, add):
    lanes = lax.broadcasted_iota(jnp.int32, (BLOCK, SPAN), 1).astype(F32).astype(BF16)

    def picked(group, rows, start):
        columns = jnp.clip(column_ref[group, rows, :] - start, -1, SPAN).astype(F32).astype(BF16)
        hot = [
            jnp.where(
                jnp.broadcast_to(columns[:, j : j + 1], (BLOCK, SPAN)) == lanes,
                jnp.ones((), BF16),
                jnp.zeros((), BF16),
            )
            for j in range(PER)
        ]
        at = pl.ds(pl.multiple_of(start, 16), SPAN)
        span = jnp.concatenate([window_ref[c, at, :] for c in range(window_ref.shape[0])], axis=1)
        return jnp.dot(jnp.concatenate(hot, axis=0), span, preferred_element_type=F32).astype(BF16)

    def first(block, _):
        rows = pl.ds(pl.multiple_of(block * BLOCK, BLOCK), BLOCK)
        for group in range(GROUPS):
            result = picked(group, rows, scalars_ref[group * blocks + block])
            for j in range(PER):
                store(group, j, rows, result[j * BLOCK : (j + 1) * BLOCK])
        return 0

    lax.fori_loop(0, blocks, first, 0, unroll=True)

    def rest(at, _):
        group, block = at // blocks, at % blocks
        rows = pl.ds(pl.multiple_of(block * BLOCK, BLOCK), BLOCK)

        def more(step, _):
            result = picked(group, rows, scalars_ref[at] + step * SPAN)
            for j in range(PER):
                add(group, j, rows, result[j * BLOCK : (j + 1) * BLOCK])
            return 0

        lax.fori_loop(1, scalars_ref[GROUPS * blocks + at], more, 0)
        return 0

    lax.fori_loop(0, GROUPS * blocks, rest, 0)


def turn(scratch_ref, value, shards, scalars_ref, at):
    half = value.shape[0] // 2
    size = half // shards
    scratch_ref[0] = value
    place = 0 if shards == 1 else scalars_ref[at + 1]
    rep = scalars_ref[at + 2]
    for core in range(2):
        for step in range(shards):
            source = (rep + core) % 2 * half + (place ^ step) * size
            target = core * half + step * size
            scratch_ref[1, target : target + size] = scratch_ref[
                0, pl.ds(pl.multiple_of(source, size), size)
            ]


def conv_kernel(chans, shards, scale, scalars_ref, index_ref, weight_ref, cotangent_ref, *refs):
    parts, refs = [refs[3 * i : 3 * i + 3] for i in range(chans)], refs[3 * chans :]
    out_ref, grad_ref, keep_ref, send_ref = refs[:4]
    window_ref, column_ref, picked_ref, conv_ref, scratch_ref = refs[4:]
    rows = index_ref.shape[2]
    blocks = rows // BLOCK
    width = chans * window_ref.shape[2]
    channels = weight_ref.shape[1]
    chan = scalars_ref[2 * GROUPS * blocks]
    rep = scalars_ref[2 * GROUPS * blocks + 2]
    slots = (chan, 1 - chan) if chans == 2 else range(chans)
    fill_window(window_ref, parts, slots, rep)
    for group in range(GROUPS):
        column_ref[group] = index_ref[group].T

    def store(group, j, at, value):
        lane = j % 3 * width
        picked_ref[group * 3 + j // 3, at, lane : lane + width] = value

    def add(group, j, at, value):
        lane = j % 3 * width
        picked_ref[group * 3 + j // 3, at, lane : lane + width] += value

    gather(scalars_ref, column_ref, window_ref, blocks, store, add)

    def multiply(three, _):
        weights = jnp.concatenate([weight_ref[three * 3 + j] for j in range(3)], axis=1)
        term = lax.dot_general(picked_ref[three], weights, NT, preferred_element_type=F32)
        conv_ref[...] += term
        return 0

    conv_ref[...] = jnp.zeros_like(conv_ref)
    lax.fori_loop(0, 9, multiply, 0, unroll=3)
    conv = conv_ref[...].T
    sigma = jax.nn.sigmoid(conv)
    out_ref[...] = (conv * sigma).astype(BF16)
    grad = cotangent_ref[...].astype(F32) * (sigma * (1.0 + conv * (1.0 - sigma)))
    grad_ref[...] = grad.T.astype(BF16)
    turn(scratch_ref, grad.astype(BF16), shards, scalars_ref, 2 * GROUPS * blocks)
    half = channels // 2
    size = half // shards

    def weigh(three, _):
        term = jnp.dot(scratch_ref[1], picked_ref[three], preferred_element_type=F32) * scale
        for j in range(3):
            both = term[:, j * width : (j + 1) * width].astype(BF16)
            for step in range(shards):
                at = step * size
                keep_ref[step, three * 3 + j] = both[at : at + size]
                send_ref[step, three * 3 + j] = both[half + at : half + at + size]
        return 0

    lax.fori_loop(0, 9, weigh, 0, unroll=3)


def coarse_grad_kernel(scalars_ref, index_ref, weight_ref, *refs):
    part, refs = refs[:3], refs[3:]
    mine_ref, other_ref, window_ref, column_ref, picked_ref, total_ref = refs
    rows = index_ref.shape[2]
    blocks = rows // BLOCK
    offsets, channels, width = weight_ref.shape
    chan = scalars_ref[2 * GROUPS * blocks]
    rep = scalars_ref[2 * GROUPS * blocks + 2]
    fill_window(window_ref, [part], (0,), rep)
    for group in range(GROUPS):
        column_ref[group] = index_ref[group].T

    def store(group, j, at, value):
        lane = (PER - 1 - j) * channels
        picked_ref[GROUPS - 1 - group, at, lane : lane + channels] = value

    def add(group, j, at, value):
        lane = (PER - 1 - j) * channels
        picked_ref[GROUPS - 1 - group, at, lane : lane + channels] += value

    gather(scalars_ref, column_ref, window_ref, blocks, store, add)
    result = None
    for group in range(GROUPS):
        weights = weight_ref[group * PER : (group + 1) * PER].reshape(PER * channels, width)
        term = jnp.dot(picked_ref[group], weights, preferred_element_type=F32)
        result = term if result is None else result + term
    result = result.T
    chans = width // channels
    for at in range(chans):
        total_ref[at] = result[at * channels : (at + 1) * channels]
    mine_ref[...] = total_ref[chan]
    for step in range(1, chans):
        other_ref[step - 1] = total_ref[lax.rem(chan + step, chans)].astype(BF16)


def pre_grad_kernel(scale, scalars_ref, children_ref, mask_ref, slope_ref, mine_ref, *refs):
    others, (grad_ref, keep_ref, send_ref, scratch_ref) = refs[:-4], refs[-4:]
    total = mine_ref[...]
    for other in others:
        total = total + other[...].astype(F32)
    grad = (total * slope_ref[...]).astype(BF16)
    grad_ref[...] = grad
    blocks = grad.shape[1] // BLOCK
    turn(scratch_ref, grad, 1, scalars_ref, 2 * GROUPS * blocks)
    half = grad.shape[0] // 2
    fine = children_ref.shape[1]
    for o in range(0, children_ref.shape[0], 2):
        masked = jnp.concatenate(
            [
                children_ref[o + j] * mask_ref[o + j : o + j + 1, :].astype(F32).astype(BF16)
                for j in range(2)
            ],
            axis=0,
        )
        term = lax.dot_general(scratch_ref[1], masked, NT, preferred_element_type=F32) * scale
        both = term.astype(BF16)
        for j in range(2):
            keep_ref[o + j] = both[:half, j * fine : (j + 1) * fine]
            send_ref[o + j] = both[half:, j * fine : (j + 1) * fine]


def cut_kernel(weight_ref, *refs):
    out_refs, scratch_ref = refs[:-1], refs[-1]
    octants, fine, _ = scratch_ref.shape
    chans = len(out_refs)
    size = fine // chans
    chan = lax.axis_index("chan")
    for o in range(octants):
        scratch_ref[o] = weight_ref[o].T
    for by in range(chans):
        at = pl.ds(pl.multiple_of((chan + by) % chans * size, size), size)
        for o in range(octants):
            out_refs[by][o] = scratch_ref[o, at, :]


def children_kernel(mask_ref, *refs):
    out_hbm, out_ref, sems = refs[-3:]
    count = (len(refs) - 3) // 2
    grads, weights = refs[:count], refs[count:-3]
    copies = []
    for o in range(out_ref.shape[0]):
        total = None
        for grad, weight in zip(grads, weights):
            term = jnp.dot(weight[o], grad[...], preferred_element_type=F32)
            term = term.astype(BF16).astype(F32)
            total = term if total is None else total + term
        out_ref[o] = (total * mask_ref[o : o + 1, :].astype(F32)).astype(BF16)
        copies.append(pltpu.make_async_copy(out_ref.at[o], out_hbm.at[o], sems.at[o]))
        copies[-1].start()
    for copy in copies:
        copy.wait()


def apart(shard, by):
    return lax.ppermute(shard, "curve", [(i, i ^ by) for i in range(lax.axis_size("curve"))])


def added(*terms):
    return sum(term.astype(F32) for term in terms).astype(BF16)


def after(value, *earlier):
    return lax.optimization_barrier((value, *earlier))[0]


def body(children, child_mask, neighbours, down_weight, conv_weight, cotangent):
    octants, fine, rows = children.shape
    offsets, channels, width = conv_weight.shape
    blocks = rows // BLOCK
    chans = lax.axis_size("chan")
    chan = lax.axis_index("chan")
    rep = lax.axis_index("rep")
    curve = lax.axis_index("curve")
    pieces = lax.axis_size(PIECES)
    scale = 1.0 / (rows * pieces) ** 0.5
    shape = jax.ShapeDtypeStruct
    half = channels // 2
    shards = 4 if lax.axis_size("curve") == 4 and half % 64 == 0 else 1
    size = half // shards

    coarse, slope = call(
        down_kernel,
        [shape((rows, channels), BF16), shape((channels, rows), F32)],
        vmem(3),
        [],
        limit=WHOLE_LIMIT,
    )(children, child_mask, down_weight)

    if chans == 2:
        parts = [coarse, swapped(coarse, "chan")]
    else:
        every = lax.all_gather(coarse, "chan", axis=0)
        parts = [every[i] for i in range(chans)]
    windows = [array for part in parts for array in [part] + met(part)]
    conv_weight = conv_weight * after(jnp.ones((), BF16), coarse)
    index, scalars = call(
        functools.partial(index_kernel, shards),
        [shape((GROUPS, 16, rows), jnp.int32), shape((2 * GROUPS * blocks + 3,), jnp.int32)],
        vmem(1),
        [],
        vmem(1) + SMEM,
    )(after(neighbours, parts[1]))

    features_out, conv_grad, keep, send = call(
        functools.partial(conv_kernel, chans, shards, scale),
        [
            shape((channels, rows), BF16),
            shape((rows, channels), BF16),
            shape((shards, offsets, size, width), BF16),
            shape((shards, offsets, size, width), BF16),
        ],
        SMEM + vmem(3 + 3 * chans),
        [
            pltpu.VMEM((chans, 3 * rows + SPAN, channels), BF16),
            pltpu.VMEM((GROUPS, rows, 16), jnp.int32),
            pltpu.VMEM((9, rows, 3 * width), BF16),
            pltpu.VMEM((rows, channels), F32),
            pltpu.VMEM((2, channels, rows), BF16),
        ],
    )(scalars, index, conv_weight, cotangent, *windows)

    near = met(conv_grad)
    received = swapped(send, "rep")
    total = [added(keep[i], received[i]) for i in range(shards)]
    terms = []
    if shards == 4:
        terms = [apart(after(total[by], near[1]), by) for by in (2, 3)]
        terms += [apart(total[1], 1)]

    mine, others = call(
        coarse_grad_kernel,
        [shape((channels, rows), F32), shape((chans - 1, channels, rows), BF16)],
        SMEM + vmem(5),
        [
            pltpu.VMEM((1, 3 * rows + SPAN, channels), BF16),
            pltpu.VMEM((GROUPS, rows, 16), jnp.int32),
            pltpu.VMEM((GROUPS, rows, PER * channels), BF16),
            pltpu.VMEM((chans, channels, rows), F32),
        ],
    )(after(scalars, *total), index, conv_weight, conv_grad, *near)
    received = [
        lax.ppermute(others[by - 1], "chan", [(i, (i + by) % chans) for i in range(chans)])
        for by in range(1, chans)
    ]
    mine_fine = fine // chans
    cut = call(
        cut_kernel,
        [shape((octants, mine_fine, channels), BF16)] * chans,
        vmem(1),
        [pltpu.VMEM((octants, fine, channels), BF16)],
    )(after(down_weight, mine))
    blank = [
        jnp.broadcast_to(after(jnp.zeros((), F32), mine), like.shape)
        for like in (conv_weight, down_weight)
    ]
    pre_grad, keep, send = call(
        functools.partial(pre_grad_kernel, scale),
        [
            shape((channels, rows), BF16),
            shape((octants, half, fine), BF16),
            shape((octants, half, fine), BF16),
        ],
        SMEM + vmem(4 + len(received)),
        [pltpu.VMEM((2, channels, rows), BF16)],
    )(after(scalars, *cut, *blank), children, child_mask, slope, mine, *received)

    if shards == 4:
        own = added(after(total[0], pre_grad), *terms)
    else:
        own = lax.psum(total[0], "curve")
    sent_grad, send = after(pre_grad, own), after(send, own)
    grads = [
        lax.ppermute(sent_grad, "chan", [(i, (i + by) % chans) for i in range(chans)])
        if by
        else pre_grad
        for by in range(chans)
    ]
    down = core_sum = added(keep, swapped(send, "rep"))
    sums = [own]
    if shards == 4:
        across = apart(own, 2)
        sums = [own, apart(own, 1), across, apart(across, 1)]
    theirs = [
        swapped(part if step else after(part, core_sum), "rep") for step, part in enumerate(sums)
    ]
    if shards == 4:
        down = added(down, apart(down, 1))
    else:
        down = lax.psum(down, "curve")
    weights = [
        lax.ppermute(after(cut[by], own), "chan", [(i, (i + by) % chans) for i in range(chans)])
        if by
        else cut[by]
        for by in range(chans)
    ]
    children_grad = call(
        children_kernel,
        shape((octants, mine_fine, rows), BF16),
        vmem(1 + 2 * chans),
        [pltpu.VMEM((octants, mine_fine, rows), BF16), pltpu.SemaphoreType.DMA((octants,))],
        anywhere(1)[0],
    )(after(child_mask, down, *theirs[2:3]), *grads, *weights)
    if shards == 4:
        down = added(after(down, children_grad), apart(after(down, sums[2], theirs[0]), 2))

    def joined(result, pieces):
        for row, piece in pieces:
            result = lax.dynamic_update_slice(result, piece.astype(F32), (0, row, 0))
        return result

    rows_of = [rep * half, (1 - rep) * half]
    down_weight_grad = joined(blank[1], zip(rows_of, (down, swapped(down, "rep"))))
    pieces = []
    for step, part in enumerate(sums):
        at = (curve ^ step) * size if shards > 1 else 0
        mine = part if step else after(part, core_sum)
        pieces += [(rows_of[0] + at, mine), (rows_of[1] + at, theirs[step])]
    conv_weight_grad = joined(blank[0], pieces)
    return (features_out, children_grad, conv_weight_grad, down_weight_grad)


def solution(mesh):
    in_specs = (
        P(None, None, ("snap", "curve", "rep")),
        P(None, ("snap", "curve", "rep")),
        P(None, ("snap", "curve", "rep")),
        P(None, "chan", None),
        P(None, "chan", None),
        P("chan", ("snap", "curve", "rep")),
    )
    out_specs = (
        P("chan", ("snap", "curve", "rep")),
        P(None, "chan", ("snap", "curve", "rep")),
        P("snap", "chan", None),
        P("snap", "chan", None),
    )
    return jax.shard_map(body, mesh=mesh, in_specs=in_specs, out_specs=out_specs, check_vma=False)
```

```python
import functools

import jax
import jax.numpy as jnp
from jax import lax
from jax.experimental import pallas as pl
from jax.experimental.pallas import tpu as pltpu
from jax.sharding import PartitionSpec as P

BLOCK = 128
SPAN = 256
GROUPS = 3
PER = 9
VMEM_LIMIT = 28 * 1024 * 1024
WHOLE_LIMIT = 60 * 1024 * 1024
PIECES = ("curve", "rep")
F32 = jnp.float32
BF16 = jnp.bfloat16
NOWHERE = -(2**20)
NT = (((1,), (1,)), ((), ()))


def silu_slope(value):
    sigma = jax.nn.sigmoid(value)
    return sigma * (1.0 + value * (1.0 - sigma))


def met(shard, later=None):
    devices = lax.axis_size(PIECES)
    pairs = [(i, i + 1) for i in range(1, devices - 1, 2)]
    pairs += [(j, i) for i, j in pairs]
    return [lax.ppermute(shard, PIECES, pairs), swapped(shard if later is None else later, "rep")]


def swapped(shard, axis):
    return lax.ppermute(shard, axis, [(0, 1), (1, 0)])


def call(kernel, out_shape, in_specs, scratch, out_specs=None, limit=VMEM_LIMIT):
    options = {} if out_specs is None else {"out_specs": out_specs}
    return pl.pallas_call(
        kernel,
        out_shape=out_shape,
        in_specs=in_specs,
        scratch_shapes=scratch,
        compiler_params=pltpu.CompilerParams(vmem_limit_bytes=limit),
        cost_estimate=pl.CostEstimate(flops=0, bytes_accessed=0, transcendentals=0),
        **options,
    )


def anywhere(count):
    return [pl.BlockSpec(memory_space=pl.ANY)] * count


def vmem(count):
    return [pl.BlockSpec(memory_space=pltpu.VMEM)] * count


SMEM = [pl.BlockSpec(memory_space=pltpu.SMEM)]


def down_kernel(children_ref, mask_ref, weight_ref, coarse_ref, slope_ref):
    octants = children_ref.shape[0]
    total = None
    for o in range(0, octants, 2):
        masked = jnp.concatenate(
            [
                children_ref[o + j] * mask_ref[o + j : o + j + 1, :].astype(F32).astype(BF16)
                for j in range(2)
            ],
            axis=0,
        )
        weights = jnp.concatenate([weight_ref[o], weight_ref[o + 1]], axis=1)
        term = jnp.dot(weights, masked, preferred_element_type=F32)
        total = term if total is None else total + term
    slope_ref[...] = silu_slope(total)
    coarse_ref[...] = (total * jax.nn.sigmoid(total)).T.astype(BF16)


def index_kernel(shards, neighbours_ref, index_ref, scalars_ref):
    offsets, rows = neighbours_ref.shape
    blocks = rows // BLOCK
    curve, rep = lax.axis_index("curve"), lax.axis_index("rep")
    names = neighbours_ref[...]
    local = jnp.where(names >= 0, names - (curve * 2 + rep - 1) * rows, NOWHERE)
    index_ref[...] = jnp.full(index_ref.shape, NOWHERE, jnp.int32)
    for group in range(GROUPS):
        part = local[group * PER : (group + 1) * PER]
        index_ref[group, :PER, :] = part
        lows = jnp.min(jnp.where(part < 0, -NOWHERE, part), axis=0, keepdims=True)
        highs = jnp.max(part, axis=0, keepdims=True)
        for block in range(blocks):
            at = slice(block * BLOCK, (block + 1) * BLOCK)
            low, high = jnp.min(lows[:, at]), jnp.max(highs[:, at]) + 1
            low = jnp.where(high <= 0, 0, low // 16 * 16)
            steps = jnp.maximum(1, (high - low + SPAN - 1) // SPAN)
            scalars_ref[group * blocks + block] = low
            scalars_ref[(GROUPS + group) * blocks + block] = steps
    last = 2 * GROUPS * blocks
    scalars_ref[last] = lax.axis_index("chan")
    scalars_ref[last + 1] = curve if shards > 1 else 0
    scalars_ref[last + 2] = rep


def fill_window(window_ref, parts, slots, rep):
    rows = parts[0][0].shape[0]
    places = (rows, rep * 2 * rows, (1 - rep) * 2 * rows)
    for part, slot in zip(parts, slots):
        for source, place in zip(part, places):
            window_ref[slot, pl.ds(pl.multiple_of(place, 16), rows), :] = source[...]
    blank = (window_ref.shape[0], window_ref.shape[1] - 3 * rows, window_ref.shape[2])
    window_ref[:, 3 * rows :, :] = jnp.zeros(blank, BF16)


def gather(scalars_ref, column_ref, window_ref, blocks, store, add):
    lanes = lax.broadcasted_iota(jnp.int32, (BLOCK, SPAN), 1).astype(F32).astype(BF16)

    def picked(group, rows, start):
        columns = jnp.clip(column_ref[group, rows, :] - start, -1, SPAN).astype(F32).astype(BF16)
        hot = [
            jnp.where(
                jnp.broadcast_to(columns[:, j : j + 1], (BLOCK, SPAN)) == lanes,
                jnp.ones((), BF16),
                jnp.zeros((), BF16),
            )
            for j in range(PER)
        ]
        at = pl.ds(pl.multiple_of(start, 16), SPAN)
        span = jnp.concatenate([window_ref[c, at, :] for c in range(window_ref.shape[0])], axis=1)
        return jnp.dot(jnp.concatenate(hot, axis=0), span, preferred_element_type=F32).astype(BF16)

    def first(block, _):
        rows = pl.ds(pl.multiple_of(block * BLOCK, BLOCK), BLOCK)
        for group in range(GROUPS):
            result = picked(group, rows, scalars_ref[group * blocks + block])
            for j in range(PER):
                store(group, j, rows, result[j * BLOCK : (j + 1) * BLOCK])
        return 0

    lax.fori_loop(0, blocks, first, 0, unroll=True)

    def rest(at, _):
        group, block = at // blocks, at % blocks
        rows = pl.ds(pl.multiple_of(block * BLOCK, BLOCK), BLOCK)

        def more(step, _):
            result = picked(group, rows, scalars_ref[at] + step * SPAN)
            for j in range(PER):
                add(group, j, rows, result[j * BLOCK : (j + 1) * BLOCK])
            return 0

        lax.fori_loop(1, scalars_ref[GROUPS * blocks + at], more, 0)
        return 0

    lax.fori_loop(0, GROUPS * blocks, rest, 0)


def turn(scratch_ref, value, shards, scalars_ref, at):
    half = value.shape[0] // 2
    size = half // shards
    scratch_ref[0] = value
    place = 0 if shards == 1 else scalars_ref[at + 1]
    rep = scalars_ref[at + 2]
    for core in range(2):
        for step in range(shards):
            source = (rep + core) % 2 * half + (place ^ step) * size
            target = core * half + step * size
            scratch_ref[1, target : target + size] = scratch_ref[
                0, pl.ds(pl.multiple_of(source, size), size)
            ]


def conv_kernel(chans, shards, scale, scalars_ref, index_ref, weight_ref, cotangent_ref, *refs):
    parts, refs = [refs[3 * i : 3 * i + 3] for i in range(chans)], refs[3 * chans :]
    out_ref, grad_ref, keep_ref, send_ref = refs[:4]
    window_ref, column_ref, picked_ref, conv_ref, scratch_ref = refs[4:]
    rows = index_ref.shape[2]
    blocks = rows // BLOCK
    width = chans * window_ref.shape[2]
    channels = weight_ref.shape[1]
    chan = scalars_ref[2 * GROUPS * blocks]
    rep = scalars_ref[2 * GROUPS * blocks + 2]
    slots = (chan, 1 - chan) if chans == 2 else range(chans)
    fill_window(window_ref, parts, slots, rep)
    for group in range(GROUPS):
        column_ref[group] = index_ref[group].T

    def store(group, j, at, value):
        lane = j % 3 * width
        picked_ref[group * 3 + j // 3, at, lane : lane + width] = value

    def add(group, j, at, value):
        lane = j % 3 * width
        picked_ref[group * 3 + j // 3, at, lane : lane + width] += value

    gather(scalars_ref, column_ref, window_ref, blocks, store, add)

    def multiply(three, _):
        weights = jnp.concatenate([weight_ref[three * 3 + j] for j in range(3)], axis=1)
        term = lax.dot_general(picked_ref[three], weights, NT, preferred_element_type=F32)
        conv_ref[...] += term
        return 0

    conv_ref[...] = jnp.zeros_like(conv_ref)
    lax.fori_loop(0, 9, multiply, 0, unroll=3)
    conv = conv_ref[...].T
    sigma = jax.nn.sigmoid(conv)
    out_ref[...] = (conv * sigma).astype(BF16)
    grad = cotangent_ref[...].astype(F32) * (sigma * (1.0 + conv * (1.0 - sigma)))
    grad_ref[...] = grad.T.astype(BF16)
    turn(scratch_ref, grad.astype(BF16), shards, scalars_ref, 2 * GROUPS * blocks)
    half = channels // 2
    size = half // shards

    def weigh(three, _):
        term = jnp.dot(scratch_ref[1], picked_ref[three], preferred_element_type=F32) * scale
        for j in range(3):
            both = term[:, j * width : (j + 1) * width].astype(BF16)
            for step in range(shards):
                at = step * size
                keep_ref[step, three * 3 + j] = both[at : at + size]
                send_ref[step, three * 3 + j] = both[half + at : half + at + size]
        return 0

    lax.fori_loop(0, 9, weigh, 0, unroll=3)


def coarse_grad_kernel(scalars_ref, index_ref, weight_ref, *refs):
    part, refs = refs[:3], refs[3:]
    mine_ref, other_ref, window_ref, column_ref, picked_ref, total_ref = refs
    rows = index_ref.shape[2]
    blocks = rows // BLOCK
    offsets, channels, width = weight_ref.shape
    chan = scalars_ref[2 * GROUPS * blocks]
    rep = scalars_ref[2 * GROUPS * blocks + 2]
    fill_window(window_ref, [part], (0,), rep)
    for group in range(GROUPS):
        column_ref[group] = index_ref[group].T

    def store(group, j, at, value):
        lane = (PER - 1 - j) * channels
        picked_ref[GROUPS - 1 - group, at, lane : lane + channels] = value

    def add(group, j, at, value):
        lane = (PER - 1 - j) * channels
        picked_ref[GROUPS - 1 - group, at, lane : lane + channels] += value

    gather(scalars_ref, column_ref, window_ref, blocks, store, add)
    result = None
    for group in range(GROUPS):
        weights = weight_ref[group * PER : (group + 1) * PER].reshape(PER * channels, width)
        term = jnp.dot(picked_ref[group], weights, preferred_element_type=F32)
        result = term if result is None else result + term
    result = result.T
    chans = width // channels
    for at in range(chans):
        total_ref[at] = result[at * channels : (at + 1) * channels]
    mine_ref[...] = total_ref[chan]
    for step in range(1, chans):
        other_ref[step - 1] = total_ref[lax.rem(chan + step, chans)].astype(BF16)


def pre_grad_kernel(scale, scalars_ref, children_ref, mask_ref, slope_ref, mine_ref, *refs):
    others, (grad_ref, keep_ref, send_ref, scratch_ref) = refs[:-4], refs[-4:]
    total = mine_ref[...]
    for other in others:
        total = total + other[...].astype(F32)
    grad = (total * slope_ref[...]).astype(BF16)
    grad_ref[...] = grad
    blocks = grad.shape[1] // BLOCK
    turn(scratch_ref, grad, 1, scalars_ref, 2 * GROUPS * blocks)
    half = grad.shape[0] // 2
    fine = children_ref.shape[1]
    for o in range(0, children_ref.shape[0], 2):
        masked = jnp.concatenate(
            [
                children_ref[o + j] * mask_ref[o + j : o + j + 1, :].astype(F32).astype(BF16)
                for j in range(2)
            ],
            axis=0,
        )
        term = lax.dot_general(scratch_ref[1], masked, NT, preferred_element_type=F32) * scale
        both = term.astype(BF16)
        for j in range(2):
            keep_ref[o + j] = both[:half, j * fine : (j + 1) * fine]
            send_ref[o + j] = both[half:, j * fine : (j + 1) * fine]


def cut_kernel(weight_ref, *refs):
    out_refs, scratch_ref = refs[:-1], refs[-1]
    octants, fine, _ = scratch_ref.shape
    chans = len(out_refs)
    size = fine // chans
    chan = lax.axis_index("chan")
    for o in range(octants):
        scratch_ref[o] = weight_ref[o].T
    for by in range(chans):
        at = pl.ds(pl.multiple_of((chan + by) % chans * size, size), size)
        for o in range(octants):
            out_refs[by][o] = scratch_ref[o, at, :]


def children_kernel(mask_ref, *refs):
    out_hbm, out_ref, sems = refs[-3:]
    count = (len(refs) - 3) // 2
    grads, weights = refs[:count], refs[count:-3]
    copies = []
    for o in range(out_ref.shape[0]):
        total = None
        for grad, weight in zip(grads, weights):
            term = jnp.dot(weight[o], grad[...], preferred_element_type=F32)
            term = term.astype(BF16).astype(F32)
            total = term if total is None else total + term
        out_ref[o] = (total * mask_ref[o : o + 1, :].astype(F32)).astype(BF16)
        copies.append(pltpu.make_async_copy(out_ref.at[o], out_hbm.at[o], sems.at[o]))
        copies[-1].start()
    for copy in copies:
        copy.wait()


def apart(shard, by):
    return lax.ppermute(shard, "curve", [(i, i ^ by) for i in range(lax.axis_size("curve"))])


def added(*terms):
    return sum(term.astype(F32) for term in terms).astype(BF16)


def after(value, *earlier):
    return lax.optimization_barrier((value, *earlier))[0]


def body(children, child_mask, neighbours, down_weight, conv_weight, cotangent):
    octants, fine, rows = children.shape
    offsets, channels, width = conv_weight.shape
    blocks = rows // BLOCK
    chans = lax.axis_size("chan")
    chan = lax.axis_index("chan")
    rep = lax.axis_index("rep")
    curve = lax.axis_index("curve")
    pieces = lax.axis_size(PIECES)
    scale = 1.0 / (rows * pieces) ** 0.5
    shape = jax.ShapeDtypeStruct
    half = channels // 2
    shards = 4 if lax.axis_size("curve") == 4 and half % 64 == 0 else 1
    size = half // shards

    coarse, slope = call(
        down_kernel,
        [shape((rows, channels), BF16), shape((channels, rows), F32)],
        vmem(3),
        [],
        limit=WHOLE_LIMIT,
    )(children, child_mask, down_weight)

    if chans == 2:
        parts = [coarse, swapped(coarse, "chan")]
    else:
        every = lax.all_gather(coarse, "chan", axis=0)
        parts = [every[i] for i in range(chans)]
    windows = [array for part in parts for array in [part] + met(part)]
    conv_weight = conv_weight * after(jnp.ones((), BF16), coarse)
    index, scalars = call(
        functools.partial(index_kernel, shards),
        [shape((GROUPS, 16, rows), jnp.int32), shape((2 * GROUPS * blocks + 3,), jnp.int32)],
        vmem(1),
        [],
        vmem(1) + SMEM,
    )(after(neighbours, parts[1]))

    features_out, conv_grad, keep, send = call(
        functools.partial(conv_kernel, chans, shards, scale),
        [
            shape((channels, rows), BF16),
            shape((rows, channels), BF16),
            shape((shards, offsets, size, width), BF16),
            shape((shards, offsets, size, width), BF16),
        ],
        SMEM + vmem(3 + 3 * chans),
        [
            pltpu.VMEM((chans, 3 * rows + SPAN, channels), BF16),
            pltpu.VMEM((GROUPS, rows, 16), jnp.int32),
            pltpu.VMEM((9, rows, 3 * width), BF16),
            pltpu.VMEM((rows, channels), F32),
            pltpu.VMEM((2, channels, rows), BF16),
        ],
    )(scalars, index, conv_weight, cotangent, *windows)

    received = swapped(send, "rep")
    near = met(conv_grad, after(conv_grad, received))
    total = [added(keep[i], received[i]) for i in range(shards)]
    terms = []
    if shards == 4:
        terms = [apart(total[1], 1)]
        terms += [apart(after(total[by], near[1]), by) for by in (3, 2)]

    mine, others = call(
        coarse_grad_kernel,
        [shape((channels, rows), F32), shape((chans - 1, channels, rows), BF16)],
        SMEM + vmem(5),
        [
            pltpu.VMEM((1, 3 * rows + SPAN, channels), BF16),
            pltpu.VMEM((GROUPS, rows, 16), jnp.int32),
            pltpu.VMEM((GROUPS, rows, PER * channels), BF16),
            pltpu.VMEM((chans, channels, rows), F32),
        ],
    )(after(scalars, *total), index, conv_weight, conv_grad, *near)
    received = [
        lax.ppermute(others[by - 1], "chan", [(i, (i + by) % chans) for i in range(chans)])
        for by in range(1, chans)
    ]
    mine_fine = fine // chans
    cut = call(
        cut_kernel,
        [shape((octants, mine_fine, channels), BF16)] * chans,
        vmem(1),
        [pltpu.VMEM((octants, fine, channels), BF16)],
    )(after(down_weight, mine))
    blank = [
        jnp.broadcast_to(after(jnp.zeros((), F32), mine), like.shape)
        for like in (conv_weight, down_weight)
    ]
    pre_grad, keep, send = call(
        functools.partial(pre_grad_kernel, scale),
        [
            shape((channels, rows), BF16),
            shape((octants, half, fine), BF16),
            shape((octants, half, fine), BF16),
        ],
        SMEM + vmem(4 + len(received)),
        [pltpu.VMEM((2, channels, rows), BF16)],
    )(after(scalars, *cut, *blank), children, child_mask, slope, mine, *received)

    if shards == 4:
        own = added(after(total[0], pre_grad), *terms)
    else:
        own = lax.psum(total[0], "curve")
    sent_grad, send = after(pre_grad, own), after(send, own)
    grads = [
        lax.ppermute(sent_grad, "chan", [(i, (i + by) % chans) for i in range(chans)])
        if by
        else pre_grad
        for by in range(chans)
    ]
    down = core_sum = added(keep, swapped(send, "rep"))
    sums = [own]
    if shards == 4:
        across = apart(own, 2)
        sums = [own, apart(own, 1), across, apart(across, 1)]
    theirs = [
        swapped(part if step else after(part, core_sum), "rep") for step, part in enumerate(sums)
    ]
    if shards == 4:
        down = added(down, apart(down, 1))
    else:
        down = lax.psum(down, "curve")
    weights = [
        lax.ppermute(after(cut[by], own), "chan", [(i, (i + by) % chans) for i in range(chans)])
        if by
        else cut[by]
        for by in range(chans)
    ]
    children_grad = call(
        children_kernel,
        shape((octants, mine_fine, rows), BF16),
        vmem(1 + 2 * chans),
        [pltpu.VMEM((octants, mine_fine, rows), BF16), pltpu.SemaphoreType.DMA((octants,))],
        anywhere(1)[0],
    )(after(child_mask, down, *theirs[2:3]), *grads, *weights)
    if shards == 4:
        down = added(after(down, children_grad), apart(after(down, sums[2], theirs[0]), 2))

    def joined(result, pieces):
        for row, piece in pieces:
            result = lax.dynamic_update_slice(result, piece.astype(F32), (0, row, 0))
        return result

    rows_of = [rep * half, (1 - rep) * half]
    down_weight_grad = joined(blank[1], zip(rows_of, (down, swapped(down, "rep"))))
    pieces = []
    for step, part in enumerate(sums):
        at = (curve ^ step) * size if shards > 1 else 0
        mine = part if step else after(part, core_sum)
        pieces += [(rows_of[0] + at, mine), (rows_of[1] + at, theirs[step])]
    conv_weight_grad = joined(blank[0], pieces)
    return (features_out, children_grad, conv_weight_grad, down_weight_grad)


def solution(mesh):
    in_specs = (
        P(None, None, ("snap", "curve", "rep")),
        P(None, ("snap", "curve", "rep")),
        P(None, ("snap", "curve", "rep")),
        P(None, "chan", None),
        P(None, "chan", None),
        P("chan", ("snap", "curve", "rep")),
    )
    out_specs = (
        P("chan", ("snap", "curve", "rep")),
        P(None, "chan", ("snap", "curve", "rep")),
        P("snap", "chan", None),
        P("snap", "chan", None),
    )
    return jax.shard_map(body, mesh=mesh, in_specs=in_specs, out_specs=out_specs, check_vma=False)
```

```python
import functools

import jax
import jax.numpy as jnp
from jax import lax
from jax.experimental import pallas as pl
from jax.experimental.pallas import tpu as pltpu
from jax.sharding import PartitionSpec as P

BLOCK = 128
SPAN = 256
GROUPS = 3
PER = 9
VMEM_LIMIT = 28 * 1024 * 1024
WHOLE_LIMIT = 60 * 1024 * 1024
PIECES = ("curve", "rep")
F32 = jnp.float32
BF16 = jnp.bfloat16
NOWHERE = -(2**20)
NT = (((1,), (1,)), ((), ()))


def silu_slope(value):
    sigma = jax.nn.sigmoid(value)
    return sigma * (1.0 + value * (1.0 - sigma))


def met(shard, later=None):
    devices = lax.axis_size(PIECES)
    pairs = [(i, i + 1) for i in range(1, devices - 1, 2)]
    pairs += [(j, i) for i, j in pairs]
    return [lax.ppermute(shard, PIECES, pairs), swapped(shard if later is None else later, "rep")]


def swapped(shard, axis):
    return lax.ppermute(shard, axis, [(0, 1), (1, 0)])


def call(kernel, out_shape, in_specs, scratch, out_specs=None, limit=VMEM_LIMIT):
    options = {} if out_specs is None else {"out_specs": out_specs}
    return pl.pallas_call(
        kernel,
        out_shape=out_shape,
        in_specs=in_specs,
        scratch_shapes=scratch,
        compiler_params=pltpu.CompilerParams(vmem_limit_bytes=limit),
        cost_estimate=pl.CostEstimate(flops=0, bytes_accessed=0, transcendentals=0),
        **options,
    )


def anywhere(count):
    return [pl.BlockSpec(memory_space=pl.ANY)] * count


def vmem(count):
    return [pl.BlockSpec(memory_space=pltpu.VMEM)] * count


SMEM = [pl.BlockSpec(memory_space=pltpu.SMEM)]


def down_kernel(children_ref, mask_ref, weight_ref, coarse_ref, slope_ref):
    octants = children_ref.shape[0]
    total = None
    for o in range(0, octants, 2):
        masked = jnp.concatenate(
            [
                children_ref[o + j] * mask_ref[o + j : o + j + 1, :].astype(F32).astype(BF16)
                for j in range(2)
            ],
            axis=0,
        )
        weights = jnp.concatenate([weight_ref[o], weight_ref[o + 1]], axis=1)
        term = jnp.dot(weights, masked, preferred_element_type=F32)
        total = term if total is None else total + term
    slope_ref[...] = silu_slope(total)
    coarse_ref[...] = (total * jax.nn.sigmoid(total)).T.astype(BF16)


def index_kernel(shards, neighbours_ref, index_ref, scalars_ref):
    offsets, rows = neighbours_ref.shape
    blocks = rows // BLOCK
    curve, rep = lax.axis_index("curve"), lax.axis_index("rep")
    names = neighbours_ref[...]
    local = jnp.where(names >= 0, names - (curve * 2 + rep - 1) * rows, NOWHERE)
    index_ref[...] = jnp.full(index_ref.shape, NOWHERE, jnp.int32)
    for group in range(GROUPS):
        part = local[group * PER : (group + 1) * PER]
        index_ref[group, :PER, :] = part
        lows = jnp.min(jnp.where(part < 0, -NOWHERE, part), axis=0, keepdims=True)
        highs = jnp.max(part, axis=0, keepdims=True)
        for block in range(blocks):
            at = slice(block * BLOCK, (block + 1) * BLOCK)
            low, high = jnp.min(lows[:, at]), jnp.max(highs[:, at]) + 1
            low = jnp.where(high <= 0, 0, low // 16 * 16)
            steps = jnp.maximum(1, (high - low + SPAN - 1) // SPAN)
            scalars_ref[group * blocks + block] = low
            scalars_ref[(GROUPS + group) * blocks + block] = steps
    last = 2 * GROUPS * blocks
    scalars_ref[last] = lax.axis_index("chan")
    scalars_ref[last + 1] = curve if shards > 1 else 0
    scalars_ref[last + 2] = rep


def fill_window(window_ref, parts, slots, rep):
    rows = parts[0][0].shape[0]
    places = (rows, rep * 2 * rows, (1 - rep) * 2 * rows)
    for part, slot in zip(parts, slots):
        for source, place in zip(part, places):
            window_ref[slot, pl.ds(pl.multiple_of(place, 16), rows), :] = source[...]
    blank = (window_ref.shape[0], window_ref.shape[1] - 3 * rows, window_ref.shape[2])
    window_ref[:, 3 * rows :, :] = jnp.zeros(blank, BF16)


def gather(scalars_ref, column_ref, window_ref, blocks, store, add):
    lanes = lax.broadcasted_iota(jnp.int32, (BLOCK, SPAN), 1).astype(F32).astype(BF16)

    def picked(group, rows, start):
        columns = jnp.clip(column_ref[group, rows, :] - start, -1, SPAN).astype(F32).astype(BF16)
        hot = [
            jnp.where(
                jnp.broadcast_to(columns[:, j : j + 1], (BLOCK, SPAN)) == lanes,
                jnp.ones((), BF16),
                jnp.zeros((), BF16),
            )
            for j in range(PER)
        ]
        at = pl.ds(pl.multiple_of(start, 16), SPAN)
        span = jnp.concatenate([window_ref[c, at, :] for c in range(window_ref.shape[0])], axis=1)
        return jnp.dot(jnp.concatenate(hot, axis=0), span, preferred_element_type=F32).astype(BF16)

    def first(block, _):
        rows = pl.ds(pl.multiple_of(block * BLOCK, BLOCK), BLOCK)
        for group in range(GROUPS):
            result = picked(group, rows, scalars_ref[group * blocks + block])
            for j in range(PER):
                store(group, j, rows, result[j * BLOCK : (j + 1) * BLOCK])
        return 0

    lax.fori_loop(0, blocks, first, 0, unroll=True)

    def rest(at, _):
        group, block = at // blocks, at % blocks
        rows = pl.ds(pl.multiple_of(block * BLOCK, BLOCK), BLOCK)

        def more(step, _):
            result = picked(group, rows, scalars_ref[at] + step * SPAN)
            for j in range(PER):
                add(group, j, rows, result[j * BLOCK : (j + 1) * BLOCK])
            return 0

        lax.fori_loop(1, scalars_ref[GROUPS * blocks + at], more, 0)
        return 0

    lax.fori_loop(0, GROUPS * blocks, rest, 0)


def turn(scratch_ref, value, shards, scalars_ref, at):
    half = value.shape[0] // 2
    size = half // shards
    scratch_ref[0] = value
    place = 0 if shards == 1 else scalars_ref[at + 1]
    rep = scalars_ref[at + 2]
    for core in range(2):
        for step in range(shards):
            source = (rep + core) % 2 * half + (place ^ step) * size
            target = core * half + step * size
            scratch_ref[1, target : target + size] = scratch_ref[
                0, pl.ds(pl.multiple_of(source, size), size)
            ]


def conv_kernel(chans, shards, scale, scalars_ref, index_ref, weight_ref, cotangent_ref, *refs):
    parts, refs = [refs[3 * i : 3 * i + 3] for i in range(chans)], refs[3 * chans :]
    out_ref, grad_ref, keep_ref, send_ref = refs[:4]
    window_ref, column_ref, picked_ref, conv_ref, scratch_ref = refs[4:]
    rows = index_ref.shape[2]
    blocks = rows // BLOCK
    width = chans * window_ref.shape[2]
    channels = weight_ref.shape[1]
    chan = scalars_ref[2 * GROUPS * blocks]
    rep = scalars_ref[2 * GROUPS * blocks + 2]
    slots = (chan, 1 - chan) if chans == 2 else range(chans)
    fill_window(window_ref, parts, slots, rep)
    for group in range(GROUPS):
        column_ref[group] = index_ref[group].T

    def store(group, j, at, value):
        lane = j % 3 * width
        picked_ref[group * 3 + j // 3, at, lane : lane + width] = value

    def add(group, j, at, value):
        lane = j % 3 * width
        picked_ref[group * 3 + j // 3, at, lane : lane + width] += value

    gather(scalars_ref, column_ref, window_ref, blocks, store, add)

    def multiply(three, _):
        weights = jnp.concatenate([weight_ref[three * 3 + j] for j in range(3)], axis=1)
        term = lax.dot_general(picked_ref[three], weights, NT, preferred_element_type=F32)
        conv_ref[...] += term
        return 0

    conv_ref[...] = jnp.zeros_like(conv_ref)
    lax.fori_loop(0, 9, multiply, 0, unroll=3)
    conv = conv_ref[...].T
    sigma = jax.nn.sigmoid(conv)
    out_ref[...] = (conv * sigma).astype(BF16)
    grad = cotangent_ref[...].astype(F32) * (sigma * (1.0 + conv * (1.0 - sigma)))
    grad_ref[...] = grad.T.astype(BF16)
    turn(scratch_ref, grad.astype(BF16), shards, scalars_ref, 2 * GROUPS * blocks)
    half = channels // 2
    size = half // shards

    def weigh(three, _):
        term = jnp.dot(scratch_ref[1], picked_ref[three], preferred_element_type=F32) * scale
        for j in range(3):
            both = term[:, j * width : (j + 1) * width].astype(BF16)
            for step in range(shards):
                at = step * size
                keep_ref[step, three * 3 + j] = both[at : at + size]
                send_ref[step, three * 3 + j] = both[half + at : half + at + size]
        return 0

    lax.fori_loop(0, 9, weigh, 0, unroll=3)


def coarse_grad_kernel(scalars_ref, index_ref, weight_ref, *refs):
    part, refs = refs[:3], refs[3:]
    mine_ref, other_ref, window_ref, column_ref, picked_ref, total_ref = refs
    rows = index_ref.shape[2]
    blocks = rows // BLOCK
    offsets, channels, width = weight_ref.shape
    chan = scalars_ref[2 * GROUPS * blocks]
    rep = scalars_ref[2 * GROUPS * blocks + 2]
    fill_window(window_ref, [part], (0,), rep)
    for group in range(GROUPS):
        column_ref[group] = index_ref[group].T

    def store(group, j, at, value):
        lane = (PER - 1 - j) * channels
        picked_ref[GROUPS - 1 - group, at, lane : lane + channels] = value

    def add(group, j, at, value):
        lane = (PER - 1 - j) * channels
        picked_ref[GROUPS - 1 - group, at, lane : lane + channels] += value

    gather(scalars_ref, column_ref, window_ref, blocks, store, add)
    result = None
    for group in range(GROUPS):
        weights = weight_ref[group * PER : (group + 1) * PER].reshape(PER * channels, width)
        term = jnp.dot(picked_ref[group], weights, preferred_element_type=F32)
        result = term if result is None else result + term
    result = result.T
    chans = width // channels
    for at in range(chans):
        total_ref[at] = result[at * channels : (at + 1) * channels]
    mine_ref[...] = total_ref[chan]
    for step in range(1, chans):
        other_ref[step - 1] = total_ref[lax.rem(chan + step, chans)].astype(BF16)


def pre_grad_kernel(scale, scalars_ref, children_ref, mask_ref, slope_ref, mine_ref, *refs):
    others, (grad_ref, keep_ref, send_ref, scratch_ref) = refs[:-4], refs[-4:]
    total = mine_ref[...]
    for other in others:
        total = total + other[...].astype(F32)
    grad = (total * slope_ref[...]).astype(BF16)
    grad_ref[...] = grad
    blocks = grad.shape[1] // BLOCK
    turn(scratch_ref, grad, 1, scalars_ref, 2 * GROUPS * blocks)
    half = grad.shape[0] // 2
    fine = children_ref.shape[1]
    for o in range(0, children_ref.shape[0], 2):
        masked = jnp.concatenate(
            [
                children_ref[o + j] * mask_ref[o + j : o + j + 1, :].astype(F32).astype(BF16)
                for j in range(2)
            ],
            axis=0,
        )
        term = lax.dot_general(scratch_ref[1], masked, NT, preferred_element_type=F32) * scale
        both = term.astype(BF16)
        for j in range(2):
            keep_ref[o + j] = both[:half, j * fine : (j + 1) * fine]
            send_ref[o + j] = both[half:, j * fine : (j + 1) * fine]


def cut_kernel(weight_ref, *refs):
    out_refs, scratch_ref = refs[:-1], refs[-1]
    octants, fine, _ = scratch_ref.shape
    chans = len(out_refs)
    size = fine // chans
    chan = lax.axis_index("chan")
    for o in range(octants):
        scratch_ref[o] = weight_ref[o].T
    for by in range(chans):
        at = pl.ds(pl.multiple_of((chan + by) % chans * size, size), size)
        for o in range(octants):
            out_refs[by][o] = scratch_ref[o, at, :]


def children_kernel(mask_ref, *refs):
    out_hbm, out_ref, sems = refs[-3:]
    count = (len(refs) - 3) // 2
    grads, weights = refs[:count], refs[count:-3]
    copies = []
    for o in range(out_ref.shape[0]):
        total = None
        for grad, weight in zip(grads, weights):
            term = jnp.dot(weight[o], grad[...], preferred_element_type=F32)
            term = term.astype(BF16).astype(F32)
            total = term if total is None else total + term
        out_ref[o] = (total * mask_ref[o : o + 1, :].astype(F32)).astype(BF16)
        copies.append(pltpu.make_async_copy(out_ref.at[o], out_hbm.at[o], sems.at[o]))
        copies[-1].start()
    for copy in copies:
        copy.wait()


def apart(shard, by):
    return lax.ppermute(shard, "curve", [(i, i ^ by) for i in range(lax.axis_size("curve"))])


def added(*terms):
    return sum(term.astype(F32) for term in terms).astype(BF16)


def after(value, *earlier):
    return lax.optimization_barrier((value, *earlier))[0]


def body(children, child_mask, neighbours, down_weight, conv_weight, cotangent):
    octants, fine, rows = children.shape
    offsets, channels, width = conv_weight.shape
    blocks = rows // BLOCK
    chans = lax.axis_size("chan")
    chan = lax.axis_index("chan")
    rep = lax.axis_index("rep")
    curve = lax.axis_index("curve")
    pieces = lax.axis_size(PIECES)
    scale = 1.0 / (rows * pieces) ** 0.5
    shape = jax.ShapeDtypeStruct
    half = channels // 2
    shards = 4 if lax.axis_size("curve") == 4 and half % 64 == 0 else 1
    size = half // shards

    coarse, slope = call(
        down_kernel,
        [shape((rows, channels), BF16), shape((channels, rows), F32)],
        vmem(3),
        [],
        limit=WHOLE_LIMIT,
    )(children, child_mask, down_weight)

    if chans == 2:
        parts = [coarse, swapped(coarse, "chan")]
    else:
        every = lax.all_gather(coarse, "chan", axis=0)
        parts = [every[i] for i in range(chans)]
    windows = [array for part in parts for array in [part] + met(part)]
    conv_weight = conv_weight * after(jnp.ones((), BF16), coarse)
    index, scalars = call(
        functools.partial(index_kernel, shards),
        [shape((GROUPS, 16, rows), jnp.int32), shape((2 * GROUPS * blocks + 3,), jnp.int32)],
        vmem(1),
        [],
        vmem(1) + SMEM,
    )(after(neighbours, parts[1]))

    features_out, conv_grad, keep, send = call(
        functools.partial(conv_kernel, chans, shards, scale),
        [
            shape((channels, rows), BF16),
            shape((rows, channels), BF16),
            shape((shards, offsets, size, width), BF16),
            shape((shards, offsets, size, width), BF16),
        ],
        SMEM + vmem(3 + 3 * chans),
        [
            pltpu.VMEM((chans, 3 * rows + SPAN, channels), BF16),
            pltpu.VMEM((GROUPS, rows, 16), jnp.int32),
            pltpu.VMEM((9, rows, 3 * width), BF16),
            pltpu.VMEM((rows, channels), F32),
            pltpu.VMEM((2, channels, rows), BF16),
        ],
    )(scalars, index, conv_weight, cotangent, *windows)

    received = swapped(send, "rep")
    near = met(conv_grad, after(conv_grad, received))
    total = [added(keep[i], received[i]) for i in range(shards)]
    terms = []
    if shards == 4:
        terms = [apart(after(total[by], near[1]), by) for by in (2, 3)]
        terms += [apart(total[1], 1)]

    mine, others = call(
        coarse_grad_kernel,
        [shape((channels, rows), F32), shape((chans - 1, channels, rows), BF16)],
        SMEM + vmem(5),
        [
            pltpu.VMEM((1, 3 * rows + SPAN, channels), BF16),
            pltpu.VMEM((GROUPS, rows, 16), jnp.int32),
            pltpu.VMEM((GROUPS, rows, PER * channels), BF16),
            pltpu.VMEM((chans, channels, rows), F32),
        ],
    )(after(scalars, *total), index, conv_weight, conv_grad, *near)
    received = [
        lax.ppermute(others[by - 1], "chan", [(i, (i + by) % chans) for i in range(chans)])
        for by in range(1, chans)
    ]
    mine_fine = fine // chans
    cut = call(
        cut_kernel,
        [shape((octants, mine_fine, channels), BF16)] * chans,
        vmem(1),
        [pltpu.VMEM((octants, fine, channels), BF16)],
    )(after(down_weight, mine))
    blank = [
        jnp.broadcast_to(after(jnp.zeros((), F32), mine), like.shape)
        for like in (conv_weight, down_weight)
    ]
    pre_grad, keep, send = call(
        functools.partial(pre_grad_kernel, scale),
        [
            shape((channels, rows), BF16),
            shape((octants, half, fine), BF16),
            shape((octants, half, fine), BF16),
        ],
        SMEM + vmem(4 + len(received)),
        [pltpu.VMEM((2, channels, rows), BF16)],
    )(after(scalars, *cut, *blank), children, child_mask, slope, mine, *received)

    if shards == 4:
        own = added(after(total[0], pre_grad), *terms)
    else:
        own = lax.psum(total[0], "curve")
    sent_grad, send = after(pre_grad, own), after(send, own)
    grads = [
        lax.ppermute(sent_grad, "chan", [(i, (i + by) % chans) for i in range(chans)])
        if by
        else pre_grad
        for by in range(chans)
    ]
    down = core_sum = added(keep, swapped(send, "rep"))
    sums = [own]
    if shards == 4:
        sums = [own] + [apart(own, by) for by in range(1, 4)]
    if shards == 4:
        down = added(down, apart(down, 1))
    else:
        down = lax.psum(down, "curve")
    weights = [
        lax.ppermute(after(cut[by], own), "chan", [(i, (i + by) % chans) for i in range(chans)])
        if by
        else cut[by]
        for by in range(chans)
    ]
    children_grad = call(
        children_kernel,
        shape((octants, mine_fine, rows), BF16),
        vmem(1 + 2 * chans),
        [pltpu.VMEM((octants, mine_fine, rows), BF16), pltpu.SemaphoreType.DMA((octants,))],
        anywhere(1)[0],
    )(after(child_mask, down), *grads, *weights)
    if shards == 4:
        down = added(after(down, children_grad), apart(down, 2))

    def joined(result, pieces):
        for row, piece in pieces:
            result = lax.dynamic_update_slice(result, piece.astype(F32), (0, row, 0))
        return result

    rows_of = [rep * half, (1 - rep) * half]
    down_weight_grad = joined(blank[1], zip(rows_of, (down, swapped(down, "rep"))))
    pieces = []
    for step, part in enumerate(sums):
        at = (curve ^ step) * size if shards > 1 else 0
        mine = part if step else after(part, core_sum)
        pieces += [(rows_of[0] + at, mine), (rows_of[1] + at, swapped(part, "rep"))]
    conv_weight_grad = joined(blank[0], pieces)
    return (features_out, children_grad, conv_weight_grad, down_weight_grad)


def solution(mesh):
    in_specs = (
        P(None, None, ("snap", "curve", "rep")),
        P(None, ("snap", "curve", "rep")),
        P(None, ("snap", "curve", "rep")),
        P(None, "chan", None),
        P(None, "chan", None),
        P("chan", ("snap", "curve", "rep")),
    )
    out_specs = (
        P("chan", ("snap", "curve", "rep")),
        P(None, "chan", ("snap", "curve", "rep")),
        P("snap", "chan", None),
        P("snap", "chan", None),
    )
    return jax.shard_map(body, mesh=mesh, in_specs=in_specs, out_specs=out_specs, check_vma=False)
```

```python
import functools

import jax
import jax.numpy as jnp
from jax import lax
from jax.experimental import pallas as pl
from jax.experimental.pallas import tpu as pltpu
from jax.sharding import PartitionSpec as P

BLOCK = 128
SPAN = 256
GROUPS = 3
PER = 9
VMEM_LIMIT = 28 * 1024 * 1024
WHOLE_LIMIT = 60 * 1024 * 1024
PIECES = ("curve", "rep")
F32 = jnp.float32
BF16 = jnp.bfloat16
NOWHERE = -(2**20)
SHIFT = 2**16
NT = (((1,), (1,)), ((), ()))


def silu_slope(value):
    sigma = jax.nn.sigmoid(value)
    return sigma * (1.0 + value * (1.0 - sigma))


def met(shard):
    devices = lax.axis_size(PIECES)
    pairs = [(i, i + 1) for i in range(1, devices - 1, 2)]
    pairs += [(j, i) for i, j in pairs]
    return [lax.ppermute(shard, PIECES, pairs), swapped(shard, "rep")]


def swapped(shard, axis):
    return lax.ppermute(shard, axis, [(0, 1), (1, 0)])


def call(kernel, out_shape, in_specs, scratch, out_specs=None, limit=VMEM_LIMIT):
    options = {} if out_specs is None else {"out_specs": out_specs}
    return pl.pallas_call(
        kernel,
        out_shape=out_shape,
        in_specs=in_specs,
        scratch_shapes=scratch,
        compiler_params=pltpu.CompilerParams(vmem_limit_bytes=limit),
        cost_estimate=pl.CostEstimate(flops=0, bytes_accessed=0, transcendentals=0),
        **options,
    )


def anywhere(count):
    return [pl.BlockSpec(memory_space=pl.ANY)] * count


def vmem(count):
    return [pl.BlockSpec(memory_space=pltpu.VMEM)] * count


SMEM = [pl.BlockSpec(memory_space=pltpu.SMEM)]


def down_kernel(children_ref, mask_ref, weight_ref, coarse_ref, slope_ref):
    octants = children_ref.shape[0]
    total = None
    for o in range(0, octants, 2):
        masked = jnp.concatenate(
            [
                children_ref[o + j] * mask_ref[o + j : o + j + 1, :].astype(F32).astype(BF16)
                for j in range(2)
            ],
            axis=0,
        )
        weights = jnp.concatenate([weight_ref[o], weight_ref[o + 1]], axis=1)
        term = jnp.dot(weights, masked, preferred_element_type=F32)
        total = term if total is None else total + term
    slope_ref[...] = silu_slope(total)
    coarse_ref[...] = (total * jax.nn.sigmoid(total)).T.astype(BF16)


def index_kernel(shards, neighbours_ref, index_ref, scalars_ref):
    offsets, rows = neighbours_ref.shape
    blocks = rows // BLOCK
    curve, rep = lax.axis_index("curve"), lax.axis_index("rep")
    names = neighbours_ref[...]
    local = jnp.where(names >= 0, names - (curve * 2 + rep - 1) * rows, NOWHERE)
    last = 2 * GROUPS * blocks
    found = 0
    for group in range(GROUPS):
        part = local[group * PER : (group + 1) * PER]
        index_ref[group] = jnp.concatenate(
            [part, jnp.full((16 - PER, rows), NOWHERE, jnp.int32)], axis=0
        ).T
        lows = jnp.min(jnp.where(part < 0, -NOWHERE, part), axis=0, keepdims=True)
        highs = jnp.max(part, axis=0, keepdims=True)
        for block in range(blocks):
            at = slice(block * BLOCK, (block + 1) * BLOCK)
            low, high = jnp.min(lows[:, at]), jnp.max(highs[:, at]) + 1
            low = jnp.where(high <= 0, 0, low // 16 * 16)
            steps = jnp.maximum(1, (high - low + SPAN - 1) // SPAN)
            scalars_ref[group * blocks + block] = low

            def note(step, found, at=group * blocks + block, low=low):
                scalars_ref[last + 3 + found] = at * SHIFT + low + step * SPAN
                return found + 1

            found = lax.fori_loop(1, steps, note, found)
    scalars_ref[GROUPS * blocks] = found
    scalars_ref[last] = lax.axis_index("chan")
    scalars_ref[last + 1] = curve if shards > 1 else 0
    scalars_ref[last + 2] = rep


def fill_window(window_ref, parts, slots, rep):
    rows = parts[0][0].shape[0]
    places = (rows, rep * 2 * rows, (1 - rep) * 2 * rows)
    for part, slot in zip(parts, slots):
        for source, place in zip(part, places):
            window_ref[slot, pl.ds(pl.multiple_of(place, 16), rows), :] = source[...]
    blank = (window_ref.shape[0], window_ref.shape[1] - 3 * rows, window_ref.shape[2])
    window_ref[:, 3 * rows :, :] = jnp.zeros(blank, BF16)


def gather(scalars_ref, column_ref, window_ref, blocks, store, add):
    lanes = lax.broadcasted_iota(jnp.int32, (BLOCK, SPAN), 1).astype(F32).astype(BF16)

    def picked(group, rows, start):
        columns = jnp.clip(column_ref[group, rows, :] - start, -1, SPAN).astype(F32).astype(BF16)
        hot = [
            jnp.where(
                jnp.broadcast_to(columns[:, j : j + 1], (BLOCK, SPAN)) == lanes,
                jnp.ones((), BF16),
                jnp.zeros((), BF16),
            )
            for j in range(PER)
        ]
        at = pl.ds(pl.multiple_of(start, 16), SPAN)
        span = jnp.concatenate([window_ref[c, at, :] for c in range(window_ref.shape[0])], axis=1)
        return jnp.dot(jnp.concatenate(hot, axis=0), span, preferred_element_type=F32).astype(BF16)

    def first(block, _):
        rows = pl.ds(pl.multiple_of(block * BLOCK, BLOCK), BLOCK)
        for group in range(GROUPS):
            result = picked(group, rows, scalars_ref[group * blocks + block])
            for j in range(PER):
                store(group, j, rows, result[j * BLOCK : (j + 1) * BLOCK])
        return 0

    lax.fori_loop(0, blocks, first, 0, unroll=True)

    def rest(entry, _):
        noted = scalars_ref[2 * GROUPS * blocks + 3 + entry]
        at, start = noted // SHIFT, noted % SHIFT
        group, block = at // blocks, at % blocks
        rows = pl.ds(pl.multiple_of(block * BLOCK, BLOCK), BLOCK)
        result = picked(group, rows, start)
        for j in range(PER):
            add(group, j, rows, result[j * BLOCK : (j + 1) * BLOCK])
        return 0

    lax.fori_loop(0, scalars_ref[GROUPS * blocks], rest, 0)


def turn(scratch_ref, value, shards, scalars_ref, at):
    half = value.shape[0] // 2
    size = half // shards
    scratch_ref[0] = value
    place = 0 if shards == 1 else scalars_ref[at + 1]
    rep = scalars_ref[at + 2]
    for core in range(2):
        for step in range(shards):
            source = (rep + core) % 2 * half + (place ^ step) * size
            target = core * half + step * size
            scratch_ref[1, target : target + size] = scratch_ref[
                0, pl.ds(pl.multiple_of(source, size), size)
            ]


def conv_kernel(chans, shards, scale, scalars_ref, index_ref, weight_ref, cotangent_ref, *refs):
    parts, refs = [refs[3 * i : 3 * i + 3] for i in range(chans)], refs[3 * chans :]
    out_ref, grad_ref, keep_ref, send_ref = refs[:4]
    window_ref, picked_ref, conv_ref, scratch_ref = refs[4:]
    rows = index_ref.shape[1]
    blocks = rows // BLOCK
    width = chans * window_ref.shape[2]
    channels = weight_ref.shape[1]
    chan = scalars_ref[2 * GROUPS * blocks]
    rep = scalars_ref[2 * GROUPS * blocks + 2]
    slots = (chan, 1 - chan) if chans == 2 else range(chans)
    fill_window(window_ref, parts, slots, rep)

    def store(group, j, at, value):
        lane = j % 3 * width
        picked_ref[group * 3 + j // 3, at, lane : lane + width] = value

    def add(group, j, at, value):
        lane = j % 3 * width
        picked_ref[group * 3 + j // 3, at, lane : lane + width] += value

    gather(scalars_ref, index_ref, window_ref, blocks, store, add)

    def multiply(three, _):
        weights = jnp.concatenate([weight_ref[three * 3 + j] for j in range(3)], axis=1)
        term = lax.dot_general(picked_ref[three], weights, NT, preferred_element_type=F32)
        conv_ref[...] += term
        return 0

    conv_ref[...] = jnp.zeros_like(conv_ref)
    lax.fori_loop(0, 9, multiply, 0, unroll=3)
    conv = conv_ref[...].T
    sigma = jax.nn.sigmoid(conv)
    out_ref[...] = (conv * sigma).astype(BF16)
    grad = cotangent_ref[...].astype(F32) * (sigma * (1.0 + conv * (1.0 - sigma)))
    grad_ref[...] = grad.T.astype(BF16)
    turn(scratch_ref, grad.astype(BF16), shards, scalars_ref, 2 * GROUPS * blocks)
    half = channels // 2
    size = half // shards

    def weigh(three, _):
        term = jnp.dot(scratch_ref[1], picked_ref[three], preferred_element_type=F32) * scale
        for j in range(3):
            both = term[:, j * width : (j + 1) * width].astype(BF16)
            for step in range(shards):
                at = step * size
                keep_ref[step, three * 3 + j] = both[at : at + size]
                send_ref[step, three * 3 + j] = both[half + at : half + at + size]
        return 0

    lax.fori_loop(0, 9, weigh, 0, unroll=3)


def coarse_grad_kernel(scalars_ref, index_ref, weight_ref, *refs):
    part, refs = refs[:3], refs[3:]
    mine_ref, other_ref, window_ref, picked_ref, total_ref = refs
    rows = index_ref.shape[1]
    blocks = rows // BLOCK
    offsets, channels, width = weight_ref.shape
    chan = scalars_ref[2 * GROUPS * blocks]
    rep = scalars_ref[2 * GROUPS * blocks + 2]
    fill_window(window_ref, [part], (0,), rep)

    def store(group, j, at, value):
        lane = (PER - 1 - j) * channels
        picked_ref[GROUPS - 1 - group, at, lane : lane + channels] = value

    def add(group, j, at, value):
        lane = (PER - 1 - j) * channels
        picked_ref[GROUPS - 1 - group, at, lane : lane + channels] += value

    gather(scalars_ref, index_ref, window_ref, blocks, store, add)
    result = None
    for group in range(GROUPS):
        weights = weight_ref[group * PER : (group + 1) * PER].reshape(PER * channels, width)
        term = jnp.dot(picked_ref[group], weights, preferred_element_type=F32)
        result = term if result is None else result + term
    result = result.T
    chans = width // channels
    for at in range(chans):
        total_ref[at] = result[at * channels : (at + 1) * channels]
    mine_ref[...] = total_ref[chan]
    for step in range(1, chans):
        other_ref[step - 1] = total_ref[lax.rem(chan + step, chans)].astype(BF16)


def pre_grad_kernel(scale, scalars_ref, children_ref, mask_ref, slope_ref, mine_ref, *refs):
    others, (grad_ref, keep_ref, send_ref, scratch_ref) = refs[:-4], refs[-4:]
    total = mine_ref[...]
    for other in others:
        total = total + other[...].astype(F32)
    grad = (total * slope_ref[...]).astype(BF16)
    grad_ref[...] = grad
    blocks = grad.shape[1] // BLOCK
    turn(scratch_ref, grad, 1, scalars_ref, 2 * GROUPS * blocks)
    half = grad.shape[0] // 2
    fine = children_ref.shape[1]
    for o in range(0, children_ref.shape[0], 2):
        masked = jnp.concatenate(
            [
                children_ref[o + j] * mask_ref[o + j : o + j + 1, :].astype(F32).astype(BF16)
                for j in range(2)
            ],
            axis=0,
        )
        term = lax.dot_general(scratch_ref[1], masked, NT, preferred_element_type=F32) * scale
        both = term.astype(BF16)
        for j in range(2):
            keep_ref[o + j] = both[:half, j * fine : (j + 1) * fine]
            send_ref[o + j] = both[half:, j * fine : (j + 1) * fine]


def cut_kernel(weight_ref, *refs):
    out_refs, scratch_ref = refs[:-1], refs[-1]
    octants, fine, _ = scratch_ref.shape
    chans = len(out_refs)
    size = fine // chans
    chan = lax.axis_index("chan")
    for o in range(octants):
        scratch_ref[o] = weight_ref[o].T
    for by in range(chans):
        at = pl.ds(pl.multiple_of((chan + by) % chans * size, size), size)
        for o in range(octants):
            out_refs[by][o] = scratch_ref[o, at, :]


def children_kernel(mask_ref, *refs):
    out_hbm, out_ref, sems = refs[-3:]
    count = (len(refs) - 3) // 2
    grads, weights = refs[:count], refs[count:-3]
    copies = []
    for o in range(out_ref.shape[0]):
        total = None
        for grad, weight in zip(grads, weights):
            term = jnp.dot(weight[o], grad[...], preferred_element_type=F32)
            term = term.astype(BF16).astype(F32)
            total = term if total is None else total + term
        out_ref[o] = (total * mask_ref[o : o + 1, :].astype(F32)).astype(BF16)
        copies.append(pltpu.make_async_copy(out_ref.at[o], out_hbm.at[o], sems.at[o]))
        copies[-1].start()
    for copy in copies:
        copy.wait()


def apart(shard, by):
    return lax.ppermute(shard, "curve", [(i, i ^ by) for i in range(lax.axis_size("curve"))])


def added(*terms):
    return sum(term.astype(F32) for term in terms).astype(BF16)


def after(value, *earlier):
    return lax.optimization_barrier((value, *earlier))[0]


def body(children, child_mask, neighbours, down_weight, conv_weight, cotangent):
    octants, fine, rows = children.shape
    offsets, channels, width = conv_weight.shape
    blocks = rows // BLOCK
    chans = lax.axis_size("chan")
    chan = lax.axis_index("chan")
    rep = lax.axis_index("rep")
    curve = lax.axis_index("curve")
    pieces = lax.axis_size(PIECES)
    scale = 1.0 / (rows * pieces) ** 0.5
    shape = jax.ShapeDtypeStruct
    half = channels // 2
    shards = 4 if lax.axis_size("curve") == 4 and half % 64 == 0 else 1
    size = half // shards

    coarse, slope = call(
        down_kernel,
        [shape((rows, channels), BF16), shape((channels, rows), F32)],
        vmem(3),
        [],
        limit=WHOLE_LIMIT,
    )(children, child_mask, down_weight)

    if chans == 2:
        parts = [coarse, swapped(coarse, "chan")]
    else:
        every = lax.all_gather(coarse, "chan", axis=0)
        parts = [every[i] for i in range(chans)]
    windows = [array for part in parts for array in [part] + met(part)]
    conv_weight = conv_weight * after(jnp.ones((), BF16), coarse)
    listed = GROUPS * blocks * (3 * rows // SPAN)
    index, scalars = call(
        functools.partial(index_kernel, shards),
        [shape((GROUPS, rows, 16), jnp.int32), shape((2 * GROUPS * blocks + 3 + listed,), jnp.int32)],
        vmem(1),
        [],
        vmem(1) + SMEM,
    )(after(neighbours, parts[1]))

    features_out, conv_grad, keep, send = call(
        functools.partial(conv_kernel, chans, shards, scale),
        [
            shape((channels, rows), BF16),
            shape((rows, channels), BF16),
            shape((shards, offsets, size, width), BF16),
            shape((shards, offsets, size, width), BF16),
        ],
        SMEM + vmem(3 + 3 * chans),
        [
            pltpu.VMEM((chans, 3 * rows + SPAN, channels), BF16),
            pltpu.VMEM((9, rows, 3 * width), BF16),
            pltpu.VMEM((rows, channels), F32),
            pltpu.VMEM((2, channels, rows), BF16),
        ],
    )(scalars, index, conv_weight, cotangent, *windows)

    near = met(conv_grad)
    received = swapped(send, "rep")
    total = [added(keep[i], received[i]) for i in range(shards)]
    terms = []
    if shards == 4:
        terms = [apart(after(total[by], near[1]), by) for by in (2, 3)]
        terms += [apart(total[1], 1)]

    mine, others = call(
        coarse_grad_kernel,
        [shape((channels, rows), F32), shape((chans - 1, channels, rows), BF16)],
        SMEM + vmem(5),
        [
            pltpu.VMEM((1, 3 * rows + SPAN, channels), BF16),
            pltpu.VMEM((GROUPS, rows, PER * channels), BF16),
            pltpu.VMEM((chans, channels, rows), F32),
        ],
    )(after(scalars, *total), index, conv_weight, conv_grad, *near)
    received = [
        lax.ppermute(others[by - 1], "chan", [(i, (i + by) % chans) for i in range(chans)])
        for by in range(1, chans)
    ]
    mine_fine = fine // chans
    cut = call(
        cut_kernel,
        [shape((octants, mine_fine, channels), BF16)] * chans,
        vmem(1),
        [pltpu.VMEM((octants, fine, channels), BF16)],
    )(after(down_weight, mine))
    blank = [
        jnp.broadcast_to(after(jnp.zeros((), F32), mine), like.shape)
        for like in (conv_weight, down_weight)
    ]
    pre_grad, keep, send = call(
        functools.partial(pre_grad_kernel, scale),
        [
            shape((channels, rows), BF16),
            shape((octants, half, fine), BF16),
            shape((octants, half, fine), BF16),
        ],
        SMEM + vmem(4 + len(received)),
        [pltpu.VMEM((2, channels, rows), BF16)],
    )(after(scalars, *cut, *blank), children, child_mask, slope, mine, *received)

    if shards == 4:
        own = added(after(total[0], pre_grad), *terms)
    else:
        own = lax.psum(total[0], "curve")
    sent_grad, send = after(pre_grad, own), after(send, own)
    grads = [
        lax.ppermute(sent_grad, "chan", [(i, (i + by) % chans) for i in range(chans)])
        if by
        else pre_grad
        for by in range(chans)
    ]
    down = core_sum = added(keep, swapped(send, "rep"))
    sums = [own]
    if shards == 4:
        across = apart(own, 2)
        sums = [own, apart(own, 1), across, apart(across, 1)]
    if shards == 4:
        down = added(down, apart(down, 1))
    else:
        down = lax.psum(down, "curve")
    weights = [
        lax.ppermute(after(cut[by], own), "chan", [(i, (i + by) % chans) for i in range(chans)])
        if by
        else cut[by]
        for by in range(chans)
    ]
    children_grad = call(
        children_kernel,
        shape((octants, mine_fine, rows), BF16),
        vmem(1 + 2 * chans),
        [pltpu.VMEM((octants, mine_fine, rows), BF16), pltpu.SemaphoreType.DMA((octants,))],
        anywhere(1)[0],
    )(after(child_mask, down), *grads, *weights)
    if shards == 4:
        down = added(after(down, children_grad), apart(after(down, sums[2]), 2))

    def joined(result, pieces):
        for row, piece in pieces:
            result = lax.dynamic_update_slice(result, piece.astype(F32), (0, row, 0))
        return result

    rows_of = [rep * half, (1 - rep) * half]
    down_weight_grad = joined(blank[1], zip(rows_of, (down, swapped(down, "rep"))))
    pieces = []
    for step, part in enumerate(sums):
        at = (curve ^ step) * size if shards > 1 else 0
        mine = part if step else after(part, core_sum)
        pieces += [(rows_of[0] + at, mine), (rows_of[1] + at, swapped(part, "rep"))]
    conv_weight_grad = joined(blank[0], pieces)
    return (features_out, children_grad, conv_weight_grad, down_weight_grad)


def solution(mesh):
    in_specs = (
        P(None, None, ("snap", "curve", "rep")),
        P(None, ("snap", "curve", "rep")),
        P(None, ("snap", "curve", "rep")),
        P(None, "chan", None),
        P(None, "chan", None),
        P("chan", ("snap", "curve", "rep")),
    )
    out_specs = (
        P("chan", ("snap", "curve", "rep")),
        P(None, "chan", ("snap", "curve", "rep")),
        P("snap", "chan", None),
        P("snap", "chan", None),
    )
    return jax.shard_map(body, mesh=mesh, in_specs=in_specs, out_specs=out_specs, check_vma=False)
```
